32 devices in a mesh: groups: 2 (over y), shard: 8 (over z, x), sub: 2 (over core).
Axes of the slice: x: 2, y: 2, z: 4, core: 2. Of those that a mesh axis runs over, the one named last changes fastest.
Arguments:
- queries: bfloat16 [32, 32, 128], P(('groups', 'shard', 'sub')), parts along dimension 0, may hold values from -6 to 6
- candidates: int32 [32, 62], P(('groups', 'shard', 'sub')), parts along dimension 0, may hold values from 0 to 1023, as said below
- token_codes: int32 [2048, 128], P(('groups', 'shard', 'sub')), parts along dimension 0, may hold values from 0 to 16383
- residuals: bfloat16 [2048, 128, 128], P(('groups', 'shard', 'sub')), parts along dimension 0, may hold values from -0.3984375 to 0.3984375
- lengths: int32 [2048], P(('groups', 'shard', 'sub')), parts along dimension 0, may hold values from 9 to 128
- centroids: bfloat16 [262144, 128], P(('groups', 'shard', 'sub')), parts along dimension 0, may hold values from -0.5 to 0.5
Outputs:
- scores: float32 [32, 62], P(('groups', 'shard', 'sub')), parts along dimension 0
The draws below stay inside these ranges and needn't reach their ends.
There are 2 independent parts, one for each index of `groups`. The reference program is written for one: setup_inputs(seed, part) draws one part's arguments, and reference() takes and returns one part's arrays. A program takes and returns all parts, laid end to end along the dimension named above; each array names one. Nothing has to cross between parts.
Inputs may be any that keep to these rules, and one draw needn't show every extreme that they name: `candidates`: each row names 62 different passages, at most 4 of them among one device's passages (passage p lies on the device of index p // 64 along shard+sub). So the rows of one device name at most 4 passages of one device and 8 of one shard; in every draw both devices of one shard receive exactly these numbers from the rows of every device.
All inputs are finite; a program needn't handle non-finite values.
Results may differ from the reference program's by a relative error of at most 0.00033.
Values may be sent and summed in bfloat16 or wider, within the bound.
No kernel may reach another device: no remote copies, remote signals or barrier semaphores. Data moves between devices by JAX's collectives and lax.ppermute only.
A program may use at most 64 MiB of HBM per device.

```python
import jax
import jax.numpy as jnp
from jax import lax

D = 128
QT = 32
LMAX = 128
CENT = 16384
PASS_DEV = 64
QUERY_DEVICE_MAX = 4
NCAND = 62
NQ = 16
PASSAGES = 1024
CENT_ALL = 131072
N_SHARD = 8


def draw_candidates(key, part):
    key = jax.random.fold_in(key, 11)
    keys = jax.random.split(key, 5)
    device_list = PASSAGES // PASS_DEV
    random_jitter = jax.random.randint(keys[0], (NQ, device_list, QUERY_DEVICE_MAX), 0, 4096)
    skew_level = jax.random.randint(keys[1], (device_list,), 0, 4) * 4096
    busiest_shard = jax.random.randint(keys[2], (), 0, device_list // 2)
    device_numbers = jnp.arange(device_list, dtype=jnp.int32)
    extra_reward = skew_level + jnp.where(device_numbers // 2 == busiest_shard, 32768, 0)
    slot_numbers = jnp.arange(device_list * QUERY_DEVICE_MAX, dtype=jnp.int32).reshape(device_list, QUERY_DEVICE_MAX)
    ranked_order = (random_jitter + extra_reward[None, :, None]) * (device_list * QUERY_DEVICE_MAX) + slot_numbers[None, :, :]
    _, picked = lax.top_k(ranked_order.reshape(NQ, device_list * QUERY_DEVICE_MAX), NCAND)
    device_of = picked // QUERY_DEVICE_MAX
    within = picked % QUERY_DEVICE_MAX
    offsets = jax.random.randint(keys[3], (NQ, device_list), 0, PASS_DEV)
    strides = jax.random.randint(keys[4], (NQ, device_list), 0, PASS_DEV // 2) * 2 + 1
    offset_of = jnp.take_along_axis(offsets, device_of, axis=1)
    stride_of = jnp.take_along_axis(strides, device_of, axis=1)
    local_ids = (offset_of + within * stride_of) % PASS_DEV
    return (device_of * PASS_DEV + local_ids).astype(jnp.int32)


def plant(drawn, own_key, smallest, high):
    place = [jax.random.randint(jax.random.fold_in(own_key, axis), (), 0, length) for axis, length in enumerate(drawn.shape)]
    main_axis = drawn.shape.index(max(drawn.shape))
    next_to = place[:main_axis] + [(place[main_axis] + 1) % drawn.shape[main_axis]] + place[main_axis + 1:]
    return drawn.at[tuple(place)].set(smallest).at[tuple(next_to)].set(high)


def levels(stream_key, extent, cuts, low, high):
    def one(axis_at, shards_of):
        draws = jax.random.uniform(jax.random.fold_in(jax.random.fold_in(stream_key, 6), axis_at), (shards_of,), jnp.float32, low / len(cuts), high / len(cuts))
        return jnp.repeat(jnp.exp(draws), extent[axis_at] // shards_of).reshape((-1,) + (1,) * (len(extent) - axis_at - 1))

    loudness = one(*cuts[0])
    for cut in cuts[1:]:
        loudness = loudness * one(*cut)
    return loudness


def centred(key, extent, scale, bound, cuts=(), held_as=jnp.bfloat16):
    result = scale * jax.random.normal(key, extent, jnp.float32)
    if cuts:
        result = result * levels(key, extent, cuts, -0.22, 0.18)
    return jnp.clip(result, -bound, bound).astype(held_as)


def setup_inputs(seed: int = 0, part: int = 0) -> dict:
    key_of = jax.random.split(jax.random.key(seed), 7)
    own_keys = jax.random.split(jax.random.fold_in(key_of[6], part), 7)
    queries = centred(own_keys[0], (NQ, QT, D), 1.0, 6.0, ((0, 16),))
    candidates = draw_candidates(jax.random.fold_in(jax.random.fold_in(key_of[6], part), 71), part)
    token_codes = plant(jax.random.randint(own_keys[2], (PASSAGES, LMAX), 0, CENT), jax.random.fold_in(own_keys[2], 1), 0, CENT - 1).astype(jnp.int32)
    residuals = centred(own_keys[3], (PASSAGES, LMAX, D), 0.06, 0.3984375, ((0, 16),))
    lengths = plant(jax.random.randint(own_keys[4], (PASSAGES,), LMAX // 16 + 1, LMAX + 1), jax.random.fold_in(own_keys[4], 1), LMAX // 16 + 1, LMAX).astype(jnp.int32)
    centroids = centred(own_keys[5], (CENT_ALL, D), D ** -0.5, 0.5, ((0, 16),))
    return {"queries": queries, "candidates": candidates, "token_codes": token_codes, "residuals": residuals, "lengths": lengths, "centroids": centroids}


def normalize_rows(vectors):
    total = lax.optimization_barrier(lax.optimization_barrier(jnp.sum(vectors * vectors, axis=-1, keepdims=True)))
    return (vectors * lax.rsqrt(total + 1e-06)).astype(jnp.bfloat16)

def reference(queries, candidates, token_codes, residuals, lengths, centroids):
    normed = normalize_rows(queries.astype(jnp.float32))
    per_shard = PASSAGES // N_SHARD

    def one_query(pieces):
        query_row, cand_ids = pieces
        shard_of = cand_ids // per_shard
        table_index = (shard_of[:, None] * CENT + token_codes[cand_ids]).astype(jnp.int32)
        vectors = centroids[table_index].astype(jnp.float32) + residuals[cand_ids].astype(jnp.float32)
        embedded = normalize_rows(vectors)
        similar = jnp.einsum('td,cjd->ctj', query_row.astype(jnp.float32), embedded.astype(jnp.float32), precision=lax.Precision.HIGHEST)
        usable = jnp.arange(LMAX)[None, :] < lengths[cand_ids][:, None]
        largest = lax.optimization_barrier(jnp.max(jnp.where(usable[:, None, :], similar, -jnp.inf), axis=2))
        return lax.optimization_barrier(jnp.sum(largest, axis=1))
    return lax.map(one_query, (normed, candidates))
```

```python
import functools

import jax
import jax.numpy as jnp
from jax import lax
from jax.experimental import pallas as pl
from jax.experimental.pallas import tpu as pltpu
from jax.sharding import PartitionSpec as P

CHUNK = 16
QUERY_BLOCK = 512


def normalized(vectors):
    total = jnp.sum(vectors * vectors, axis=-1, keepdims=True)
    return (vectors * lax.rsqrt(total + 1e-06)).astype(jnp.bfloat16)


def score_kernel(
    token_count,
    half_ref,
    codes_ref,
    lengths_ref,
    queries_ref,
    own_ref,
    other_ref,
    residuals_ref,
    out_ref,
    staged,
    table,
    residual_rows,
    rows,
    embedded,
    turned,
    largest,
    sems,
):
    passages, slots, width = residuals_ref.shape
    half_rows = own_ref.shape[0]
    half = half_ref[0]
    own_copy = pltpu.make_async_copy(own_ref, staged.at[0], sems.at[0])
    other_copy = pltpu.make_async_copy(other_ref, staged.at[1], sems.at[1])
    residual_copy = pltpu.make_async_copy(residuals_ref, residual_rows, sems.at[2])
    own_copy.start()
    other_copy.start()
    residual_copy.start()

    query_tokens = queries_ref.shape[0]
    block = min(QUERY_BLOCK, query_tokens)
    blocks = query_tokens // block

    def turn(b, carry):
        at = pl.ds(pl.multiple_of(b * block, block), block)
        vectors = normalized(queries_ref[at, :].astype(jnp.float32))
        turned[b] = vectors.astype(jnp.float32).T.astype(jnp.bfloat16)
        return carry

    lax.fori_loop(0, blocks, turn, 0)

    step = 256

    def widen(source, base):
        def body(i, carry):
            start = pl.multiple_of(i * step, step)
            table[pl.ds(pl.multiple_of(base + start, step), step), :] = staged[
                source, pl.ds(start, step), :
            ].astype(jnp.float32)
            return carry

        lax.fori_loop(0, half_rows // step, body, 0)

    own_copy.wait()
    widen(0, half * half_rows)
    other_copy.wait()
    widen(1, (1 - half) * half_rows)
    residual_copy.wait()

    slot_numbers = lax.broadcasted_iota(jnp.int32, (slots, width), 0)

    def decode(p, carry):
        length = lengths_ref[p]

        def fetch(c, inner):
            base = pl.multiple_of(c * CHUNK, CHUNK)
            for k in range(CHUNK):
                code = codes_ref[p, base + k]
                rows[pl.ds(base + k, 1), :] = table[pl.ds(code, 1), :]
            return inner

        lax.fori_loop(0, (length + CHUNK - 1) // CHUNK, fetch, 0)
        vectors = rows[...] + residual_rows[p].astype(jnp.float32)
        vectors = jnp.where(slot_numbers < length, vectors, vectors[0:1, :])
        embedded[p] = normalized(vectors)
        return carry

    lax.fori_loop(0, passages, decode, 0)

    def score(i, carry):
        b = i // passages
        p = i % passages
        similar = jnp.dot(embedded[p], turned[b], preferred_element_type=jnp.float32)
        largest[b, pl.ds(p, 1), :] = jnp.max(similar, axis=0, keepdims=True)
        return carry

    lax.fori_loop(0, blocks * passages, score, 0)

    per_block = block // token_count
    owner = lax.broadcasted_iota(jnp.int32, (per_block, block), 0)
    token_of = lax.broadcasted_iota(jnp.int32, (per_block, block), 1) // token_count
    summing = (owner == token_of).astype(jnp.float32)

    def total(b, carry):
        sums = lax.dot_general(
            summing,
            largest[b],
            (((1,), (1,)), ((), ())),
            precision=lax.Precision.HIGHEST,
            preferred_element_type=jnp.float32,
        )
        out_ref[pl.ds(pl.multiple_of(b * per_block, per_block), per_block), :] = sums
        return carry

    lax.fori_loop(0, blocks, total, 0)


def score_all(half, token_codes, lengths, query_rows, own, other, residuals, token_count):
    passages, slots, width = residuals.shape
    half_rows = own.shape[0]
    query_tokens = query_rows.shape[0]
    block = min(QUERY_BLOCK, query_tokens)
    blocks = query_tokens // block
    smem = pl.BlockSpec(memory_space=pltpu.SMEM)
    vmem = pl.BlockSpec(memory_space=pltpu.VMEM)
    hbm = pl.BlockSpec(memory_space=pl.ANY)
    return pl.pallas_call(
        functools.partial(score_kernel, token_count),
        out_shape=jax.ShapeDtypeStruct((query_tokens // token_count, passages), jnp.float32),
        in_specs=[smem, smem, smem, vmem, hbm, hbm, hbm],
        out_specs=vmem,
        scratch_shapes=[
            pltpu.VMEM((2, half_rows, width), jnp.bfloat16),
            pltpu.VMEM((2 * half_rows, width), jnp.float32),
            pltpu.VMEM((passages, slots, width), jnp.bfloat16),
            pltpu.VMEM((slots, width), jnp.float32),
            pltpu.VMEM((passages, slots, width), jnp.bfloat16),
            pltpu.VMEM((blocks, width, block), jnp.bfloat16),
            pltpu.VMEM((blocks, passages, block), jnp.float32),
            pltpu.SemaphoreType.DMA((3,)),
        ],
        compiler_params=pltpu.CompilerParams(vmem_limit_bytes=48 * 1024 * 1024),
    )(half, token_codes, lengths, query_rows, own, other, residuals)


def body(queries, candidates, token_codes, residuals, lengths, centroids):
    local_queries, token_count, width = queries.shape
    targets = lax.axis_size("shard") * lax.axis_size("sub")
    passages = token_codes.shape[0]
    other = lax.ppermute(centroids, "sub", [(0, 1), (1, 0)])
    sent = jnp.broadcast_to(queries[None], (targets,) + queries.shape)
    gathered = lax.all_to_all(sent, ("shard", "sub"), split_axis=0, concat_axis=0, tiled=True)
    query_rows = gathered.reshape(targets * local_queries * token_count, width)
    half = lax.axis_index("sub").astype(jnp.int32).reshape(1)
    scores = score_all(
        half, token_codes, lengths, query_rows, centroids, other, residuals, token_count
    )
    returned = lax.all_to_all(
        scores.reshape(targets, local_queries, passages),
        ("shard", "sub"),
        split_axis=0,
        concat_axis=0,
        tiled=True,
    )
    known = jnp.transpose(returned, (1, 0, 2)).reshape(local_queries, targets * passages)
    numbers = jnp.arange(targets * passages, dtype=jnp.int32)
    hits = candidates[:, :, None] == numbers[None, None, :]
    return jnp.sum(jnp.where(hits, known[:, None, :], 0.0), axis=2)


def solution(mesh):
    placed = (
        P(("groups", "shard", "sub"), None, None),
        P(("groups", "shard", "sub"), None),
        P(("groups", "shard", "sub"), None),
        P(("groups", "shard", "sub"), None, None),
        P(("groups", "shard", "sub")),
        P(("groups", "shard", "sub"), None),
    )
    return jax.shard_map(
        body,
        mesh=mesh,
        in_specs=placed,
        out_specs=P(("groups", "shard", "sub"), None),
        check_vma=False,
    )
```

```python
import functools

import jax
import jax.numpy as jnp
from jax import lax
from jax.experimental import pallas as pl
from jax.experimental.pallas import tpu as pltpu
from jax.sharding import PartitionSpec as P

CHUNK = 32
GROUP = 8
BATCH = 16
QUERY_BLOCK = 512
ROUND_BITS = 2


def normalized(vectors):
    total = jnp.sum(vectors * vectors, axis=-1, keepdims=True)
    return (vectors * lax.rsqrt(total + 1e-06)).astype(jnp.bfloat16)


def score_kernel(
    token_count,
    half_ref,
    codes_hbm,
    lengths_hbm,
    queries_ref,
    own_ref,
    other_ref,
    residuals_ref,
    out_ref,
    codes_ref,
    lengths_ref,
    owner_ref,
    staged,
    table,
    residual_rows,
    rows,
    embedded,
    turned,
    largest,
    sems,
):
    passages, slots, width = residuals_ref.shape
    half_rows = own_ref.shape[0]
    half = half_ref[0]
    own_copy = pltpu.make_async_copy(own_ref, staged.at[0], sems.at[0])
    other_copy = pltpu.make_async_copy(other_ref, staged.at[1], sems.at[1])
    residual_copy = pltpu.make_async_copy(residuals_ref, residual_rows, sems.at[2])
    codes_copy = pltpu.make_async_copy(codes_hbm, codes_ref, sems.at[3])
    lengths_copy = pltpu.make_async_copy(lengths_hbm, lengths_ref, sems.at[4])
    lengths_copy.start()
    codes_copy.start()
    own_copy.start()
    other_copy.start()
    residual_copy.start()

    query_tokens = queries_ref.shape[0]
    block = min(QUERY_BLOCK, query_tokens)
    blocks = query_tokens // block

    def turn(b, carry):
        at = pl.ds(pl.multiple_of(b * block, block), block)
        vectors = normalized(queries_ref[at, :].astype(jnp.float32))
        turned[b] = vectors.astype(jnp.float32).T.astype(jnp.bfloat16)
        return carry

    lax.fori_loop(0, blocks, turn, 0)

    step = 256

    def widen(source, base):
        def body(i, carry):
            start = pl.multiple_of(i * step, step)
            table[pl.ds(pl.multiple_of(base + start, step), step), :] = staged[
                source, pl.ds(start, step), :
            ].astype(jnp.float32)
            return carry

        lax.fori_loop(0, half_rows // step, body, 0)

    own_copy.wait()
    widen(0, half * half_rows)
    lengths_copy.wait()
    codes_copy.wait()

    def count(p, chunks):
        return chunks + (lengths_ref[p] + CHUNK - 1) // CHUNK

    chunks = lax.fori_loop(0, passages, count, 0)
    other_copy.wait()
    widen(1, (1 - half) * half_rows)
    residual_copy.wait()

    slot_numbers = lax.broadcasted_iota(jnp.int32, (CHUNK, width), 0)

    def decode(i, carry):
        p, start, last_p, last_start = carry
        last_at = pl.ds(pl.multiple_of(last_start, CHUNK), CHUNK)
        vectors = rows[...] + residual_rows[last_p, last_at, :].astype(jnp.float32)
        live = slot_numbers < lengths_ref[last_p] - last_start
        vectors = jnp.where(live, vectors, vectors[0:1, :])
        done = jnp.maximum(i - 1, 0)
        embedded[pl.ds(pl.multiple_of(done * CHUNK, CHUNK), CHUNK), :] = normalized(vectors)
        owner_ref[done] = last_p
        for k in range(0, CHUNK, BATCH):
            fetched = [
                table[pl.ds(codes_ref[p, start + k + j], 1), :] for j in range(BATCH)
            ]
            for j in range(BATCH):
                rows[pl.ds(k + j, 1), :] = fetched[j]
        more = start + CHUNK < lengths_ref[p]
        next_p = jnp.where(more, p, jnp.minimum(p + 1, passages - 1))
        next_start = jnp.where(more, start + CHUNK, 0)
        return next_p, next_start, p, start

    lax.fori_loop(0, chunks + 1, decode, (0, 0, 0, 0))
    for k in range(GROUP):
        owner_ref[chunks + k] = passages

    groups = (chunks + GROUP - 1) // GROUP

    def score_block(b, carry):
        largest[...] = jnp.full(largest.shape, -jnp.inf, jnp.float32)

        def score(g, inner):
            at = pl.ds(pl.multiple_of(g * GROUP * CHUNK, GROUP * CHUNK), GROUP * CHUNK)
            similar = jnp.dot(embedded[at, :], turned[b], preferred_element_type=jnp.float32)
            parts = jnp.max(similar.reshape(GROUP, CHUNK // 8, 8, block), axis=1)
            for k in range(GROUP):
                p = owner_ref[g * GROUP + k]
                largest[p] = jnp.maximum(largest[p], parts[k])
            return inner

        lax.fori_loop(0, groups, score, 0)
        per_block = block // token_count
        owner = lax.broadcasted_iota(jnp.int32, (per_block, block), 0)
        token_of = lax.broadcasted_iota(jnp.int32, (per_block, block), 1) // token_count
        summing = (owner == token_of).astype(jnp.float32)
        sums = lax.dot_general(
            summing,
            jnp.max(largest[0:passages], axis=1),
            (((1,), (1,)), ((), ())),
            precision=lax.Precision.HIGHEST,
            preferred_element_type=jnp.float32,
        )
        out_ref[pl.ds(pl.multiple_of(b * per_block, per_block), per_block), :] = sums
        return carry

    lax.fori_loop(0, blocks, score_block, 0)


def score_all(half, token_codes, lengths, query_rows, own, other, residuals, token_count):
    passages, slots, width = residuals.shape
    half_rows = own.shape[0]
    query_tokens = query_rows.shape[0]
    block = min(QUERY_BLOCK, query_tokens)
    blocks = query_tokens // block
    most = passages * (slots // CHUNK) + GROUP
    smem = pl.BlockSpec(memory_space=pltpu.SMEM)
    vmem = pl.BlockSpec(memory_space=pltpu.VMEM)
    hbm = pl.BlockSpec(memory_space=pl.ANY)
    return pl.pallas_call(
        functools.partial(score_kernel, token_count),
        out_shape=jax.ShapeDtypeStruct((query_tokens // token_count, passages), jnp.float32),
        in_specs=[smem, hbm, hbm, vmem, hbm, hbm, hbm],
        out_specs=vmem,
        scratch_shapes=[
            pltpu.SMEM(token_codes.shape, jnp.int32),
            pltpu.SMEM(lengths.shape, jnp.int32),
            pltpu.SMEM((most,), jnp.int32),
            pltpu.VMEM((2, half_rows, width), jnp.bfloat16),
            pltpu.VMEM((2 * half_rows, width), jnp.float32),
            pltpu.VMEM((passages, slots, width), jnp.bfloat16),
            pltpu.VMEM((CHUNK, width), jnp.float32),
            pltpu.VMEM((most * CHUNK, width), jnp.bfloat16),
            pltpu.VMEM((blocks, width, block), jnp.bfloat16),
            pltpu.VMEM((passages + 1, 8, block), jnp.float32),
            pltpu.SemaphoreType.DMA((5,)),
        ],
        compiler_params=pltpu.CompilerParams(vmem_limit_bytes=60 * 1024 * 1024),
    )(half, token_codes, lengths, query_rows, own, other, residuals)


def rounds_of(targets):
    first = 0
    bits = targets.bit_length() - 1
    while first < bits:
        taken = min(ROUND_BITS, bits - first)
        yield first, taken
        first += taken


def partner(targets, offset):
    return [(device, device ^ offset) for device in range(targets)]


def gather_relative(own, targets):
    held = own[None]
    for first, taken in rounds_of(targets):
        parts = [held]
        for value in range(1, 1 << taken):
            pairs = partner(targets, value << first)
            parts.append(lax.ppermute(held, ("shard", "sub"), pairs))
        held = jnp.concatenate(parts, axis=0)
    return held


def return_relative(blocks, targets):
    held = blocks.reshape((targets, 1) + blocks.shape[1:])
    for first, taken in rounds_of(targets):
        split = held.reshape((-1, 1 << taken) + held.shape[1:])
        parts = [split[:, 0]]
        for value in range(1, 1 << taken):
            pairs = partner(targets, value << first)
            parts.append(lax.ppermute(split[:, value], ("shard", "sub"), pairs))
        held = jnp.concatenate(parts, axis=1)
    return held[0]


def body(queries, candidates, token_codes, residuals, lengths, centroids):
    local_queries, token_count, width = queries.shape
    targets = lax.axis_size("shard") * lax.axis_size("sub")
    passages = token_codes.shape[0]
    half = lax.axis_index("sub").astype(jnp.int32)
    me = lax.axis_index("shard").astype(jnp.int32) * lax.axis_size("sub") + half
    other = lax.ppermute(centroids, "sub", [(0, 1), (1, 0)])
    gathered = gather_relative(queries, targets)
    query_rows = gathered.reshape(targets * local_queries * token_count, width)
    scores = score_all(
        half.reshape(1), token_codes, lengths, query_rows, centroids, other, residuals, token_count
    )
    returned = return_relative(scores.reshape(targets, local_queries, passages), targets)
    known = jnp.transpose(returned, (1, 0, 2)).reshape(local_queries, targets * passages)
    relative = ((candidates // passages) ^ me) * passages + candidates % passages
    numbers = jnp.arange(targets * passages, dtype=jnp.int32)
    hits = relative[:, :, None] == numbers[None, None, :]
    return jnp.sum(jnp.where(hits, known[:, None, :], 0.0), axis=2)


def solution(mesh):
    placed = (
        P(("groups", "shard", "sub"), None, None),
        P(("groups", "shard", "sub"), None),
        P(("groups", "shard", "sub"), None),
        P(("groups", "shard", "sub"), None, None),
        P(("groups", "shard", "sub")),
        P(("groups", "shard", "sub"), None),
    )
    return jax.shard_map(
        body,
        mesh=mesh,
        in_specs=placed,
        out_specs=P(("groups", "shard", "sub"), None),
        check_vma=False,
    )
```

```python
import functools

import jax
import jax.numpy as jnp
from jax import lax
from jax.experimental import pallas as pl
from jax.experimental.pallas import tpu as pltpu
from jax.sharding import PartitionSpec as P

CHUNK = 32
GROUP = 8
QUERY_BLOCK = 512
SMEM = pl.BlockSpec(memory_space=pltpu.SMEM)
VMEM = pl.BlockSpec(memory_space=pltpu.VMEM)
HBM = pl.BlockSpec(memory_space=pltpu.HBM)


def normalized(vectors):
    total = jnp.sum(vectors * vectors, axis=-1, keepdims=True)
    return (vectors * lax.rsqrt(total + 1e-06)).astype(jnp.bfloat16)


def decode_kernel(
    half_ref,
    codes_hbm,
    lengths_hbm,
    own_ref,
    other_ref,
    residuals_ref,
    embedded,
    owner_ref,
    codes_ref,
    lengths_ref,
    at_ref,
    live_ref,
    staged,
    table,
    residual_rows,
    rows,
    sems,
):
    passages = lengths_ref.shape[0]
    slots = codes_ref.shape[0] // passages
    half_rows, width = own_ref.shape
    half = half_ref[0]
    lengths_copy = pltpu.make_async_copy(lengths_hbm, lengths_ref, sems.at[2])
    codes_copy = pltpu.make_async_copy(codes_hbm, codes_ref, sems.at[3])
    own_copy = pltpu.make_async_copy(own_ref, staged, sems.at[0])
    residual_copy = pltpu.make_async_copy(residuals_ref, residual_rows, sems.at[1])
    lengths_copy.start()
    codes_copy.start()
    own_copy.start()
    residual_copy.start()

    lengths_copy.wait()

    def listing(p, chunks):
        length = lengths_ref[p]
        for k in range(slots // CHUNK):
            at_ref[chunks + k] = p * slots + k * CHUNK
            live_ref[chunks + k] = length - k * CHUNK
            owner_ref[chunks + k] = p
        return chunks + (length + CHUNK - 1) // CHUNK

    chunks = lax.fori_loop(0, passages, listing, 0)
    for k in range(GROUP):
        at_ref[chunks + k] = 0
        live_ref[chunks + k] = CHUNK
        owner_ref[chunks + k] = passages
    groups = (chunks + GROUP - 1) // GROUP
    owner_ref[owner_ref.shape[0] - 1] = groups

    step = 256

    def widen(source, base):
        def body(i, carry):
            start = pl.multiple_of(i * step, step)
            table[pl.ds(pl.multiple_of(base + start, step), step), :] = source[
                pl.ds(start, step), :
            ].astype(jnp.float32)
            return carry

        lax.fori_loop(0, half_rows // step, body, 0)

    widen(other_ref, (1 - half) * half_rows)
    own_copy.wait()
    widen(staged, half * half_rows)
    codes_copy.wait()
    residual_copy.wait()

    slot_numbers = lax.broadcasted_iota(jnp.int32, (CHUNK, width), 0)
    single = table.reshape(2 * half_rows, 1, width)

    def decode(g, carry):
        before = jnp.maximum(g - 1, 0)
        done = []
        for k in range(GROUP):
            i = before * GROUP + k
            own = pl.ds(pl.multiple_of(at_ref[i], CHUNK), CHUNK)
            vectors = rows[pl.ds(k * CHUNK, CHUNK), :] + residual_rows[own, :].astype(jnp.float32)
            vectors = jnp.where(slot_numbers < live_ref[i], vectors, vectors[0:1, :])
            done.append(normalized(vectors))
            at = at_ref[g * GROUP + k]
            for j in range(CHUNK):
                rows[pl.ds(k * CHUNK + j, 1), :] = single[codes_ref[at + j]]
        for k in range(GROUP):
            start = pl.multiple_of((before * GROUP + k) * CHUNK, CHUNK)
            embedded[pl.ds(start, CHUNK), :] = done[k]
        return carry

    lax.fori_loop(0, groups + 1, decode, 0)


def decode_all(half, token_codes, lengths, own, other, residuals):
    passages, slots, width = residuals.shape
    half_rows = own.shape[0]
    most = passages * (slots // CHUNK) + 2 * GROUP
    return pl.pallas_call(
        decode_kernel,
        out_shape=(
            jax.ShapeDtypeStruct((most * CHUNK, width), jnp.bfloat16),
            jax.ShapeDtypeStruct((most + 1,), jnp.int32),
        ),
        in_specs=[SMEM, HBM, HBM, HBM, VMEM, HBM],
        out_specs=(VMEM, SMEM),
        scratch_shapes=[
            pltpu.SMEM((passages * slots,), jnp.int32),
            pltpu.SMEM((passages,), jnp.int32),
            pltpu.SMEM((most,), jnp.int32),
            pltpu.SMEM((most,), jnp.int32),
            pltpu.VMEM((half_rows, width), jnp.bfloat16),
            pltpu.VMEM((2 * half_rows, width), jnp.float32),
            pltpu.VMEM((passages * slots, width), jnp.bfloat16),
            pltpu.VMEM((GROUP * CHUNK, width), jnp.float32),
            pltpu.SemaphoreType.DMA((4,)),
        ],
        compiler_params=pltpu.CompilerParams(vmem_limit_bytes=40 * 1024 * 1024),
        cost_estimate=pl.CostEstimate(flops=10**7, bytes_accessed=40 * 10**6, transcendentals=0),
        name="decode",
    )(
        half,
        token_codes.reshape(passages * slots),
        lengths,
        own,
        other,
        residuals.reshape(passages * slots, width),
    )


def score_kernel(token_count, passages, owner_ref, queries_ref, embedded, out_ref, turned, largest):
    query_tokens = queries_ref.shape[0]
    block = min(QUERY_BLOCK, query_tokens)
    blocks = query_tokens // block
    groups = owner_ref[owner_ref.shape[0] - 1]
    per_block = block // token_count
    owner = lax.broadcasted_iota(jnp.int32, (per_block, block), 0)
    token_of = lax.broadcasted_iota(jnp.int32, (per_block, block), 1) // token_count
    summing = (owner == token_of).astype(jnp.float32)

    def score_block(b, carry):
        at = pl.ds(pl.multiple_of(b * block, block), block)
        vectors = normalized(queries_ref[at, :].astype(jnp.float32))
        turned[...] = vectors.astype(jnp.float32).T.astype(jnp.bfloat16)
        largest[...] = jnp.full(largest.shape, -jnp.inf, jnp.float32)

        def score(g, inner):
            at = pl.ds(pl.multiple_of(g * GROUP * CHUNK, GROUP * CHUNK), GROUP * CHUNK)
            similar = jnp.dot(embedded[at, :], turned[...], preferred_element_type=jnp.float32)
            parts = jnp.max(similar.reshape(GROUP, CHUNK // 8, 8, block), axis=1)
            for k in range(GROUP):
                p = owner_ref[g * GROUP + k]
                largest[p] = jnp.maximum(largest[p], parts[k])
            return inner

        lax.fori_loop(0, groups, score, 0)
        sums = lax.dot_general(
            summing,
            jnp.max(largest[0:passages], axis=1),
            (((1,), (1,)), ((), ())),
            precision=lax.Precision.HIGHEST,
            preferred_element_type=jnp.float32,
        )
        out_ref[pl.ds(pl.multiple_of(b * per_block, per_block), per_block), :] = sums
        return carry

    lax.fori_loop(0, blocks, score_block, 0)


def score_all(owner, query_rows, embedded, passages, token_count):
    query_tokens, width = query_rows.shape
    block = min(QUERY_BLOCK, query_tokens)
    return pl.pallas_call(
        functools.partial(score_kernel, token_count, passages),
        out_shape=jax.ShapeDtypeStruct((query_tokens // token_count, passages), jnp.float32),
        in_specs=[SMEM, VMEM, VMEM],
        out_specs=VMEM,
        scratch_shapes=[
            pltpu.VMEM((width, block), jnp.bfloat16),
            pltpu.VMEM((passages + 1, 8, block), jnp.float32),
        ],
        compiler_params=pltpu.CompilerParams(vmem_limit_bytes=32 * 1024 * 1024),
        name="score",
    )(owner, query_rows, embedded)


def body(queries, candidates, token_codes, residuals, lengths, centroids):
    local_queries, token_count, width = queries.shape
    targets = lax.axis_size("shard") * lax.axis_size("sub")
    passages = token_codes.shape[0]
    half = lax.axis_index("sub").astype(jnp.int32)
    other = lax.ppermute(centroids, "sub", [(0, 1), (1, 0)])
    sent = jnp.broadcast_to(queries[None], (targets,) + queries.shape)
    gathered = lax.all_to_all(sent, ("shard", "sub"), split_axis=0, concat_axis=0, tiled=True)
    query_rows = gathered.reshape(targets * local_queries * token_count, width)
    embedded, owner = decode_all(half.reshape(1), token_codes, lengths, centroids, other, residuals)
    scores = score_all(owner, query_rows, embedded, passages, token_count)
    returned = lax.all_to_all(
        scores.reshape(targets, local_queries, passages),
        ("shard", "sub"),
        split_axis=0,
        concat_axis=0,
        tiled=True,
    )
    known = jnp.transpose(returned, (1, 0, 2)).reshape(local_queries, targets * passages)
    numbers = jnp.arange(targets * passages, dtype=jnp.int32)
    hits = candidates[:, :, None] == numbers[None, None, :]
    return jnp.sum(jnp.where(hits, known[:, None, :], 0.0), axis=2)


def solution(mesh):
    placed = (
        P(("groups", "shard", "sub"), None, None),
        P(("groups", "shard", "sub"), None),
        P(("groups", "shard", "sub"), None),
        P(("groups", "shard", "sub"), None, None),
        P(("groups", "shard", "sub")),
        P(("groups", "shard", "sub"), None),
    )
    return jax.shard_map(
        body,
        mesh=mesh,
        in_specs=placed,
        out_specs=P(("groups", "shard", "sub"), None),
        check_vma=False,
    )
```

```python
import functools

import jax
import jax.numpy as jnp
from jax import lax
from jax.experimental import pallas as pl
from jax.experimental.pallas import tpu as pltpu
from jax.sharding import PartitionSpec as P

CHUNK = 32
GROUP = 8
SCORE_GROUP = 16
QUERY_BLOCK = 512
SMEM = pl.BlockSpec(memory_space=pltpu.SMEM)
VMEM = pl.BlockSpec(memory_space=pltpu.VMEM)
HBM = pl.BlockSpec(memory_space=pltpu.HBM)


def normalized(vectors):
    total = jnp.sum(vectors * vectors, axis=-1, keepdims=True)
    return (vectors * lax.rsqrt(total + 1e-06)).astype(jnp.bfloat16)


def decode_kernel(
    half_ref,
    codes_hbm,
    lengths_hbm,
    own_ref,
    other_ref,
    residuals_ref,
    embedded,
    owner_ref,
    codes_ref,
    lengths_ref,
    at_ref,
    live_ref,
    staged,
    table,
    residual_rows,
    rows,
    sems,
):
    passages = lengths_ref.shape[0]
    slots = codes_ref.shape[0] // passages
    half_rows, width = own_ref.shape
    half = half_ref[0]
    lengths_copy = pltpu.make_async_copy(lengths_hbm, lengths_ref, sems.at[2])
    codes_copy = pltpu.make_async_copy(codes_hbm, codes_ref, sems.at[3])
    own_copy = pltpu.make_async_copy(own_ref, staged, sems.at[0])
    residual_copy = pltpu.make_async_copy(residuals_ref, residual_rows, sems.at[1])
    lengths_copy.start()
    codes_copy.start()
    own_copy.start()
    residual_copy.start()

    lengths_copy.wait()

    def listing(p, chunks):
        length = lengths_ref[p]
        for k in range(slots // CHUNK):
            at_ref[chunks + k] = p * slots + k * CHUNK
            live_ref[chunks + k] = length - k * CHUNK
            owner_ref[chunks + k] = p
        return chunks + (length + CHUNK - 1) // CHUNK

    chunks = lax.fori_loop(0, passages, listing, 0)
    for k in range(SCORE_GROUP):
        at_ref[chunks + k] = 0
        live_ref[chunks + k] = CHUNK
        owner_ref[chunks + k] = passages
    groups = (chunks + GROUP - 1) // GROUP
    owner_ref[owner_ref.shape[0] - 1] = chunks

    step = 256

    def widen(source, base):
        def body(i, carry):
            start = pl.multiple_of(i * step, step)
            table[pl.ds(pl.multiple_of(base + start, step), step), :] = source[
                pl.ds(start, step), :
            ].astype(jnp.float32)
            return carry

        lax.fori_loop(0, half_rows // step, body, 0)

    widen(other_ref, (1 - half) * half_rows)
    own_copy.wait()
    widen(staged, half * half_rows)
    codes_copy.wait()
    residual_copy.wait()

    slot_numbers = lax.broadcasted_iota(jnp.int32, (CHUNK, width), 0)
    single = table.reshape(2 * half_rows, 1, width)

    def decode(g, carry):
        before = jnp.maximum(g - 1, 0)
        done = []
        for k in range(GROUP):
            i = before * GROUP + k
            own = pl.ds(pl.multiple_of(at_ref[i], CHUNK), CHUNK)
            vectors = rows[pl.ds(k * CHUNK, CHUNK), :] + residual_rows[own, :].astype(jnp.float32)
            vectors = jnp.where(slot_numbers < live_ref[i], vectors, vectors[0:1, :])
            done.append(normalized(vectors))
            at = at_ref[g * GROUP + k]
            for j in range(CHUNK):
                rows[pl.ds(k * CHUNK + j, 1), :] = single[codes_ref[at + j]]
        for k in range(GROUP):
            start = pl.multiple_of((before * GROUP + k) * CHUNK, CHUNK)
            embedded[pl.ds(start, CHUNK), :] = done[k]
        return carry

    lax.fori_loop(0, groups + 1, decode, 0)


def pinned(array):
    return pltpu.with_memory_space_constraint(array, pltpu.HBM)


def decode_all(half, token_codes, lengths, own, other, residuals):
    passages, slots, width = residuals.shape
    half_rows = own.shape[0]
    most = passages * (slots // CHUNK) + 2 * SCORE_GROUP
    return pl.pallas_call(
        decode_kernel,
        out_shape=(
            jax.ShapeDtypeStruct((most * CHUNK, width), jnp.bfloat16),
            jax.ShapeDtypeStruct((most + 1,), jnp.int32),
        ),
        in_specs=[SMEM, HBM, HBM, HBM, VMEM, HBM],
        out_specs=(VMEM, SMEM),
        scratch_shapes=[
            pltpu.SMEM((passages * slots,), jnp.int32),
            pltpu.SMEM((passages,), jnp.int32),
            pltpu.SMEM((most,), jnp.int32),
            pltpu.SMEM((most,), jnp.int32),
            pltpu.VMEM((half_rows, width), jnp.bfloat16),
            pltpu.VMEM((2 * half_rows, width), jnp.float32),
            pltpu.VMEM((passages * slots, width), jnp.bfloat16),
            pltpu.VMEM((GROUP * CHUNK, width), jnp.float32),
            pltpu.SemaphoreType.DMA((4,)),
        ],
        compiler_params=pltpu.CompilerParams(vmem_limit_bytes=40 * 1024 * 1024),
        cost_estimate=pl.CostEstimate(flops=10**7, bytes_accessed=40 * 10**6, transcendentals=0),
        name="decode",
    )(
        half,
        pinned(token_codes.reshape(passages * slots)),
        pinned(lengths),
        pinned(own),
        other,
        pinned(residuals.reshape(passages * slots, width)),
    )


def score_kernel(token_count, passages, owner_ref, queries_ref, embedded, out_ref, turned, largest):
    query_tokens = queries_ref.shape[0]
    block = min(QUERY_BLOCK, query_tokens)
    blocks = query_tokens // block
    chunks = owner_ref[owner_ref.shape[0] - 1]
    groups = (chunks + SCORE_GROUP - 1) // SCORE_GROUP
    per_block = block // token_count
    owner = lax.broadcasted_iota(jnp.int32, (per_block, block), 0)
    token_of = lax.broadcasted_iota(jnp.int32, (per_block, block), 1) // token_count
    summing = (owner == token_of).astype(jnp.float32)

    def score_block(b, carry):
        at = pl.ds(pl.multiple_of(b * block, block), block)
        vectors = normalized(queries_ref[at, :].astype(jnp.float32))
        turned[...] = vectors.astype(jnp.float32).T.astype(jnp.bfloat16)
        largest[...] = jnp.full(largest.shape, -jnp.inf, jnp.float32)

        def score(g, inner):
            at = pl.ds(pl.multiple_of(g * SCORE_GROUP * CHUNK, SCORE_GROUP * CHUNK), SCORE_GROUP * CHUNK)
            similar = jnp.dot(embedded[at, :], turned[...], preferred_element_type=jnp.float32)
            parts = jnp.max(similar.reshape(SCORE_GROUP, CHUNK // 8, 8, block), axis=1)
            for k in range(SCORE_GROUP):
                p = owner_ref[g * SCORE_GROUP + k]
                largest[p] = jnp.maximum(largest[p], parts[k])
            return inner

        lax.fori_loop(0, groups, score, 0)
        sums = lax.dot_general(
            summing,
            jnp.max(largest[0:passages], axis=1),
            (((1,), (1,)), ((), ())),
            precision=lax.Precision.HIGHEST,
            preferred_element_type=jnp.float32,
        )
        out_ref[pl.ds(pl.multiple_of(b * per_block, per_block), per_block), :] = sums
        return carry

    lax.fori_loop(0, blocks, score_block, 0)


def score_all(owner, query_rows, embedded, passages, token_count):
    query_tokens, width = query_rows.shape
    block = min(QUERY_BLOCK, query_tokens)
    return pl.pallas_call(
        functools.partial(score_kernel, token_count, passages),
        out_shape=jax.ShapeDtypeStruct((query_tokens // token_count, passages), jnp.float32),
        in_specs=[SMEM, VMEM, VMEM],
        out_specs=VMEM,
        scratch_shapes=[
            pltpu.VMEM((width, block), jnp.bfloat16),
            pltpu.VMEM((passages + 1, 8, block), jnp.float32),
        ],
        compiler_params=pltpu.CompilerParams(vmem_limit_bytes=32 * 1024 * 1024),
        name="score",
    )(owner, query_rows, embedded)


def pick_kernel(passages, candidates_ref, returned_ref, out_ref):
    local_queries, count = candidates_ref.shape
    targets = returned_ref.shape[0]
    passage_numbers = lax.broadcasted_iota(jnp.int32, (passages, count), 0)
    target_numbers = lax.broadcasted_iota(jnp.int32, (targets, count), 0)
    for q in range(local_queries):
        wanted = candidates_ref[q : q + 1, :]
        target = wanted // passages
        hits = (passage_numbers == wanted - target * passages).astype(jnp.float32)
        picked = jnp.dot(
            returned_ref[:, q * passages : (q + 1) * passages],
            hits,
            precision=lax.Precision.HIGHEST,
            preferred_element_type=jnp.float32,
        )
        kept = jnp.where(target_numbers == target, picked, 0.0)
        out_ref[q : q + 1, :] = jnp.sum(kept, axis=0, keepdims=True)


def pick(candidates, returned, passages):
    return pl.pallas_call(
        functools.partial(pick_kernel, passages),
        out_shape=jax.ShapeDtypeStruct(candidates.shape, jnp.float32),
        in_specs=[VMEM, VMEM],
        out_specs=VMEM,
        name="pick",
    )(candidates, returned)


def body(queries, candidates, token_codes, residuals, lengths, centroids):
    local_queries, token_count, width = queries.shape
    targets = lax.axis_size("shard") * lax.axis_size("sub")
    passages = token_codes.shape[0]
    half = lax.axis_index("sub").astype(jnp.int32)
    other = lax.ppermute(centroids, "sub", [(0, 1), (1, 0)])
    own_rows = queries.reshape(1, local_queries * token_count, width)
    sent = jnp.broadcast_to(own_rows, (targets,) + own_rows.shape[1:])
    gathered = lax.all_to_all(sent, ("shard", "sub"), split_axis=0, concat_axis=0, tiled=True)
    query_rows = gathered.reshape(targets * local_queries * token_count, width)
    embedded, owner = decode_all(half.reshape(1), token_codes, lengths, centroids, other, residuals)
    scores = score_all(owner, query_rows, embedded, passages, token_count)
    returned = lax.all_to_all(
        scores.reshape(targets, local_queries * passages),
        ("shard", "sub"),
        split_axis=0,
        concat_axis=0,
        tiled=True,
    )
    return pick(candidates, returned, passages)


def solution(mesh):
    placed = (
        P(("groups", "shard", "sub"), None, None),
        P(("groups", "shard", "sub"), None),
        P(("groups", "shard", "sub"), None),
        P(("groups", "shard", "sub"), None, None),
        P(("groups", "shard", "sub")),
        P(("groups", "shard", "sub"), None),
    )
    return jax.shard_map(
        body,
        mesh=mesh,
        in_specs=placed,
        out_specs=P(("groups", "shard", "sub"), None),
        check_vma=False,
    )
```

```python
import functools

import jax
import jax.numpy as jnp
from jax import lax
from jax.experimental import pallas as pl
from jax.experimental.pallas import tpu as pltpu
from jax.sharding import PartitionSpec as P

CHUNK = 16
GROUP = 16
SCORE_GROUP = 32
QUERY_BLOCK = 512
SMEM = pl.BlockSpec(memory_space=pltpu.SMEM)
VMEM = pl.BlockSpec(memory_space=pltpu.VMEM)
HBM = pl.BlockSpec(memory_space=pltpu.HBM)


def normalized(vectors):
    total = jnp.sum(vectors * vectors, axis=-1, keepdims=True)
    return (vectors * lax.rsqrt(total + 1e-06)).astype(jnp.bfloat16)


def decode_kernel(
    half_ref,
    codes_hbm,
    lengths_hbm,
    own_ref,
    other_ref,
    residuals_ref,
    embedded,
    owner_ref,
    codes_ref,
    lengths_ref,
    at_ref,
    live_ref,
    staged,
    table,
    residual_rows,
    rows,
    sems,
):
    passages = lengths_ref.shape[0]
    slots = codes_ref.shape[0] // passages
    half_rows, width = own_ref.shape
    half = half_ref[0]
    lengths_copy = pltpu.make_async_copy(lengths_hbm, lengths_ref, sems.at[2])
    codes_copy = pltpu.make_async_copy(codes_hbm, codes_ref, sems.at[3])
    own_copy = pltpu.make_async_copy(own_ref, staged, sems.at[0])
    residual_copy = pltpu.make_async_copy(residuals_ref, residual_rows, sems.at[1])
    lengths_copy.start()
    codes_copy.start()
    own_copy.start()
    residual_copy.start()

    lengths_copy.wait()

    def listing(p, chunks):
        length = lengths_ref[p]
        for k in range(slots // CHUNK):
            at_ref[chunks + k] = p * slots + k * CHUNK
            live_ref[chunks + k] = length - k * CHUNK
            owner_ref[chunks + k] = 2 * p + (1 if k == 0 else 0)
        return chunks + (length + CHUNK - 1) // CHUNK

    chunks = lax.fori_loop(0, passages, listing, 0)
    for k in range(SCORE_GROUP):
        at_ref[chunks + k] = 0
        live_ref[chunks + k] = CHUNK
        owner_ref[chunks + k] = 2 * passages + 1
    groups = (chunks + GROUP - 1) // GROUP
    owner_ref[owner_ref.shape[0] - 1] = chunks

    step = min(1024, half_rows)

    def widen(source, base):
        def body(i, carry):
            start = pl.multiple_of(i * step, step)
            table[pl.ds(pl.multiple_of(base + start, step), step), :] = source[
                pl.ds(start, step), :
            ].astype(jnp.float32)
            return carry

        lax.fori_loop(0, half_rows // step, body, 0)

    widen(other_ref, (1 - half) * half_rows)
    own_copy.wait()
    widen(staged, half * half_rows)
    codes_copy.wait()
    residual_copy.wait()

    slot_numbers = lax.broadcasted_iota(jnp.int32, (CHUNK, width), 0)
    single = table.reshape(2 * half_rows, 1, width)

    def fetch(g, k):
        at = at_ref[g * GROUP + k]
        for j in range(CHUNK):
            rows[pl.ds(k * CHUNK + j, 1), :] = single[codes_ref[at + j]]

    def finish(g, k):
        i = g * GROUP + k
        at = pl.ds(pl.multiple_of(at_ref[i], CHUNK), CHUNK)
        vectors = rows[pl.ds(k * CHUNK, CHUNK), :] + residual_rows[at, :].astype(jnp.float32)
        vectors = jnp.where(slot_numbers < live_ref[i], vectors, vectors[0:1, :])
        return normalized(vectors)

    def keep(g, done):
        for k in range(GROUP):
            start = pl.multiple_of((g * GROUP + k) * CHUNK, CHUNK)
            embedded[pl.ds(start, CHUNK), :] = done[k]

    for k in range(GROUP):
        fetch(0, k)

    def decode(g, carry):
        done = []
        for k in range(GROUP):
            done.append(finish(g - 1, k))
            fetch(g, k)
        keep(g - 1, done)
        return carry

    lax.fori_loop(1, groups, decode, 0)
    keep(groups - 1, [finish(groups - 1, k) for k in range(GROUP)])


def pinned(array):
    return pltpu.with_memory_space_constraint(array, pltpu.HBM)


def decode_all(half, token_codes, lengths, own, other, residuals):
    passages, slots, width = residuals.shape
    half_rows = own.shape[0]
    most = passages * (slots // CHUNK) + 2 * SCORE_GROUP
    return pl.pallas_call(
        decode_kernel,
        out_shape=(
            jax.ShapeDtypeStruct((most * CHUNK, width), jnp.bfloat16),
            jax.ShapeDtypeStruct((most + 1,), jnp.int32),
        ),
        in_specs=[SMEM, HBM, HBM, HBM, VMEM, HBM],
        out_specs=(VMEM, SMEM),
        scratch_shapes=[
            pltpu.SMEM((passages * slots,), jnp.int32),
            pltpu.SMEM((passages,), jnp.int32),
            pltpu.SMEM((most,), jnp.int32),
            pltpu.SMEM((most,), jnp.int32),
            pltpu.VMEM((half_rows, width), jnp.bfloat16),
            pltpu.VMEM((2 * half_rows, width), jnp.float32),
            pltpu.VMEM((passages * slots, width), jnp.bfloat16),
            pltpu.VMEM((GROUP * CHUNK, width), jnp.float32),
            pltpu.SemaphoreType.DMA((4,)),
        ],
        compiler_params=pltpu.CompilerParams(vmem_limit_bytes=24 * 1024 * 1024),
        cost_estimate=pl.CostEstimate(flops=10**7, bytes_accessed=40 * 10**6, transcendentals=0),
        name="decode",
    )(
        half,
        pinned(token_codes.reshape(passages * slots)),
        pinned(lengths),
        pinned(own),
        pltpu.with_memory_space_constraint(other, pltpu.VMEM),
        pinned(residuals.reshape(passages * slots, width)),
    )


def score_kernel(token_count, passages, owner_ref, queries_ref, embedded, out_ref, turned, largest):
    query_tokens = queries_ref.shape[0]
    block = min(QUERY_BLOCK, query_tokens)
    blocks = query_tokens // block
    chunks = owner_ref[owner_ref.shape[0] - 1]
    groups = (chunks + SCORE_GROUP - 1) // SCORE_GROUP
    per_block = block // token_count
    owner = lax.broadcasted_iota(jnp.int32, (per_block, block), 0)
    token_of = lax.broadcasted_iota(jnp.int32, (per_block, block), 1) // token_count
    summing = (owner == token_of).astype(jnp.bfloat16)

    def score_block(b, carry):
        at = pl.ds(pl.multiple_of(b * block, block), block)
        vectors = normalized(queries_ref[at, :].astype(jnp.float32))
        turned[...] = vectors.astype(jnp.float32).T.astype(jnp.bfloat16)

        def score(g, so_far):
            at = pl.ds(pl.multiple_of(g * SCORE_GROUP * CHUNK, SCORE_GROUP * CHUNK), SCORE_GROUP * CHUNK)
            similar = jnp.dot(embedded[at, :], turned[...], preferred_element_type=jnp.float32)
            parts = jnp.max(similar.reshape(SCORE_GROUP, CHUNK // 8, 8, block), axis=1)
            for k in range(SCORE_GROUP):
                mark = owner_ref[g * SCORE_GROUP + k]
                first = lax.rem(mark, 2) == 1
                so_far = jnp.where(first, parts[k], jnp.maximum(so_far, parts[k]))
                at = pl.multiple_of(lax.shift_right_logical(mark, 1) * 8, 8)
                for lane in range(block // 128):
                    largest[lane, pl.ds(at, 8), :] = so_far[:, lane * 128 : (lane + 1) * 128]
            return so_far

        lax.fori_loop(0, groups, score, jnp.zeros((8, block), jnp.float32))
        kept = []
        for lane in range(block // 128):
            best = largest[lane, pl.ds(0, passages, stride=8), :]
            for k in range(1, 8):
                best = jnp.maximum(best, largest[lane, pl.ds(k, passages, stride=8), :])
            kept.append(best)
        best = jnp.concatenate(kept, axis=1)
        sums = jnp.zeros((per_block, passages), jnp.float32)
        for _ in range(3):
            part = best.astype(jnp.bfloat16)
            best = best - part.astype(jnp.float32)
            sums = sums + lax.dot_general(
                summing, part, (((1,), (1,)), ((), ())), preferred_element_type=jnp.float32
            )
        out_ref[pl.ds(pl.multiple_of(b * per_block, per_block), per_block), :] = sums
        return carry

    lax.fori_loop(0, blocks, score_block, 0)


def score_all(owner, query_rows, embedded, passages, token_count):
    query_tokens, width = query_rows.shape
    block = min(QUERY_BLOCK, query_tokens)
    return pl.pallas_call(
        functools.partial(score_kernel, token_count, passages),
        out_shape=jax.ShapeDtypeStruct((query_tokens // token_count, passages), jnp.float32),
        in_specs=[SMEM, VMEM, VMEM],
        out_specs=VMEM,
        scratch_shapes=[
            pltpu.VMEM((width, block), jnp.bfloat16),
            pltpu.VMEM((block // 128, (passages + 1) * 8, 128), jnp.float32),
        ],
        compiler_params=pltpu.CompilerParams(vmem_limit_bytes=32 * 1024 * 1024),
        name="score",
    )(owner, query_rows, embedded)


def pick_kernel(passages, candidates_ref, returned_ref, out_ref):
    local_queries, count = candidates_ref.shape
    targets = returned_ref.shape[0]
    passage_numbers = lax.broadcasted_iota(jnp.int32, (passages, count), 0)
    target_numbers = lax.broadcasted_iota(jnp.int32, (targets, count), 0)
    for q in range(local_queries):
        wanted = candidates_ref[q : q + 1, :]
        target = lax.div(wanted, passages)
        hits = (passage_numbers == wanted - target * passages).astype(jnp.bfloat16)
        left = returned_ref[:, q * passages : (q + 1) * passages]
        picked = jnp.zeros((targets, count), jnp.float32)
        for _ in range(3):
            part = left.astype(jnp.bfloat16)
            left = left - part.astype(jnp.float32)
            picked = picked + jnp.dot(part, hits, preferred_element_type=jnp.float32)
        kept = jnp.where(target_numbers == target, picked, 0.0)
        out_ref[q : q + 1, :] = jnp.sum(kept, axis=0, keepdims=True)


def pick(candidates, returned, passages):
    return pl.pallas_call(
        functools.partial(pick_kernel, passages),
        out_shape=jax.ShapeDtypeStruct(candidates.shape, jnp.float32),
        in_specs=[VMEM, VMEM],
        out_specs=VMEM,
        name="pick",
    )(candidates, pltpu.with_memory_space_constraint(returned, pltpu.VMEM))


def body(queries, candidates, token_codes, residuals, lengths, centroids):
    local_queries, token_count, width = queries.shape
    targets = lax.axis_size("shard") * lax.axis_size("sub")
    passages = token_codes.shape[0]
    half = lax.axis_index("sub").astype(jnp.int32)
    other = lax.ppermute(centroids, "sub", [(0, 1), (1, 0)])
    own_rows = queries.reshape(1, local_queries * token_count, width)
    sent = jnp.broadcast_to(own_rows, (targets,) + own_rows.shape[1:])
    gathered = lax.all_to_all(sent, ("shard", "sub"), split_axis=0, concat_axis=0, tiled=True)
    query_rows = gathered.reshape(targets * local_queries * token_count, width)
    embedded, owner = decode_all(half.reshape(1), token_codes, lengths, centroids, other, residuals)
    scores = score_all(owner, query_rows, embedded, passages, token_count)
    returned = lax.all_to_all(
        scores.reshape(targets, local_queries * passages),
        ("shard", "sub"),
        split_axis=0,
        concat_axis=0,
        tiled=True,
    )
    return pick(candidates, returned, passages)


def solution(mesh):
    placed = (
        P(("groups", "shard", "sub"), None, None),
        P(("groups", "shard", "sub"), None),
        P(("groups", "shard", "sub"), None),
        P(("groups", "shard", "sub"), None, None),
        P(("groups", "shard", "sub")),
        P(("groups", "shard", "sub"), None),
    )
    return jax.shard_map(
        body,
        mesh=mesh,
        in_specs=placed,
        out_specs=P(("groups", "shard", "sub"), None),
        check_vma=False,
    )
```

```python
import functools

import jax
import jax.numpy as jnp
from jax import lax
from jax.experimental import pallas as pl
from jax.experimental.pallas import tpu as pltpu
from jax.sharding import PartitionSpec as P

CHUNK = 16
GROUP = 16
SCORE_GROUP = 32
PIECES = 4
QUERY_BLOCK = 512
SMEM = pl.BlockSpec(memory_space=pltpu.SMEM)
VMEM = pl.BlockSpec(memory_space=pltpu.VMEM)
HBM = pl.BlockSpec(memory_space=pltpu.HBM)


def normalized(vectors):
    total = jnp.sum(vectors * vectors, axis=-1, keepdims=True)
    return (vectors * lax.rsqrt(total + 1e-06)).astype(jnp.bfloat16)


def quotient(number, divisor):
    if divisor & (divisor - 1) == 0:
        return lax.shift_right_logical(number, divisor.bit_length() - 1)
    return lax.div(number, divisor)


def decode_kernel(
    half_ref,
    codes_hbm,
    lengths_hbm,
    own_ref,
    other_ref,
    residuals_ref,
    embedded,
    at_ref,
    codes_ref,
    lengths_ref,
    staged,
    table,
    residual_rows,
    rows,
    sems,
):
    passages = lengths_ref.shape[0]
    tokens = codes_ref.shape[0]
    slots = tokens // passages
    half_rows, width = own_ref.shape
    half = half_ref[0]
    lengths_copy = pltpu.make_async_copy(lengths_hbm, lengths_ref, sems.at[0])
    codes_copy = pltpu.make_async_copy(codes_hbm, codes_ref, sems.at[1])
    residual_copy = pltpu.make_async_copy(residuals_ref, residual_rows, sems.at[2])
    lengths_copy.start()
    codes_copy.start()
    piece = half_rows // PIECES
    copies = []
    for source, ref in enumerate((own_ref, other_ref)):
        for k in range(PIECES):
            at = pl.ds(k * piece, piece)
            sem = sems.at[3 + source * PIECES + k]
            copies.append(pltpu.make_async_copy(ref.at[at], staged.at[source, at], sem))
            copies[-1].start()
    residual_copy.start()

    lengths_copy.wait()

    def listing(p, chunks):
        for k in range(slots // CHUNK):
            at_ref[chunks + k] = p * slots + k * CHUNK
        return chunks + quotient(lengths_ref[p] + CHUNK - 1, CHUNK)

    chunks = lax.fori_loop(0, passages, listing, 0, unroll=4)
    for k in range(SCORE_GROUP):
        at_ref[chunks + k] = tokens
    groups = quotient(chunks + GROUP - 1, GROUP)
    at_ref[at_ref.shape[0] - 1] = chunks

    for source in range(2):
        base = (half if source == 0 else 1 - half) * half_rows
        for k in range(PIECES):
            copies[source * PIECES + k].wait()
            to = pl.ds(pl.multiple_of(base + k * piece, piece), piece)
            table[to, :] = staged[source, pl.ds(k * piece, piece), :].astype(jnp.float32)
    codes_copy.wait()
    residual_copy.wait()

    slot_numbers = lax.broadcasted_iota(jnp.int32, (CHUNK, width), 0)
    single = table.reshape(2 * half_rows, 1, width)

    def fetch(g, k):
        at = jnp.minimum(at_ref[g * GROUP + k], tokens - CHUNK)
        for j in range(CHUNK):
            rows[pl.ds(k * CHUNK + j, 1), :] = single[codes_ref[at + j]]

    def finish(g, k):
        at = jnp.minimum(at_ref[g * GROUP + k], tokens - CHUNK)
        p = quotient(at, slots)
        live = lengths_ref[p] - (at - p * slots)
        near = residual_rows[pl.ds(pl.multiple_of(at, CHUNK), CHUNK), :]
        vectors = rows[pl.ds(k * CHUNK, CHUNK), :] + near.astype(jnp.float32)
        vectors = jnp.where(slot_numbers < live, vectors, vectors[0:1, :])
        return normalized(vectors)

    def keep(g, done):
        for k in range(GROUP):
            start = pl.multiple_of((g * GROUP + k) * CHUNK, CHUNK)
            embedded[pl.ds(start, CHUNK), :] = done[k]

    for k in range(GROUP):
        fetch(0, k)

    def decode(g, carry):
        done = []
        for k in range(GROUP):
            done.append(finish(g - 1, k))
            fetch(g, k)
        keep(g - 1, done)
        return carry

    lax.fori_loop(1, groups, decode, 0)
    keep(groups - 1, [finish(groups - 1, k) for k in range(GROUP)])


def pinned(array):
    return pltpu.with_memory_space_constraint(array, pltpu.HBM)


def decode_all(half, token_codes, lengths, own, other, residuals):
    passages, slots, width = residuals.shape
    half_rows = own.shape[0]
    most = passages * (slots // CHUNK) + 2 * SCORE_GROUP
    return pl.pallas_call(
        decode_kernel,
        out_shape=(
            jax.ShapeDtypeStruct((most * CHUNK, width), jnp.bfloat16),
            jax.ShapeDtypeStruct((most + 1,), jnp.int32),
        ),
        in_specs=[SMEM, HBM, HBM, HBM, HBM, HBM],
        out_specs=(VMEM, SMEM),
        scratch_shapes=[
            pltpu.SMEM((passages * slots,), jnp.int32),
            pltpu.SMEM((passages,), jnp.int32),
            pltpu.VMEM((2, half_rows, width), jnp.bfloat16),
            pltpu.VMEM((2 * half_rows, width), jnp.float32),
            pltpu.VMEM((passages * slots, width), jnp.bfloat16),
            pltpu.VMEM((GROUP * CHUNK, width), jnp.float32),
            pltpu.SemaphoreType.DMA((3 + 2 * PIECES,)),
        ],
        compiler_params=pltpu.CompilerParams(vmem_limit_bytes=24 * 1024 * 1024),
        cost_estimate=pl.CostEstimate(flops=10**7, bytes_accessed=40 * 10**6, transcendentals=0),
        name="decode",
    )(
        half,
        pinned(token_codes.reshape(passages * slots)),
        pinned(lengths),
        pinned(own),
        pinned(other),
        pinned(residuals.reshape(passages * slots, width)),
    )


def score_kernel(token_count, slots, at_ref, queries_ref, embedded, out_ref, turned, largest):
    passages = out_ref.shape[1]
    query_tokens = queries_ref.shape[0]
    block = min(QUERY_BLOCK, query_tokens)
    blocks = query_tokens // block
    groups = quotient(at_ref[at_ref.shape[0] - 1] + SCORE_GROUP - 1, SCORE_GROUP)
    per_block = block // token_count
    owner = lax.broadcasted_iota(jnp.int32, (per_block, block), 0)
    token_of = lax.broadcasted_iota(jnp.int32, (per_block, block), 1) // token_count
    summing = (owner == token_of).astype(jnp.bfloat16)

    def score_block(b, carry):
        at = pl.ds(pl.multiple_of(b * block, block), block)
        vectors = normalized(queries_ref[at, :].astype(jnp.float32))
        turned[...] = vectors.astype(jnp.float32).T.astype(jnp.bfloat16)

        def score(g, so_far):
            size = SCORE_GROUP * CHUNK
            at = pl.ds(pl.multiple_of(g * size, size), size)
            similar = jnp.dot(embedded[at, :], turned[...], preferred_element_type=jnp.float32)
            parts = jnp.max(similar.reshape(SCORE_GROUP, CHUNK // 8, 8, block), axis=1)
            for k in range(SCORE_GROUP):
                start = at_ref[g * SCORE_GROUP + k]
                p = quotient(start, slots)
                so_far = jnp.where(start == p * slots, parts[k], jnp.maximum(so_far, parts[k]))
                at = pl.multiple_of(p * 8, 8)
                for lane in range(block // 128):
                    largest[lane, pl.ds(at, 8), :] = so_far[:, lane * 128 : (lane + 1) * 128]
            return so_far

        lax.fori_loop(0, groups, score, jnp.zeros((8, block), jnp.float32))
        kept = []
        for lane in range(block // 128):
            best = largest[lane, pl.ds(0, passages, stride=8), :]
            for k in range(1, 8):
                best = jnp.maximum(best, largest[lane, pl.ds(k, passages, stride=8), :])
            kept.append(best)
        best = jnp.concatenate(kept, axis=1)
        sums = jnp.zeros((per_block, passages), jnp.float32)
        for _ in range(3):
            part = best.astype(jnp.bfloat16)
            best = best - part.astype(jnp.float32)
            sums = sums + lax.dot_general(
                summing, part, (((1,), (1,)), ((), ())), preferred_element_type=jnp.float32
            )
        out_ref[pl.ds(pl.multiple_of(b * per_block, per_block), per_block), :] = sums
        return carry

    lax.fori_loop(0, blocks, score_block, 0)


def score_all(starts, query_rows, embedded, passages, slots, token_count):
    query_tokens, width = query_rows.shape
    block = min(QUERY_BLOCK, query_tokens)
    return pl.pallas_call(
        functools.partial(score_kernel, token_count, slots),
        out_shape=jax.ShapeDtypeStruct((query_tokens // token_count, passages), jnp.float32),
        in_specs=[SMEM, VMEM, VMEM],
        out_specs=VMEM,
        scratch_shapes=[
            pltpu.VMEM((width, block), jnp.bfloat16),
            pltpu.VMEM((block // 128, (passages + 1) * 8, 128), jnp.float32),
        ],
        compiler_params=pltpu.CompilerParams(vmem_limit_bytes=32 * 1024 * 1024),
        name="score",
    )(starts, query_rows, embedded)


def pick_kernel(passages, candidates_ref, returned_ref, out_ref):
    local_queries, count = candidates_ref.shape
    targets = returned_ref.shape[0]
    passage_numbers = lax.broadcasted_iota(jnp.int32, (passages, count), 0)
    target_numbers = lax.broadcasted_iota(jnp.int32, (targets, count), 0)
    for q in range(local_queries):
        wanted = candidates_ref[q : q + 1, :]
        target = quotient(wanted, passages)
        hits = (passage_numbers == wanted - target * passages).astype(jnp.bfloat16)
        left = returned_ref[:, q * passages : (q + 1) * passages]
        picked = jnp.zeros((targets, count), jnp.float32)
        for _ in range(3):
            part = left.astype(jnp.bfloat16)
            left = left - part.astype(jnp.float32)
            picked = picked + jnp.dot(part, hits, preferred_element_type=jnp.float32)
        kept = jnp.where(target_numbers == target, picked, 0.0)
        out_ref[q : q + 1, :] = jnp.sum(kept, axis=0, keepdims=True)


def pick(candidates, returned, passages):
    return pl.pallas_call(
        functools.partial(pick_kernel, passages),
        out_shape=jax.ShapeDtypeStruct(candidates.shape, jnp.float32),
        in_specs=[VMEM, VMEM],
        out_specs=VMEM,
        compiler_params=pltpu.CompilerParams(vmem_limit_bytes=4 * 1024 * 1024),
        name="pick",
    )(candidates, pltpu.with_memory_space_constraint(returned, pltpu.VMEM))


def body(queries, candidates, token_codes, residuals, lengths, centroids):
    local_queries, token_count, width = queries.shape
    targets = lax.axis_size("shard") * lax.axis_size("sub")
    passages, slots = token_codes.shape
    half = lax.axis_index("sub").astype(jnp.int32)
    other = lax.ppermute(centroids, "sub", [(0, 1), (1, 0)])
    own_rows = queries.reshape(1, local_queries * token_count, width)
    sent = jnp.broadcast_to(own_rows, (targets,) + own_rows.shape[1:])
    gathered = lax.all_to_all(sent, ("shard", "sub"), split_axis=0, concat_axis=0, tiled=True)
    query_rows = gathered.reshape(targets * local_queries * token_count, width)
    embedded, starts = decode_all(half.reshape(1), token_codes, lengths, centroids, other, residuals)
    scores = score_all(starts, query_rows, embedded, passages, slots, token_count)
    returned = lax.all_to_all(
        scores.reshape(targets, local_queries * passages),
        ("shard", "sub"),
        split_axis=0,
        concat_axis=0,
        tiled=True,
    )
    return pick(candidates, returned, passages)


def solution(mesh):
    placed = (
        P(("groups", "shard", "sub"), None, None),
        P(("groups", "shard", "sub"), None),
        P(("groups", "shard", "sub"), None),
        P(("groups", "shard", "sub"), None, None),
        P(("groups", "shard", "sub")),
        P(("groups", "shard", "sub"), None),
    )
    return jax.shard_map(
        body,
        mesh=mesh,
        in_specs=placed,
        out_specs=P(("groups", "shard", "sub"), None),
        check_vma=False,
    )
```

```python
import functools

import jax
import jax.numpy as jnp
from jax import lax
from jax.experimental import pallas as pl
from jax.experimental.pallas import tpu as pltpu
from jax.sharding import PartitionSpec as P

CHUNK = 16
GROUP = 16
PIECES = 4
QUERY_BLOCK = 512
DIGIT = 128
NOBODY = 255.0
SMEM = pl.BlockSpec(memory_space=pltpu.SMEM)
VMEM = pl.BlockSpec(memory_space=pltpu.VMEM)
HBM = pl.BlockSpec(memory_space=pltpu.HBM)


def pinned(array, space=pltpu.HBM):
    return pltpu.with_memory_space_constraint(array, space)


def granted(mebibytes):
    return pltpu.CompilerParams(vmem_limit_bytes=mebibytes * 1024 * 1024)


def quotient(number, divisor):
    if divisor & (divisor - 1) == 0:
        return lax.shift_right_logical(number, divisor.bit_length() - 1)
    return lax.div(number, divisor)


def normalized(vectors):
    total = jnp.sum(vectors * vectors, axis=-1, keepdims=True)
    return (vectors * lax.rsqrt(total + 1e-06)).astype(jnp.bfloat16)


def id_rows_of(local_queries, count):
    rows = local_queries * -(-count // 128)
    return -(-rows // 8) * 8


def spread_kernel(queries_ref, candidates_ref, out_ref, digits):
    targets = out_ref.shape[0]
    query_rows = queries_ref.shape[0]
    local_queries, count = candidates_ref.shape
    id_rows = digits.shape[0] // 2
    digits[...] = jnp.full(digits.shape, NOBODY, jnp.float32)
    row = 0
    for q in range(local_queries):
        for start in range(0, count, 128):
            size = min(128, count - start)
            ids = candidates_ref[q : q + 1, start : start + size]
            high = quotient(ids, DIGIT)
            digits[row : row + 1, 0:size] = (ids - high * DIGIT).astype(jnp.float32)
            digits[id_rows + row : id_rows + row + 1, 0:size] = high.astype(jnp.float32)
            row += 1
    queries = queries_ref[...]
    coded = digits[...].astype(jnp.bfloat16)

    def copy(t, carry):
        out_ref[t, 0:query_rows, :] = queries
        out_ref[t, query_rows:, :] = coded
        return carry

    lax.fori_loop(0, targets, copy, 0)


def spread(queries, candidates, targets):
    query_rows, width = queries.shape
    id_rows = id_rows_of(*candidates.shape)
    return pl.pallas_call(
        spread_kernel,
        out_shape=jax.ShapeDtypeStruct((targets, query_rows + 2 * id_rows, width), jnp.bfloat16),
        in_specs=[VMEM, VMEM],
        out_specs=VMEM,
        scratch_shapes=[pltpu.VMEM((2 * id_rows, width), jnp.float32)],
        compiler_params=granted(16),
        name="spread",
    )(pinned(queries), pinned(candidates))


def widen_kernel(half_ref, own_ref, other_ref, table, staged, sems):
    half_rows = own_ref.shape[0]
    half = half_ref[0]
    piece = half_rows // PIECES
    copies = []
    for source, ref in enumerate((own_ref, other_ref)):
        for k in range(PIECES):
            at = pl.ds(k * piece, piece)
            sem = sems.at[source * PIECES + k]
            copies.append(pltpu.make_async_copy(ref.at[at], staged.at[source, at], sem))
            copies[-1].start()
    for source in range(2):
        base = (half if source == 0 else 1 - half) * half_rows
        for k in range(PIECES):
            copies[source * PIECES + k].wait()
            to = pl.ds(pl.multiple_of(base + k * piece, piece), piece)
            table[to, :] = staged[source, pl.ds(k * piece, piece), :].astype(jnp.float32)


def widen(half, own, other):
    half_rows, width = own.shape
    return pl.pallas_call(
        widen_kernel,
        out_shape=pltpu.VMEM((2 * half_rows, width), jnp.float32),
        in_specs=[SMEM, HBM, HBM],
        out_specs=VMEM,
        scratch_shapes=[
            pltpu.VMEM((2, half_rows, width), jnp.bfloat16),
            pltpu.SemaphoreType.DMA((2 * PIECES,)),
        ],
        compiler_params=granted(16),
        cost_estimate=pl.CostEstimate(flops=10**7, bytes_accessed=10**7, transcendentals=0),
        name="widen",
    )(half, pinned(own), pinned(other))


def score_kernel(
    token_count,
    query_rows,
    base_ref,
    codes_hbm,
    lengths_hbm,
    gathered_ref,
    table,
    residuals_ref,
    out_ref,
    codes_ref,
    lengths_ref,
    at_ref,
    residual_rows,
    rows,
    embedded,
    turned,
    so_far,
    largest,
    sems,
):
    passages = lengths_ref.shape[0]
    tokens = codes_ref.shape[0]
    slots = tokens // passages
    targets, sent_rows, width = gathered_ref.shape
    id_rows = (sent_rows - query_rows) // 2
    blocks, _, block = turned.shape
    lengths_copy = pltpu.make_async_copy(lengths_hbm, lengths_ref, sems.at[0])
    codes_copy = pltpu.make_async_copy(codes_hbm, codes_ref, sems.at[1])
    residual_copy = pltpu.make_async_copy(residuals_ref, residual_rows, sems.at[2])
    lengths_copy.start()
    codes_copy.start()
    residual_copy.start()

    words = -(-passages // 32)
    shape = (id_rows, width)

    def collect(t, masks):
        low = gathered_ref[t, query_rows : query_rows + id_rows, :].astype(jnp.float32)
        high = gathered_ref[t, query_rows + id_rows :, :].astype(jnp.float32)
        local = (high * DIGIT + low).astype(jnp.int32) - base_ref[0]
        bits = lax.shift_left(jnp.ones(shape, jnp.int32), local & 31)
        word = lax.shift_right_arithmetic(local, 5)
        return tuple(mask | jnp.where(word == w, bits, 0) for w, mask in enumerate(masks))

    empty = tuple(jnp.zeros(shape, jnp.int32) for _ in range(words))
    masks = lax.fori_loop(0, targets, collect, empty, unroll=min(8, targets))
    joined = []
    for mask in masks:
        folded = mask[0:8]
        for k in range(8, id_rows, 8):
            folded = folded | mask[k : k + 8]
        for shift in (4, 2, 1):
            folded = folded | pltpu.roll(folded, shift, 0)
        for shift in (64, 32, 16, 8, 4, 2, 1):
            folded = folded | pltpu.roll(folded, shift, 1)
        joined.append(folded[0, 0])

    per_device = block // query_rows

    def turn(b, carry):
        vectors = gathered_ref[pl.ds(b * per_device, per_device), 0:query_rows, :]
        ready = normalized(vectors.reshape(block, width).astype(jnp.float32))
        turned[b] = ready.astype(jnp.float32).T.astype(jnp.bfloat16)
        largest[b] = jnp.zeros(largest.shape[1:], jnp.float32)
        return carry

    lax.fori_loop(0, blocks, turn, 0)

    lengths_copy.wait()
    chunks = jnp.int32(0)
    for w in range(words):

        def listing(k, listed):
            p = w * 32 + k
            for j in range(slots // CHUNK):
                at_ref[listed + j] = p * slots + j * CHUNK
            wanted = lax.shift_right_logical(joined[w], k) & 1
            return listed + wanted * quotient(lengths_ref[p] + CHUNK - 1, CHUNK)

        chunks = lax.fori_loop(0, min(32, passages - w * 32), listing, chunks, unroll=4)
    for k in range(GROUP):
        at_ref[chunks + k] = tokens
    groups = quotient(chunks + GROUP - 1, GROUP)
    codes_copy.wait()
    residual_copy.wait()

    slot_numbers = lax.broadcasted_iota(jnp.int32, (CHUNK, width), 0)
    single = table.reshape(table.shape[0], 1, width)

    def fetch(g, k):
        at = jnp.minimum(at_ref[g * GROUP + k], tokens - CHUNK)
        for j in range(CHUNK):
            rows[pl.ds(k * CHUNK + j, 1), :] = single[codes_ref[at + j]]

    def finish(g, k):
        at = jnp.minimum(at_ref[g * GROUP + k], tokens - CHUNK)
        p = quotient(at, slots)
        live = lengths_ref[p] - (at - p * slots)
        near = residual_rows[pl.ds(pl.multiple_of(at, CHUNK), CHUNK), :]
        vectors = rows[pl.ds(k * CHUNK, CHUNK), :] + near.astype(jnp.float32)
        vectors = jnp.where(slot_numbers < live, vectors, vectors[0:1, :])
        return normalized(vectors)

    def score(g, b):
        similar = jnp.dot(embedded[...], turned[b], preferred_element_type=jnp.float32)
        parts = jnp.max(similar.reshape(GROUP, CHUNK // 8, 8, block), axis=1)
        best = so_far[b]
        for k in range(GROUP):
            start = at_ref[g * GROUP + k]
            p = quotient(start, slots)
            best = jnp.where(start == p * slots, parts[k], jnp.maximum(best, parts[k]))
            at = pl.multiple_of(p * 8, 8)
            for lane in range(block // 128):
                largest[b, lane, pl.ds(at, 8), :] = best[:, lane * 128 : (lane + 1) * 128]
        so_far[b] = best

    def step(i, carry):
        scored = jnp.maximum(i - 2, 0)
        if blocks == 1:
            score(scored, 0)
        else:

            def score_block(b, inner):
                score(scored, b)
                return inner

            lax.fori_loop(0, blocks, score_block, 0)
        fetched = jnp.minimum(i, groups - 1)
        finished = jnp.maximum(jnp.minimum(i - 1, groups - 1), 0)
        done = []
        for k in range(GROUP):
            done.append(finish(finished, k))
            fetch(fetched, k)
        for k in range(GROUP):
            embedded[pl.ds(k * CHUNK, CHUNK), :] = done[k]
        return carry

    lax.fori_loop(0, jnp.where(groups > 0, groups + 2, 0), step, 0)

    per_block = block // token_count
    owner = lax.broadcasted_iota(jnp.int32, (per_block, block), 0)
    token_of = quotient(lax.broadcasted_iota(jnp.int32, (per_block, block), 1), token_count)
    summing = (owner == token_of).astype(jnp.bfloat16)

    def total(b, carry):
        kept = []
        for lane in range(block // 128):
            best = largest[b, lane, pl.ds(0, passages, stride=8), :]
            for k in range(1, 8):
                best = jnp.maximum(best, largest[b, lane, pl.ds(k, passages, stride=8), :])
            kept.append(best)
        left = jnp.concatenate(kept, axis=1)
        sums = jnp.zeros((per_block, passages), jnp.float32)
        for _ in range(3):
            part = left.astype(jnp.bfloat16)
            left = left - part.astype(jnp.float32)
            sums = sums + lax.dot_general(
                summing, part, (((1,), (1,)), ((), ())), preferred_element_type=jnp.float32
            )
        out_ref[pl.ds(pl.multiple_of(b * per_block, per_block), per_block), :] = sums
        return carry

    lax.fori_loop(0, blocks, total, 0)


def score_all(base, token_codes, lengths, gathered, table, residuals, query_rows, token_count):
    passages, slots, width = residuals.shape
    targets = gathered.shape[0]
    tokens = passages * slots
    block = min(QUERY_BLOCK, targets * query_rows)
    blocks = targets * query_rows // block
    return pl.pallas_call(
        functools.partial(score_kernel, token_count, query_rows),
        out_shape=jax.ShapeDtypeStruct(
            (targets * query_rows // token_count, passages), jnp.float32
        ),
        in_specs=[SMEM, HBM, HBM, VMEM, VMEM, HBM],
        out_specs=VMEM,
        scratch_shapes=[
            pltpu.SMEM((tokens,), jnp.int32),
            pltpu.SMEM((passages,), jnp.int32),
            pltpu.SMEM((tokens // CHUNK + slots // CHUNK + GROUP,), jnp.int32),
            pltpu.VMEM((tokens, width), jnp.bfloat16),
            pltpu.VMEM((GROUP * CHUNK, width), jnp.float32),
            pltpu.VMEM((GROUP * CHUNK, width), jnp.bfloat16),
            pltpu.VMEM((blocks, width, block), jnp.bfloat16),
            pltpu.VMEM((blocks, 8, block), jnp.float32),
            pltpu.VMEM((blocks, block // 128, (passages + 1) * 8, 128), jnp.float32),
            pltpu.SemaphoreType.DMA((3,)),
        ],
        compiler_params=granted(40),
        name="score",
    )(
        base,
        pinned(token_codes.reshape(tokens)),
        pinned(lengths),
        gathered,
        pinned(table, pltpu.VMEM),
        pinned(residuals.reshape(tokens, width)),
    )


def pick_kernel(passages, candidates_ref, returned_ref, out_ref):
    local_queries, count = candidates_ref.shape
    targets = returned_ref.shape[0]
    passage_numbers = lax.broadcasted_iota(jnp.int32, (passages, count), 0)
    target_numbers = lax.broadcasted_iota(jnp.int32, (targets, count), 0)
    for q in range(local_queries):
        wanted = candidates_ref[q : q + 1, :]
        target = quotient(wanted, passages)
        hits = (passage_numbers == wanted - target * passages).astype(jnp.bfloat16)
        left = returned_ref[:, q * passages : (q + 1) * passages]
        picked = jnp.zeros((targets, count), jnp.float32)
        for _ in range(3):
            part = left.astype(jnp.bfloat16)
            left = left - part.astype(jnp.float32)
            picked = picked + jnp.dot(part, hits, preferred_element_type=jnp.float32)
        kept = jnp.where(target_numbers == target, picked, 0.0)
        out_ref[q : q + 1, :] = jnp.sum(kept, axis=0, keepdims=True)


def pick(candidates, returned, passages):
    return pl.pallas_call(
        functools.partial(pick_kernel, passages),
        out_shape=jax.ShapeDtypeStruct(candidates.shape, jnp.float32),
        in_specs=[VMEM, VMEM],
        out_specs=VMEM,
        compiler_params=granted(8),
        name="pick",
    )(candidates, pinned(returned, pltpu.VMEM))


def body(queries, candidates, token_codes, residuals, lengths, centroids):
    local_queries, token_count, width = queries.shape
    targets = lax.axis_size("shard") * lax.axis_size("sub")
    passages = token_codes.shape[0]
    query_rows = local_queries * token_count
    half = lax.axis_index("sub").astype(jnp.int32)
    me = lax.axis_index("shard").astype(jnp.int32) * lax.axis_size("sub") + half
    other = lax.ppermute(centroids, "sub", [(0, 1), (1, 0)])
    sent = spread(queries.reshape(query_rows, width), candidates, targets)
    gathered = lax.all_to_all(sent, ("shard", "sub"), split_axis=0, concat_axis=0, tiled=True)
    table = widen(half.reshape(1), centroids, other)
    base = (me * passages).reshape(1)
    scores = score_all(
        base, token_codes, lengths, gathered, table, residuals, query_rows, token_count
    )
    returned = lax.all_to_all(
        scores.reshape(targets, local_queries * passages),
        ("shard", "sub"),
        split_axis=0,
        concat_axis=0,
        tiled=True,
    )
    return pick(candidates, returned, passages)


def solution(mesh):
    placed = (
        P(("groups", "shard", "sub"), None, None),
        P(("groups", "shard", "sub"), None),
        P(("groups", "shard", "sub"), None),
        P(("groups", "shard", "sub"), None, None),
        P(("groups", "shard", "sub")),
        P(("groups", "shard", "sub"), None),
    )
    return jax.shard_map(
        body,
        mesh=mesh,
        in_specs=placed,
        out_specs=P(("groups", "shard", "sub"), None),
        check_vma=False,
    )
```

```python
import functools

import jax
import jax.numpy as jnp
from jax import lax
from jax.experimental import pallas as pl
from jax.experimental.pallas import tpu as pltpu
from jax.sharding import PartitionSpec as P

CHUNK = 16
GROUP = 16
SCORE_GROUP = 32
PIECES = 4
QUERY_BLOCK = 512
SMEM = pl.BlockSpec(memory_space=pltpu.SMEM)
VMEM = pl.BlockSpec(memory_space=pltpu.VMEM)
HBM = pl.BlockSpec(memory_space=pltpu.HBM)


def normalized(vectors):
    total = jnp.sum(vectors * vectors, axis=-1, keepdims=True)
    return (vectors * lax.rsqrt(total + 1e-06)).astype(jnp.bfloat16)


def quotient(number, divisor):
    if divisor & (divisor - 1) == 0:
        return lax.shift_right_logical(number, divisor.bit_length() - 1)
    return lax.div(number, divisor)


def pinned(array, space=pltpu.HBM):
    return pltpu.with_memory_space_constraint(array, space)


def granted(mebibytes):
    return pltpu.CompilerParams(vmem_limit_bytes=mebibytes * 1024 * 1024)


def widen_kernel(half_ref, own_hbm, other_ref, residuals_hbm, table, residuals, staged, sems):
    half_rows = own_hbm.shape[0]
    half = half_ref[0]
    piece = half_rows // PIECES
    copies = []
    for k in range(PIECES):
        at = pl.ds(k * piece, piece)
        copies.append(pltpu.make_async_copy(own_hbm.at[at], staged.at[at], sems.at[k]))
        copies[-1].start()
    residual_copy = pltpu.make_async_copy(residuals_hbm, residuals, sems.at[PIECES])
    residual_copy.start()
    for source, ref in enumerate((other_ref, staged)):
        base = (1 - half if source == 0 else half) * half_rows
        for k in range(PIECES):
            if source == 1:
                copies[k].wait()
            to = pl.ds(pl.multiple_of(base + k * piece, piece), piece)
            table[to, :] = ref[pl.ds(k * piece, piece), :].astype(jnp.float32)
    residual_copy.wait()


def widen(half, own, other, residuals):
    half_rows, width = own.shape
    return pl.pallas_call(
        widen_kernel,
        out_shape=(
            pltpu.VMEM((2 * half_rows, width), jnp.float32),
            pltpu.VMEM(residuals.shape, jnp.bfloat16),
        ),
        in_specs=[SMEM, HBM, VMEM, HBM],
        out_specs=(VMEM, VMEM),
        scratch_shapes=[
            pltpu.VMEM((half_rows, width), jnp.bfloat16),
            pltpu.SemaphoreType.DMA((PIECES + 1,)),
        ],
        compiler_params=granted(4),
        cost_estimate=pl.CostEstimate(flops=10**7, bytes_accessed=10**7, transcendentals=0),
        name="widen",
    )(half, pinned(own), pinned(other, pltpu.VMEM), pinned(residuals))


def decode_kernel(
    codes_hbm,
    lengths_hbm,
    table,
    residuals,
    embedded,
    at_ref,
    codes_ref,
    lengths_ref,
    rows,
    sems,
):
    passages = lengths_ref.shape[0]
    tokens, width = residuals.shape
    slots = tokens // passages
    lengths_copy = pltpu.make_async_copy(lengths_hbm, lengths_ref, sems.at[0])
    codes_copy = pltpu.make_async_copy(codes_hbm, codes_ref, sems.at[1])
    lengths_copy.start()
    codes_copy.start()
    lengths_copy.wait()

    def listing(p, chunks):
        for k in range(slots // CHUNK):
            at_ref[chunks + k] = p * slots + k * CHUNK
        return chunks + quotient(lengths_ref[p] + CHUNK - 1, CHUNK)

    chunks = lax.fori_loop(0, passages, listing, 0, unroll=4)
    for k in range(SCORE_GROUP):
        at_ref[chunks + k] = tokens
    groups = quotient(chunks + GROUP - 1, GROUP)
    at_ref[at_ref.shape[0] - 1] = chunks
    codes_copy.wait()

    slot_numbers = lax.broadcasted_iota(jnp.int32, (CHUNK, width), 0)
    table_single = table.reshape(table.shape[0], 1, width)
    rows_single = rows.reshape(rows.shape[0], 1, width)

    def fetch(g, k):
        at = jnp.minimum(at_ref[g * GROUP + k], tokens - CHUNK)
        codes = codes_ref.at[pl.ds(at, CHUNK)]
        for j in range(CHUNK):
            rows_single[k * CHUNK + j] = table_single[codes[j]]

    def finish(g, k):
        at = jnp.minimum(at_ref[g * GROUP + k], tokens - CHUNK)
        p = quotient(at, slots)
        live = lengths_ref[p] - (at - p * slots)
        near = residuals[pl.ds(pl.multiple_of(at, CHUNK), CHUNK), :]
        vectors = rows[pl.ds(k * CHUNK, CHUNK), :] + near.astype(jnp.float32)
        vectors = jnp.where(slot_numbers < live, vectors, vectors[0:1, :])
        return normalized(vectors)

    def keep(g, done):
        for k in range(GROUP):
            start = pl.multiple_of((g * GROUP + k) * CHUNK, CHUNK)
            embedded[pl.ds(start, CHUNK), :] = done[k]

    for k in range(GROUP):
        fetch(0, k)

    def decode(g, carry):
        done = []
        for k in range(GROUP):
            done.append(finish(g - 1, k))
            fetch(g, k)
        keep(g - 1, done)
        return carry

    lax.fori_loop(1, groups, decode, 0)
    keep(groups - 1, [finish(groups - 1, k) for k in range(GROUP)])


def decode_all(token_codes, lengths, table, residuals):
    passages, slots = token_codes.shape
    tokens, width = residuals.shape
    most = tokens // CHUNK + 2 * SCORE_GROUP
    return pl.pallas_call(
        decode_kernel,
        out_shape=(
            jax.ShapeDtypeStruct((most * CHUNK, width), jnp.bfloat16),
            jax.ShapeDtypeStruct((most + 1,), jnp.int32),
        ),
        in_specs=[HBM, HBM, VMEM, VMEM],
        out_specs=(VMEM, SMEM),
        scratch_shapes=[
            pltpu.SMEM((tokens,), jnp.int32),
            pltpu.SMEM((passages,), jnp.int32),
            pltpu.VMEM((GROUP * CHUNK, width), jnp.float32),
            pltpu.SemaphoreType.DMA((2,)),
        ],
        compiler_params=granted(4),
        cost_estimate=pl.CostEstimate(flops=10**7, bytes_accessed=40 * 10**6, transcendentals=0),
        name="decode",
    )(
        pinned(token_codes.reshape(tokens)),
        pinned(lengths),
        pinned(table, pltpu.VMEM),
        pinned(residuals, pltpu.VMEM),
    )


def score_kernel(token_count, slots, at_ref, queries_ref, embedded, out_ref, turned, largest):
    passages = out_ref.shape[1]
    query_tokens = queries_ref.shape[0]
    block = min(QUERY_BLOCK, query_tokens)
    blocks = query_tokens // block
    groups = quotient(at_ref[at_ref.shape[0] - 1] + SCORE_GROUP - 1, SCORE_GROUP)
    per_block = block // token_count
    owner = lax.broadcasted_iota(jnp.int32, (per_block, block), 0)
    token_of = lax.broadcasted_iota(jnp.int32, (per_block, block), 1) // token_count
    summing = (owner == token_of).astype(jnp.bfloat16)

    def score_block(b, carry):
        at = pl.ds(pl.multiple_of(b * block, block), block)
        vectors = normalized(queries_ref[at, :].astype(jnp.float32))
        turned[...] = vectors.astype(jnp.float32).T.astype(jnp.bfloat16)

        def score(g, so_far):
            size = SCORE_GROUP * CHUNK
            at = pl.ds(pl.multiple_of(g * size, size), size)
            similar = jnp.dot(embedded[at, :], turned[...], preferred_element_type=jnp.float32)
            parts = jnp.max(similar.reshape(SCORE_GROUP, CHUNK // 8, 8, block), axis=1)
            for k in range(SCORE_GROUP):
                start = at_ref[g * SCORE_GROUP + k]
                p = quotient(start, slots)
                so_far = jnp.where(start == p * slots, parts[k], jnp.maximum(so_far, parts[k]))
                at = pl.multiple_of(p * 8, 8)
                for lane in range(block // 128):
                    largest[lane, pl.ds(at, 8), :] = so_far[:, lane * 128 : (lane + 1) * 128]
            return so_far

        lax.fori_loop(0, groups, score, jnp.zeros((8, block), jnp.float32))
        kept = []
        for lane in range(block // 128):
            best = largest[lane, pl.ds(0, passages, stride=8), :]
            for k in range(1, 8):
                best = jnp.maximum(best, largest[lane, pl.ds(k, passages, stride=8), :])
            kept.append(best)
        best = jnp.concatenate(kept, axis=1)
        sums = jnp.zeros((per_block, passages), jnp.float32)
        for _ in range(3):
            part = best.astype(jnp.bfloat16)
            best = best - part.astype(jnp.float32)
            sums = sums + lax.dot_general(
                summing, part, (((1,), (1,)), ((), ())), preferred_element_type=jnp.float32
            )
        out_ref[pl.ds(pl.multiple_of(b * per_block, per_block), per_block), :] = sums
        return carry

    lax.fori_loop(0, blocks, score_block, 0)


def score_all(starts, query_rows, embedded, passages, slots, token_count):
    query_tokens, width = query_rows.shape
    block = min(QUERY_BLOCK, query_tokens)
    blocks = query_tokens // block
    return pl.pallas_call(
        functools.partial(score_kernel, token_count, slots),
        out_shape=jax.ShapeDtypeStruct((query_tokens // token_count, passages), jnp.float32),
        in_specs=[SMEM, VMEM, VMEM],
        out_specs=VMEM,
        scratch_shapes=[
            pltpu.VMEM((width, block), jnp.bfloat16),
            pltpu.VMEM((block // 128, (passages + 1) * 8, 128), jnp.float32),
        ],
        compiler_params=granted(8 + 2 * blocks),
        name="score",
    )(starts, query_rows, embedded)


def pick_kernel(passages, candidates_ref, returned_ref, out_ref):
    local_queries, count = candidates_ref.shape
    targets = returned_ref.shape[0]
    passage_numbers = lax.broadcasted_iota(jnp.int32, (passages, count), 0)
    target_numbers = lax.broadcasted_iota(jnp.int32, (targets, count), 0)
    for q in range(local_queries):
        wanted = candidates_ref[q : q + 1, :]
        target = quotient(wanted, passages)
        hits = (passage_numbers == wanted - target * passages).astype(jnp.bfloat16)
        left = returned_ref[:, q * passages : (q + 1) * passages]
        picked = jnp.zeros((targets, count), jnp.float32)
        for _ in range(3):
            part = left.astype(jnp.bfloat16)
            left = left - part.astype(jnp.float32)
            picked = picked + jnp.dot(part, hits, preferred_element_type=jnp.float32)
        kept = jnp.where(target_numbers == target, picked, 0.0)
        out_ref[q : q + 1, :] = jnp.sum(kept, axis=0, keepdims=True)


def pick(candidates, returned, passages):
    return pl.pallas_call(
        functools.partial(pick_kernel, passages),
        out_shape=jax.ShapeDtypeStruct(candidates.shape, jnp.float32),
        in_specs=[VMEM, VMEM],
        out_specs=VMEM,
        compiler_params=granted(8),
        name="pick",
    )(candidates, pltpu.with_memory_space_constraint(returned, pltpu.VMEM))


def body(queries, candidates, token_codes, residuals, lengths, centroids):
    local_queries, token_count, width = queries.shape
    targets = lax.axis_size("shard") * lax.axis_size("sub")
    passages, slots = token_codes.shape
    half = lax.axis_index("sub").astype(jnp.int32)
    other = lax.ppermute(centroids, "sub", [(0, 1), (1, 0)])
    own_rows = queries.reshape(1, local_queries * token_count, width)
    sent = jnp.broadcast_to(own_rows, (targets,) + own_rows.shape[1:])
    gathered = lax.all_to_all(sent, ("shard", "sub"), split_axis=0, concat_axis=0, tiled=True)
    query_rows = gathered.reshape(targets * local_queries * token_count, width)
    flat = residuals.reshape(passages * slots, width)
    table, near = widen(half.reshape(1), centroids, other, flat)
    embedded, starts = decode_all(token_codes, lengths, table, near)
    scores = score_all(starts, query_rows, embedded, passages, slots, token_count)
    returned = lax.all_to_all(
        scores.reshape(targets, local_queries * passages),
        ("shard", "sub"),
        split_axis=0,
        concat_axis=0,
        tiled=True,
    )
    return pick(candidates, returned, passages)


def solution(mesh):
    placed = (
        P(("groups", "shard", "sub"), None, None),
        P(("groups", "shard", "sub"), None),
        P(("groups", "shard", "sub"), None),
        P(("groups", "shard", "sub"), None, None),
        P(("groups", "shard", "sub")),
        P(("groups", "shard", "sub"), None),
    )
    return jax.shard_map(
        body,
        mesh=mesh,
        in_specs=placed,
        out_specs=P(("groups", "shard", "sub"), None),
        check_vma=False,
    )
```

```python
import functools

import jax
import jax.numpy as jnp
from jax import lax
from jax.experimental import pallas as pl
from jax.experimental.pallas import tpu as pltpu
from jax.sharding import PartitionSpec as P

CHUNK = 16
GROUP = 16
PIECES = 4
QUERY_BLOCK = 512
DIGIT = 128
NOBODY = 255.0
SMEM = pl.BlockSpec(memory_space=pltpu.SMEM)
VMEM = pl.BlockSpec(memory_space=pltpu.VMEM)
HBM = pl.BlockSpec(memory_space=pltpu.HBM)


def pinned(array, space=pltpu.HBM):
    return pltpu.with_memory_space_constraint(array, space)


def granted(mebibytes):
    return pltpu.CompilerParams(vmem_limit_bytes=mebibytes * 1024 * 1024)


def quotient(number, divisor):
    if divisor & (divisor - 1) == 0:
        return lax.shift_right_logical(number, divisor.bit_length() - 1)
    return lax.div(number, divisor)


def normalized(vectors):
    total = jnp.sum(vectors * vectors, axis=-1, keepdims=True)
    return (vectors * lax.rsqrt(total + 1e-06)).astype(jnp.bfloat16)


def id_rows_of(local_queries, count):
    rows = local_queries * -(-count // 128)
    return -(-rows // 8) * 8


def pack_kernel(queries_ref, candidates_ref, out_ref, digits):
    query_rows = queries_ref.shape[0]
    local_queries, count = candidates_ref.shape
    id_rows = digits.shape[0] // 2
    digits[...] = jnp.full(digits.shape, NOBODY, jnp.float32)
    row = 0
    for q in range(local_queries):
        for start in range(0, count, 128):
            size = min(128, count - start)
            ids = candidates_ref[q : q + 1, start : start + size]
            high = quotient(ids, DIGIT)
            digits[row : row + 1, 0:size] = (ids - high * DIGIT).astype(jnp.float32)
            digits[id_rows + row : id_rows + row + 1, 0:size] = high.astype(jnp.float32)
            row += 1
    out_ref[0:query_rows, :] = queries_ref[...]
    out_ref[query_rows:, :] = digits[...].astype(jnp.bfloat16)


def pack(queries, candidates):
    query_rows, width = queries.shape
    id_rows = id_rows_of(*candidates.shape)
    return pl.pallas_call(
        pack_kernel,
        out_shape=pltpu.VMEM((query_rows + 2 * id_rows, width), jnp.bfloat16),
        in_specs=[VMEM, VMEM],
        out_specs=VMEM,
        scratch_shapes=[pltpu.VMEM((2 * id_rows, width), jnp.float32)],
        compiler_params=granted(4),
        name="pack",
    )(pinned(queries), pinned(candidates))


def widen_own_kernel(half_ref, own_hbm, residuals_hbm, table, residuals, staged, sems):
    half_rows = own_hbm.shape[0]
    base = half_ref[0] * half_rows
    piece = half_rows // PIECES
    copies = []
    for k in range(PIECES):
        at = pl.ds(k * piece, piece)
        copies.append(pltpu.make_async_copy(own_hbm.at[at], staged.at[at], sems.at[k]))
        copies[-1].start()
    residual_copy = pltpu.make_async_copy(residuals_hbm, residuals, sems.at[PIECES])
    residual_copy.start()
    for k in range(PIECES):
        copies[k].wait()
        to = pl.ds(pl.multiple_of(base + k * piece, piece), piece)
        table[to, :] = staged[pl.ds(k * piece, piece), :].astype(jnp.float32)
    residual_copy.wait()


def widen_own(half, own, residuals):
    half_rows, width = own.shape
    return pl.pallas_call(
        widen_own_kernel,
        out_shape=(
            pltpu.VMEM((2 * half_rows, width), jnp.float32),
            pltpu.VMEM(residuals.shape, jnp.bfloat16),
        ),
        in_specs=[SMEM, HBM, HBM],
        out_specs=(VMEM, VMEM),
        scratch_shapes=[
            pltpu.VMEM((half_rows, width), jnp.bfloat16),
            pltpu.SemaphoreType.DMA((PIECES + 1,)),
        ],
        compiler_params=granted(4),
        cost_estimate=pl.CostEstimate(flops=10**7, bytes_accessed=5 * 10**6, transcendentals=0),
        name="widen_own",
    )(half, pinned(own), pinned(residuals))


def widen_other_kernel(half_ref, other_ref, partial_ref, table):
    half_rows = other_ref.shape[0]
    base = (1 - half_ref[0]) * half_rows
    piece = half_rows // PIECES
    for k in range(PIECES):
        to = pl.ds(pl.multiple_of(base + k * piece, piece), piece)
        table[to, :] = other_ref[pl.ds(k * piece, piece), :].astype(jnp.float32)


def widen_other(half, other, partial):
    return pl.pallas_call(
        widen_other_kernel,
        out_shape=pltpu.VMEM(partial.shape, jnp.float32),
        in_specs=[SMEM, VMEM, VMEM],
        out_specs=VMEM,
        input_output_aliases={2: 0},
        compiler_params=granted(4),
        cost_estimate=pl.CostEstimate(flops=10**7, bytes_accessed=3 * 10**6, transcendentals=0),
        name="widen_other",
    )(half, pinned(other, pltpu.VMEM), pinned(partial, pltpu.VMEM))


def score_kernel(
    token_count,
    query_rows,
    me_ref,
    codes_hbm,
    lengths_hbm,
    gathered_ref,
    table,
    residuals,
    out_ref,
    codes_ref,
    lengths_ref,
    at_ref,
    rows,
    turned,
    so_far,
    largest,
    sems,
):
    passages = lengths_ref.shape[0]
    tokens = codes_ref.shape[0]
    slots = tokens // passages
    targets, sent_rows, width = gathered_ref.shape
    id_rows = (sent_rows - query_rows) // 2
    blocks, _, block = turned.shape
    lengths_copy = pltpu.make_async_copy(lengths_hbm, lengths_ref, sems.at[0])
    codes_copy = pltpu.make_async_copy(codes_hbm, codes_ref, sems.at[1])
    lengths_copy.start()
    codes_copy.start()
    base = me_ref[0] * passages

    words = -(-passages // 32)
    shape = (id_rows, width)

    def collect(t, masks):
        low = gathered_ref[t, query_rows : query_rows + id_rows, :].astype(jnp.float32)
        high = gathered_ref[t, query_rows + id_rows :, :].astype(jnp.float32)
        local = (high * DIGIT + low).astype(jnp.int32) - base
        bits = lax.shift_left(jnp.ones(shape, jnp.int32), local & 31)
        word = lax.shift_right_arithmetic(local, 5)
        return tuple(mask | jnp.where(word == w, bits, 0) for w, mask in enumerate(masks))

    empty = tuple(jnp.zeros(shape, jnp.int32) for _ in range(words))
    masks = lax.fori_loop(0, targets, collect, empty, unroll=min(8, targets))
    joined = []
    for mask in masks:
        folded = mask[0:8]
        for k in range(8, id_rows, 8):
            folded = folded | mask[k : k + 8]
        for shift in (4, 2, 1):
            folded = folded | pltpu.roll(folded, shift, 0)
        for shift in (64, 32, 16, 8, 4, 2, 1):
            folded = folded | pltpu.roll(folded, shift, 1)
        joined.append(folded[0, 0])

    per_device = block // query_rows

    def turn(b, carry):
        vectors = gathered_ref[pl.ds(b * per_device, per_device), 0:query_rows, :]
        ready = normalized(vectors.reshape(block, width).astype(jnp.float32))
        turned[b] = ready.astype(jnp.float32).T.astype(jnp.bfloat16)
        largest[b] = jnp.zeros(largest.shape[1:], jnp.float32)
        return carry

    lax.fori_loop(0, blocks, turn, 0)

    lengths_copy.wait()
    chunks = jnp.int32(0)
    for w in range(words):

        def listing(k, listed):
            p = w * 32 + k
            for j in range(slots // CHUNK):
                at_ref[listed + j] = p * slots + j * CHUNK
            wanted = lax.shift_right_logical(joined[w], k) & 1
            return listed + wanted * quotient(lengths_ref[p] + CHUNK - 1, CHUNK)

        chunks = lax.fori_loop(0, min(32, passages - w * 32), listing, chunks, unroll=4)
    for k in range(GROUP):
        at_ref[chunks + k] = tokens
    groups = quotient(chunks + GROUP - 1, GROUP)
    codes_copy.wait()

    slot_numbers = lax.broadcasted_iota(jnp.int32, (CHUNK, width), 0)
    table_single = table.reshape(table.shape[0], 1, width)
    rows_single = rows.reshape(rows.shape[0], 1, width)

    def fetch(g, k):
        at = jnp.minimum(at_ref[g * GROUP + k], tokens - CHUNK)
        codes = codes_ref.at[pl.ds(at, CHUNK)]
        for j in range(CHUNK):
            rows_single[k * CHUNK + j] = table_single[codes[j]]

    def finish(g, k):
        at = jnp.minimum(at_ref[g * GROUP + k], tokens - CHUNK)
        p = quotient(at, slots)
        live = lengths_ref[p] - (at - p * slots)
        near = residuals[pl.ds(pl.multiple_of(at, CHUNK), CHUNK), :]
        vectors = rows[pl.ds(k * CHUNK, CHUNK), :] + near.astype(jnp.float32)
        vectors = jnp.where(slot_numbers < live, vectors, vectors[0:1, :])
        return normalized(vectors)

    def score(g, b, embedded):
        similar = jnp.dot(embedded, turned[b], preferred_element_type=jnp.float32)
        parts = jnp.max(similar.reshape(GROUP, CHUNK // 8, 8, block), axis=1)
        best = so_far[b]
        for k in range(GROUP):
            start = at_ref[g * GROUP + k]
            p = quotient(start, slots)
            best = jnp.where(start == p * slots, parts[k], jnp.maximum(best, parts[k]))
            at = pl.multiple_of(p * 8, 8)
            for lane in range(block // 128):
                largest[b, lane, pl.ds(at, 8), :] = best[:, lane * 128 : (lane + 1) * 128]
        so_far[b] = best

    def step(i, carry):
        fetched = jnp.minimum(i, groups - 1)
        finished = jnp.maximum(i - 1, 0)
        done = []
        for k in range(GROUP):
            done.append(finish(finished, k))
            fetch(fetched, k)
        embedded = jnp.concatenate(done, axis=0)
        if blocks == 1:
            score(finished, 0, embedded)
        else:

            def score_block(b, inner):
                score(finished, b, embedded)
                return inner

            lax.fori_loop(0, blocks, score_block, 0)
        return carry

    lax.fori_loop(0, jnp.where(groups > 0, groups + 1, 0), step, 0)

    per_block = block // token_count
    local_queries = query_rows // token_count
    owner = lax.broadcasted_iota(jnp.int32, (per_block, block), 0)
    token_of = quotient(lax.broadcasted_iota(jnp.int32, (per_block, block), 1), token_count)
    block_targets = per_block // local_queries
    near_me = me_ref[0] & (block_targets - 1)
    far_me = quotient(me_ref[0], block_targets)
    owner_target = quotient(owner, local_queries)
    relative = (owner_target ^ near_me) * local_queries + owner - owner_target * local_queries
    summing = (relative == token_of).astype(jnp.bfloat16)

    def total(b, carry):
        kept = []
        for lane in range(block // 128):
            best = largest[b, lane, pl.ds(0, passages, stride=8), :]
            for k in range(1, 8):
                best = jnp.maximum(best, largest[b, lane, pl.ds(k, passages, stride=8), :])
            kept.append(best)
        left = jnp.concatenate(kept, axis=1)
        sums = jnp.zeros((per_block, passages), jnp.float32)
        for _ in range(3):
            part = left.astype(jnp.bfloat16)
            left = left - part.astype(jnp.float32)
            sums = sums + lax.dot_general(
                summing, part, (((1,), (1,)), ((), ())), preferred_element_type=jnp.float32
            )
        to = pl.multiple_of((b ^ far_me) * per_block, per_block)
        out_ref[pl.ds(to, per_block), :] = sums
        return carry

    lax.fori_loop(0, blocks, total, 0)


def score_all(me, token_codes, lengths, gathered, table, residuals, query_rows, token_count):
    passages, slots = token_codes.shape
    width = residuals.shape[1]
    targets = gathered.shape[0]
    tokens = passages * slots
    block = min(QUERY_BLOCK, targets * query_rows)
    blocks = targets * query_rows // block
    return pl.pallas_call(
        functools.partial(score_kernel, token_count, query_rows),
        out_shape=jax.ShapeDtypeStruct(
            (targets * query_rows // token_count, passages), jnp.float32
        ),
        in_specs=[SMEM, HBM, HBM, VMEM, VMEM, VMEM],
        out_specs=VMEM,
        scratch_shapes=[
            pltpu.SMEM((tokens,), jnp.int32),
            pltpu.SMEM((passages,), jnp.int32),
            pltpu.SMEM((tokens // CHUNK + slots // CHUNK + GROUP,), jnp.int32),
            pltpu.VMEM((GROUP * CHUNK, width), jnp.float32),
            pltpu.VMEM((blocks, width, block), jnp.bfloat16),
            pltpu.VMEM((blocks, 8, block), jnp.float32),
            pltpu.VMEM((blocks, block // 128, (passages + 1) * 8, 128), jnp.float32),
            pltpu.SemaphoreType.DMA((2,)),
        ],
        compiler_params=granted(8 + 2 * blocks),
        name="score",
    )(
        me,
        pinned(token_codes.reshape(tokens)),
        pinned(lengths),
        gathered,
        pinned(table, pltpu.VMEM),
        pinned(residuals, pltpu.VMEM),
    )


def pick_kernel(passages, candidates_ref, returned_ref, out_ref):
    local_queries, count = candidates_ref.shape
    targets = returned_ref.shape[0]
    passage_numbers = lax.broadcasted_iota(jnp.int32, (passages, count), 0)
    target_numbers = lax.broadcasted_iota(jnp.int32, (targets, count), 0)
    for q in range(local_queries):
        wanted = candidates_ref[q : q + 1, :]
        target = quotient(wanted, passages)
        hits = (passage_numbers == wanted - target * passages).astype(jnp.bfloat16)
        left = returned_ref[:, q * passages : (q + 1) * passages]
        picked = jnp.zeros((targets, count), jnp.float32)
        for _ in range(3):
            part = left.astype(jnp.bfloat16)
            left = left - part.astype(jnp.float32)
            picked = picked + jnp.dot(part, hits, preferred_element_type=jnp.float32)
        kept = jnp.where(target_numbers == target, picked, 0.0)
        out_ref[q : q + 1, :] = jnp.sum(kept, axis=0, keepdims=True)


def pick(candidates, returned, passages):
    return pl.pallas_call(
        functools.partial(pick_kernel, passages),
        out_shape=jax.ShapeDtypeStruct(candidates.shape, jnp.float32),
        in_specs=[VMEM, VMEM],
        out_specs=VMEM,
        compiler_params=granted(8),
        name="pick",
    )(candidates, pinned(returned, pltpu.VMEM))


def gather_relative(own, targets):
    bits = targets.bit_length() - 1
    held = own[None, None]
    for first in range(bits - 1, -1, -1):
        pairs = [(device, device ^ (1 << first)) for device in range(targets)]
        received = lax.ppermute(held, ("shard", "sub"), pairs)
        held = jnp.concatenate([held, received], axis=1)
        if first > 0:
            held = held.reshape((-1, 1) + own.shape)
    return held.reshape((targets,) + own.shape)


def body(queries, candidates, token_codes, residuals, lengths, centroids):
    local_queries, token_count, width = queries.shape
    targets = lax.axis_size("shard") * lax.axis_size("sub")
    passages, slots = token_codes.shape
    query_rows = local_queries * token_count
    half = lax.axis_index("sub").astype(jnp.int32)
    me = lax.axis_index("shard").astype(jnp.int32) * lax.axis_size("sub") + half
    half = half.reshape(1)
    other = lax.ppermute(centroids, "sub", [(0, 1), (1, 0)])
    sent = pack(queries.reshape(query_rows, width), candidates)
    gathered = gather_relative(sent, targets)
    partial, near = widen_own(half, centroids, residuals.reshape(passages * slots, width))
    table = widen_other(half, other, partial)
    scores = score_all(
        me.reshape(1), token_codes, lengths, gathered, table, near, query_rows, token_count
    )
    returned = lax.all_to_all(
        scores.reshape(targets, local_queries * passages),
        ("shard", "sub"),
        split_axis=0,
        concat_axis=0,
        tiled=True,
    )
    return pick(candidates, returned, passages)


def solution(mesh):
    placed = (
        P(("groups", "shard", "sub"), None, None),
        P(("groups", "shard", "sub"), None),
        P(("groups", "shard", "sub"), None),
        P(("groups", "shard", "sub"), None, None),
        P(("groups", "shard", "sub")),
        P(("groups", "shard", "sub"), None),
    )
    return jax.shard_map(
        body,
        mesh=mesh,
        in_specs=placed,
        out_specs=P(("groups", "shard", "sub"), None),
        check_vma=False,
    )
```

```python
import functools

import jax
import jax.numpy as jnp
from jax import lax
from jax.experimental import pallas as pl
from jax.experimental.pallas import tpu as pltpu
from jax.sharding import PartitionSpec as P

CHUNK = 16
GROUP = 16
SCORE_GROUP = 32
PIECES = 4
QUERY_BLOCK = 512
SMEM = pl.BlockSpec(memory_space=pltpu.SMEM)
VMEM = pl.BlockSpec(memory_space=pltpu.VMEM)
HBM = pl.BlockSpec(memory_space=pltpu.HBM)


def normalized(vectors):
    total = jnp.sum(vectors * vectors, axis=-1, keepdims=True)
    return (vectors * lax.rsqrt(total + 1e-06)).astype(jnp.bfloat16)


def quotient(number, divisor):
    if divisor & (divisor - 1) == 0:
        return lax.shift_right_logical(number, divisor.bit_length() - 1)
    return lax.div(number, divisor)


def pinned(array, space=pltpu.HBM):
    return pltpu.with_memory_space_constraint(array, space)


def granted(mebibytes):
    return pltpu.CompilerParams(vmem_limit_bytes=mebibytes * 1024 * 1024)


def widen_kernel(half_ref, own_hbm, other_ref, residuals_hbm, table, residuals, staged, sems):
    half_rows = own_hbm.shape[0]
    half = half_ref[0]
    piece = half_rows // PIECES
    copies = []
    for k in range(PIECES):
        at = pl.ds(k * piece, piece)
        copies.append(pltpu.make_async_copy(own_hbm.at[at], staged.at[at], sems.at[k]))
        copies[-1].start()
    residual_copy = pltpu.make_async_copy(residuals_hbm, residuals, sems.at[PIECES])
    residual_copy.start()
    for source, ref in enumerate((other_ref, staged)):
        base = (1 - half if source == 0 else half) * half_rows
        for k in range(PIECES):
            if source == 1:
                copies[k].wait()
            to = pl.ds(pl.multiple_of(base + k * piece, piece), piece)
            table[to, :] = ref[pl.ds(k * piece, piece), :].astype(jnp.float32)
    residual_copy.wait()


def widen(half, own, other, residuals):
    half_rows, width = own.shape
    return pl.pallas_call(
        widen_kernel,
        out_shape=(
            pltpu.VMEM((2 * half_rows, width), jnp.float32),
            pltpu.VMEM(residuals.shape, jnp.bfloat16),
        ),
        in_specs=[SMEM, HBM, VMEM, HBM],
        out_specs=(VMEM, VMEM),
        scratch_shapes=[
            pltpu.VMEM((half_rows, width), jnp.bfloat16),
            pltpu.SemaphoreType.DMA((PIECES + 1,)),
        ],
        compiler_params=granted(4),
        cost_estimate=pl.CostEstimate(flops=10**7, bytes_accessed=10**7, transcendentals=0),
        name="widen",
    )(half, pinned(own), pinned(other, pltpu.VMEM), pinned(residuals))


def decode_kernel(
    codes_hbm,
    lengths_hbm,
    table,
    residuals,
    embedded,
    at_ref,
    codes_ref,
    lengths_ref,
    live_ref,
    rows,
    sems,
):
    passages = lengths_ref.shape[0]
    tokens, width = residuals.shape
    slots = tokens // passages
    lengths_copy = pltpu.make_async_copy(lengths_hbm, lengths_ref, sems.at[0])
    codes_copy = pltpu.make_async_copy(codes_hbm, codes_ref, sems.at[1])
    lengths_copy.start()
    codes_copy.start()
    lengths_copy.wait()

    def listing(p, chunks):
        for k in range(slots // CHUNK):
            at_ref[chunks + k] = p * slots + k * CHUNK
            live_ref[chunks + k] = lengths_ref[p] - k * CHUNK
        return chunks + quotient(lengths_ref[p] + CHUNK - 1, CHUNK)

    chunks = lax.fori_loop(0, passages, listing, 0, unroll=4)
    for k in range(SCORE_GROUP):
        at_ref[chunks + k] = tokens
        live_ref[chunks + k] = 0
    groups = quotient(chunks + GROUP - 1, GROUP)
    at_ref[at_ref.shape[0] - 1] = chunks
    codes_copy.wait()

    slot_numbers = lax.broadcasted_iota(jnp.int32, (CHUNK, width), 0)
    table_single = table.reshape(table.shape[0], 1, width)
    rows_single = rows.reshape(rows.shape[0], 1, width)

    def fetch(g, k):
        at = jnp.minimum(at_ref[g * GROUP + k], tokens - CHUNK)
        codes = codes_ref.at[pl.ds(at, CHUNK)]
        fetched = [table_single[codes[j]] for j in range(CHUNK)]
        for j in range(CHUNK):
            rows_single[k * CHUNK + j] = fetched[j]

    def finish(g, k):
        at = jnp.minimum(at_ref[g * GROUP + k], tokens - CHUNK)
        near = residuals[pl.ds(pl.multiple_of(at, CHUNK), CHUNK), :]
        vectors = rows[pl.ds(k * CHUNK, CHUNK), :] + near.astype(jnp.float32)
        vectors = jnp.where(slot_numbers < live_ref[g * GROUP + k], vectors, vectors[0:1, :])
        return normalized(vectors)

    def keep(g, done):
        for k in range(GROUP):
            start = pl.multiple_of((g * GROUP + k) * CHUNK, CHUNK)
            embedded[pl.ds(start, CHUNK), :] = done[k]

    for k in range(GROUP):
        fetch(0, k)

    def decode(g, carry):
        done = []
        for k in range(GROUP):
            done.append(finish(g - 1, k))
            fetch(g, k)
        keep(g - 1, done)
        return carry

    lax.fori_loop(1, groups, decode, 0)
    keep(groups - 1, [finish(groups - 1, k) for k in range(GROUP)])


def decode_all(token_codes, lengths, table, residuals):
    passages, slots = token_codes.shape
    tokens, width = residuals.shape
    most = tokens // CHUNK + 2 * SCORE_GROUP
    return pl.pallas_call(
        decode_kernel,
        out_shape=(
            jax.ShapeDtypeStruct((most * CHUNK, width), jnp.bfloat16),
            jax.ShapeDtypeStruct((most + 1,), jnp.int32),
        ),
        in_specs=[HBM, HBM, VMEM, VMEM],
        out_specs=(VMEM, SMEM),
        scratch_shapes=[
            pltpu.SMEM((tokens,), jnp.int32),
            pltpu.SMEM((passages,), jnp.int32),
            pltpu.SMEM((most,), jnp.int32),
            pltpu.VMEM((GROUP * CHUNK, width), jnp.float32),
            pltpu.SemaphoreType.DMA((2,)),
        ],
        compiler_params=granted(4),
        cost_estimate=pl.CostEstimate(flops=10**7, bytes_accessed=40 * 10**6, transcendentals=0),
        name="decode",
    )(
        pinned(token_codes.reshape(tokens)),
        pinned(lengths),
        pinned(table, pltpu.VMEM),
        pinned(residuals, pltpu.VMEM),
    )


def score_kernel(token_count, slots, at_ref, queries_ref, embedded, out_ref, turned, largest):
    passages = out_ref.shape[1]
    query_tokens = queries_ref.shape[0]
    block = min(QUERY_BLOCK, query_tokens)
    blocks = query_tokens // block
    groups = quotient(at_ref[at_ref.shape[0] - 1] + SCORE_GROUP - 1, SCORE_GROUP)
    per_block = block // token_count
    owner = lax.broadcasted_iota(jnp.int32, (per_block, block), 0)
    token_of = lax.broadcasted_iota(jnp.int32, (per_block, block), 1) // token_count
    summing = (owner == token_of).astype(jnp.bfloat16)

    def score_block(b, carry):
        at = pl.ds(pl.multiple_of(b * block, block), block)
        vectors = normalized(queries_ref[at, :].astype(jnp.float32))
        turned[...] = vectors.astype(jnp.float32).T.astype(jnp.bfloat16)

        def score(g, so_far):
            size = SCORE_GROUP * CHUNK
            at = pl.ds(pl.multiple_of(g * size, size), size)
            similar = jnp.dot(embedded[at, :], turned[...], preferred_element_type=jnp.float32)
            parts = jnp.max(similar.reshape(SCORE_GROUP, CHUNK // 8, 8, block), axis=1)
            for k in range(SCORE_GROUP):
                start = at_ref[g * SCORE_GROUP + k]
                p = quotient(start, slots)
                so_far = jnp.where(start == p * slots, parts[k], jnp.maximum(so_far, parts[k]))
                at = pl.multiple_of(p * 8, 8)
                for lane in range(block // 128):
                    largest[lane, pl.ds(at, 8), :] = so_far[:, lane * 128 : (lane + 1) * 128]
            return so_far

        lax.fori_loop(0, groups, score, jnp.zeros((8, block), jnp.float32))
        kept = []
        for lane in range(block // 128):
            best = largest[lane, pl.ds(0, passages, stride=8), :]
            for k in range(1, 8):
                best = jnp.maximum(best, largest[lane, pl.ds(k, passages, stride=8), :])
            kept.append(best)
        best = jnp.concatenate(kept, axis=1)
        sums = jnp.zeros((per_block, passages), jnp.float32)
        for _ in range(3):
            part = best.astype(jnp.bfloat16)
            best = best - part.astype(jnp.float32)
            sums = sums + lax.dot_general(
                summing, part, (((1,), (1,)), ((), ())), preferred_element_type=jnp.float32
            )
        out_ref[pl.ds(pl.multiple_of(b * per_block, per_block), per_block), :] = sums
        return carry

    lax.fori_loop(0, blocks, score_block, 0)


def score_all(starts, query_rows, embedded, passages, slots, token_count):
    query_tokens, width = query_rows.shape
    block = min(QUERY_BLOCK, query_tokens)
    blocks = query_tokens // block
    return pl.pallas_call(
        functools.partial(score_kernel, token_count, slots),
        out_shape=jax.ShapeDtypeStruct((query_tokens // token_count, passages), jnp.float32),
        in_specs=[SMEM, VMEM, VMEM],
        out_specs=VMEM,
        scratch_shapes=[
            pltpu.VMEM((width, block), jnp.bfloat16),
            pltpu.VMEM((block // 128, (passages + 1) * 8, 128), jnp.float32),
        ],
        compiler_params=granted(8 + 2 * blocks),
        name="score",
    )(starts, query_rows, embedded)


def pick_kernel(passages, candidates_ref, returned_ref, out_ref):
    local_queries, count = candidates_ref.shape
    targets = returned_ref.shape[0]
    passage_numbers = lax.broadcasted_iota(jnp.int32, (passages, count), 0)
    target_numbers = lax.broadcasted_iota(jnp.int32, (targets, count), 0)
    for q in range(local_queries):
        wanted = candidates_ref[q : q + 1, :]
        target = quotient(wanted, passages)
        hits = (passage_numbers == wanted - target * passages).astype(jnp.bfloat16)
        left = returned_ref[:, q * passages : (q + 1) * passages]
        picked = jnp.zeros((targets, count), jnp.float32)
        for _ in range(3):
            part = left.astype(jnp.bfloat16)
            left = left - part.astype(jnp.float32)
            picked = picked + jnp.dot(part, hits, preferred_element_type=jnp.float32)
        kept = jnp.where(target_numbers == target, picked, 0.0)
        out_ref[q : q + 1, :] = jnp.sum(kept, axis=0, keepdims=True)


def pick(candidates, returned, passages):
    return pl.pallas_call(
        functools.partial(pick_kernel, passages),
        out_shape=jax.ShapeDtypeStruct(candidates.shape, jnp.float32),
        in_specs=[VMEM, VMEM],
        out_specs=VMEM,
        compiler_params=granted(8),
        name="pick",
    )(candidates, pltpu.with_memory_space_constraint(returned, pltpu.VMEM))


def body(queries, candidates, token_codes, residuals, lengths, centroids):
    local_queries, token_count, width = queries.shape
    targets = lax.axis_size("shard") * lax.axis_size("sub")
    passages, slots = token_codes.shape
    half = lax.axis_index("sub").astype(jnp.int32)
    other = lax.ppermute(centroids, "sub", [(0, 1), (1, 0)])
    own_rows = queries.reshape(1, local_queries * token_count, width)
    sent = jnp.broadcast_to(own_rows, (targets,) + own_rows.shape[1:])
    gathered = lax.all_to_all(sent, ("shard", "sub"), split_axis=0, concat_axis=0, tiled=True)
    query_rows = gathered.reshape(targets * local_queries * token_count, width)
    flat = residuals.reshape(passages * slots, width)
    table, near = widen(half.reshape(1), centroids, other, flat)
    embedded, starts = decode_all(token_codes, lengths, table, near)
    scores = score_all(starts, query_rows, embedded, passages, slots, token_count)
    returned = lax.all_to_all(
        scores.reshape(targets, local_queries * passages),
        ("shard", "sub"),
        split_axis=0,
        concat_axis=0,
        tiled=True,
    )
    return pick(candidates, returned, passages)


def solution(mesh):
    placed = (
        P(("groups", "shard", "sub"), None, None),
        P(("groups", "shard", "sub"), None),
        P(("groups", "shard", "sub"), None),
        P(("groups", "shard", "sub"), None, None),
        P(("groups", "shard", "sub")),
        P(("groups", "shard", "sub"), None),
    )
    return jax.shard_map(
        body,
        mesh=mesh,
        in_specs=placed,
        out_specs=P(("groups", "shard", "sub"), None),
        check_vma=False,
    )
```

```python
import functools

import jax
import jax.numpy as jnp
from jax import lax
from jax.experimental import pallas as pl
from jax.experimental.pallas import tpu as pltpu
from jax.sharding import PartitionSpec as P

CHUNK = 16
GROUP = 16
SCORE_GROUP = 32
PIECES = 4
QUERY_BLOCK = 512
SMEM = pl.BlockSpec(memory_space=pltpu.SMEM)
VMEM = pl.BlockSpec(memory_space=pltpu.VMEM)
HBM = pl.BlockSpec(memory_space=pltpu.HBM)


def normalized(vectors):
    total = jnp.sum(vectors * vectors, axis=-1, keepdims=True)
    return (vectors * lax.rsqrt(total + 1e-06)).astype(jnp.bfloat16)


def quotient(number, divisor):
    if divisor & (divisor - 1) == 0:
        return lax.shift_right_logical(number, divisor.bit_length() - 1)
    return lax.div(number, divisor)


def pinned(array, space=pltpu.HBM):
    return pltpu.with_memory_space_constraint(array, space)


def granted(mebibytes):
    return pltpu.CompilerParams(vmem_limit_bytes=mebibytes * 1024 * 1024)


def spread_kernel(queries_ref, out_ref):
    queries = queries_ref[...]

    def copy(t, carry):
        out_ref[t] = queries
        return carry

    lax.fori_loop(0, out_ref.shape[0], copy, 0, unroll=8)


def spread(queries, targets):
    return pl.pallas_call(
        spread_kernel,
        out_shape=pltpu.VMEM((targets,) + queries.shape, jnp.bfloat16),
        in_specs=[VMEM],
        out_specs=VMEM,
        compiler_params=granted(4),
        name="spread",
    )(pinned(queries))


def widen_kernel(
    slots,
    half_ref,
    lengths_hbm,
    own_hbm,
    other_ref,
    table,
    starts_hbm,
    lives_hbm,
    lengths_ref,
    starts_ref,
    lives_ref,
    staged,
    sems,
):
    passages = lengths_ref.shape[0]
    half_rows = own_hbm.shape[0]
    half = half_ref[0]
    lengths_copy = pltpu.make_async_copy(lengths_hbm, lengths_ref, sems.at[0])
    lengths_copy.start()
    piece = half_rows // PIECES
    copies = []
    for k in range(PIECES):
        at = pl.ds(k * piece, piece)
        copies.append(pltpu.make_async_copy(own_hbm.at[at], staged.at[at], sems.at[3 + k]))
        copies[-1].start()

    def widened(ref, base, k):
        to = pl.ds(pl.multiple_of(base + k * piece, piece), piece)
        table[to, :] = ref[pl.ds(k * piece, piece), :].astype(jnp.float32)

    for k in range(PIECES):
        widened(other_ref, (1 - half) * half_rows, k)
    lengths_copy.wait()

    def listing(p, chunks):
        length = lengths_ref[p]
        for k in range(slots // CHUNK):
            starts_ref[chunks + k] = p * slots + k * CHUNK
            lives_ref[chunks + k] = length - k * CHUNK
        return chunks + quotient(length + CHUNK - 1, CHUNK)

    chunks = lax.fori_loop(0, passages, listing, 0, unroll=4)
    for k in range(SCORE_GROUP):
        starts_ref[chunks + k] = passages * slots
        lives_ref[chunks + k] = 0
    starts_ref[starts_ref.shape[0] - 1] = chunks
    starts_copy = pltpu.make_async_copy(starts_ref, starts_hbm, sems.at[1])
    lives_copy = pltpu.make_async_copy(lives_ref, lives_hbm, sems.at[2])
    starts_copy.start()
    lives_copy.start()
    for k in range(PIECES):
        copies[k].wait()
        widened(staged, half * half_rows, k)
    starts_copy.wait()
    lives_copy.wait()


def widen(half, lengths, own, other, slots):
    half_rows, width = own.shape
    most = lengths.shape[0] * (slots // CHUNK) + SCORE_GROUP + slots // CHUNK
    most = -(-most // 128) * 128
    listed = pltpu.HBM((most,), jnp.int32)
    return pl.pallas_call(
        functools.partial(widen_kernel, slots),
        out_shape=(pltpu.VMEM((2 * half_rows, width), jnp.float32), listed, listed),
        in_specs=[SMEM, HBM, HBM, VMEM],
        out_specs=(VMEM, HBM, HBM),
        scratch_shapes=[
            pltpu.SMEM(lengths.shape, jnp.int32),
            pltpu.SMEM((most,), jnp.int32),
            pltpu.SMEM((most,), jnp.int32),
            pltpu.VMEM((half_rows, width), jnp.bfloat16),
            pltpu.SemaphoreType.DMA((3 + PIECES,)),
        ],
        compiler_params=granted(4),
        cost_estimate=pl.CostEstimate(flops=10**7, bytes_accessed=10**7, transcendentals=0),
        name="widen",
    )(half, pinned(lengths), pinned(own), pinned(other, pltpu.VMEM))


def decode_kernel(
    codes_hbm,
    starts_hbm,
    lives_hbm,
    residuals_hbm,
    table,
    embedded,
    codes_ref,
    starts_ref,
    lives_ref,
    residuals,
    rows,
    sems,
):
    tokens, width = residuals.shape
    moves = []
    pairs = ((starts_hbm, starts_ref), (lives_hbm, lives_ref), (codes_hbm, codes_ref))
    for k, (source, to) in enumerate(pairs):
        moves.append(pltpu.make_async_copy(source, to, sems.at[k]))
        moves[-1].start()
    piece = tokens // PIECES
    copies = []
    for k in range(PIECES):
        at = pl.ds(k * piece, piece)
        copies.append(
            pltpu.make_async_copy(residuals_hbm.at[at], residuals.at[at], sems.at[3 + k])
        )
        copies[-1].start()

    slot_numbers = lax.broadcasted_iota(jnp.int32, (CHUNK, width), 0)
    table_single = table.reshape(table.shape[0], 1, width)
    rows_single = rows.reshape(rows.shape[0], 1, width)

    def fetch(g):
        for k in range(GROUP):
            at = jnp.minimum(starts_ref[g * GROUP + k], tokens - CHUNK)
            codes = codes_ref.at[pl.ds(at, CHUNK)]
            fetched = [table_single[codes[j]] for j in range(CHUNK)]
            for j in range(CHUNK):
                rows_single[k * CHUNK + j] = fetched[j]

    def finish(g):
        summed = []
        for k in range(GROUP):
            at = jnp.minimum(starts_ref[g * GROUP + k], tokens - CHUNK)
            near = residuals[pl.ds(pl.multiple_of(at, CHUNK), CHUNK), :]
            vectors = rows[pl.ds(k * CHUNK, CHUNK), :] + near.astype(jnp.float32)
            live = slot_numbers < lives_ref[g * GROUP + k]
            summed.append(jnp.where(live, vectors, vectors[0:1, :]))
        return normalized(jnp.concatenate(summed, axis=0))

    def keep(g, done):
        size = GROUP * CHUNK
        embedded[pl.ds(pl.multiple_of(g * size, size), size), :] = done

    for move in moves:
        move.wait()
    groups = quotient(starts_ref[starts_ref.shape[0] - 1] + GROUP - 1, GROUP)
    fetch(0)
    for copy in copies:
        copy.wait()

    def decode(g, carry):
        done = finish(g - 1)
        fetch(g)
        keep(g - 1, done)
        return carry

    lax.fori_loop(1, groups, decode, 0)
    keep(groups - 1, finish(groups - 1))


def decode_all(token_codes, starts, lives, residuals, table):
    tokens, width = residuals.shape
    rounding = SCORE_GROUP * CHUNK
    return pl.pallas_call(
        decode_kernel,
        out_shape=jax.ShapeDtypeStruct((-(-tokens // rounding) * rounding, width), jnp.bfloat16),
        in_specs=[HBM, HBM, HBM, HBM, VMEM],
        out_specs=VMEM,
        scratch_shapes=[
            pltpu.SMEM((tokens,), jnp.int32),
            pltpu.SMEM(starts.shape, jnp.int32),
            pltpu.SMEM(lives.shape, jnp.int32),
            pltpu.VMEM((tokens, width), jnp.bfloat16),
            pltpu.VMEM((GROUP * CHUNK, width), jnp.float32),
            pltpu.SemaphoreType.DMA((3 + PIECES,)),
        ],
        compiler_params=granted(6),
        cost_estimate=pl.CostEstimate(flops=10**7, bytes_accessed=40 * 10**6, transcendentals=0),
        name="decode",
    )(
        pinned(token_codes.reshape(tokens)),
        pinned(starts),
        pinned(lives),
        pinned(residuals),
        pinned(table, pltpu.VMEM),
    )


def score_kernel(
    token_count, slots, starts_hbm, queries_ref, embedded, out_ref, at_ref, turned, largest, sem
):
    starts_copy = pltpu.make_async_copy(starts_hbm, at_ref, sem)
    starts_copy.start()
    passages = out_ref.shape[1]
    query_tokens = queries_ref.shape[0]
    block = min(QUERY_BLOCK, query_tokens)
    blocks = query_tokens // block
    per_block = block // token_count
    owner = lax.broadcasted_iota(jnp.int32, (per_block, block), 0)
    token_of = lax.broadcasted_iota(jnp.int32, (per_block, block), 1) // token_count
    summing = (owner == token_of).astype(jnp.bfloat16)

    def score_block(b, carry):
        at = pl.ds(pl.multiple_of(b * block, block), block)
        vectors = normalized(queries_ref[at, :].astype(jnp.float32))
        turned[...] = vectors.astype(jnp.float32).T.astype(jnp.bfloat16)

        def score(g, so_far):
            size = SCORE_GROUP * CHUNK
            at = pl.ds(pl.multiple_of(g * size, size), size)
            similar = jnp.dot(embedded[at, :], turned[...], preferred_element_type=jnp.float32)
            parts = jnp.max(similar.reshape(SCORE_GROUP, CHUNK // 8, 8, block), axis=1)
            for k in range(SCORE_GROUP):
                start = at_ref[g * SCORE_GROUP + k]
                p = quotient(start, slots)
                so_far = jnp.where(start == p * slots, parts[k], jnp.maximum(so_far, parts[k]))
                at = pl.multiple_of(p * 8, 8)
                for lane in range(block // 128):
                    largest[lane, pl.ds(at, 8), :] = so_far[:, lane * 128 : (lane + 1) * 128]
            return so_far

        @pl.when(b == 0)
        def arrived():
            starts_copy.wait()

        groups = quotient(at_ref[at_ref.shape[0] - 1] + SCORE_GROUP - 1, SCORE_GROUP)
        lax.fori_loop(0, groups, score, jnp.zeros((8, block), jnp.float32))
        kept = []
        for lane in range(block // 128):
            best = largest[lane, pl.ds(0, passages, stride=8), :]
            for k in range(1, 8):
                best = jnp.maximum(best, largest[lane, pl.ds(k, passages, stride=8), :])
            kept.append(best)
        best = jnp.concatenate(kept, axis=1)
        sums = jnp.zeros((per_block, passages), jnp.float32)
        for _ in range(3):
            part = best.astype(jnp.bfloat16)
            best = best - part.astype(jnp.float32)
            sums = sums + lax.dot_general(
                summing, part, (((1,), (1,)), ((), ())), preferred_element_type=jnp.float32
            )
        out_ref[pl.ds(pl.multiple_of(b * per_block, per_block), per_block), :] = sums
        return carry

    lax.fori_loop(0, blocks, score_block, 0)


def score_all(starts, query_rows, embedded, passages, slots, token_count):
    query_tokens, width = query_rows.shape
    block = min(QUERY_BLOCK, query_tokens)
    blocks = query_tokens // block
    return pl.pallas_call(
        functools.partial(score_kernel, token_count, slots),
        out_shape=jax.ShapeDtypeStruct((query_tokens // token_count, passages), jnp.float32),
        in_specs=[HBM, VMEM, VMEM],
        out_specs=VMEM,
        scratch_shapes=[
            pltpu.SMEM(starts.shape, jnp.int32),
            pltpu.VMEM((width, block), jnp.bfloat16),
            pltpu.VMEM((block // 128, (passages + 1) * 8, 128), jnp.float32),
            pltpu.SemaphoreType.DMA,
        ],
        compiler_params=granted(8 + 2 * blocks),
        name="score",
    )(pinned(starts), query_rows, embedded)


def pick_kernel(passages, candidates_ref, returned_ref, out_ref):
    local_queries, count = candidates_ref.shape
    targets = returned_ref.shape[0]
    passage_numbers = lax.broadcasted_iota(jnp.int32, (passages, count), 0)
    target_numbers = lax.broadcasted_iota(jnp.int32, (targets, count), 0)
    for q in range(local_queries):
        wanted = candidates_ref[q : q + 1, :]
        target = quotient(wanted, passages)
        hits = (passage_numbers == wanted - target * passages).astype(jnp.bfloat16)
        left = returned_ref[:, q * passages : (q + 1) * passages]
        picked = jnp.zeros((targets, count), jnp.float32)
        for _ in range(3):
            part = left.astype(jnp.bfloat16)
            left = left - part.astype(jnp.float32)
            picked = picked + jnp.dot(part, hits, preferred_element_type=jnp.float32)
        kept = jnp.where(target_numbers == target, picked, 0.0)
        out_ref[q : q + 1, :] = jnp.sum(kept, axis=0, keepdims=True)


def pick(candidates, returned, passages):
    return pl.pallas_call(
        functools.partial(pick_kernel, passages),
        out_shape=jax.ShapeDtypeStruct(candidates.shape, jnp.float32),
        in_specs=[VMEM, VMEM],
        out_specs=VMEM,
        compiler_params=granted(8),
        name="pick",
    )(candidates, pltpu.with_memory_space_constraint(returned, pltpu.VMEM))


def body(queries, candidates, token_codes, residuals, lengths, centroids):
    local_queries, token_count, width = queries.shape
    targets = lax.axis_size("shard") * lax.axis_size("sub")
    passages, slots = token_codes.shape
    half = lax.axis_index("sub").astype(jnp.int32)
    other = lax.ppermute(centroids, "sub", [(0, 1), (1, 0)])
    sent = spread(queries.reshape(local_queries * token_count, width), targets)
    gathered = lax.all_to_all(sent, ("shard", "sub"), split_axis=0, concat_axis=0, tiled=True)
    query_rows = gathered.reshape(targets * local_queries * token_count, width)
    flat = residuals.reshape(passages * slots, width)
    table, starts, lives = widen(half.reshape(1), lengths, centroids, other, slots)
    embedded = decode_all(token_codes, starts, lives, flat, table)
    scores = score_all(starts, query_rows, embedded, passages, slots, token_count)
    returned = lax.all_to_all(
        scores.reshape(targets, local_queries * passages),
        ("shard", "sub"),
        split_axis=0,
        concat_axis=0,
        tiled=True,
    )
    return pick(candidates, returned, passages)


def solution(mesh):
    placed = (
        P(("groups", "shard", "sub"), None, None),
        P(("groups", "shard", "sub"), None),
        P(("groups", "shard", "sub"), None),
        P(("groups", "shard", "sub"), None, None),
        P(("groups", "shard", "sub")),
        P(("groups", "shard", "sub"), None),
    )
    return jax.shard_map(
        body,
        mesh=mesh,
        in_specs=placed,
        out_specs=P(("groups", "shard", "sub"), None),
        check_vma=False,
    )
```

```python
import functools

import jax
import jax.numpy as jnp
from jax import lax
from jax.experimental import pallas as pl
from jax.experimental.pallas import tpu as pltpu
from jax.sharding import PartitionSpec as P

CHUNK = 16
GROUP = 16
SCORE_GROUP = 32
PIECES = 4
QUERY_BLOCK = 512
SMEM = pl.BlockSpec(memory_space=pltpu.SMEM)
VMEM = pl.BlockSpec(memory_space=pltpu.VMEM)
HBM = pl.BlockSpec(memory_space=pltpu.HBM)


def normalized(vectors):
    total = jnp.sum(vectors * vectors, axis=-1, keepdims=True)
    return (vectors * lax.rsqrt(total + 1e-06)).astype(jnp.bfloat16)


def quotient(number, divisor):
    if divisor & (divisor - 1) == 0:
        return lax.shift_right_logical(number, divisor.bit_length() - 1)
    return lax.div(number, divisor)


def pinned(array, space=pltpu.HBM):
    return pltpu.with_memory_space_constraint(array, space)


def granted(mebibytes):
    return pltpu.CompilerParams(vmem_limit_bytes=mebibytes * 1024 * 1024)


def spread_kernel(queries_hbm, out_hbm, sems):
    copies = []
    for k in range(sems.shape[0]):
        copies.append(pltpu.make_async_copy(queries_hbm, out_hbm.at[k], sems.at[k]))
        copies[-1].start()
    for copy in copies:
        copy.wait()


def spread(queries, targets):
    return pl.pallas_call(
        spread_kernel,
        out_shape=pltpu.HBM((targets,) + queries.shape, jnp.bfloat16),
        in_specs=[HBM],
        out_specs=HBM,
        scratch_shapes=[pltpu.SemaphoreType.DMA((targets,))],
        compiler_params=granted(4),
        name="spread",
    )(pinned(queries))


def widen_kernel(half_ref, own_hbm, other_ref, table, staged, sems):
    half_rows = own_hbm.shape[0]
    half = half_ref[0]
    piece = half_rows // PIECES
    copies = []
    for k in range(PIECES):
        at = pl.ds(k * piece, piece)
        copies.append(pltpu.make_async_copy(own_hbm.at[at], staged.at[at], sems.at[k]))
        copies[-1].start()

    def widened(ref, base, k):
        to = pl.ds(pl.multiple_of(base + k * piece, piece), piece)
        table[to, :] = ref[pl.ds(k * piece, piece), :].astype(jnp.float32)

    for k in range(PIECES):
        widened(other_ref, (1 - half) * half_rows, k)
    for k in range(PIECES):
        copies[k].wait()
        widened(staged, half * half_rows, k)


def widen(half, own, other):
    half_rows, width = own.shape
    return pl.pallas_call(
        widen_kernel,
        out_shape=pltpu.VMEM((2 * half_rows, width), jnp.float32),
        in_specs=[SMEM, HBM, VMEM],
        out_specs=VMEM,
        scratch_shapes=[
            pltpu.VMEM((half_rows, width), jnp.bfloat16),
            pltpu.SemaphoreType.DMA((PIECES,)),
        ],
        compiler_params=granted(4),
        cost_estimate=pl.CostEstimate(flops=10**7, bytes_accessed=10**7, transcendentals=0),
        name="widen",
    )(half, pinned(own), pinned(other, pltpu.VMEM))


def decode_kernel(
    codes_hbm,
    lengths_hbm,
    residuals_hbm,
    table,
    embedded,
    starts_hbm,
    codes_ref,
    lengths_ref,
    starts_ref,
    residuals,
    sems,
):
    tokens, width = residuals.shape
    passages = lengths_ref.shape[0]
    slots = tokens // passages
    lengths_copy = pltpu.make_async_copy(lengths_hbm, lengths_ref, sems.at[0])
    codes_copy = pltpu.make_async_copy(codes_hbm, codes_ref, sems.at[1])
    lengths_copy.start()
    codes_copy.start()
    piece = tokens // PIECES
    copies = []
    for k in range(PIECES):
        at = pl.ds(k * piece, piece)
        copies.append(
            pltpu.make_async_copy(residuals_hbm.at[at], residuals.at[at], sems.at[3 + k])
        )
        copies[-1].start()
    lengths_copy.wait()

    def listing(p, chunks):
        for k in range(slots // CHUNK):
            starts_ref[chunks + k] = p * slots + k * CHUNK
        return chunks + quotient(lengths_ref[p] + CHUNK - 1, CHUNK)

    chunks = lax.fori_loop(0, passages, listing, 0, unroll=4)
    for k in range(SCORE_GROUP):
        starts_ref[chunks + k] = tokens
    starts_ref[starts_ref.shape[0] - 1] = chunks
    starts_copy = pltpu.make_async_copy(starts_ref, starts_hbm, sems.at[2])
    starts_copy.start()

    slot_numbers = lax.broadcasted_iota(jnp.int32, (CHUNK, width), 0)
    sublanes = lax.broadcasted_iota(jnp.int32, (8, width), 0)

    def fetched(codes, first):
        tile = table[pl.ds(codes[first], 8, stride=0), :]
        for j in range(1, 8):
            tile = jnp.where(sublanes == j, table[pl.ds(codes[first + j], 8, stride=0), :], tile)
        return tile

    codes_copy.wait()
    for copy in copies:
        copy.wait()

    def decode(g, carry):
        summed = []
        for k in range(GROUP):
            at = jnp.minimum(starts_ref[g * GROUP + k], tokens - CHUNK)
            codes = codes_ref.at[pl.ds(at, CHUNK)]
            rows = jnp.concatenate([fetched(codes, j) for j in range(0, CHUNK, 8)], axis=0)
            near = residuals[pl.ds(pl.multiple_of(at, CHUNK), CHUNK), :]
            vectors = rows + near.astype(jnp.float32)
            p = quotient(at, slots)
            live = slot_numbers < lengths_ref[p] - (at - p * slots)
            summed.append(jnp.where(live, vectors, vectors[0:1, :]))
        size = GROUP * CHUNK
        done = normalized(jnp.concatenate(summed, axis=0))
        embedded[pl.ds(pl.multiple_of(g * size, size), size), :] = done
        return carry

    lax.fori_loop(0, quotient(chunks + GROUP - 1, GROUP), decode, 0)
    starts_copy.wait()


def decode_all(token_codes, lengths, residuals, table):
    tokens, width = residuals.shape
    rounding = SCORE_GROUP * CHUNK
    passages, slots = token_codes.shape
    most = tokens // CHUNK + SCORE_GROUP + slots // CHUNK
    most = -(-most // 128) * 128
    return pl.pallas_call(
        decode_kernel,
        out_shape=(
            jax.ShapeDtypeStruct((-(-tokens // rounding) * rounding, width), jnp.bfloat16),
            pltpu.HBM((most,), jnp.int32),
        ),
        in_specs=[HBM, HBM, HBM, VMEM],
        out_specs=(VMEM, HBM),
        scratch_shapes=[
            pltpu.SMEM((tokens,), jnp.int32),
            pltpu.SMEM((passages,), jnp.int32),
            pltpu.SMEM((most,), jnp.int32),
            pltpu.VMEM((tokens, width), jnp.bfloat16),
            pltpu.SemaphoreType.DMA((3 + PIECES,)),
        ],
        compiler_params=granted(6),
        cost_estimate=pl.CostEstimate(flops=10**7, bytes_accessed=40 * 10**6, transcendentals=0),
        name="decode",
    )(
        pinned(token_codes.reshape(tokens)),
        pinned(lengths),
        pinned(residuals),
        pinned(table, pltpu.VMEM),
    )


def score_kernel(
    token_count, slots, starts_hbm, queries_ref, embedded, out_ref, at_ref, turned, largest, sem
):
    starts_copy = pltpu.make_async_copy(starts_hbm, at_ref, sem)
    starts_copy.start()
    passages = out_ref.shape[1]
    query_tokens = queries_ref.shape[0]
    block = min(QUERY_BLOCK, query_tokens)
    blocks = query_tokens // block
    per_block = block // token_count
    owner = lax.broadcasted_iota(jnp.int32, (per_block, block), 0)
    token_of = lax.broadcasted_iota(jnp.int32, (per_block, block), 1) // token_count
    summing = (owner == token_of).astype(jnp.bfloat16)

    def score_block(b, carry):
        at = pl.ds(pl.multiple_of(b * block, block), block)
        vectors = normalized(queries_ref[at, :].astype(jnp.float32))
        turned[...] = vectors.astype(jnp.float32).T.astype(jnp.bfloat16)

        def score(g, so_far):
            size = SCORE_GROUP * CHUNK
            at = pl.ds(pl.multiple_of(g * size, size), size)
            similar = jnp.dot(embedded[at, :], turned[...], preferred_element_type=jnp.float32)
            parts = jnp.max(similar.reshape(SCORE_GROUP, CHUNK // 8, 8, block), axis=1)
            for k in range(SCORE_GROUP):
                start = at_ref[g * SCORE_GROUP + k]
                p = quotient(start, slots)
                so_far = jnp.where(start == p * slots, parts[k], jnp.maximum(so_far, parts[k]))
                at = pl.multiple_of(p * 8, 8)
                for lane in range(block // 128):
                    largest[lane, pl.ds(at, 8), :] = so_far[:, lane * 128 : (lane + 1) * 128]
            return so_far

        @pl.when(b == 0)
        def arrived():
            starts_copy.wait()

        groups = quotient(at_ref[at_ref.shape[0] - 1] + SCORE_GROUP - 1, SCORE_GROUP)
        lax.fori_loop(0, groups, score, jnp.zeros((8, block), jnp.float32))
        kept = []
        for lane in range(block // 128):
            best = largest[lane, pl.ds(0, passages, stride=8), :]
            for k in range(1, 8):
                best = jnp.maximum(best, largest[lane, pl.ds(k, passages, stride=8), :])
            kept.append(best)
        best = jnp.concatenate(kept, axis=1)
        sums = jnp.zeros((per_block, passages), jnp.float32)
        for _ in range(3):
            part = best.astype(jnp.bfloat16)
            best = best - part.astype(jnp.float32)
            sums = sums + lax.dot_general(
                summing, part, (((1,), (1,)), ((), ())), preferred_element_type=jnp.float32
            )
        out_ref[pl.ds(pl.multiple_of(b * per_block, per_block), per_block), :] = sums
        return carry

    lax.fori_loop(0, blocks, score_block, 0)


def score_all(starts, query_rows, embedded, passages, slots, token_count):
    query_tokens, width = query_rows.shape
    block = min(QUERY_BLOCK, query_tokens)
    blocks = query_tokens // block
    return pl.pallas_call(
        functools.partial(score_kernel, token_count, slots),
        out_shape=jax.ShapeDtypeStruct((query_tokens // token_count, passages), jnp.float32),
        in_specs=[HBM, VMEM, VMEM],
        out_specs=VMEM,
        scratch_shapes=[
            pltpu.SMEM(starts.shape, jnp.int32),
            pltpu.VMEM((width, block), jnp.bfloat16),
            pltpu.VMEM((block // 128, (passages + 1) * 8, 128), jnp.float32),
            pltpu.SemaphoreType.DMA,
        ],
        compiler_params=granted(8 + 2 * blocks),
        name="score",
    )(pinned(starts), query_rows, embedded)


def pick_kernel(passages, candidates_ref, returned_ref, out_ref):
    local_queries, count = candidates_ref.shape
    targets = returned_ref.shape[0]
    passage_numbers = lax.broadcasted_iota(jnp.int32, (passages, count), 0)
    target_numbers = lax.broadcasted_iota(jnp.int32, (targets, count), 0)
    for q in range(local_queries):
        wanted = candidates_ref[q : q + 1, :]
        target = quotient(wanted, passages)
        hits = (passage_numbers == wanted - target * passages).astype(jnp.bfloat16)
        left = returned_ref[:, q * passages : (q + 1) * passages]
        picked = jnp.zeros((targets, count), jnp.float32)
        for _ in range(3):
            part = left.astype(jnp.bfloat16)
            left = left - part.astype(jnp.float32)
            picked = picked + jnp.dot(part, hits, preferred_element_type=jnp.float32)
        kept = jnp.where(target_numbers == target, picked, 0.0)
        out_ref[q : q + 1, :] = jnp.sum(kept, axis=0, keepdims=True)


def pick(candidates, returned, passages):
    return pl.pallas_call(
        functools.partial(pick_kernel, passages),
        out_shape=jax.ShapeDtypeStruct(candidates.shape, jnp.float32),
        in_specs=[VMEM, VMEM],
        out_specs=VMEM,
        compiler_params=granted(8),
        name="pick",
    )(candidates, pltpu.with_memory_space_constraint(returned, pltpu.VMEM))


def body(queries, candidates, token_codes, residuals, lengths, centroids):
    local_queries, token_count, width = queries.shape
    targets = lax.axis_size("shard") * lax.axis_size("sub")
    passages, slots = token_codes.shape
    half = lax.axis_index("sub").astype(jnp.int32)
    other = lax.ppermute(centroids, "sub", [(0, 1), (1, 0)])
    sent = spread(queries.reshape(local_queries * token_count, width), targets)
    gathered = lax.all_to_all(sent, ("shard", "sub"), split_axis=0, concat_axis=0, tiled=True)
    query_rows = gathered.reshape(targets * local_queries * token_count, width)
    flat = residuals.reshape(passages * slots, width)
    table = widen(half.reshape(1), centroids, other)
    embedded, starts = decode_all(token_codes, lengths, flat, table)
    scores = score_all(starts, query_rows, embedded, passages, slots, token_count)
    returned = lax.all_to_all(
        scores.reshape(targets, local_queries * passages),
        ("shard", "sub"),
        split_axis=0,
        concat_axis=0,
        tiled=True,
    )
    return pick(candidates, returned, passages)


def solution(mesh):
    placed = (
        P(("groups", "shard", "sub"), None, None),
        P(("groups", "shard", "sub"), None),
        P(("groups", "shard", "sub"), None),
        P(("groups", "shard", "sub"), None, None),
        P(("groups", "shard", "sub")),
        P(("groups", "shard", "sub"), None),
    )
    return jax.shard_map(
        body,
        mesh=mesh,
        in_specs=placed,
        out_specs=P(("groups", "shard", "sub"), None),
        check_vma=False,
    )
```

```python
import functools

import jax
import jax.numpy as jnp
from jax import lax
from jax.experimental import pallas as pl
from jax.experimental.pallas import tpu as pltpu
from jax.sharding import PartitionSpec as P

CHUNK = 16
GROUP = 16
PIECES = 4
QUERY_BLOCK = 512
DIGIT = 128
NOBODY = 255.0
SMEM = pl.BlockSpec(memory_space=pltpu.SMEM)
VMEM = pl.BlockSpec(memory_space=pltpu.VMEM)
HBM = pl.BlockSpec(memory_space=pltpu.HBM)


def pinned(array, space=pltpu.HBM):
    return pltpu.with_memory_space_constraint(array, space)


def granted(mebibytes):
    return pltpu.CompilerParams(vmem_limit_bytes=mebibytes * 1024 * 1024)


def quotient(number, divisor):
    if divisor & (divisor - 1) == 0:
        return lax.shift_right_logical(number, divisor.bit_length() - 1)
    return lax.div(number, divisor)


def normalized(vectors):
    total = jnp.sum(vectors * vectors, axis=-1, keepdims=True)
    return (vectors * lax.rsqrt(total + 1e-06)).astype(jnp.bfloat16)


def id_rows_of(local_queries, count):
    rows = local_queries * -(-count // 128)
    return -(-rows // 8) * 8


def spread_kernel(me_ref, queries_ref, candidates_ref, out_ref, digits):
    del me_ref
    targets = out_ref.shape[0]
    query_rows = queries_ref.shape[0]
    local_queries, count = candidates_ref.shape
    id_rows = digits.shape[0] // 2
    digits[...] = jnp.full(digits.shape, NOBODY, jnp.float32)
    row = 0
    for q in range(local_queries):
        for start in range(0, count, 128):
            size = min(128, count - start)
            ids = candidates_ref[q : q + 1, start : start + size]
            high = quotient(ids, DIGIT)
            digits[row : row + 1, 0:size] = (ids - high * DIGIT).astype(jnp.float32)
            digits[id_rows + row : id_rows + row + 1, 0:size] = high.astype(jnp.float32)
            row += 1
    queries = queries_ref[...]
    coded = digits[...].astype(jnp.bfloat16)

    def copy(t, carry):
        out_ref[t, 0:query_rows, :] = queries
        out_ref[t, query_rows:, :] = coded
        return carry

    lax.fori_loop(0, targets, copy, 0, unroll=8)


def spread(me, queries, candidates, targets):
    query_rows, width = queries.shape
    id_rows = id_rows_of(*candidates.shape)
    return pl.pallas_call(
        spread_kernel,
        out_shape=pltpu.VMEM((targets, query_rows + 2 * id_rows, width), jnp.bfloat16),
        in_specs=[SMEM, VMEM, VMEM],
        out_specs=VMEM,
        scratch_shapes=[pltpu.VMEM((2 * id_rows, width), jnp.float32)],
        compiler_params=granted(16),
        name="spread",
    )(me, pinned(queries), pinned(candidates))


def score_kernel(
    token_count,
    query_rows,
    me_ref,
    half_ref,
    codes_hbm,
    lengths_hbm,
    own_hbm,
    residuals_hbm,
    other_ref,
    gathered_ref,
    out_ref,
    codes_ref,
    lengths_ref,
    list_ref,
    table,
    staged,
    residuals,
    rows,
    turned,
    so_far,
    largest,
    sems,
):
    passages, slots = codes_ref.shape
    half_rows, width = own_hbm.shape
    tokens = passages * slots
    per_passage = slots // CHUNK
    targets, sent_rows, _ = gathered_ref.shape
    id_rows = (sent_rows - query_rows) // 2
    blocks, _, block = turned.shape
    base = me_ref[0] * passages
    half = half_ref[0]
    lengths_copy = pltpu.make_async_copy(lengths_hbm, lengths_ref, sems.at[0])
    codes_copy = pltpu.make_async_copy(codes_hbm, codes_ref, sems.at[1])
    lengths_copy.start()
    codes_copy.start()

    def pieces(source, to, first):
        size = source.shape[0] // PIECES
        copies = []
        for k in range(PIECES):
            at = pl.ds(k * size, size)
            sem = sems.at[first + k]
            copies.append(pltpu.make_async_copy(source.at[at], to.at[at], sem))
            copies[-1].start()
        return copies

    own_copies = pieces(own_hbm, staged, 2)
    residual_copies = pieces(residuals_hbm, residuals, 2 + PIECES)

    words = -(-passages // 32)
    shape = (id_rows, width)

    def collect(t, masks):
        low = gathered_ref[t, query_rows : query_rows + id_rows, :].astype(jnp.float32)
        high = gathered_ref[t, query_rows + id_rows :, :].astype(jnp.float32)
        local = (high * DIGIT + low).astype(jnp.int32) - base
        bits = lax.shift_left(jnp.ones(shape, jnp.int32), local & 31)
        word = lax.shift_right_arithmetic(local, 5)
        return tuple(mask | jnp.where(word == w, bits, 0) for w, mask in enumerate(masks))

    empty = tuple(jnp.zeros(shape, jnp.int32) for _ in range(words))
    masks = lax.fori_loop(0, targets, collect, empty, unroll=min(16, targets))
    joined = []
    for mask in masks:
        folded = mask[0:8]
        for k in range(8, id_rows, 8):
            folded = folded | mask[k : k + 8]
        for shift in (4, 2, 1):
            folded = folded | pltpu.roll(folded, shift, 0)
        for shift in (64, 32, 16, 8, 4, 2, 1):
            folded = folded | pltpu.roll(folded, shift, 1)
        joined.append(folded[0, 0])

    per_device = block // query_rows

    def turn(b, carry):
        vectors = gathered_ref[pl.ds(b * per_device, per_device), 0:query_rows, :]
        ready = normalized(vectors.reshape(block, width).astype(jnp.float32))
        turned[b] = ready.astype(jnp.float32).T.astype(jnp.bfloat16)
        largest[b] = jnp.zeros(largest.shape[1:], jnp.float32)
        return carry

    lax.fori_loop(0, blocks, turn, 0)

    piece = half_rows // PIECES

    def widened(ref, start, k):
        to = pl.ds(pl.multiple_of(start + k * piece, piece), piece)
        table[to, :] = ref[pl.ds(k * piece, piece), :].astype(jnp.float32)

    for k in range(PIECES):
        widened(other_ref, (1 - half) * half_rows, k)

    lengths_copy.wait()
    chunks = jnp.int32(0)
    for w in range(words):

        def listing(k, listed):
            p = w * 32 + k
            for j in range(per_passage):
                list_ref[listed + j] = p * per_passage + j
            wanted = lax.shift_right_logical(joined[w], k) & 1
            return listed + wanted * quotient(lengths_ref[p] + CHUNK - 1, CHUNK)

        chunks = lax.fori_loop(0, min(32, passages - w * 32), listing, chunks, unroll=4)
    for k in range(GROUP):
        list_ref[chunks + k] = passages * per_passage
    groups = quotient(chunks + GROUP - 1, GROUP)

    for k in range(PIECES):
        own_copies[k].wait()
        widened(staged, half * half_rows, k)
    codes_copy.wait()
    for copy in residual_copies:
        copy.wait()

    slot_numbers = lax.broadcasted_iota(jnp.int32, (CHUNK, width), 0)
    table_single = table.reshape(2 * half_rows, 1, width)
    rows_single = rows.reshape(rows.shape[0], 1, width)
    codes_chunks = codes_ref.reshape(passages * per_passage, CHUNK)

    def chunk_at(g, k):
        return jnp.minimum(list_ref[g * GROUP + k], passages * per_passage - 1)

    def fetch(g, k):
        chunk = chunk_at(g, k)
        for j in range(CHUNK):
            rows_single[k * CHUNK + j] = table_single[codes_chunks[chunk, j]]

    def finish(g, k):
        chunk = chunk_at(g, k)
        p = quotient(chunk, per_passage)
        live = lengths_ref[p] - (chunk - p * per_passage) * CHUNK
        near = residuals[pl.ds(pl.multiple_of(chunk * CHUNK, CHUNK), CHUNK), :]
        vectors = rows[pl.ds(k * CHUNK, CHUNK), :] + near.astype(jnp.float32)
        return jnp.where(slot_numbers < live, vectors, vectors[0:1, :])

    def score(g, b, embedded):
        similar = jnp.dot(embedded, turned[b], preferred_element_type=jnp.float32)
        parts = jnp.max(similar.reshape(GROUP, CHUNK // 8, 8, block), axis=1)
        best = so_far[b]
        for k in range(GROUP):
            chunk = list_ref[g * GROUP + k]
            p = quotient(chunk, per_passage)
            fresh = chunk == p * per_passage
            best = jnp.where(fresh, parts[k], jnp.maximum(best, parts[k]))
            at = pl.multiple_of(p * 8, 8)
            for lane in range(block // 128):
                largest[b, lane, pl.ds(at, 8), :] = best[:, lane * 128 : (lane + 1) * 128]
        so_far[b] = best

    def step(i, carry):
        fetched = jnp.minimum(i, groups - 1)
        finished = jnp.maximum(i - 1, 0)
        summed = []
        for k in range(GROUP):
            summed.append(finish(finished, k))
            fetch(fetched, k)
        embedded = normalized(jnp.concatenate(summed, axis=0))
        if blocks == 1:
            score(finished, 0, embedded)
        else:

            def score_block(b, inner):
                score(finished, b, embedded)
                return inner

            lax.fori_loop(0, blocks, score_block, 0)
        return carry

    lax.fori_loop(0, jnp.where(groups > 0, groups + 1, 0), step, 0)

    per_block = block // token_count
    owner = lax.broadcasted_iota(jnp.int32, (per_block, block), 0)
    token_of = quotient(lax.broadcasted_iota(jnp.int32, (per_block, block), 1), token_count)
    summing = (owner == token_of).astype(jnp.bfloat16)

    def total(b, carry):
        kept = []
        for lane in range(block // 128):
            best = largest[b, lane, pl.ds(0, passages, stride=8), :]
            for k in range(1, 8):
                best = jnp.maximum(best, largest[b, lane, pl.ds(k, passages, stride=8), :])
            kept.append(best)
        left = jnp.concatenate(kept, axis=1)
        sums = jnp.zeros((per_block, passages), jnp.float32)
        for _ in range(3):
            part = left.astype(jnp.bfloat16)
            left = left - part.astype(jnp.float32)
            sums = sums + lax.dot_general(
                summing, part, (((1,), (1,)), ((), ())), preferred_element_type=jnp.float32
            )
        out_ref[pl.ds(pl.multiple_of(b * per_block, per_block), per_block), :] = sums
        return carry

    lax.fori_loop(0, blocks, total, 0)


def score_all(
    me, half, token_codes, lengths, own, residuals, other, gathered, query_rows, token_count
):
    passages, slots = token_codes.shape
    half_rows, width = own.shape
    targets = gathered.shape[0]
    block = min(QUERY_BLOCK, targets * query_rows)
    blocks = targets * query_rows // block
    most = passages * (slots // CHUNK) + slots // CHUNK + GROUP
    return pl.pallas_call(
        functools.partial(score_kernel, token_count, query_rows),
        out_shape=jax.ShapeDtypeStruct(
            (targets * query_rows // token_count, passages), jnp.float32
        ),
        in_specs=[SMEM, SMEM, HBM, HBM, HBM, HBM, VMEM, VMEM],
        out_specs=VMEM,
        scratch_shapes=[
            pltpu.SMEM((passages, slots), jnp.int32),
            pltpu.SMEM((passages,), jnp.int32),
            pltpu.SMEM((most,), jnp.int32),
            pltpu.VMEM((2 * half_rows, width), jnp.float32),
            pltpu.VMEM((half_rows, width), jnp.bfloat16),
            pltpu.VMEM((passages * slots, width), jnp.bfloat16),
            pltpu.VMEM((GROUP * CHUNK, width), jnp.float32),
            pltpu.VMEM((blocks, width, block), jnp.bfloat16),
            pltpu.VMEM((blocks, 8, block), jnp.float32),
            pltpu.VMEM((blocks, block // 128, (passages + 1) * 8, 128), jnp.float32),
            pltpu.SemaphoreType.DMA((2 + 2 * PIECES,)),
        ],
        compiler_params=granted(20 + 2 * blocks),
        name="score",
    )(
        me,
        half,
        pinned(token_codes),
        pinned(lengths),
        pinned(own),
        pinned(residuals.reshape(passages * slots, width)),
        pinned(other, pltpu.VMEM),
        pinned(gathered, pltpu.VMEM),
    )


def pick_kernel(passages, candidates_ref, returned_ref, out_ref):
    local_queries, count = candidates_ref.shape
    targets = returned_ref.shape[0]
    passage_numbers = lax.broadcasted_iota(jnp.int32, (passages, count), 0)
    target_numbers = lax.broadcasted_iota(jnp.int32, (targets, count), 0)
    for q in range(local_queries):
        wanted = candidates_ref[q : q + 1, :]
        target = quotient(wanted, passages)
        hits = (passage_numbers == wanted - target * passages).astype(jnp.bfloat16)
        left = returned_ref[:, q * passages : (q + 1) * passages]
        picked = jnp.zeros((targets, count), jnp.float32)
        for _ in range(3):
            part = left.astype(jnp.bfloat16)
            left = left - part.astype(jnp.float32)
            picked = picked + jnp.dot(part, hits, preferred_element_type=jnp.float32)
        kept = jnp.where(target_numbers == target, picked, 0.0)
        out_ref[q : q + 1, :] = jnp.sum(kept, axis=0, keepdims=True)


def pick(candidates, returned, passages):
    return pl.pallas_call(
        functools.partial(pick_kernel, passages),
        out_shape=jax.ShapeDtypeStruct(candidates.shape, jnp.float32),
        in_specs=[VMEM, VMEM],
        out_specs=VMEM,
        compiler_params=granted(8),
        name="pick",
    )(candidates, pinned(returned, pltpu.VMEM))


def body(queries, candidates, token_codes, residuals, lengths, centroids):
    local_queries, token_count, width = queries.shape
    targets = lax.axis_size("shard") * lax.axis_size("sub")
    passages = token_codes.shape[0]
    query_rows = local_queries * token_count
    half = lax.axis_index("sub").astype(jnp.int32)
    me = lax.axis_index("shard").astype(jnp.int32) * lax.axis_size("sub") + half
    half = half.reshape(1)
    me = me.reshape(1)
    other = lax.ppermute(centroids, "sub", [(0, 1), (1, 0)])
    sent = spread(me, queries.reshape(query_rows, width), candidates, targets)
    gathered = lax.all_to_all(sent, ("shard", "sub"), split_axis=0, concat_axis=0, tiled=True)
    scores = score_all(
        me, half, token_codes, lengths, centroids, residuals, other, gathered, query_rows, token_count
    )
    returned = lax.all_to_all(
        scores.reshape(targets, local_queries * passages),
        ("shard", "sub"),
        split_axis=0,
        concat_axis=0,
        tiled=True,
    )
    return pick(candidates, returned, passages)


def solution(mesh):
    placed = (
        P(("groups", "shard", "sub"), None, None),
        P(("groups", "shard", "sub"), None),
        P(("groups", "shard", "sub"), None),
        P(("groups", "shard", "sub"), None, None),
        P(("groups", "shard", "sub")),
        P(("groups", "shard", "sub"), None),
    )
    return jax.shard_map(
        body,
        mesh=mesh,
        in_specs=placed,
        out_specs=P(("groups", "shard", "sub"), None),
        check_vma=False,
    )
```

```python
import functools

import jax
import jax.numpy as jnp
from jax import lax
from jax.experimental import pallas as pl
from jax.experimental.pallas import tpu as pltpu
from jax.sharding import PartitionSpec as P

CHUNK = 16
GROUP = 16
SCORE_GROUP = 64
SCORE_PARTS = 2
PIECES = 4
QUERY_BLOCK = 512
SMEM = pl.BlockSpec(memory_space=pltpu.SMEM)
VMEM = pl.BlockSpec(memory_space=pltpu.VMEM)
HBM = pl.BlockSpec(memory_space=pltpu.HBM)


def normalized(vectors):
    total = jnp.sum(vectors * vectors, axis=-1, keepdims=True)
    return (vectors * lax.rsqrt(total + 1e-06)).astype(jnp.bfloat16)


def quotient(number, divisor):
    if divisor & (divisor - 1) == 0:
        return lax.shift_right_logical(number, divisor.bit_length() - 1)
    return lax.div(number, divisor)


def pinned(array, space=pltpu.HBM):
    return pltpu.with_memory_space_constraint(array, space)


def granted(mebibytes):
    return pltpu.CompilerParams(vmem_limit_bytes=mebibytes * 1024 * 1024)


def spread_kernel(queries_ref, out_ref):
    queries = queries_ref[...]

    def copy(t, carry):
        out_ref[t] = queries
        return carry

    lax.fori_loop(0, out_ref.shape[0], copy, 0, unroll=8)


def spread(queries, targets):
    return pl.pallas_call(
        spread_kernel,
        out_shape=pltpu.VMEM((targets,) + queries.shape, jnp.bfloat16),
        in_specs=[VMEM],
        out_specs=VMEM,
        compiler_params=granted(4),
        name="spread",
    )(pinned(queries))


def widen_kernel(
    half_ref, codes_hbm, own_hbm, other_ref, table, paired_hbm, staged, codes, paired, sems
):
    half_rows = own_hbm.shape[0]
    half = half_ref[0]
    piece = half_rows // PIECES
    codes_copy = pltpu.make_async_copy(codes_hbm, codes, sems.at[PIECES])
    codes_copy.start()
    copies = []
    for k in range(PIECES):
        at = pl.ds(k * piece, piece)
        copies.append(pltpu.make_async_copy(own_hbm.at[at], staged.at[at], sems.at[k]))
        copies[-1].start()

    def widened(ref, base, k):
        to = pl.ds(pl.multiple_of(base + k * piece, piece), piece)
        table[to, :] = ref[pl.ds(k * piece, piece), :].astype(jnp.float32)

    for k in range(PIECES):
        widened(other_ref, (1 - half) * half_rows, k)
    codes_copy.wait()
    slots = codes.shape[1]
    following = pltpu.roll(codes[...], slots - 1, 1)
    paired[...] = codes[...] | lax.shift_left(following, jnp.full_like(following, 16))
    paired_copy = pltpu.make_async_copy(paired, paired_hbm, sems.at[PIECES + 1])
    paired_copy.start()
    for k in range(PIECES):
        copies[k].wait()
        widened(staged, half * half_rows, k)
    paired_copy.wait()


def widen(half, token_codes, own, other):
    half_rows, width = own.shape
    return pl.pallas_call(
        widen_kernel,
        out_shape=(
            pltpu.VMEM((2 * half_rows, width), jnp.float32),
            pltpu.HBM(token_codes.shape, jnp.int32),
        ),
        in_specs=[SMEM, HBM, HBM, VMEM],
        out_specs=(VMEM, HBM),
        scratch_shapes=[
            pltpu.VMEM((half_rows, width), jnp.bfloat16),
            pltpu.VMEM(token_codes.shape, jnp.int32),
            pltpu.VMEM(token_codes.shape, jnp.int32),
            pltpu.SemaphoreType.DMA((PIECES + 2,)),
        ],
        compiler_params=granted(4),
        cost_estimate=pl.CostEstimate(flops=10**7, bytes_accessed=10**7, transcendentals=0),
        name="widen",
    )(half, pinned(token_codes), pinned(own), pinned(other, pltpu.VMEM))


def decode_kernel(
    codes_hbm,
    lengths_hbm,
    residuals_hbm,
    table,
    embedded,
    starts_hbm,
    codes_ref,
    lengths_ref,
    starts_ref,
    residuals,
    rows,
    sems,
):
    tokens, width = residuals.shape
    passages = lengths_ref.shape[0]
    slots = tokens // passages
    lengths_copy = pltpu.make_async_copy(lengths_hbm, lengths_ref, sems.at[0])
    codes_copy = pltpu.make_async_copy(codes_hbm, codes_ref, sems.at[1])
    lengths_copy.start()
    codes_copy.start()
    piece = tokens // PIECES
    copies = []
    for k in range(PIECES):
        at = pl.ds(k * piece, piece)
        copies.append(
            pltpu.make_async_copy(residuals_hbm.at[at], residuals.at[at], sems.at[3 + k])
        )
        copies[-1].start()
    lengths_copy.wait()

    def listing(p, chunks):
        for k in range(slots // CHUNK):
            starts_ref[chunks + k] = p * slots + k * CHUNK
        return chunks + quotient(lengths_ref[p] + CHUNK - 1, CHUNK)

    chunks = lax.fori_loop(0, passages, listing, 0, unroll=4)
    for k in range(SCORE_GROUP):
        starts_ref[chunks + k] = tokens
    starts_ref[starts_ref.shape[0] - 1] = chunks
    starts_copy = pltpu.make_async_copy(starts_ref, starts_hbm, sems.at[2])
    starts_copy.start()

    slot_numbers = lax.broadcasted_iota(jnp.int32, (CHUNK, width), 0)
    table_single = table.reshape(table.shape[0], 1, width)
    rows_single = rows.reshape(rows.shape[0], 1, width)

    def fetch(g):
        for k in range(GROUP):
            at = jnp.minimum(starts_ref[g * GROUP + k], tokens - CHUNK)
            for j in range(0, CHUNK, 2):
                pair = codes_ref[at + j]
                rows_single[k * CHUNK + j] = table_single[pair & 0xFFFF]
                rows_single[k * CHUNK + j + 1] = table_single[lax.shift_right_logical(pair, 16)]

    def finish(g):
        summed = []
        for k in range(GROUP):
            at = jnp.minimum(starts_ref[g * GROUP + k], tokens - CHUNK)
            near = residuals[pl.ds(pl.multiple_of(at, CHUNK), CHUNK), :]
            vectors = rows[pl.ds(k * CHUNK, CHUNK), :] + near.astype(jnp.float32)
            p = quotient(at, slots)
            live = slot_numbers < lengths_ref[p] - (at - p * slots)
            summed.append(jnp.where(live, vectors, vectors[0:1, :]))
        return normalized(jnp.concatenate(summed, axis=0))

    def keep(g, done):
        size = GROUP * CHUNK
        embedded[pl.ds(pl.multiple_of(g * size, size), size), :] = done

    codes_copy.wait()
    groups = quotient(chunks + GROUP - 1, GROUP)
    fetch(0)
    for copy in copies:
        copy.wait()

    def decode(g, carry):
        done = finish(g - 1)
        fetch(g)
        keep(g - 1, done)
        return carry

    lax.fori_loop(1, groups, decode, 0)
    keep(groups - 1, finish(groups - 1))
    starts_copy.wait()


def decode_all(token_codes, lengths, residuals, table):
    tokens, width = residuals.shape
    rounding = SCORE_GROUP * CHUNK
    passages, slots = token_codes.shape
    most = tokens // CHUNK + SCORE_GROUP + slots // CHUNK
    most = -(-most // 128) * 128
    return pl.pallas_call(
        decode_kernel,
        out_shape=(
            jax.ShapeDtypeStruct((-(-tokens // rounding) * rounding, width), jnp.bfloat16),
            pltpu.HBM((most,), jnp.int32),
        ),
        in_specs=[HBM, HBM, HBM, VMEM],
        out_specs=(VMEM, HBM),
        scratch_shapes=[
            pltpu.SMEM((tokens,), jnp.int32),
            pltpu.SMEM((passages,), jnp.int32),
            pltpu.SMEM((most,), jnp.int32),
            pltpu.VMEM((tokens, width), jnp.bfloat16),
            pltpu.VMEM((GROUP * CHUNK, width), jnp.float32),
            pltpu.SemaphoreType.DMA((3 + PIECES,)),
        ],
        compiler_params=granted(6),
        cost_estimate=pl.CostEstimate(flops=10**7, bytes_accessed=40 * 10**6, transcendentals=0),
        name="decode",
    )(
        pinned(token_codes.reshape(tokens)),
        pinned(lengths),
        pinned(residuals),
        pinned(table, pltpu.VMEM),
    )


def score_kernel(
    token_count, slots, starts_hbm, queries_ref, embedded, out_ref, at_ref, turned, largest, sem
):
    starts_copy = pltpu.make_async_copy(starts_hbm, at_ref, sem)
    starts_copy.start()
    passages = out_ref.shape[1]
    query_tokens = queries_ref.shape[0]
    block = min(QUERY_BLOCK, query_tokens)
    blocks = query_tokens // block
    per_block = block // token_count
    owner = lax.broadcasted_iota(jnp.int32, (per_block, block), 0)
    token_of = lax.broadcasted_iota(jnp.int32, (per_block, block), 1) // token_count
    summing = (owner == token_of).astype(jnp.bfloat16)

    def score_block(b, carry):
        at = pl.ds(pl.multiple_of(b * block, block), block)
        vectors = normalized(queries_ref[at, :].astype(jnp.float32))
        turned[...] = vectors.astype(jnp.float32).T.astype(jnp.bfloat16)

        def score(g, so_far):
            count = SCORE_GROUP // SCORE_PARTS
            size = count * CHUNK
            for part in range(SCORE_PARTS):
                first = g * SCORE_PARTS + part
                at = pl.ds(pl.multiple_of(first * size, size), size)
                similar = jnp.dot(embedded[at, :], turned[...], preferred_element_type=jnp.float32)
                parts = jnp.max(similar.reshape(count, CHUNK // 8, 8, block), axis=1)
                for k in range(count):
                    start = at_ref[first * count + k]
                    p = quotient(start, slots)
                    so_far = jnp.where(start == p * slots, parts[k], jnp.maximum(so_far, parts[k]))
                    to = pl.multiple_of(p * 8, 8)
                    for lane in range(block // 128):
                        largest[lane, pl.ds(to, 8), :] = so_far[:, lane * 128 : (lane + 1) * 128]
            return so_far

        @pl.when(b == 0)
        def arrived():
            starts_copy.wait()

        groups = quotient(at_ref[at_ref.shape[0] - 1] + SCORE_GROUP - 1, SCORE_GROUP)
        lax.fori_loop(0, groups, score, jnp.zeros((8, block), jnp.float32))
        kept = []
        for lane in range(block // 128):
            best = largest[lane, pl.ds(0, passages, stride=8), :]
            for k in range(1, 8):
                best = jnp.maximum(best, largest[lane, pl.ds(k, passages, stride=8), :])
            kept.append(best)
        best = jnp.concatenate(kept, axis=1)
        sums = jnp.zeros((per_block, passages), jnp.float32)
        for _ in range(3):
            part = best.astype(jnp.bfloat16)
            best = best - part.astype(jnp.float32)
            sums = sums + lax.dot_general(
                summing, part, (((1,), (1,)), ((), ())), preferred_element_type=jnp.float32
            )
        out_ref[pl.ds(pl.multiple_of(b * per_block, per_block), per_block), :] = sums
        return carry

    lax.fori_loop(0, blocks, score_block, 0)


def score_all(starts, query_rows, embedded, passages, slots, token_count):
    query_tokens, width = query_rows.shape
    block = min(QUERY_BLOCK, query_tokens)
    blocks = query_tokens // block
    return pl.pallas_call(
        functools.partial(score_kernel, token_count, slots),
        out_shape=jax.ShapeDtypeStruct((query_tokens // token_count, passages), jnp.float32),
        in_specs=[HBM, VMEM, VMEM],
        out_specs=VMEM,
        scratch_shapes=[
            pltpu.SMEM(starts.shape, jnp.int32),
            pltpu.VMEM((width, block), jnp.bfloat16),
            pltpu.VMEM((block // 128, (passages + 1) * 8, 128), jnp.float32),
            pltpu.SemaphoreType.DMA,
        ],
        compiler_params=granted(8 + 2 * blocks),
        name="score",
    )(pinned(starts), query_rows, embedded)


def pick_kernel(passages, candidates_ref, returned_ref, out_ref):
    local_queries, count = candidates_ref.shape
    targets = returned_ref.shape[0]
    passage_numbers = lax.broadcasted_iota(jnp.int32, (passages, count), 0)
    target_numbers = lax.broadcasted_iota(jnp.int32, (targets, count), 0)
    for q in range(local_queries):
        wanted = candidates_ref[q : q + 1, :]
        target = quotient(wanted, passages)
        hits = (passage_numbers == wanted - target * passages).astype(jnp.bfloat16)
        left = returned_ref[:, q * passages : (q + 1) * passages]
        picked = jnp.zeros((targets, count), jnp.float32)
        for _ in range(3):
            part = left.astype(jnp.bfloat16)
            left = left - part.astype(jnp.float32)
            picked = picked + jnp.dot(part, hits, preferred_element_type=jnp.float32)
        kept = jnp.where(target_numbers == target, picked, 0.0)
        out_ref[q : q + 1, :] = jnp.sum(kept, axis=0, keepdims=True)


def pick(candidates, returned, passages):
    return pl.pallas_call(
        functools.partial(pick_kernel, passages),
        out_shape=jax.ShapeDtypeStruct(candidates.shape, jnp.float32),
        in_specs=[VMEM, VMEM],
        out_specs=VMEM,
        compiler_params=granted(8),
        name="pick",
    )(candidates, pltpu.with_memory_space_constraint(returned, pltpu.VMEM))


def body(queries, candidates, token_codes, residuals, lengths, centroids):
    local_queries, token_count, width = queries.shape
    targets = lax.axis_size("shard") * lax.axis_size("sub")
    passages, slots = token_codes.shape
    half = lax.axis_index("sub").astype(jnp.int32)
    other = lax.ppermute(centroids, "sub", [(0, 1), (1, 0)])
    sent = spread(queries.reshape(local_queries * token_count, width), targets)
    gathered = lax.all_to_all(sent, ("shard", "sub"), split_axis=0, concat_axis=0, tiled=True)
    query_rows = gathered.reshape(targets * local_queries * token_count, width)
    flat = residuals.reshape(passages * slots, width)
    table, paired = widen(half.reshape(1), token_codes, centroids, other)
    embedded, starts = decode_all(paired, lengths, flat, table)
    scores = score_all(starts, query_rows, embedded, passages, slots, token_count)
    returned = lax.all_to_all(
        scores.reshape(targets, local_queries * passages),
        ("shard", "sub"),
        split_axis=0,
        concat_axis=0,
        tiled=True,
    )
    return pick(candidates, returned, passages)


def solution(mesh):
    placed = (
        P(("groups", "shard", "sub"), None, None),
        P(("groups", "shard", "sub"), None),
        P(("groups", "shard", "sub"), None),
        P(("groups", "shard", "sub"), None, None),
        P(("groups", "shard", "sub")),
        P(("groups", "shard", "sub"), None),
    )
    return jax.shard_map(
        body,
        mesh=mesh,
        in_specs=placed,
        out_specs=P(("groups", "shard", "sub"), None),
        check_vma=False,
    )
```

```python
import functools

import jax
import jax.numpy as jnp
from jax import lax
from jax.experimental import pallas as pl
from jax.experimental.pallas import tpu as pltpu
from jax.sharding import PartitionSpec as P

CHUNK = 16
GROUP = 16
SCORE_GROUP = 64
SCORE_PARTS = 2
PIECES = 4
QUERY_BLOCK = 512
SMEM = pl.BlockSpec(memory_space=pltpu.SMEM)
VMEM = pl.BlockSpec(memory_space=pltpu.VMEM)
HBM = pl.BlockSpec(memory_space=pltpu.HBM)


def normalized(vectors):
    squares = vectors * vectors
    high = squares.astype(jnp.bfloat16)
    low = (squares - high.astype(jnp.float32)).astype(jnp.bfloat16)
    ones = jnp.ones((2 * vectors.shape[1], vectors.shape[1]), jnp.bfloat16)
    split = jnp.concatenate([high, low], axis=1)
    total = jnp.dot(split, ones, preferred_element_type=jnp.float32)
    return (vectors * lax.rsqrt(total + 1e-06)).astype(jnp.bfloat16)


def quotient(number, divisor):
    if divisor & (divisor - 1) == 0:
        return lax.shift_right_logical(number, divisor.bit_length() - 1)
    return lax.div(number, divisor)


def pinned(array, space=pltpu.HBM):
    return pltpu.with_memory_space_constraint(array, space)


def granted(mebibytes):
    return pltpu.CompilerParams(vmem_limit_bytes=mebibytes * 1024 * 1024)


def spread_kernel(queries_ref, out_ref):
    queries = queries_ref[...]

    def copy(t, carry):
        out_ref[t] = queries
        return carry

    lax.fori_loop(0, out_ref.shape[0], copy, 0, unroll=8)


def spread(queries, targets):
    return pl.pallas_call(
        spread_kernel,
        out_shape=pltpu.VMEM((targets,) + queries.shape, jnp.bfloat16),
        in_specs=[VMEM],
        out_specs=VMEM,
        compiler_params=granted(4),
        name="spread",
    )(pinned(queries))


def widen_kernel(half_ref, own_hbm, other_ref, table, staged, sems):
    half_rows = own_hbm.shape[0]
    half = half_ref[0]
    piece = half_rows // PIECES
    copies = []
    for k in range(PIECES):
        at = pl.ds(k * piece, piece)
        copies.append(pltpu.make_async_copy(own_hbm.at[at], staged.at[at], sems.at[k]))
        copies[-1].start()

    def widened(ref, base, k):
        to = pl.ds(pl.multiple_of(base + k * piece, piece), piece)
        table[to, :] = ref[pl.ds(k * piece, piece), :].astype(jnp.float32)

    for k in range(PIECES):
        widened(other_ref, (1 - half) * half_rows, k)
    for k in range(PIECES):
        copies[k].wait()
        widened(staged, half * half_rows, k)


def widen(half, own, other):
    half_rows, width = own.shape
    return pl.pallas_call(
        widen_kernel,
        out_shape=pltpu.VMEM((2 * half_rows, width), jnp.float32),
        in_specs=[SMEM, HBM, VMEM],
        out_specs=VMEM,
        scratch_shapes=[
            pltpu.VMEM((half_rows, width), jnp.bfloat16),
            pltpu.SemaphoreType.DMA((PIECES,)),
        ],
        compiler_params=granted(4),
        cost_estimate=pl.CostEstimate(flops=10**7, bytes_accessed=10**7, transcendentals=0),
        name="widen",
    )(half, pinned(own), pinned(other, pltpu.VMEM))


def decode_kernel(
    codes_hbm,
    lengths_hbm,
    residuals_hbm,
    table,
    embedded,
    starts_hbm,
    codes_ref,
    lengths_ref,
    starts_ref,
    residuals,
    rows,
    sems,
):
    tokens, width = residuals.shape
    passages = lengths_ref.shape[0]
    slots = tokens // passages
    lengths_copy = pltpu.make_async_copy(lengths_hbm, lengths_ref, sems.at[0])
    codes_copy = pltpu.make_async_copy(codes_hbm, codes_ref, sems.at[1])
    lengths_copy.start()
    codes_copy.start()
    piece = tokens // PIECES
    copies = []
    for k in range(PIECES):
        at = pl.ds(k * piece, piece)
        copies.append(
            pltpu.make_async_copy(residuals_hbm.at[at], residuals.at[at], sems.at[3 + k])
        )
        copies[-1].start()
    lengths_copy.wait()

    def listing(p, chunks):
        for k in range(slots // CHUNK):
            starts_ref[chunks + k] = p * slots + k * CHUNK
        return chunks + quotient(lengths_ref[p] + CHUNK - 1, CHUNK)

    chunks = lax.fori_loop(0, passages, listing, 0, unroll=4)
    for k in range(SCORE_GROUP):
        starts_ref[chunks + k] = tokens
    starts_ref[starts_ref.shape[0] - 1] = chunks
    starts_copy = pltpu.make_async_copy(starts_ref, starts_hbm, sems.at[2])
    starts_copy.start()

    slot_numbers = lax.broadcasted_iota(jnp.int32, (CHUNK, width), 0)
    table_single = table.reshape(table.shape[0], 1, width)
    rows_single = rows.reshape(rows.shape[0], 1, width)

    def fetch(g):
        for k in range(GROUP):
            at = jnp.minimum(starts_ref[g * GROUP + k], tokens - CHUNK)
            for j in range(CHUNK):
                rows_single[k * CHUNK + j] = table_single[codes_ref[at + j]]

    def finish(g):
        summed = []
        for k in range(GROUP):
            at = jnp.minimum(starts_ref[g * GROUP + k], tokens - CHUNK)
            near = residuals[pl.ds(pl.multiple_of(at, CHUNK), CHUNK), :]
            vectors = rows[pl.ds(k * CHUNK, CHUNK), :] + near.astype(jnp.float32)
            p = quotient(at, slots)
            live = slot_numbers < lengths_ref[p] - (at - p * slots)
            summed.append(jnp.where(live, vectors, vectors[0:1, :]))
        return normalized(jnp.concatenate(summed, axis=0))

    def keep(g, done):
        size = GROUP * CHUNK
        embedded[pl.ds(pl.multiple_of(g * size, size), size), :] = done

    codes_copy.wait()
    groups = quotient(chunks + GROUP - 1, GROUP)
    fetch(0)
    for copy in copies:
        copy.wait()

    def decode(g, carry):
        done = finish(g - 1)
        fetch(g)
        keep(g - 1, done)
        return carry

    lax.fori_loop(1, groups, decode, 0)
    keep(groups - 1, finish(groups - 1))
    starts_copy.wait()


def decode_all(token_codes, lengths, residuals, table):
    tokens, width = residuals.shape
    rounding = SCORE_GROUP * CHUNK
    passages, slots = token_codes.shape
    most = tokens // CHUNK + SCORE_GROUP + slots // CHUNK
    most = -(-most // 128) * 128
    return pl.pallas_call(
        decode_kernel,
        out_shape=(
            jax.ShapeDtypeStruct((-(-tokens // rounding) * rounding, width), jnp.bfloat16),
            pltpu.HBM((most,), jnp.int32),
        ),
        in_specs=[HBM, HBM, HBM, VMEM],
        out_specs=(VMEM, HBM),
        scratch_shapes=[
            pltpu.SMEM((tokens,), jnp.int32),
            pltpu.SMEM((passages,), jnp.int32),
            pltpu.SMEM((most,), jnp.int32),
            pltpu.VMEM((tokens, width), jnp.bfloat16),
            pltpu.VMEM((GROUP * CHUNK, width), jnp.float32),
            pltpu.SemaphoreType.DMA((3 + PIECES,)),
        ],
        compiler_params=granted(6),
        cost_estimate=pl.CostEstimate(flops=10**7, bytes_accessed=40 * 10**6, transcendentals=0),
        name="decode",
    )(
        pinned(token_codes.reshape(tokens)),
        pinned(lengths),
        pinned(residuals),
        pinned(table, pltpu.VMEM),
    )


def score_kernel(
    token_count, slots, starts_hbm, queries_ref, embedded, out_ref, at_ref, turned, largest, sem
):
    starts_copy = pltpu.make_async_copy(starts_hbm, at_ref, sem)
    starts_copy.start()
    passages = out_ref.shape[1]
    query_tokens = queries_ref.shape[0]
    block = min(QUERY_BLOCK, query_tokens)
    blocks = query_tokens // block
    per_block = block // token_count
    owner = lax.broadcasted_iota(jnp.int32, (per_block, block), 0)
    token_of = lax.broadcasted_iota(jnp.int32, (per_block, block), 1) // token_count
    summing = (owner == token_of).astype(jnp.bfloat16)

    def score_block(b, carry):
        at = pl.ds(pl.multiple_of(b * block, block), block)
        vectors = normalized(queries_ref[at, :].astype(jnp.float32))
        turned[...] = vectors.astype(jnp.float32).T.astype(jnp.bfloat16)

        def score(g, so_far):
            count = SCORE_GROUP // SCORE_PARTS
            size = count * CHUNK
            for part in range(SCORE_PARTS):
                first = g * SCORE_PARTS + part
                at = pl.ds(pl.multiple_of(first * size, size), size)
                similar = jnp.dot(embedded[at, :], turned[...], preferred_element_type=jnp.float32)
                parts = jnp.max(similar.reshape(count, CHUNK // 8, 8, block), axis=1)
                for k in range(count):
                    start = at_ref[first * count + k]
                    p = quotient(start, slots)
                    so_far = jnp.where(start == p * slots, parts[k], jnp.maximum(so_far, parts[k]))
                    to = pl.multiple_of(p * 8, 8)
                    for lane in range(block // 128):
                        largest[lane, pl.ds(to, 8), :] = so_far[:, lane * 128 : (lane + 1) * 128]
            return so_far

        @pl.when(b == 0)
        def arrived():
            starts_copy.wait()

        groups = quotient(at_ref[at_ref.shape[0] - 1] + SCORE_GROUP - 1, SCORE_GROUP)
        lax.fori_loop(0, groups, score, jnp.zeros((8, block), jnp.float32))
        kept = []
        for lane in range(block // 128):
            best = largest[lane, pl.ds(0, passages, stride=8), :]
            for k in range(1, 8):
                best = jnp.maximum(best, largest[lane, pl.ds(k, passages, stride=8), :])
            kept.append(best)
        best = jnp.concatenate(kept, axis=1)
        sums = jnp.zeros((per_block, passages), jnp.float32)
        for _ in range(3):
            part = best.astype(jnp.bfloat16)
            best = best - part.astype(jnp.float32)
            sums = sums + lax.dot_general(
                summing, part, (((1,), (1,)), ((), ())), preferred_element_type=jnp.float32
            )
        out_ref[pl.ds(pl.multiple_of(b * per_block, per_block), per_block), :] = sums
        return carry

    lax.fori_loop(0, blocks, score_block, 0)


def score_all(starts, query_rows, embedded, passages, slots, token_count):
    query_tokens, width = query_rows.shape
    block = min(QUERY_BLOCK, query_tokens)
    blocks = query_tokens // block
    return pl.pallas_call(
        functools.partial(score_kernel, token_count, slots),
        out_shape=jax.ShapeDtypeStruct((query_tokens // token_count, passages), jnp.float32),
        in_specs=[HBM, VMEM, VMEM],
        out_specs=VMEM,
        scratch_shapes=[
            pltpu.SMEM(starts.shape, jnp.int32),
            pltpu.VMEM((width, block), jnp.bfloat16),
            pltpu.VMEM((block // 128, (passages + 1) * 8, 128), jnp.float32),
            pltpu.SemaphoreType.DMA,
        ],
        compiler_params=granted(8 + 2 * blocks),
        name="score",
    )(pinned(starts), query_rows, embedded)


def pick_kernel(passages, candidates_ref, returned_ref, out_ref):
    local_queries, count = candidates_ref.shape
    targets = returned_ref.shape[0]
    passage_numbers = lax.broadcasted_iota(jnp.int32, (passages, count), 0)
    target_numbers = lax.broadcasted_iota(jnp.int32, (targets, count), 0)
    for q in range(local_queries):
        wanted = candidates_ref[q : q + 1, :]
        target = quotient(wanted, passages)
        hits = (passage_numbers == wanted - target * passages).astype(jnp.bfloat16)
        left = returned_ref[:, q * passages : (q + 1) * passages]
        picked = jnp.zeros((targets, count), jnp.float32)
        for _ in range(3):
            part = left.astype(jnp.bfloat16)
            left = left - part.astype(jnp.float32)
            picked = picked + jnp.dot(part, hits, preferred_element_type=jnp.float32)
        kept = jnp.where(target_numbers == target, picked, 0.0)
        out_ref[q : q + 1, :] = jnp.sum(kept, axis=0, keepdims=True)


def pick(candidates, returned, passages):
    return pl.pallas_call(
        functools.partial(pick_kernel, passages),
        out_shape=jax.ShapeDtypeStruct(candidates.shape, jnp.float32),
        in_specs=[VMEM, VMEM],
        out_specs=VMEM,
        compiler_params=granted(8),
        name="pick",
    )(candidates, pltpu.with_memory_space_constraint(returned, pltpu.VMEM))


def body(queries, candidates, token_codes, residuals, lengths, centroids):
    local_queries, token_count, width = queries.shape
    targets = lax.axis_size("shard") * lax.axis_size("sub")
    passages, slots = token_codes.shape
    half = lax.axis_index("sub").astype(jnp.int32)
    other = lax.ppermute(centroids, "sub", [(0, 1), (1, 0)])
    sent = spread(queries.reshape(local_queries * token_count, width), targets)
    gathered = lax.all_to_all(sent, ("shard", "sub"), split_axis=0, concat_axis=0, tiled=True)
    query_rows = gathered.reshape(targets * local_queries * token_count, width)
    flat = residuals.reshape(passages * slots, width)
    table = widen(half.reshape(1), centroids, other)
    embedded, starts = decode_all(token_codes, lengths, flat, table)
    scores = score_all(starts, query_rows, embedded, passages, slots, token_count)
    returned = lax.all_to_all(
        scores.reshape(targets, local_queries * passages),
        ("shard", "sub"),
        split_axis=0,
        concat_axis=0,
        tiled=True,
    )
    return pick(candidates, returned, passages)


def solution(mesh):
    placed = (
        P(("groups", "shard", "sub"), None, None),
        P(("groups", "shard", "sub"), None),
        P(("groups", "shard", "sub"), None),
        P(("groups", "shard", "sub"), None, None),
        P(("groups", "shard", "sub")),
        P(("groups", "shard", "sub"), None),
    )
    return jax.shard_map(
        body,
        mesh=mesh,
        in_specs=placed,
        out_specs=P(("groups", "shard", "sub"), None),
        check_vma=False,
    )
```

```python
import functools

import jax
import jax.numpy as jnp
from jax import lax
from jax.experimental import pallas as pl
from jax.experimental.pallas import tpu as pltpu
from jax.sharding import PartitionSpec as P

CHUNK = 16
GROUP = 16
SCORE_GROUP = 64
SCORE_PARTS = 2
STEPS = 3
PIECES = 4
QUERY_BLOCK = 512
SMEM = pl.BlockSpec(memory_space=pltpu.SMEM)
VMEM = pl.BlockSpec(memory_space=pltpu.VMEM)
HBM = pl.BlockSpec(memory_space=pltpu.HBM)


def normalized(vectors):
    total = jnp.sum(vectors * vectors, axis=-1, keepdims=True)
    return (vectors * lax.rsqrt(total + 1e-06)).astype(jnp.bfloat16)


def quotient(number, divisor):
    if divisor & (divisor - 1) == 0:
        return lax.shift_right_logical(number, divisor.bit_length() - 1)
    return lax.div(number, divisor)


def pinned(array, space=pltpu.HBM):
    return pltpu.with_memory_space_constraint(array, space)


def granted(mebibytes):
    return pltpu.CompilerParams(vmem_limit_bytes=mebibytes * 1024 * 1024)


def prepare_kernel(
    half_ref,
    lengths_hbm,
    codes_hbm,
    own_hbm,
    residuals_hbm,
    table,
    residuals,
    codes,
    starts,
    lives,
    nothing,
    lengths_ref,
    starts_ref,
    lives_ref,
    staged,
    sems,
):
    passages = lengths_ref.shape[0]
    slots = codes_hbm.shape[0] // passages
    half_rows = own_hbm.shape[0]
    moves = []

    def move(source, to):
        moves.append(pltpu.make_async_copy(source, to, sems.at[len(moves)]))
        moves[-1].start()
        return moves[-1]

    lengths_copy = move(lengths_hbm, lengths_ref)
    piece = half_rows // PIECES
    copies = []
    for k in range(PIECES):
        at = pl.ds(k * piece, piece)
        copies.append(move(own_hbm.at[at], staged.at[at]))
    codes_copy = move(codes_hbm, codes)
    residual_copy = move(residuals_hbm, residuals)
    nothing[...] = jnp.zeros(nothing.shape, nothing.dtype)
    lengths_copy.wait()

    def listing(p, chunks):
        length = lengths_ref[p]
        for k in range(slots // CHUNK):
            starts_ref[chunks + k] = p * slots + k * CHUNK
            lives_ref[chunks + k] = length - k * CHUNK
        return chunks + quotient(length + CHUNK - 1, CHUNK)

    chunks = lax.fori_loop(0, passages, listing, 0, unroll=4)
    for k in range(SCORE_GROUP):
        starts_ref[chunks + k] = passages * slots
        lives_ref[chunks + k] = 0
    starts_ref[starts_ref.shape[0] - 1] = chunks
    starts_copy = move(starts_ref, starts)
    lives_copy = move(lives_ref, lives)
    for k in range(PIECES):
        copies[k].wait()
        to = pl.ds(pl.multiple_of(half_ref[0] * half_rows + k * piece, piece), piece)
        table[to, :] = staged[pl.ds(k * piece, piece), :].astype(jnp.float32)
    for copy in (codes_copy, starts_copy, lives_copy, residual_copy):
        copy.wait()


def prepare(half, lengths, token_codes, own, residuals):
    half_rows, width = own.shape
    passages = lengths.shape[0]
    slots = token_codes.shape[0] // passages
    most = passages * (slots // CHUNK) + SCORE_GROUP + slots // CHUNK
    most = -(-most // 1024) * 1024
    return pl.pallas_call(
        prepare_kernel,
        out_shape=(
            pltpu.VMEM((2 * half_rows, width), jnp.float32),
            pltpu.VMEM(residuals.shape, jnp.bfloat16),
            pltpu.VMEM(token_codes.shape, jnp.int32),
            pltpu.VMEM((most,), jnp.int32),
            pltpu.VMEM((most,), jnp.int32),
            pltpu.VMEM((16, width), jnp.bfloat16),
        ),
        in_specs=[SMEM, HBM, HBM, HBM, HBM],
        out_specs=(VMEM,) * 6,
        scratch_shapes=[
            pltpu.SMEM(lengths.shape, jnp.int32),
            pltpu.SMEM((most,), jnp.int32),
            pltpu.SMEM((most,), jnp.int32),
            pltpu.VMEM((half_rows, width), jnp.bfloat16),
            pltpu.SemaphoreType.DMA((5 + PIECES,)),
        ],
        compiler_params=granted(4),
        cost_estimate=pl.CostEstimate(flops=10**7, bytes_accessed=8 * 10**6, transcendentals=0),
        name="prepare",
    )(half, pinned(lengths), pinned(token_codes), pinned(own), pinned(residuals))


def decode_kernel(step, *refs):
    if step == 0:
        half_ref, other_ref, codes, starts, lives, residuals, _, _, table, embedded = refs[:10]
    else:
        codes, starts, lives, residuals, table, _, _, embedded = refs[:8]
    nothing, codes_ref, starts_ref, lives_ref, rows, sems = refs[-6:]
    tokens = codes_ref.shape[0]
    width = rows.shape[1]
    moves = []
    pairs = ((starts, starts_ref), (lives, lives_ref), (codes, codes_ref))
    for k, (source, to) in enumerate(pairs):
        moves.append(pltpu.make_async_copy(source, to, sems.at[k]))
        moves[-1].start()
    nothing[...] = jnp.zeros(nothing.shape, nothing.dtype)
    if step == 0:
        half_rows = other_ref.shape[0]
        piece = half_rows // PIECES
        for k in range(PIECES):
            to = pl.ds(pl.multiple_of((1 - half_ref[0]) * half_rows + k * piece, piece), piece)
            table[to, :] = other_ref[pl.ds(k * piece, piece), :].astype(jnp.float32)

    slot_numbers = lax.broadcasted_iota(jnp.int32, (CHUNK, width), 0)
    table_single = table.reshape(table.shape[0], 1, width)
    rows_single = rows.reshape(rows.shape[0], 1, width)

    def fetch(g):
        for k in range(GROUP):
            at = jnp.minimum(starts_ref[g * GROUP + k], tokens - CHUNK)
            for j in range(CHUNK):
                rows_single[k * CHUNK + j] = table_single[codes_ref[at + j]]

    def finish(g):
        summed = []
        for k in range(GROUP):
            at = jnp.minimum(starts_ref[g * GROUP + k], tokens - CHUNK)
            near = residuals[pl.ds(pl.multiple_of(at, CHUNK), CHUNK), :]
            vectors = rows[pl.ds(k * CHUNK, CHUNK), :] + near.astype(jnp.float32)
            live = slot_numbers < lives_ref[g * GROUP + k]
            summed.append(jnp.where(live, vectors, vectors[0:1, :]))
        return normalized(jnp.concatenate(summed, axis=0))

    def keep(g, done):
        size = GROUP * CHUNK
        embedded[pl.ds(pl.multiple_of(g * size, size), size), :] = done

    for move in moves:
        move.wait()
    groups = quotient(starts_ref[starts_ref.shape[0] - 1] + GROUP - 1, GROUP)
    groups = jnp.maximum(groups, STEPS)
    low = quotient(groups * (65536 * step // STEPS + 1), 65536)
    high = quotient(groups * (65536 * (step + 1) // STEPS + 1), 65536)
    fetch(low)

    def decode(g, carry):
        done = finish(g - 1)
        fetch(g)
        keep(g - 1, done)
        return carry

    lax.fori_loop(low + 1, high, decode, 0)
    keep(high - 1, finish(high - 1))


def decode_step(step, half, other, codes, starts, lives, residuals, table, embedded, held):
    tokens, width = residuals.shape
    rounding = SCORE_GROUP * CHUNK
    space = (-(-tokens // rounding) * rounding, width)
    inside = lambda array: pinned(array, pltpu.VMEM)
    shared = [inside(codes), inside(starts), inside(lives), inside(residuals), inside(table)]
    if step == 0:
        operands = [half, inside(other)] + shared + [inside(held)]
        in_specs = [SMEM] + [VMEM] * 7
        out_shape = [pltpu.VMEM(table.shape, table.dtype), pltpu.VMEM(space, jnp.bfloat16)]
        aliases = {6: 0}
    else:
        operands = shared + [inside(embedded), inside(held)]
        in_specs = [VMEM] * 7
        out_shape = [pltpu.VMEM(space, jnp.bfloat16)]
        aliases = {5: 0}
    out_shape.append(pltpu.VMEM((16, width), jnp.bfloat16))
    results = pl.pallas_call(
        functools.partial(decode_kernel, step),
        out_shape=tuple(out_shape),
        in_specs=in_specs,
        out_specs=(VMEM,) * len(out_shape),
        input_output_aliases=aliases,
        scratch_shapes=[
            pltpu.SMEM((tokens,), jnp.int32),
            pltpu.SMEM(starts.shape, jnp.int32),
            pltpu.SMEM(lives.shape, jnp.int32),
            pltpu.VMEM((GROUP * CHUNK, width), jnp.float32),
            pltpu.SemaphoreType.DMA((3,)),
        ],
        compiler_params=granted(4),
        cost_estimate=pl.CostEstimate(flops=10**7, bytes_accessed=10**7, transcendentals=0),
        name="decode",
    )(*operands)
    if step == 0:
        return results
    return (table,) + tuple(results)


def score_kernel(
    token_count,
    local_queries,
    slots,
    me_ref,
    starts,
    queries_ref,
    embedded,
    out_ref,
    at_ref,
    turned,
    largest,
    sem,
):
    starts_copy = pltpu.make_async_copy(starts, at_ref, sem)
    starts_copy.start()
    passages = out_ref.shape[1]
    query_tokens = queries_ref.shape[0]
    block = min(QUERY_BLOCK, query_tokens)
    blocks = query_tokens // block
    per_block = block // token_count
    owner = lax.broadcasted_iota(jnp.int32, (per_block, block), 0)
    token_of = quotient(lax.broadcasted_iota(jnp.int32, (per_block, block), 1), token_count)
    block_targets = per_block // local_queries
    near_me = me_ref[0] & (block_targets - 1)
    far_me = quotient(me_ref[0], block_targets)
    owner_target = quotient(owner, local_queries)
    relative = (owner_target ^ near_me) * local_queries + owner - owner_target * local_queries
    summing = (relative == token_of).astype(jnp.bfloat16)

    def score_block(b, carry):
        at = pl.ds(pl.multiple_of(b * block, block), block)
        vectors = normalized(queries_ref[at, :].astype(jnp.float32))
        turned[...] = vectors.astype(jnp.float32).T.astype(jnp.bfloat16)

        def score(g, so_far):
            count = SCORE_GROUP // SCORE_PARTS
            size = count * CHUNK
            for part in range(SCORE_PARTS):
                first = g * SCORE_PARTS + part
                at = pl.ds(pl.multiple_of(first * size, size), size)
                similar = jnp.dot(embedded[at, :], turned[...], preferred_element_type=jnp.float32)
                parts = jnp.max(similar.reshape(count, CHUNK // 8, 8, block), axis=1)
                for k in range(count):
                    start = at_ref[first * count + k]
                    p = quotient(start, slots)
                    so_far = jnp.where(start == p * slots, parts[k], jnp.maximum(so_far, parts[k]))
                    to = pl.multiple_of(p * 8, 8)
                    for lane in range(block // 128):
                        largest[lane, pl.ds(to, 8), :] = so_far[:, lane * 128 : (lane + 1) * 128]
            return so_far

        @pl.when(b == 0)
        def arrived():
            starts_copy.wait()

        groups = quotient(at_ref[at_ref.shape[0] - 1] + SCORE_GROUP - 1, SCORE_GROUP)
        lax.fori_loop(0, groups, score, jnp.zeros((8, block), jnp.float32))
        kept = []
        for lane in range(block // 128):
            best = largest[lane, pl.ds(0, passages, stride=8), :]
            for k in range(1, 8):
                best = jnp.maximum(best, largest[lane, pl.ds(k, passages, stride=8), :])
            kept.append(best)
        best = jnp.concatenate(kept, axis=1)
        sums = jnp.zeros((per_block, passages), jnp.float32)
        for _ in range(3):
            part = best.astype(jnp.bfloat16)
            best = best - part.astype(jnp.float32)
            sums = sums + lax.dot_general(
                summing, part, (((1,), (1,)), ((), ())), preferred_element_type=jnp.float32
            )
        to = pl.multiple_of((b ^ far_me) * per_block, per_block)
        out_ref[pl.ds(to, per_block), :] = sums
        return carry

    lax.fori_loop(0, blocks, score_block, 0)


def score_all(me, starts, query_rows, embedded, passages, slots, token_count, local_queries):
    query_tokens, width = query_rows.shape
    block = min(QUERY_BLOCK, query_tokens)
    blocks = query_tokens // block
    return pl.pallas_call(
        functools.partial(score_kernel, token_count, local_queries, slots),
        out_shape=jax.ShapeDtypeStruct((query_tokens // token_count, passages), jnp.float32),
        in_specs=[SMEM, VMEM, VMEM, VMEM],
        out_specs=VMEM,
        scratch_shapes=[
            pltpu.SMEM(starts.shape, jnp.int32),
            pltpu.VMEM((width, block), jnp.bfloat16),
            pltpu.VMEM((block // 128, (passages + 1) * 8, 128), jnp.float32),
            pltpu.SemaphoreType.DMA,
        ],
        compiler_params=granted(8 + 2 * blocks),
        name="score",
    )(
        me,
        pinned(starts, pltpu.VMEM),
        pinned(query_rows, pltpu.VMEM),
        pinned(embedded, pltpu.VMEM),
    )


def pick_kernel(passages, candidates_ref, returned_ref, out_ref):
    local_queries, count = candidates_ref.shape
    targets = returned_ref.shape[0]
    passage_numbers = lax.broadcasted_iota(jnp.int32, (passages, count), 0)
    target_numbers = lax.broadcasted_iota(jnp.int32, (targets, count), 0)
    for q in range(local_queries):
        wanted = candidates_ref[q : q + 1, :]
        target = quotient(wanted, passages)
        hits = (passage_numbers == wanted - target * passages).astype(jnp.bfloat16)
        left = returned_ref[:, q * passages : (q + 1) * passages]
        picked = jnp.zeros((targets, count), jnp.float32)
        for _ in range(3):
            part = left.astype(jnp.bfloat16)
            left = left - part.astype(jnp.float32)
            picked = picked + jnp.dot(part, hits, preferred_element_type=jnp.float32)
        kept = jnp.where(target_numbers == target, picked, 0.0)
        out_ref[q : q + 1, :] = jnp.sum(kept, axis=0, keepdims=True)


def pick(candidates, returned, passages):
    return pl.pallas_call(
        functools.partial(pick_kernel, passages),
        out_shape=jax.ShapeDtypeStruct(candidates.shape, jnp.float32),
        in_specs=[VMEM, VMEM],
        out_specs=VMEM,
        compiler_params=granted(8),
        name="pick",
    )(candidates, pltpu.with_memory_space_constraint(returned, pltpu.VMEM))


def body(queries, candidates, token_codes, residuals, lengths, centroids):
    local_queries, token_count, width = queries.shape
    targets = lax.axis_size("shard") * lax.axis_size("sub")
    passages, slots = token_codes.shape
    half = lax.axis_index("sub").astype(jnp.int32)
    me = lax.axis_index("shard").astype(jnp.int32) * lax.axis_size("sub") + half
    half = half.reshape(1)
    near = residuals.reshape(passages * slots, width)
    other = lax.ppermute(centroids, "sub", [(0, 1), (1, 0)])

    held = queries.reshape(1, 1, local_queries * token_count, width)
    bits = targets.bit_length() - 1
    embedded = None
    for turn, first in enumerate(range(bits - 1, -1, -1)):
        pairs = [(device, device ^ (1 << first)) for device in range(targets)]
        received = lax.ppermute(held, ("shard", "sub"), pairs)
        if turn == 0:
            ready = prepare(half, lengths, token_codes.reshape(passages * slots), centroids, near)
            table, near, codes, starts, lives, nothing = ready
        elif turn <= STEPS:
            table, embedded, nothing = decode_step(
                turn - 1, half, other, codes, starts, lives, near, table, embedded, held
            )
        received = received + nothing[0:1, :]
        held = jnp.concatenate([held, received], axis=1)
        if first > 0:
            held = held.reshape((-1, 1) + held.shape[2:])
    query_rows = held.reshape(targets * local_queries * token_count, width)
    scores = score_all(
        me.reshape(1), starts, query_rows, embedded, passages, slots, token_count, local_queries
    )
    returned = lax.all_to_all(
        scores.reshape(targets, local_queries * passages),
        ("shard", "sub"),
        split_axis=0,
        concat_axis=0,
        tiled=True,
    )
    return pick(candidates, returned, passages)


def solution(mesh):
    placed = (
        P(("groups", "shard", "sub"), None, None),
        P(("groups", "shard", "sub"), None),
        P(("groups", "shard", "sub"), None),
        P(("groups", "shard", "sub"), None, None),
        P(("groups", "shard", "sub")),
        P(("groups", "shard", "sub"), None),
    )
    return jax.shard_map(
        body,
        mesh=mesh,
        in_specs=placed,
        out_specs=P(("groups", "shard", "sub"), None),
        check_vma=False,
    )
```

```python
import functools

import jax
import jax.numpy as jnp
from jax import lax
from jax.experimental import pallas as pl
from jax.experimental.pallas import tpu as pltpu
from jax.sharding import PartitionSpec as P

CHUNK = 16
GROUP = 16
SCORE_GROUP = 64
SCORE_PARTS = 2
STEPS = 3
PIECES = 4
QUERY_BLOCK = 512
SMEM = pl.BlockSpec(memory_space=pltpu.SMEM)
VMEM = pl.BlockSpec(memory_space=pltpu.VMEM)
HBM = pl.BlockSpec(memory_space=pltpu.HBM)


def normalized(vectors):
    total = jnp.sum(vectors * vectors, axis=-1, keepdims=True)
    return (vectors * lax.rsqrt(total + 1e-06)).astype(jnp.bfloat16)


def quotient(number, divisor):
    if divisor & (divisor - 1) == 0:
        return lax.shift_right_logical(number, divisor.bit_length() - 1)
    return lax.div(number, divisor)


def pinned(array, space=pltpu.HBM):
    return pltpu.with_memory_space_constraint(array, space)


def granted(mebibytes):
    return pltpu.CompilerParams(vmem_limit_bytes=mebibytes * 1024 * 1024)


def shares_of(passages):
    units = -(-passages // 8)
    edges = [units * step // STEPS * 8 for step in range(STEPS)] + [passages]
    return list(zip(edges[:-1], edges[1:]))


def prepare_kernel(
    me_ref,
    lengths_hbm,
    codes_hbm,
    own_hbm,
    residuals_hbm,
    staged,
    residuals,
    codes,
    starts,
    lives,
    nothing,
    lengths_ref,
    starts_ref,
    lives_ref,
    sems,
):
    del me_ref
    passages = lengths_ref.shape[0]
    slots = codes_hbm.shape[0] // passages
    moves = []

    def move(source, to):
        moves.append(pltpu.make_async_copy(source, to, sems.at[len(moves)]))
        moves[-1].start()

    lengths_copy = pltpu.make_async_copy(lengths_hbm, lengths_ref, sems.at[5])
    lengths_copy.start()
    move(codes_hbm, codes)
    move(own_hbm, staged)
    move(residuals_hbm, residuals)
    nothing[...] = jnp.zeros(nothing.shape, nothing.dtype)
    lengths_copy.wait()

    def listing(p, chunks):
        length = lengths_ref[p]
        for k in range(slots // CHUNK):
            starts_ref[chunks + k] = p * slots + k * CHUNK
            lives_ref[chunks + k] = length - k * CHUNK
        return chunks + quotient(length + CHUNK - 1, CHUNK)

    last = starts_ref.shape[0] - 1
    chunks = jnp.int32(0)
    for step, (low, high) in enumerate(shares_of(passages)):
        chunks = lax.fori_loop(low, high, listing, chunks, unroll=4)
        for k in range(GROUP):
            starts_ref[chunks + k] = passages * slots
            lives_ref[chunks + k] = 0
        chunks = quotient(chunks + GROUP - 1, GROUP) * GROUP
        starts_ref[last - STEPS + step] = quotient(chunks, GROUP)
    for k in range(SCORE_GROUP):
        starts_ref[chunks + k] = passages * slots
    starts_ref[last] = chunks
    move(starts_ref, starts)
    move(lives_ref, lives)
    for copy in moves:
        copy.wait()


def list_size(passages, slots):
    most = passages * (slots // CHUNK) + STEPS * GROUP + SCORE_GROUP + STEPS + 1
    return -(-most // 1024) * 1024


def prepare(me, lengths, token_codes, own, residuals):
    width = own.shape[1]
    passages = lengths.shape[0]
    slots = token_codes.shape[0] // passages
    most = list_size(passages, slots)
    return pl.pallas_call(
        prepare_kernel,
        out_shape=(
            pltpu.VMEM(own.shape, jnp.bfloat16),
            pltpu.VMEM(residuals.shape, jnp.bfloat16),
            pltpu.VMEM(token_codes.shape, jnp.int32),
            pltpu.VMEM((most,), jnp.int32),
            pltpu.VMEM((most,), jnp.int32),
            pltpu.VMEM((16, width), jnp.bfloat16),
        ),
        in_specs=[SMEM, HBM, HBM, HBM, HBM],
        out_specs=(VMEM,) * 6,
        scratch_shapes=[
            pltpu.SMEM(lengths.shape, jnp.int32),
            pltpu.SMEM((most,), jnp.int32),
            pltpu.SMEM((most,), jnp.int32),
            pltpu.SemaphoreType.DMA((6,)),
        ],
        compiler_params=granted(4),
        cost_estimate=pl.CostEstimate(flops=10**7, bytes_accessed=8 * 10**6, transcendentals=0),
        name="prepare",
    )(me, pinned(lengths), pinned(token_codes), pinned(own), pinned(residuals))


def decode_kernel(step, passages, *refs):
    if step == 0:
        half_ref, own_ref, other_ref, codes, starts, lives, residuals, _, table, embedded = refs[:10]
    else:
        codes, starts, lives, residuals, table, _, _, embedded = refs[:8]
    nothing, codes_ref, starts_ref, lives_ref, rows, sems = refs[-6:]
    tokens = codes_ref.shape[0]
    slots = tokens // passages
    width = rows.shape[1]
    moves = []
    first, after = shares_of(passages)[step]
    part = pl.ds(first * slots, (after - first) * slots)
    pairs = ((starts, starts_ref), (lives, lives_ref), (codes.at[part], codes_ref.at[part]))
    for k, (source, to) in enumerate(pairs):
        moves.append(pltpu.make_async_copy(source, to, sems.at[k]))
        moves[-1].start()
    nothing[...] = jnp.zeros(nothing.shape, nothing.dtype)
    if step == 0:
        half_rows = other_ref.shape[0]
        piece = half_rows // PIECES
        for source, base in ((own_ref, half_ref[0]), (other_ref, 1 - half_ref[0])):
            for k in range(PIECES):
                to = pl.ds(pl.multiple_of(base * half_rows + k * piece, piece), piece)
                table[to, :] = source[pl.ds(k * piece, piece), :].astype(jnp.float32)

    slot_numbers = lax.broadcasted_iota(jnp.int32, (CHUNK, width), 0)
    table_single = table.reshape(table.shape[0], 1, width)
    rows_single = rows.reshape(rows.shape[0], 1, width)

    def fetch(g):
        for k in range(GROUP):
            at = jnp.minimum(starts_ref[g * GROUP + k], after * slots - CHUNK)
            for j in range(CHUNK):
                rows_single[k * CHUNK + j] = table_single[codes_ref[at + j]]

    def finish(g):
        summed = []
        for k in range(GROUP):
            at = jnp.minimum(starts_ref[g * GROUP + k], tokens - CHUNK)
            near = residuals[pl.ds(pl.multiple_of(at, CHUNK), CHUNK), :]
            vectors = rows[pl.ds(k * CHUNK, CHUNK), :] + near.astype(jnp.float32)
            live = slot_numbers < lives_ref[g * GROUP + k]
            summed.append(jnp.where(live, vectors, vectors[0:1, :]))
        return normalized(jnp.concatenate(summed, axis=0))

    def keep(g, done):
        size = GROUP * CHUNK
        embedded[pl.ds(pl.multiple_of(g * size, size), size), :] = done

    for move in moves:
        move.wait()
    last = starts_ref.shape[0] - 1
    low = starts_ref[last - STEPS + step - 1] if step > 0 else 0
    high = starts_ref[last - STEPS + step]
    fetch(low)

    def decode(g, carry):
        done = finish(g - 1)
        fetch(g)
        keep(g - 1, done)
        return carry

    lax.fori_loop(low + 1, high, decode, 0)
    keep(high - 1, finish(high - 1))


def decode_step(
    step, passages, half, own, other, codes, starts, lives, residuals, table, embedded, held
):
    tokens, width = residuals.shape
    rounding = SCORE_GROUP * CHUNK
    space = (-(-(tokens + STEPS * GROUP * CHUNK) // rounding) * rounding, width)
    inside = lambda array: pinned(array, pltpu.VMEM)
    shared = [inside(codes), inside(starts), inside(lives), inside(residuals)]
    if step == 0:
        operands = [half, inside(own), inside(other)] + shared + [inside(held)]
        in_specs = [SMEM] + [VMEM] * 7
        whole = (2 * own.shape[0], width)
        out_shape = [pltpu.VMEM(whole, jnp.float32), pltpu.VMEM(space, jnp.bfloat16)]
        aliases = {}
    else:
        operands = shared + [inside(table), inside(embedded), inside(held)]
        in_specs = [VMEM] * 7
        out_shape = [pltpu.VMEM(space, jnp.bfloat16)]
        aliases = {5: 0}
    out_shape.append(pltpu.VMEM((16, width), jnp.bfloat16))
    results = pl.pallas_call(
        functools.partial(decode_kernel, step, passages),
        out_shape=tuple(out_shape),
        in_specs=in_specs,
        out_specs=(VMEM,) * len(out_shape),
        input_output_aliases=aliases,
        scratch_shapes=[
            pltpu.SMEM((tokens,), jnp.int32),
            pltpu.SMEM(starts.shape, jnp.int32),
            pltpu.SMEM(lives.shape, jnp.int32),
            pltpu.VMEM((GROUP * CHUNK, width), jnp.float32),
            pltpu.SemaphoreType.DMA((3,)),
        ],
        compiler_params=granted(4),
        cost_estimate=pl.CostEstimate(flops=10**7, bytes_accessed=10**7, transcendentals=0),
        name="decode",
    )(*operands)
    if step == 0:
        return results
    return (table,) + tuple(results)


def score_kernel(
    token_count,
    local_queries,
    slots,
    me_ref,
    starts,
    queries_ref,
    embedded,
    out_ref,
    at_ref,
    turned,
    largest,
    sem,
):
    starts_copy = pltpu.make_async_copy(starts, at_ref, sem)
    starts_copy.start()
    passages = out_ref.shape[1]
    query_tokens = queries_ref.shape[0]
    block = min(QUERY_BLOCK, query_tokens)
    blocks = query_tokens // block
    per_block = block // token_count
    owner = lax.broadcasted_iota(jnp.int32, (per_block, block), 0)
    token_of = quotient(lax.broadcasted_iota(jnp.int32, (per_block, block), 1), token_count)
    block_targets = per_block // local_queries
    near_me = me_ref[0] & (block_targets - 1)
    far_me = quotient(me_ref[0], block_targets)
    owner_target = quotient(owner, local_queries)
    relative = (owner_target ^ near_me) * local_queries + owner - owner_target * local_queries
    summing = (relative == token_of).astype(jnp.bfloat16)

    def score_block(b, carry):
        at = pl.ds(pl.multiple_of(b * block, block), block)
        vectors = normalized(queries_ref[at, :].astype(jnp.float32))
        turned[...] = vectors.astype(jnp.float32).T.astype(jnp.bfloat16)

        def score(g, so_far):
            count = SCORE_GROUP // SCORE_PARTS
            size = count * CHUNK
            for part in range(SCORE_PARTS):
                first = g * SCORE_PARTS + part
                at = pl.ds(pl.multiple_of(first * size, size), size)
                similar = jnp.dot(embedded[at, :], turned[...], preferred_element_type=jnp.float32)
                parts = jnp.max(similar.reshape(count, CHUNK // 8, 8, block), axis=1)
                for k in range(count):
                    start = at_ref[first * count + k]
                    p = quotient(start, slots)
                    so_far = jnp.where(start == p * slots, parts[k], jnp.maximum(so_far, parts[k]))
                    to = pl.multiple_of(p * 8, 8)
                    for lane in range(block // 128):
                        largest[lane, pl.ds(to, 8), :] = so_far[:, lane * 128 : (lane + 1) * 128]
            return so_far

        @pl.when(b == 0)
        def arrived():
            starts_copy.wait()

        groups = quotient(at_ref[at_ref.shape[0] - 1] + SCORE_GROUP - 1, SCORE_GROUP)
        lax.fori_loop(0, groups, score, jnp.zeros((8, block), jnp.float32))
        kept = []
        for lane in range(block // 128):
            best = largest[lane, pl.ds(0, passages, stride=8), :]
            for k in range(1, 8):
                best = jnp.maximum(best, largest[lane, pl.ds(k, passages, stride=8), :])
            kept.append(best)
        best = jnp.concatenate(kept, axis=1)
        sums = jnp.zeros((per_block, passages), jnp.float32)
        for _ in range(3):
            part = best.astype(jnp.bfloat16)
            best = best - part.astype(jnp.float32)
            sums = sums + lax.dot_general(
                summing, part, (((1,), (1,)), ((), ())), preferred_element_type=jnp.float32
            )
        to = pl.multiple_of((b ^ far_me) * per_block, per_block)
        out_ref[pl.ds(to, per_block), :] = sums
        return carry

    lax.fori_loop(0, blocks, score_block, 0)


def score_all(me, starts, query_rows, embedded, passages, slots, token_count, local_queries):
    query_tokens, width = query_rows.shape
    block = min(QUERY_BLOCK, query_tokens)
    blocks = query_tokens // block
    return pl.pallas_call(
        functools.partial(score_kernel, token_count, local_queries, slots),
        out_shape=jax.ShapeDtypeStruct((query_tokens // token_count, passages), jnp.float32),
        in_specs=[SMEM, VMEM, VMEM, VMEM],
        out_specs=VMEM,
        scratch_shapes=[
            pltpu.SMEM(starts.shape, jnp.int32),
            pltpu.VMEM((width, block), jnp.bfloat16),
            pltpu.VMEM((block // 128, (passages + 1) * 8, 128), jnp.float32),
            pltpu.SemaphoreType.DMA,
        ],
        compiler_params=granted(8 + 2 * blocks),
        name="score",
    )(
        me,
        pinned(starts, pltpu.VMEM),
        pinned(query_rows, pltpu.VMEM),
        pinned(embedded, pltpu.VMEM),
    )


def pick_kernel(passages, candidates_ref, returned_ref, out_ref):
    local_queries, count = candidates_ref.shape
    targets = returned_ref.shape[0]
    passage_numbers = lax.broadcasted_iota(jnp.int32, (passages, count), 0)
    target_numbers = lax.broadcasted_iota(jnp.int32, (targets, count), 0)
    for q in range(local_queries):
        wanted = candidates_ref[q : q + 1, :]
        target = quotient(wanted, passages)
        hits = (passage_numbers == wanted - target * passages).astype(jnp.bfloat16)
        left = returned_ref[:, q * passages : (q + 1) * passages]
        picked = jnp.zeros((targets, count), jnp.float32)
        for _ in range(3):
            part = left.astype(jnp.bfloat16)
            left = left - part.astype(jnp.float32)
            picked = picked + jnp.dot(part, hits, preferred_element_type=jnp.float32)
        kept = jnp.where(target_numbers == target, picked, 0.0)
        out_ref[q : q + 1, :] = jnp.sum(kept, axis=0, keepdims=True)


def pick(candidates, returned, passages):
    return pl.pallas_call(
        functools.partial(pick_kernel, passages),
        out_shape=jax.ShapeDtypeStruct(candidates.shape, jnp.float32),
        in_specs=[VMEM, VMEM],
        out_specs=VMEM,
        compiler_params=granted(8),
        name="pick",
    )(candidates, pltpu.with_memory_space_constraint(returned, pltpu.VMEM))


def body(queries, candidates, token_codes, residuals, lengths, centroids):
    local_queries, token_count, width = queries.shape
    targets = lax.axis_size("shard") * lax.axis_size("sub")
    passages, slots = token_codes.shape
    half = lax.axis_index("sub").astype(jnp.int32)
    me = lax.axis_index("shard").astype(jnp.int32) * lax.axis_size("sub") + half
    half = half.reshape(1)
    me = me.reshape(1)
    near = residuals.reshape(passages * slots, width)
    other = lax.ppermute(centroids, "sub", [(0, 1), (1, 0)])

    held = queries.reshape(1, 1, local_queries * token_count, width)
    bits = targets.bit_length() - 1
    embedded = None
    for turn, first in enumerate(range(bits - 1, -1, -1)):
        pairs = [(device, device ^ (1 << first)) for device in range(targets)]
        received = lax.ppermute(held, ("shard", "sub"), pairs)
        if turn == 0:
            ready = prepare(me, lengths, token_codes.reshape(passages * slots), centroids, near)
            own, near, codes, starts, lives, nothing = ready
            table = None
        elif turn <= STEPS:
            table, embedded, nothing = decode_step(
                turn - 1,
                passages,
                half,
                own,
                other,
                codes,
                starts,
                lives,
                near,
                table,
                embedded,
                held,
            )
        received = received + nothing[0:1, :]
        held = jnp.concatenate([held, received], axis=1)
        if first > 0:
            held = held.reshape((-1, 1) + held.shape[2:])
    query_rows = held.reshape(targets * local_queries * token_count, width)
    scores = score_all(
        me, starts, query_rows, embedded, passages, slots, token_count, local_queries
    )
    returned = lax.all_to_all(
        scores.reshape(targets, local_queries * passages),
        ("shard", "sub"),
        split_axis=0,
        concat_axis=0,
        tiled=True,
    )
    return pick(candidates, returned, passages)


def solution(mesh):
    placed = (
        P(("groups", "shard", "sub"), None, None),
        P(("groups", "shard", "sub"), None),
        P(("groups", "shard", "sub"), None),
        P(("groups", "shard", "sub"), None, None),
        P(("groups", "shard", "sub")),
        P(("groups", "shard", "sub"), None),
    )
    return jax.shard_map(
        body,
        mesh=mesh,
        in_specs=placed,
        out_specs=P(("groups", "shard", "sub"), None),
        check_vma=False,
    )
```

```python
import functools

import jax
import jax.numpy as jnp
from jax import lax
from jax.experimental import pallas as pl
from jax.experimental.pallas import tpu as pltpu
from jax.sharding import PartitionSpec as P

CHUNK = 16
GROUP = 16
SCORE_GROUP = 64
SCORE_PARTS = 2
STEPS = 3
PIECES = 4
QUERY_BLOCK = 512
SMEM = pl.BlockSpec(memory_space=pltpu.SMEM)
VMEM = pl.BlockSpec(memory_space=pltpu.VMEM)
HBM = pl.BlockSpec(memory_space=pltpu.HBM)


def normalized(vectors):
    total = jnp.sum(vectors * vectors, axis=-1, keepdims=True)
    return (vectors * lax.rsqrt(total + 1e-06)).astype(jnp.bfloat16)


def quotient(number, divisor):
    if divisor & (divisor - 1) == 0:
        return lax.shift_right_logical(number, divisor.bit_length() - 1)
    return lax.div(number, divisor)


def pinned(array, space=pltpu.HBM):
    return pltpu.with_memory_space_constraint(array, space)


def granted(mebibytes):
    return pltpu.CompilerParams(vmem_limit_bytes=mebibytes * 1024 * 1024)


def shares_of(passages):
    edges = [0, passages * 11 // 32, passages * 21 // 32]
    return tuple(zip(edges, edges[1:] + [passages]))


def prepare_kernel(
    me_ref,
    lengths_hbm,
    codes_hbm,
    own_hbm,
    residuals_hbm,
    staged,
    residuals,
    codes,
    starts,
    lives,
    nothing,
    lengths_ref,
    starts_ref,
    lives_ref,
    sems,
):
    del me_ref
    passages = lengths_ref.shape[0]
    slots = codes_hbm.shape[0] // passages
    moves = []

    def move(source, to):
        moves.append(pltpu.make_async_copy(source, to, sems.at[len(moves)]))
        moves[-1].start()

    lengths_copy = pltpu.make_async_copy(lengths_hbm, lengths_ref, sems.at[5])
    lengths_copy.start()
    move(codes_hbm, codes)
    move(own_hbm, staged)
    move(residuals_hbm, residuals)
    nothing[...] = jnp.zeros(nothing.shape, nothing.dtype)
    lengths_copy.wait()

    def listing(p, chunks):
        length = lengths_ref[p]
        for k in range(slots // CHUNK):
            starts_ref[chunks + k] = p * slots + k * CHUNK
            lives_ref[chunks + k] = length - k * CHUNK
        return chunks + quotient(length + CHUNK - 1, CHUNK)

    last = starts_ref.shape[0] - 1
    chunks = jnp.int32(0)
    for step, (low, high) in enumerate(shares_of(passages)):
        chunks = lax.fori_loop(low, high, listing, chunks, unroll=4)
        for k in range(GROUP):
            starts_ref[chunks + k] = passages * slots
            lives_ref[chunks + k] = 0
        chunks = quotient(chunks + GROUP - 1, GROUP) * GROUP
        starts_ref[last - STEPS + step] = quotient(chunks, GROUP)
    for k in range(SCORE_GROUP):
        starts_ref[chunks + k] = passages * slots
    starts_ref[last] = chunks
    move(starts_ref, starts)
    move(lives_ref, lives)
    for copy in moves:
        copy.wait()


def list_size(passages, slots):
    most = passages * (slots // CHUNK) + STEPS * GROUP + SCORE_GROUP + STEPS + 1
    return -(-most // 1024) * 1024


def prepare(me, lengths, token_codes, own, residuals):
    width = own.shape[1]
    passages = lengths.shape[0]
    slots = token_codes.shape[0] // passages
    most = list_size(passages, slots)
    return pl.pallas_call(
        prepare_kernel,
        out_shape=(
            pltpu.VMEM(own.shape, jnp.bfloat16),
            pltpu.VMEM(residuals.shape, jnp.bfloat16),
            pltpu.VMEM(token_codes.shape, jnp.int32),
            pltpu.VMEM((most,), jnp.int32),
            pltpu.VMEM((most,), jnp.int32),
            pltpu.VMEM((16, width), jnp.bfloat16),
        ),
        in_specs=[SMEM, HBM, HBM, HBM, HBM],
        out_specs=(VMEM,) * 6,
        scratch_shapes=[
            pltpu.SMEM(lengths.shape, jnp.int32),
            pltpu.SMEM((most,), jnp.int32),
            pltpu.SMEM((most,), jnp.int32),
            pltpu.SemaphoreType.DMA((6,)),
        ],
        compiler_params=granted(4),
        cost_estimate=pl.CostEstimate(flops=10**7, bytes_accessed=8 * 10**6, transcendentals=0),
        name="prepare",
    )(me, pinned(lengths), pinned(token_codes), pinned(own), pinned(residuals))


def decode_kernel(step, passages, *refs):
    if step == 0:
        half_ref, own_ref, other_ref, codes, starts, lives, residuals, _, table = refs[:9]
    else:
        codes, starts, lives, residuals, table = refs[:5]
    embedded, rows, nothing, codes_ref, starts_ref, lives_ref, sems = refs[-7:]
    tokens = codes_ref.shape[0]
    slots = tokens // passages
    width = rows.shape[1]
    moves = []
    first, after = shares_of(passages)[step]
    first_move, after_move = first // 8 * 8, min(-(-after // 8) * 8, passages)
    part = pl.ds(first_move * slots, (after_move - first_move) * slots)
    pairs = ((starts, starts_ref), (lives, lives_ref), (codes.at[part], codes_ref.at[part]))
    for k, (source, to) in enumerate(pairs):
        moves.append(pltpu.make_async_copy(source, to, sems.at[k]))
        moves[-1].start()
    nothing[...] = jnp.zeros(nothing.shape, nothing.dtype)
    if step == 0:
        half_rows = other_ref.shape[0]
        piece = half_rows // PIECES
        for source, base in ((own_ref, half_ref[0]), (other_ref, 1 - half_ref[0])):
            for k in range(PIECES):
                to = pl.ds(pl.multiple_of(base * half_rows + k * piece, piece), piece)
                table[to, :] = source[pl.ds(k * piece, piece), :].astype(jnp.float32)

    slot_numbers = lax.broadcasted_iota(jnp.int32, (CHUNK, width), 0)
    table_single = table.reshape(table.shape[0], 1, width)
    rows_single = rows.reshape(rows.shape[0], 1, width)

    def fetch(g):
        for k in range(GROUP):
            at = jnp.minimum(starts_ref[g * GROUP + k], after * slots - CHUNK)
            for j in range(CHUNK):
                rows_single[k * CHUNK + j] = table_single[codes_ref[at + j]]

    def finish(g):
        summed = []
        for k in range(GROUP):
            at = jnp.minimum(starts_ref[g * GROUP + k], tokens - CHUNK)
            near = residuals[pl.ds(pl.multiple_of(at, CHUNK), CHUNK), :]
            vectors = rows[pl.ds(k * CHUNK, CHUNK), :] + near.astype(jnp.float32)
            live = slot_numbers < lives_ref[g * GROUP + k]
            summed.append(jnp.where(live, vectors, vectors[0:1, :]))
        return normalized(jnp.concatenate(summed, axis=0))

    def keep(g, done):
        size = GROUP * CHUNK
        embedded[pl.ds(pl.multiple_of(g * size, size), size), :] = done

    for move in moves:
        move.wait()
    last = starts_ref.shape[0] - 1
    low = starts_ref[last - STEPS + step - 1] if step > 0 else 0
    high = starts_ref[last - STEPS + step]
    def decode(g, carry):
        done = finish(g - 1)
        fetch(g)
        keep(g - 1, done)
        return carry

    if step == 0:
        fetch(low)
    lax.fori_loop(low + (step == 0), high, decode, 0)
    if step == STEPS - 1:
        keep(high - 1, finish(high - 1))


def decode_step(
    step, passages, half, own, other, codes, starts, lives, residuals, table, carried, held
):
    tokens, width = residuals.shape
    rounding = SCORE_GROUP * CHUNK
    space = (-(-(tokens + STEPS * GROUP * CHUNK) // rounding) * rounding, width)
    inside = lambda array: pinned(array, pltpu.VMEM)
    shared = [inside(codes), inside(starts), inside(lives), inside(residuals)]
    if step == 0:
        operands = [half, inside(own), inside(other)] + shared + [inside(held)]
        in_specs = [SMEM] + [VMEM] * 7
        whole = (2 * own.shape[0], width)
        out_shape = [pltpu.VMEM(whole, jnp.float32)]
        aliases = {}
    else:
        operands = shared + [inside(table), inside(held)] + [inside(array) for array in carried]
        in_specs = [VMEM] * 8
        out_shape = []
        aliases = {6: 0, 7: 1}
    out_shape.append(pltpu.VMEM(space, jnp.bfloat16))
    out_shape.append(pltpu.VMEM((GROUP * CHUNK, width), jnp.float32))
    out_shape.append(pltpu.VMEM((16, width), jnp.bfloat16))
    results = pl.pallas_call(
        functools.partial(decode_kernel, step, passages),
        out_shape=tuple(out_shape),
        in_specs=in_specs,
        out_specs=(VMEM,) * len(out_shape),
        input_output_aliases=aliases,
        scratch_shapes=[
            pltpu.SMEM((tokens,), jnp.int32),
            pltpu.SMEM(starts.shape, jnp.int32),
            pltpu.SMEM(lives.shape, jnp.int32),
            pltpu.SemaphoreType.DMA((3,)),
        ],
        compiler_params=granted(4),
        cost_estimate=pl.CostEstimate(flops=10**7, bytes_accessed=10**7, transcendentals=0),
        name="decode",
    )(*operands)
    if step == 0:
        table, results = results[0], results[1:]
    return table, results[:2], results[2]


def score_kernel(
    token_count,
    local_queries,
    slots,
    me_ref,
    starts,
    queries_ref,
    embedded,
    out_ref,
    at_ref,
    turned,
    largest,
    sem,
):
    starts_copy = pltpu.make_async_copy(starts, at_ref, sem)
    starts_copy.start()
    passages = out_ref.shape[1]
    query_tokens = queries_ref.shape[0]
    block = min(QUERY_BLOCK, query_tokens)
    blocks = query_tokens // block
    per_block = block // token_count
    owner = lax.broadcasted_iota(jnp.int32, (per_block, block), 0)
    token_of = quotient(lax.broadcasted_iota(jnp.int32, (per_block, block), 1), token_count)
    block_targets = per_block // local_queries
    near_me = me_ref[0] & (block_targets - 1)
    far_me = quotient(me_ref[0], block_targets)
    owner_target = quotient(owner, local_queries)
    relative = (owner_target ^ near_me) * local_queries + owner - owner_target * local_queries
    summing = (relative == token_of).astype(jnp.bfloat16)

    def score_block(b, carry):
        at = pl.ds(pl.multiple_of(b * block, block), block)
        vectors = normalized(queries_ref[at, :].astype(jnp.float32))
        turned[...] = vectors.astype(jnp.float32).T.astype(jnp.bfloat16)

        count = SCORE_GROUP // SCORE_PARTS
        size = count * CHUNK

        def score(first, so_far):
            at = pl.ds(pl.multiple_of(first * size, size), size)
            similar = jnp.dot(embedded[at, :], turned[...], preferred_element_type=jnp.float32)
            parts = jnp.max(similar.reshape(count, CHUNK // 8, 8, block), axis=1)
            for k in range(count):
                start = at_ref[first * count + k]
                p = quotient(start, slots)
                so_far = jnp.where(start == p * slots, parts[k], jnp.maximum(so_far, parts[k]))
                to = pl.multiple_of(p * 8, 8)
                for lane in range(block // 128):
                    largest[lane, pl.ds(to, 8), :] = so_far[:, lane * 128 : (lane + 1) * 128]
            return so_far

        def score_parts(g, so_far):
            for part in range(SCORE_PARTS):
                so_far = score(g * SCORE_PARTS + part, so_far)
            return so_far

        @pl.when(b == 0)
        def arrived():
            starts_copy.wait()

        parts_used = quotient(at_ref[at_ref.shape[0] - 1] + count - 1, count)
        whole = quotient(parts_used, SCORE_PARTS)
        so_far = jnp.zeros((8, block), jnp.float32)
        so_far = lax.fori_loop(0, whole, score_parts, so_far)
        lax.fori_loop(whole * SCORE_PARTS, parts_used, score, so_far)
        kept = []
        for lane in range(block // 128):
            best = largest[lane, pl.ds(0, passages, stride=8), :]
            for k in range(1, 8):
                best = jnp.maximum(best, largest[lane, pl.ds(k, passages, stride=8), :])
            kept.append(best)
        best = jnp.concatenate(kept, axis=1)
        sums = jnp.zeros((per_block, passages), jnp.float32)
        for _ in range(3):
            part = best.astype(jnp.bfloat16)
            best = best - part.astype(jnp.float32)
            sums = sums + lax.dot_general(
                summing, part, (((1,), (1,)), ((), ())), preferred_element_type=jnp.float32
            )
        to = pl.multiple_of((b ^ far_me) * per_block, per_block)
        out_ref[pl.ds(to, per_block), :] = sums
        return carry

    lax.fori_loop(0, blocks, score_block, 0)


def score_all(me, starts, query_rows, embedded, passages, slots, token_count, local_queries):
    query_tokens, width = query_rows.shape
    block = min(QUERY_BLOCK, query_tokens)
    blocks = query_tokens // block
    return pl.pallas_call(
        functools.partial(score_kernel, token_count, local_queries, slots),
        out_shape=jax.ShapeDtypeStruct((query_tokens // token_count, passages), jnp.float32),
        in_specs=[SMEM, VMEM, VMEM, VMEM],
        out_specs=VMEM,
        scratch_shapes=[
            pltpu.SMEM(starts.shape, jnp.int32),
            pltpu.VMEM((width, block), jnp.bfloat16),
            pltpu.VMEM((block // 128, (passages + 1) * 8, 128), jnp.float32),
            pltpu.SemaphoreType.DMA,
        ],
        compiler_params=granted(8 + 2 * blocks),
        name="score",
    )(
        me,
        pinned(starts, pltpu.VMEM),
        pinned(query_rows, pltpu.VMEM),
        pinned(embedded, pltpu.VMEM),
    )


def pick_kernel(passages, candidates_ref, returned_ref, out_ref):
    local_queries, count = candidates_ref.shape
    targets = returned_ref.shape[0]
    passage_numbers = lax.broadcasted_iota(jnp.int32, (passages, count), 0)
    target_numbers = lax.broadcasted_iota(jnp.int32, (targets, count), 0)
    for q in range(local_queries):
        wanted = candidates_ref[q : q + 1, :]
        target = quotient(wanted, passages)
        hits = (passage_numbers == wanted - target * passages).astype(jnp.bfloat16)
        left = returned_ref[:, q * passages : (q + 1) * passages]
        picked = jnp.zeros((targets, count), jnp.float32)
        for _ in range(3):
            part = left.astype(jnp.bfloat16)
            left = left - part.astype(jnp.float32)
            picked = picked + jnp.dot(part, hits, preferred_element_type=jnp.float32)
        kept = jnp.where(target_numbers == target, picked, 0.0)
        out_ref[q : q + 1, :] = jnp.sum(kept, axis=0, keepdims=True)


def pick(candidates, returned, passages):
    return pl.pallas_call(
        functools.partial(pick_kernel, passages),
        out_shape=jax.ShapeDtypeStruct(candidates.shape, jnp.float32),
        in_specs=[VMEM, VMEM],
        out_specs=VMEM,
        compiler_params=granted(8),
        name="pick",
    )(candidates, pltpu.with_memory_space_constraint(returned, pltpu.VMEM))


def body(queries, candidates, token_codes, residuals, lengths, centroids):
    local_queries, token_count, width = queries.shape
    targets = lax.axis_size("shard") * lax.axis_size("sub")
    passages, slots = token_codes.shape
    half = lax.axis_index("sub").astype(jnp.int32)
    me = lax.axis_index("shard").astype(jnp.int32) * lax.axis_size("sub") + half
    half = half.reshape(1)
    me = me.reshape(1)
    near = residuals.reshape(passages * slots, width)
    other = lax.ppermute(centroids, "sub", [(0, 1), (1, 0)])

    held = queries.reshape(1, 1, local_queries * token_count, width)
    bits = targets.bit_length() - 1
    carried = None
    for turn, first in enumerate(range(bits - 1, -1, -1)):
        pairs = [(device, device ^ (1 << first)) for device in range(targets)]
        received = lax.ppermute(held, ("shard", "sub"), pairs)
        if turn == 0:
            ready = prepare(me, lengths, token_codes.reshape(passages * slots), centroids, near)
            own, near, codes, starts, lives, nothing = ready
            table = None
        elif turn <= STEPS:
            table, carried, nothing = decode_step(
                turn - 1,
                passages,
                half,
                own,
                other,
                codes,
                starts,
                lives,
                near,
                table,
                carried,
                held,
            )
        received = received + nothing[0:1, :]
        held = jnp.concatenate([held, received], axis=1)
        if first > 0:
            held = held.reshape((-1, 1) + held.shape[2:])
    query_rows = held.reshape(targets * local_queries * token_count, width)
    scores = score_all(
        me, starts, query_rows, carried[0], passages, slots, token_count, local_queries
    )
    returned = lax.all_to_all(
        scores.reshape(targets, local_queries * passages),
        ("shard", "sub"),
        split_axis=0,
        concat_axis=0,
        tiled=True,
    )
    return pick(candidates, returned, passages)


def solution(mesh):
    placed = (
        P(("groups", "shard", "sub"), None, None),
        P(("groups", "shard", "sub"), None),
        P(("groups", "shard", "sub"), None),
        P(("groups", "shard", "sub"), None, None),
        P(("groups", "shard", "sub")),
        P(("groups", "shard", "sub"), None),
    )
    return jax.shard_map(
        body,
        mesh=mesh,
        in_specs=placed,
        out_specs=P(("groups", "shard", "sub"), None),
        check_vma=False,
    )
```

```python
import functools

import jax
import jax.numpy as jnp
from jax import lax
from jax.experimental import pallas as pl
from jax.experimental.pallas import tpu as pltpu
from jax.sharding import PartitionSpec as P

CHUNK = 16
GROUP = 16
SCORE_GROUP = 64
SCORE_PARTS = 2
STEPS = 3
PIECES = 4
QUERY_BLOCK = 512
SMEM = pl.BlockSpec(memory_space=pltpu.SMEM)
VMEM = pl.BlockSpec(memory_space=pltpu.VMEM)
HBM = pl.BlockSpec(memory_space=pltpu.HBM)


def normalized(vectors):
    total = jnp.sum(vectors * vectors, axis=-1, keepdims=True)
    return (vectors * lax.rsqrt(total + 1e-06)).astype(jnp.bfloat16)


def quotient(number, divisor):
    if divisor & (divisor - 1) == 0:
        return lax.shift_right_logical(number, divisor.bit_length() - 1)
    return lax.div(number, divisor)


def pinned(array, space=pltpu.HBM):
    return pltpu.with_memory_space_constraint(array, space)


def granted(mebibytes):
    return pltpu.CompilerParams(vmem_limit_bytes=mebibytes * 1024 * 1024)


def shares_of(passages):
    edges = [0, passages * 11 // 32, passages * 21 // 32]
    return tuple(zip(edges, edges[1:] + [passages]))


def prepare_kernel(
    me_ref,
    lengths_hbm,
    codes_hbm,
    own_hbm,
    residuals_hbm,
    staged,
    near,
    codes,
    starts,
    cleans,
    nothing,
    lengths_ref,
    starts_ref,
    cleans_ref,
    length_rows,
    drawn,
    residuals,
    sems,
):
    del me_ref
    passages, slots = codes_hbm.shape
    width = own_hbm.shape[1]
    lengths_copy = pltpu.make_async_copy(lengths_hbm, lengths_ref, sems.at[0])
    codes_copy = pltpu.make_async_copy(codes_hbm, drawn, sems.at[1])
    residual_copy = pltpu.make_async_copy(residuals_hbm, residuals, sems.at[2])
    own_copy = pltpu.make_async_copy(own_hbm, staged, sems.at[3])
    lengths_copy.start()
    codes_copy.start()
    residual_copy.start()
    own_copy.start()
    nothing[...] = jnp.zeros(nothing.shape, nothing.dtype)
    lengths_copy.wait()

    def listing(p, chunks):
        length = lengths_ref[p]
        length_rows[pl.ds(p, 1), :] = jnp.full((1, slots), length, jnp.int32)
        for k in range(slots // CHUNK):
            starts_ref[chunks + k] = p * slots + k * CHUNK
            cleans_ref[chunks + k] = p * slots + k * CHUNK
        return chunks + quotient(length + CHUNK - 1, CHUNK)

    last = starts_ref.shape[0] - 1
    chunks = jnp.int32(0)
    for step, (low, high) in enumerate(shares_of(passages)):
        chunks = lax.fori_loop(low, high, listing, chunks, unroll=4)
        for k in range(GROUP):
            starts_ref[chunks + k] = passages * slots
            cleans_ref[chunks + k] = low * slots
        chunks = quotient(chunks + GROUP - 1, GROUP) * GROUP
        cleans_ref[last - STEPS + step] = quotient(chunks, GROUP)
    for k in range(SCORE_GROUP):
        starts_ref[chunks + k] = passages * slots
    starts_ref[last] = chunks
    starts_copy = pltpu.make_async_copy(starts_ref, starts, sems.at[4])
    cleans_copy = pltpu.make_async_copy(cleans_ref, cleans, sems.at[5])
    starts_copy.start()
    cleans_copy.start()
    codes_copy.wait()
    lanes = lax.broadcasted_iota(jnp.int32, (passages, slots), 1)
    codes[...] = jnp.where(lanes < length_rows[...], drawn[...], drawn[:, 0:1])
    residual_copy.wait()
    slot_numbers = lax.broadcasted_iota(jnp.int32, (CHUNK, width), 0)

    def place(g, carry):
        for k in range(GROUP):
            at = cleans_ref[g * GROUP + k]
            p = quotient(at, slots)
            live = lengths_ref[p] - (at - p * slots)
            first = residuals[pl.ds(pl.multiple_of(p * slots, CHUNK), CHUNK), :]
            rows = residuals[pl.ds(pl.multiple_of(at, CHUNK), CHUNK), :].astype(jnp.float32)
            rows = jnp.where(slot_numbers < live, rows, first.astype(jnp.float32)[0:1, :])
            to = pl.multiple_of((g * GROUP + k) * CHUNK, CHUNK)
            near[pl.ds(to, CHUNK), :] = rows
        return carry

    lax.fori_loop(0, quotient(chunks, GROUP), place, 0)
    own_copy.wait()
    starts_copy.wait()
    cleans_copy.wait()


def list_size(passages, slots):
    most = passages * (slots // CHUNK) + STEPS * GROUP + SCORE_GROUP + STEPS + 1
    return -(-most // 1024) * 1024


def list_rows(passages, slots):
    rounding = SCORE_GROUP * CHUNK
    return -(-(passages * slots + STEPS * GROUP * CHUNK) // rounding) * rounding


def prepare(me, lengths, token_codes, own, residuals):
    width = own.shape[1]
    passages, slots = token_codes.shape
    most = list_size(passages, slots)
    return pl.pallas_call(
        prepare_kernel,
        out_shape=(
            pltpu.VMEM(own.shape, jnp.bfloat16),
            pltpu.VMEM((list_rows(passages, slots), width), jnp.float32),
            pltpu.VMEM(token_codes.shape, jnp.int32),
            pltpu.VMEM((most,), jnp.int32),
            pltpu.VMEM((most,), jnp.int32),
            pltpu.VMEM((16, width), jnp.bfloat16),
        ),
        in_specs=[SMEM, HBM, HBM, HBM, HBM],
        out_specs=(VMEM,) * 6,
        scratch_shapes=[
            pltpu.SMEM(lengths.shape, jnp.int32),
            pltpu.SMEM((most,), jnp.int32),
            pltpu.SMEM((most,), jnp.int32),
            pltpu.VMEM(token_codes.shape, jnp.int32),
            pltpu.VMEM(token_codes.shape, jnp.int32),
            pltpu.VMEM(residuals.shape, jnp.bfloat16),
            pltpu.SemaphoreType.DMA((6,)),
        ],
        compiler_params=granted(4),
        cost_estimate=pl.CostEstimate(flops=10**7, bytes_accessed=8 * 10**6, transcendentals=0),
        name="prepare",
    )(me, pinned(lengths), pinned(token_codes), pinned(own), pinned(residuals))


def decode_kernel(step, passages, *refs):
    if step == 0:
        half_ref, own_ref, other_ref, codes, cleans, near, _, table = refs[:8]
    else:
        codes, cleans, near, table = refs[:4]
    embedded, rows, nothing, codes_smem, cleans_ref, sems = refs[-6:]
    slots = codes.shape[1]
    width = rows.shape[1]
    codes_ref = codes_smem.reshape(passages * slots)
    moves = []
    first, after = shares_of(passages)[step]
    first_move, after_move = first // 8 * 8, min(-(-after // 8) * 8, passages)
    part = pl.ds(first_move, after_move - first_move)
    pairs = ((cleans, cleans_ref), (codes.at[part], codes_smem.at[part]))
    for k, (source, to) in enumerate(pairs):
        moves.append(pltpu.make_async_copy(source, to, sems.at[k]))
        moves[-1].start()
    nothing[...] = jnp.zeros(nothing.shape, nothing.dtype)
    if step == 0:
        half_rows = other_ref.shape[0]
        piece = half_rows // PIECES
        for source, base in ((own_ref, half_ref[0]), (other_ref, 1 - half_ref[0])):
            for k in range(PIECES):
                to = pl.ds(pl.multiple_of(base * half_rows + k * piece, piece), piece)
                table[to, :] = source[pl.ds(k * piece, piece), :].astype(jnp.float32)

    table_single = table.reshape(table.shape[0], 1, width)
    rows_single = rows.reshape(rows.shape[0], 1, width)

    def fetch(g):
        for k in range(GROUP):
            at = cleans_ref[g * GROUP + k]
            for j in range(CHUNK):
                rows_single[k * CHUNK + j] = table_single[codes_ref[at + j]]

    def finish(g):
        size = GROUP * CHUNK
        return normalized(rows[...] + near[pl.ds(pl.multiple_of(g * size, size), size), :])

    def keep(g, done):
        size = GROUP * CHUNK
        embedded[pl.ds(pl.multiple_of(g * size, size), size), :] = done

    for move in moves:
        move.wait()
    last = cleans_ref.shape[0] - 1
    low = cleans_ref[last - STEPS + step - 1] if step > 0 else 0
    high = cleans_ref[last - STEPS + step]
    def decode(g, carry):
        done = finish(g - 1)
        fetch(g)
        keep(g - 1, done)
        return carry

    if step == 0:
        fetch(low)
    lax.fori_loop(low + (step == 0), high, decode, 0)
    if step == STEPS - 1:
        keep(high - 1, finish(high - 1))


def decode_step(
    step, half, own, other, codes, cleans, near, table, carried, held
):
    passages, slots = codes.shape
    width = near.shape[1]
    space = near.shape
    inside = lambda array: pinned(array, pltpu.VMEM)
    shared = [inside(codes), inside(cleans), inside(near)]
    if step == 0:
        operands = [half, inside(own), inside(other)] + shared + [inside(held)]
        in_specs = [SMEM] + [VMEM] * 6
        whole = (2 * own.shape[0], width)
        out_shape = [pltpu.VMEM(whole, jnp.float32)]
        aliases = {}
    else:
        operands = shared + [inside(table), inside(held)] + [inside(array) for array in carried]
        in_specs = [VMEM] * 7
        out_shape = []
        aliases = {5: 0, 6: 1}
    out_shape.append(pltpu.VMEM(space, jnp.bfloat16))
    out_shape.append(pltpu.VMEM((GROUP * CHUNK, width), jnp.float32))
    out_shape.append(pltpu.VMEM((16, width), jnp.bfloat16))
    results = pl.pallas_call(
        functools.partial(decode_kernel, step, passages),
        out_shape=tuple(out_shape),
        in_specs=in_specs,
        out_specs=(VMEM,) * len(out_shape),
        input_output_aliases=aliases,
        scratch_shapes=[
            pltpu.SMEM(codes.shape, jnp.int32),
            pltpu.SMEM(cleans.shape, jnp.int32),
            pltpu.SemaphoreType.DMA((2,)),
        ],
        compiler_params=granted(4),
        cost_estimate=pl.CostEstimate(flops=10**7, bytes_accessed=10**7, transcendentals=0),
        name="decode",
    )(*operands)
    if step == 0:
        table, results = results[0], results[1:]
    return table, results[:2], results[2]


def score_kernel(
    token_count,
    local_queries,
    slots,
    me_ref,
    starts,
    queries_ref,
    embedded,
    out_ref,
    at_ref,
    turned,
    largest,
    sem,
):
    starts_copy = pltpu.make_async_copy(starts, at_ref, sem)
    starts_copy.start()
    passages = out_ref.shape[1]
    query_tokens = queries_ref.shape[0]
    block = min(QUERY_BLOCK, query_tokens)
    blocks = query_tokens // block
    per_block = block // token_count
    owner = lax.broadcasted_iota(jnp.int32, (per_block, block), 0)
    token_of = quotient(lax.broadcasted_iota(jnp.int32, (per_block, block), 1), token_count)
    block_targets = per_block // local_queries
    near_me = me_ref[0] & (block_targets - 1)
    far_me = quotient(me_ref[0], block_targets)
    owner_target = quotient(owner, local_queries)
    relative = (owner_target ^ near_me) * local_queries + owner - owner_target * local_queries
    summing = (relative == token_of).astype(jnp.bfloat16)

    def score_block(b, carry):
        at = pl.ds(pl.multiple_of(b * block, block), block)
        vectors = normalized(queries_ref[at, :].astype(jnp.float32))
        turned[...] = vectors.astype(jnp.float32).T.astype(jnp.bfloat16)

        count = SCORE_GROUP // SCORE_PARTS
        size = count * CHUNK

        def score(first, so_far):
            at = pl.ds(pl.multiple_of(first * size, size), size)
            similar = jnp.dot(embedded[at, :], turned[...], preferred_element_type=jnp.float32)
            parts = jnp.max(similar.reshape(count, CHUNK // 8, 8, block), axis=1)
            for k in range(count):
                start = at_ref[first * count + k]
                p = quotient(start, slots)
                so_far = jnp.where(start == p * slots, parts[k], jnp.maximum(so_far, parts[k]))
                to = pl.multiple_of(p * 8, 8)
                for lane in range(block // 128):
                    largest[lane, pl.ds(to, 8), :] = so_far[:, lane * 128 : (lane + 1) * 128]
            return so_far

        def score_parts(g, so_far):
            for part in range(SCORE_PARTS):
                so_far = score(g * SCORE_PARTS + part, so_far)
            return so_far

        @pl.when(b == 0)
        def arrived():
            starts_copy.wait()

        parts_used = quotient(at_ref[at_ref.shape[0] - 1] + count - 1, count)
        whole = quotient(parts_used, SCORE_PARTS)
        so_far = jnp.zeros((8, block), jnp.float32)
        so_far = lax.fori_loop(0, whole, score_parts, so_far)
        lax.fori_loop(whole * SCORE_PARTS, parts_used, score, so_far)
        kept = []
        for lane in range(block // 128):
            best = largest[lane, pl.ds(0, passages, stride=8), :]
            for k in range(1, 8):
                best = jnp.maximum(best, largest[lane, pl.ds(k, passages, stride=8), :])
            kept.append(best)
        best = jnp.concatenate(kept, axis=1)
        sums = jnp.zeros((per_block, passages), jnp.float32)
        for _ in range(3):
            part = best.astype(jnp.bfloat16)
            best = best - part.astype(jnp.float32)
            sums = sums + lax.dot_general(
                summing, part, (((1,), (1,)), ((), ())), preferred_element_type=jnp.float32
            )
        to = pl.multiple_of((b ^ far_me) * per_block, per_block)
        out_ref[pl.ds(to, per_block), :] = sums
        return carry

    lax.fori_loop(0, blocks, score_block, 0)


def score_all(me, starts, query_rows, embedded, passages, slots, token_count, local_queries):
    query_tokens, width = query_rows.shape
    block = min(QUERY_BLOCK, query_tokens)
    blocks = query_tokens // block
    return pl.pallas_call(
        functools.partial(score_kernel, token_count, local_queries, slots),
        out_shape=jax.ShapeDtypeStruct((query_tokens // token_count, passages), jnp.float32),
        in_specs=[SMEM, VMEM, VMEM, VMEM],
        out_specs=VMEM,
        scratch_shapes=[
            pltpu.SMEM(starts.shape, jnp.int32),
            pltpu.VMEM((width, block), jnp.bfloat16),
            pltpu.VMEM((block // 128, (passages + 1) * 8, 128), jnp.float32),
            pltpu.SemaphoreType.DMA,
        ],
        compiler_params=granted(8 + 2 * blocks),
        name="score",
    )(
        me,
        pinned(starts, pltpu.VMEM),
        pinned(query_rows, pltpu.VMEM),
        pinned(embedded, pltpu.VMEM),
    )


def pick_kernel(passages, candidates_ref, returned_ref, out_ref):
    local_queries, count = candidates_ref.shape
    targets = returned_ref.shape[0]
    passage_numbers = lax.broadcasted_iota(jnp.int32, (passages, count), 0)
    target_numbers = lax.broadcasted_iota(jnp.int32, (targets, count), 0)
    for q in range(local_queries):
        wanted = candidates_ref[q : q + 1, :]
        target = quotient(wanted, passages)
        hits = (passage_numbers == wanted - target * passages).astype(jnp.bfloat16)
        left = returned_ref[:, q * passages : (q + 1) * passages]
        picked = jnp.zeros((targets, count), jnp.float32)
        for _ in range(3):
            part = left.astype(jnp.bfloat16)
            left = left - part.astype(jnp.float32)
            picked = picked + jnp.dot(part, hits, preferred_element_type=jnp.float32)
        kept = jnp.where(target_numbers == target, picked, 0.0)
        out_ref[q : q + 1, :] = jnp.sum(kept, axis=0, keepdims=True)


def pick(candidates, returned, passages):
    return pl.pallas_call(
        functools.partial(pick_kernel, passages),
        out_shape=jax.ShapeDtypeStruct(candidates.shape, jnp.float32),
        in_specs=[VMEM, VMEM],
        out_specs=VMEM,
        compiler_params=granted(8),
        name="pick",
    )(candidates, pltpu.with_memory_space_constraint(returned, pltpu.VMEM))


def body(queries, candidates, token_codes, residuals, lengths, centroids):
    local_queries, token_count, width = queries.shape
    targets = lax.axis_size("shard") * lax.axis_size("sub")
    passages, slots = token_codes.shape
    half = lax.axis_index("sub").astype(jnp.int32)
    me = lax.axis_index("shard").astype(jnp.int32) * lax.axis_size("sub") + half
    half = half.reshape(1)
    me = me.reshape(1)
    flat = residuals.reshape(passages * slots, width)
    other = lax.ppermute(centroids, "sub", [(0, 1), (1, 0)])

    held = queries.reshape(1, 1, local_queries * token_count, width)
    bits = targets.bit_length() - 1
    carried = None
    for turn, first in enumerate(range(bits - 1, -1, -1)):
        pairs = [(device, device ^ (1 << first)) for device in range(targets)]
        received = lax.ppermute(held, ("shard", "sub"), pairs)
        if turn == 0:
            ready = prepare(me, lengths, token_codes, centroids, flat)
            own, near, codes, starts, cleans, nothing = ready
            table = None
        elif turn <= STEPS:
            table, carried, nothing = decode_step(
                turn - 1, half, own, other, codes, cleans, near, table, carried, held
            )
        received = received + nothing[0:1, :]
        held = jnp.concatenate([held, received], axis=1)
        if first > 0:
            held = held.reshape((-1, 1) + held.shape[2:])
    query_rows = held.reshape(targets * local_queries * token_count, width)
    scores = score_all(
        me, starts, query_rows, carried[0], passages, slots, token_count, local_queries
    )
    returned = lax.all_to_all(
        scores.reshape(targets, local_queries * passages),
        ("shard", "sub"),
        split_axis=0,
        concat_axis=0,
        tiled=True,
    )
    return pick(candidates, returned, passages)


def solution(mesh):
    placed = (
        P(("groups", "shard", "sub"), None, None),
        P(("groups", "shard", "sub"), None),
        P(("groups", "shard", "sub"), None),
        P(("groups", "shard", "sub"), None, None),
        P(("groups", "shard", "sub")),
        P(("groups", "shard", "sub"), None),
    )
    return jax.shard_map(
        body,
        mesh=mesh,
        in_specs=placed,
        out_specs=P(("groups", "shard", "sub"), None),
        check_vma=False,
    )
```

```python
import functools

import jax
import jax.numpy as jnp
from jax import lax
from jax.experimental import pallas as pl
from jax.experimental.pallas import tpu as pltpu
from jax.sharding import PartitionSpec as P

CHUNK = 16
GROUP = 16
SCORE_GROUP = 64
SCORE_PARTS = 2
STEPS = 2
PIECES = 4
QUERY_BLOCK = 512
SMEM = pl.BlockSpec(memory_space=pltpu.SMEM)
VMEM = pl.BlockSpec(memory_space=pltpu.VMEM)
HBM = pl.BlockSpec(memory_space=pltpu.HBM)


def normalized(vectors):
    total = jnp.sum(vectors * vectors, axis=-1, keepdims=True)
    return (vectors * lax.rsqrt(total + 1e-06)).astype(jnp.bfloat16)


def quotient(number, divisor):
    if divisor & (divisor - 1) == 0:
        return lax.shift_right_logical(number, divisor.bit_length() - 1)
    return lax.div(number, divisor)


def pinned(array, space=pltpu.HBM):
    return pltpu.with_memory_space_constraint(array, space)


def granted(mebibytes):
    return pltpu.CompilerParams(vmem_limit_bytes=mebibytes * 1024 * 1024)


def shares_of(passages):
    edges = [0, passages * 15 // 32]
    return tuple(zip(edges, edges[1:] + [passages]))


def prepare_kernel(
    me_ref,
    lengths_hbm,
    codes_hbm,
    own_hbm,
    residuals_hbm,
    staged,
    near,
    codes,
    starts,
    cleans,
    nothing,
    lengths_ref,
    starts_ref,
    cleans_ref,
    length_rows,
    drawn,
    residuals,
    sems,
):
    del me_ref
    passages, slots = codes_hbm.shape
    width = own_hbm.shape[1]
    lengths_copy = pltpu.make_async_copy(lengths_hbm, lengths_ref, sems.at[0])
    codes_copy = pltpu.make_async_copy(codes_hbm, drawn, sems.at[1])
    residual_copy = pltpu.make_async_copy(residuals_hbm, residuals, sems.at[2])
    own_copy = pltpu.make_async_copy(own_hbm, staged, sems.at[3])
    lengths_copy.start()
    codes_copy.start()
    residual_copy.start()
    own_copy.start()
    nothing[...] = jnp.zeros(nothing.shape, nothing.dtype)
    lengths_copy.wait()

    def listing(p, chunks):
        length = lengths_ref[p]
        length_rows[pl.ds(p, 1), :] = jnp.full((1, slots), length, jnp.int32)
        for k in range(slots // CHUNK):
            starts_ref[chunks + k] = p * slots + k * CHUNK
            cleans_ref[chunks + k] = p * slots + k * CHUNK
        return chunks + quotient(length + CHUNK - 1, CHUNK)

    last = starts_ref.shape[0] - 1
    chunks = jnp.int32(0)
    for step, (low, high) in enumerate(shares_of(passages)):
        chunks = lax.fori_loop(low, high, listing, chunks, unroll=4)
        for k in range(GROUP):
            starts_ref[chunks + k] = passages * slots
            cleans_ref[chunks + k] = low * slots
        chunks = quotient(chunks + GROUP - 1, GROUP) * GROUP
        cleans_ref[last - STEPS + step] = quotient(chunks, GROUP)
    for k in range(SCORE_GROUP):
        starts_ref[chunks + k] = passages * slots
    starts_ref[last] = chunks
    starts_copy = pltpu.make_async_copy(starts_ref, starts, sems.at[4])
    cleans_copy = pltpu.make_async_copy(cleans_ref, cleans, sems.at[5])
    starts_copy.start()
    cleans_copy.start()
    codes_copy.wait()
    lanes = lax.broadcasted_iota(jnp.int32, (passages, slots), 1)
    codes[...] = jnp.where(lanes < length_rows[...], drawn[...], drawn[:, 0:1])
    residual_copy.wait()
    slot_numbers = lax.broadcasted_iota(jnp.int32, (CHUNK, width), 0)

    def place(g, carry):
        for k in range(GROUP):
            at = cleans_ref[g * GROUP + k]
            p = quotient(at, slots)
            live = lengths_ref[p] - (at - p * slots)
            first = residuals[pl.ds(pl.multiple_of(p * slots, CHUNK), CHUNK), :]
            rows = residuals[pl.ds(pl.multiple_of(at, CHUNK), CHUNK), :].astype(jnp.float32)
            rows = jnp.where(slot_numbers < live, rows, first.astype(jnp.float32)[0:1, :])
            to = pl.multiple_of((g * GROUP + k) * CHUNK, CHUNK)
            near[pl.ds(to, CHUNK), :] = rows
        return carry

    lax.fori_loop(0, quotient(chunks, GROUP), place, 0)
    own_copy.wait()
    starts_copy.wait()
    cleans_copy.wait()


def list_size(passages, slots):
    most = passages * (slots // CHUNK) + STEPS * GROUP + SCORE_GROUP + STEPS + 1
    return -(-most // 1024) * 1024


def list_rows(passages, slots):
    rounding = SCORE_GROUP * CHUNK
    return -(-(passages * slots + STEPS * GROUP * CHUNK) // rounding) * rounding


def prepare(me, lengths, token_codes, own, residuals):
    width = own.shape[1]
    passages, slots = token_codes.shape
    most = list_size(passages, slots)
    return pl.pallas_call(
        prepare_kernel,
        out_shape=(
            pltpu.VMEM(own.shape, jnp.bfloat16),
            pltpu.VMEM((list_rows(passages, slots), width), jnp.float32),
            pltpu.VMEM(token_codes.shape, jnp.int32),
            pltpu.VMEM((most,), jnp.int32),
            pltpu.VMEM((most,), jnp.int32),
            pltpu.VMEM((16, width), jnp.bfloat16),
        ),
        in_specs=[SMEM, HBM, HBM, HBM, HBM],
        out_specs=(VMEM,) * 6,
        scratch_shapes=[
            pltpu.SMEM(lengths.shape, jnp.int32),
            pltpu.SMEM((most,), jnp.int32),
            pltpu.SMEM((most,), jnp.int32),
            pltpu.VMEM(token_codes.shape, jnp.int32),
            pltpu.VMEM(token_codes.shape, jnp.int32),
            pltpu.VMEM(residuals.shape, jnp.bfloat16),
            pltpu.SemaphoreType.DMA((6,)),
        ],
        compiler_params=granted(4),
        cost_estimate=pl.CostEstimate(flops=10**7, bytes_accessed=8 * 10**6, transcendentals=0),
        name="prepare",
    )(me, pinned(lengths), pinned(token_codes), pinned(own), pinned(residuals))


def decode_kernel(step, passages, *refs):
    if step == 0:
        half_ref, own_ref, other_ref, codes, cleans, near, _, table = refs[:8]
    else:
        codes, cleans, near, table = refs[:4]
    embedded, rows, nothing, codes_smem, cleans_ref, sems = refs[-6:]
    slots = codes.shape[1]
    width = rows.shape[1]
    codes_ref = codes_smem.reshape(passages * slots)
    moves = []
    first, after = shares_of(passages)[step]
    first_move, after_move = first // 8 * 8, min(-(-after // 8) * 8, passages)
    part = pl.ds(first_move, after_move - first_move)
    pairs = ((cleans, cleans_ref), (codes.at[part], codes_smem.at[part]))
    for k, (source, to) in enumerate(pairs):
        moves.append(pltpu.make_async_copy(source, to, sems.at[k]))
        moves[-1].start()
    nothing[...] = jnp.zeros(nothing.shape, nothing.dtype)
    if step == 0:
        half_rows = other_ref.shape[0]
        piece = half_rows // PIECES
        for source, base in ((own_ref, half_ref[0]), (other_ref, 1 - half_ref[0])):
            for k in range(PIECES):
                to = pl.ds(pl.multiple_of(base * half_rows + k * piece, piece), piece)
                table[to, :] = source[pl.ds(k * piece, piece), :].astype(jnp.float32)

    table_single = table.reshape(table.shape[0], 1, width)
    rows_single = rows.reshape(rows.shape[0], 1, width)

    def fetch(g):
        for k in range(GROUP):
            at = cleans_ref[g * GROUP + k]
            for j in range(CHUNK):
                rows_single[k * CHUNK + j] = table_single[codes_ref[at + j]]

    def finish(g):
        size = GROUP * CHUNK
        return normalized(rows[...] + near[pl.ds(pl.multiple_of(g * size, size), size), :])

    def keep(g, done):
        size = GROUP * CHUNK
        embedded[pl.ds(pl.multiple_of(g * size, size), size), :] = done

    for move in moves:
        move.wait()
    last = cleans_ref.shape[0] - 1
    low = cleans_ref[last - STEPS + step - 1] if step > 0 else 0
    high = cleans_ref[last - STEPS + step]
    def decode(g, carry):
        done = finish(g - 1)
        fetch(g)
        keep(g - 1, done)
        return carry

    if step == 0:
        fetch(low)
    lax.fori_loop(low + (step == 0), high, decode, 0)
    if step == STEPS - 1:
        keep(high - 1, finish(high - 1))


def decode_step(
    step, half, own, other, codes, cleans, near, table, carried, held
):
    passages, slots = codes.shape
    width = near.shape[1]
    space = near.shape
    inside = lambda array: pinned(array, pltpu.VMEM)
    shared = [inside(codes), inside(cleans), inside(near)]
    if step == 0:
        operands = [half, inside(own), inside(other)] + shared + [inside(held)]
        in_specs = [SMEM] + [VMEM] * 6
        whole = (2 * own.shape[0], width)
        out_shape = [pltpu.VMEM(whole, jnp.float32)]
        aliases = {}
    else:
        operands = shared + [inside(table), inside(held)] + [inside(array) for array in carried]
        in_specs = [VMEM] * 7
        out_shape = []
        aliases = {5: 0, 6: 1}
    out_shape.append(pltpu.VMEM(space, jnp.bfloat16))
    out_shape.append(pltpu.VMEM((GROUP * CHUNK, width), jnp.float32))
    out_shape.append(pltpu.VMEM((16, width), jnp.bfloat16))
    results = pl.pallas_call(
        functools.partial(decode_kernel, step, passages),
        out_shape=tuple(out_shape),
        in_specs=in_specs,
        out_specs=(VMEM,) * len(out_shape),
        input_output_aliases=aliases,
        scratch_shapes=[
            pltpu.SMEM(codes.shape, jnp.int32),
            pltpu.SMEM(cleans.shape, jnp.int32),
            pltpu.SemaphoreType.DMA((2,)),
        ],
        compiler_params=granted(4),
        cost_estimate=pl.CostEstimate(flops=10**7, bytes_accessed=10**7, transcendentals=0),
        name="decode",
    )(*operands)
    if step == 0:
        table, results = results[0], results[1:]
    return table, results[:2], results[2]


def score_kernel(
    bit,
    token_count,
    local_queries,
    slots,
    me_ref,
    starts,
    queries_ref,
    embedded,
    before_ref,
    out_ref,
    at_ref,
    turned,
    largest,
    sem,
):
    starts_copy = pltpu.make_async_copy(starts, at_ref, sem)
    starts_copy.start()
    passages = out_ref.shape[1]
    query_tokens = queries_ref.shape[0]
    block = min(QUERY_BLOCK, query_tokens)
    blocks = query_tokens // block
    window = 2 * block // token_count
    window_targets = window // local_queries
    near_me = me_ref[0] & (window_targets - 1)
    far_me = quotient(me_ref[0], window_targets)
    owner = lax.broadcasted_iota(jnp.int32, (window, block), 0)
    owner_target = quotient(owner, local_queries)
    owner_row = (owner_target ^ near_me) * local_queries + owner - owner_target * local_queries
    query_of = quotient(lax.broadcasted_iota(jnp.int32, (window, block), 1), token_count)
    target_of = quotient(query_of, local_queries)
    row_of = query_of + (target_of + bit) * local_queries
    summing = (owner_row == row_of).astype(jnp.bfloat16)
    count = SCORE_GROUP // SCORE_PARTS
    size = count * CHUNK

    def score_block(b, carry):
        at = pl.ds(pl.multiple_of(b * block, block), block)
        vectors = normalized(queries_ref[at, :].astype(jnp.float32))
        turned[...] = vectors.astype(jnp.float32).T.astype(jnp.bfloat16)

        def score(first, so_far):
            at = pl.ds(pl.multiple_of(first * size, size), size)
            similar = jnp.dot(embedded[at, :], turned[...], preferred_element_type=jnp.float32)
            parts = jnp.max(similar.reshape(count, CHUNK // 8, 8, block), axis=1)
            for k in range(count):
                start = at_ref[first * count + k]
                p = quotient(start, slots)
                so_far = jnp.where(start == p * slots, parts[k], jnp.maximum(so_far, parts[k]))
                to = pl.multiple_of(p * 8, 8)
                for lane in range(block // 128):
                    largest[lane, pl.ds(to, 8), :] = so_far[:, lane * 128 : (lane + 1) * 128]
            return so_far

        def score_parts(g, so_far):
            for part in range(SCORE_PARTS):
                so_far = score(g * SCORE_PARTS + part, so_far)
            return so_far

        @pl.when(b == 0)
        def arrived():
            starts_copy.wait()

        parts_used = quotient(at_ref[at_ref.shape[0] - 1] + count - 1, count)
        whole = quotient(parts_used, SCORE_PARTS)
        so_far = jnp.zeros((8, block), jnp.float32)
        so_far = lax.fori_loop(0, whole, score_parts, so_far)
        lax.fori_loop(whole * SCORE_PARTS, parts_used, score, so_far)
        kept = []
        for lane in range(block // 128):
            best = largest[lane, pl.ds(0, passages, stride=8), :]
            for k in range(1, 8):
                best = jnp.maximum(best, largest[lane, pl.ds(k, passages, stride=8), :])
            kept.append(best)
        left = jnp.concatenate(kept, axis=1)
        to = pl.ds(pl.multiple_of((b ^ far_me) * window, window), window)
        sums = before_ref[to, :] if bit else jnp.zeros((window, passages), jnp.float32)
        for _ in range(3):
            part = left.astype(jnp.bfloat16)
            left = left - part.astype(jnp.float32)
            sums = sums + lax.dot_general(
                summing, part, (((1,), (1,)), ((), ())), preferred_element_type=jnp.float32
            )
        out_ref[to, :] = sums
        return carry

    lax.fori_loop(0, blocks, score_block, 0)


def score_half(bit, me, starts, query_rows, embedded, before, passages, slots, shape):
    token_count, local_queries = shape
    query_tokens, width = query_rows.shape
    block = min(QUERY_BLOCK, query_tokens)
    blocks = query_tokens // block
    return pl.pallas_call(
        functools.partial(score_kernel, bit, token_count, local_queries, slots),
        out_shape=pltpu.VMEM((2 * query_tokens // token_count, passages), jnp.float32),
        in_specs=[SMEM] + [VMEM] * 4,
        out_specs=VMEM,
        scratch_shapes=[
            pltpu.SMEM(starts.shape, jnp.int32),
            pltpu.VMEM((width, block), jnp.bfloat16),
            pltpu.VMEM((block // 128, (passages + 1) * 8, 128), jnp.float32),
            pltpu.SemaphoreType.DMA,
        ],
        compiler_params=granted(4),
        cost_estimate=pl.CostEstimate(flops=10**7, bytes_accessed=8 * 10**6, transcendentals=0),
        name="score",
    )(
        me,
        pinned(starts, pltpu.VMEM),
        pinned(query_rows, pltpu.VMEM),
        pinned(embedded, pltpu.VMEM),
        pinned(before, pltpu.VMEM),
    )


def pick_kernel(passages, candidates_ref, returned_ref, out_ref):
    local_queries, count = candidates_ref.shape
    targets = returned_ref.shape[0]
    passage_numbers = lax.broadcasted_iota(jnp.int32, (passages, count), 0)
    target_numbers = lax.broadcasted_iota(jnp.int32, (targets, count), 0)
    for q in range(local_queries):
        wanted = candidates_ref[q : q + 1, :]
        target = quotient(wanted, passages)
        hits = (passage_numbers == wanted - target * passages).astype(jnp.bfloat16)
        left = returned_ref[:, q * passages : (q + 1) * passages]
        picked = jnp.zeros((targets, count), jnp.float32)
        for _ in range(3):
            part = left.astype(jnp.bfloat16)
            left = left - part.astype(jnp.float32)
            picked = picked + jnp.dot(part, hits, preferred_element_type=jnp.float32)
        kept = jnp.where(target_numbers == target, picked, 0.0)
        out_ref[q : q + 1, :] = jnp.sum(kept, axis=0, keepdims=True)


def pick(candidates, returned, passages):
    return pl.pallas_call(
        functools.partial(pick_kernel, passages),
        out_shape=jax.ShapeDtypeStruct(candidates.shape, jnp.float32),
        in_specs=[VMEM, VMEM],
        out_specs=VMEM,
        compiler_params=granted(8),
        name="pick",
    )(candidates, pltpu.with_memory_space_constraint(returned, pltpu.VMEM))


def body(queries, candidates, token_codes, residuals, lengths, centroids):
    local_queries, token_count, width = queries.shape
    targets = lax.axis_size("shard") * lax.axis_size("sub")
    passages, slots = token_codes.shape
    half = lax.axis_index("sub").astype(jnp.int32)
    me = lax.axis_index("shard").astype(jnp.int32) * lax.axis_size("sub") + half
    half = half.reshape(1)
    me = me.reshape(1)
    flat = residuals.reshape(passages * slots, width)
    other = lax.ppermute(centroids, "sub", [(0, 1), (1, 0)])

    held = queries.reshape(1, 1, local_queries * token_count, width)
    bits = targets.bit_length() - 1
    carried = None
    for turn, first in enumerate(range(bits - 1, -1, -1)):
        pairs = [(device, device ^ (1 << first)) for device in range(targets)]
        received = lax.ppermute(held, ("shard", "sub"), pairs)
        if turn == 0:
            ready = prepare(me, lengths, token_codes, centroids, flat)
            own, near, codes, starts, cleans, nothing = ready
            table = None
        elif turn <= STEPS:
            table, carried, nothing = decode_step(
                turn - 1, half, own, other, codes, cleans, near, table, carried, held
            )
        if first > 0:
            received = received + nothing[0:1, :]
            held = jnp.concatenate([held, received], axis=1)
            held = held.reshape((-1, 1) + held.shape[2:])
    shape = (token_count, local_queries)
    scores = carried[1]
    for bit, half_rows in enumerate((held, received)):
        rows = half_rows.reshape(targets // 2 * local_queries * token_count, width)
        scores = score_half(bit, me, starts, rows, carried[0], scores, passages, slots, shape)
    returned = lax.all_to_all(
        scores.reshape(targets, local_queries * passages),
        ("shard", "sub"),
        split_axis=0,
        concat_axis=0,
        tiled=True,
    )
    return pick(candidates, returned, passages)


def solution(mesh):
    placed = (
        P(("groups", "shard", "sub"), None, None),
        P(("groups", "shard", "sub"), None),
        P(("groups", "shard", "sub"), None),
        P(("groups", "shard", "sub"), None, None),
        P(("groups", "shard", "sub")),
        P(("groups", "shard", "sub"), None),
    )
    return jax.shard_map(
        body,
        mesh=mesh,
        in_specs=placed,
        out_specs=P(("groups", "shard", "sub"), None),
        check_vma=False,
    )
```

```python
import functools

import jax
import jax.numpy as jnp
from jax import lax
from jax.experimental import pallas as pl
from jax.experimental.pallas import tpu as pltpu
from jax.sharding import PartitionSpec as P

CHUNK = 16
GROUP = 16
SCORE_GROUP = 64
SCORE_PARTS = 2
STEPS = 2
PIECES = 4
QUERY_BLOCK = 512
SMEM = pl.BlockSpec(memory_space=pltpu.SMEM)
VMEM = pl.BlockSpec(memory_space=pltpu.VMEM)
HBM = pl.BlockSpec(memory_space=pltpu.HBM)


def normalized(vectors):
    total = jnp.sum(vectors * vectors, axis=-1, keepdims=True)
    return (vectors * lax.rsqrt(total + 1e-06)).astype(jnp.bfloat16)


def quotient(number, divisor):
    if divisor & (divisor - 1) == 0:
        return lax.shift_right_logical(number, divisor.bit_length() - 1)
    return lax.div(number, divisor)


def pinned(array, space=pltpu.HBM):
    return pltpu.with_memory_space_constraint(array, space)


def granted(mebibytes):
    return pltpu.CompilerParams(vmem_limit_bytes=mebibytes * 1024 * 1024)


def shares_of(passages):
    edges = [0, passages // 2]
    return tuple(zip(edges, edges[1:] + [passages]))


def widened(table, half, source):
    half_rows = source.shape[0]
    piece = half_rows // PIECES
    for k in range(PIECES):
        to = pl.ds(pl.multiple_of(half * half_rows + k * piece, piece), piece)
        table[to, :] = source[pl.ds(k * piece, piece), :].astype(jnp.float32)


def prepare_kernel(
    me_ref,
    half_ref,
    lengths_hbm,
    codes_hbm,
    own_hbm,
    residuals_hbm,
    table,
    near,
    codes,
    marks,
    resets,
    cleans,
    nothing,
    lengths_ref,
    marks_ref,
    resets_ref,
    cleans_ref,
    length_rows,
    drawn,
    staged,
    residuals,
    sems,
):
    del me_ref
    passages, slots = codes_hbm.shape
    width = own_hbm.shape[1]
    lengths_copy = pltpu.make_async_copy(lengths_hbm, lengths_ref, sems.at[0])
    codes_copy = pltpu.make_async_copy(codes_hbm, drawn, sems.at[1])
    residual_copy = pltpu.make_async_copy(residuals_hbm, residuals, sems.at[2])
    own_copy = pltpu.make_async_copy(own_hbm, staged, sems.at[3])
    lengths_copy.start()
    codes_copy.start()
    residual_copy.start()
    own_copy.start()
    nothing[...] = jnp.zeros(nothing.shape, nothing.dtype)
    lengths_copy.wait()

    def listing(p, chunks):
        length = lengths_ref[p]
        length_rows[pl.ds(p, 1), :] = jnp.full((1, slots), length, jnp.int32)
        for k in range(slots // CHUNK):
            marks_ref[chunks + k] = p
            resets_ref[chunks + k] = -jnp.inf if k == 0 else 0.0
            cleans_ref[chunks + k] = p * slots + k * CHUNK
        return chunks + quotient(length + CHUNK - 1, CHUNK)

    last = marks_ref.shape[0] - 1
    chunks = jnp.int32(0)
    for step, (low, high) in enumerate(shares_of(passages)):
        chunks = lax.fori_loop(low, high, listing, chunks, unroll=4)
        for k in range(GROUP):
            marks_ref[chunks + k] = passages
            resets_ref[chunks + k] = -jnp.inf
            cleans_ref[chunks + k] = low * slots
        chunks = quotient(chunks + GROUP - 1, GROUP) * GROUP
        cleans_ref[last - STEPS + step] = quotient(chunks, GROUP)
    for k in range(SCORE_GROUP):
        marks_ref[chunks + k] = passages
        resets_ref[chunks + k] = -jnp.inf
    marks_ref[last] = chunks
    lists = []
    for source, to in ((marks_ref, marks), (resets_ref, resets), (cleans_ref, cleans)):
        lists.append(pltpu.make_async_copy(source, to, sems.at[4 + len(lists)]))
        lists[-1].start()
    codes_copy.wait()
    lanes = lax.broadcasted_iota(jnp.int32, (passages, slots), 1)
    codes[...] = jnp.where(lanes < length_rows[...], drawn[...], drawn[:, 0:1])
    residual_copy.wait()
    slot_numbers = lax.broadcasted_iota(jnp.int32, (CHUNK, width), 0)

    def place(g, carry):
        for k in range(GROUP):
            at = cleans_ref[g * GROUP + k]
            p = quotient(at, slots)
            live = lengths_ref[p] - (at - p * slots)
            first = residuals[pl.ds(pl.multiple_of(p * slots, CHUNK), CHUNK), :]
            rows = residuals[pl.ds(pl.multiple_of(at, CHUNK), CHUNK), :].astype(jnp.float32)
            rows = jnp.where(slot_numbers < live, rows, first.astype(jnp.float32)[0:1, :])
            to = pl.multiple_of((g * GROUP + k) * CHUNK, CHUNK)
            near[pl.ds(to, CHUNK), :] = rows
        return carry

    lax.fori_loop(0, quotient(chunks, GROUP), place, 0)
    own_copy.wait()
    widened(table, half_ref[0], staged)
    for copy in lists:
        copy.wait()


def list_size(passages, slots):
    most = passages * (slots // CHUNK) + STEPS * GROUP + SCORE_GROUP + STEPS + 1
    return -(-most // 1024) * 1024


def list_rows(passages, slots):
    rounding = SCORE_GROUP * CHUNK
    return -(-(passages * slots + STEPS * GROUP * CHUNK) // rounding) * rounding


def prepare(me, half, lengths, token_codes, own, residuals):
    half_rows, width = own.shape
    passages, slots = token_codes.shape
    most = list_size(passages, slots)
    return pl.pallas_call(
        prepare_kernel,
        out_shape=(
            pltpu.VMEM((2 * half_rows, width), jnp.float32),
            pltpu.VMEM((list_rows(passages, slots), width), jnp.float32),
            pltpu.VMEM(token_codes.shape, jnp.int32),
            pltpu.VMEM((most,), jnp.int32),
            pltpu.VMEM((most,), jnp.float32),
            pltpu.VMEM((most,), jnp.int32),
            pltpu.VMEM((16, width), jnp.bfloat16),
        ),
        in_specs=[SMEM, SMEM, HBM, HBM, HBM, HBM],
        out_specs=(VMEM,) * 7,
        scratch_shapes=[
            pltpu.SMEM(lengths.shape, jnp.int32),
            pltpu.SMEM((most,), jnp.int32),
            pltpu.SMEM((most,), jnp.float32),
            pltpu.SMEM((most,), jnp.int32),
            pltpu.VMEM(token_codes.shape, jnp.int32),
            pltpu.VMEM(token_codes.shape, jnp.int32),
            pltpu.VMEM(own.shape, jnp.bfloat16),
            pltpu.VMEM(residuals.shape, jnp.bfloat16),
            pltpu.SemaphoreType.DMA((7,)),
        ],
        compiler_params=granted(6),
        cost_estimate=pl.CostEstimate(flops=10**7, bytes_accessed=8 * 10**6, transcendentals=0),
        name="prepare",
    )(me, half, pinned(lengths), pinned(token_codes), pinned(own), pinned(residuals))


def decode_kernel(step, passages, *refs):
    if step == 0:
        half_ref, other_ref, codes, cleans, near, _, _, table = refs[:8]
    else:
        codes, cleans, near, table = refs[:4]
    embedded, rows, nothing, codes_smem, cleans_ref, sems = refs[-6:]
    slots = codes.shape[1]
    width = rows.shape[1]
    codes_ref = codes_smem.reshape(passages * slots)
    moves = []
    first, after = shares_of(passages)[step]
    first_move, after_move = first // 8 * 8, min(-(-after // 8) * 8, passages)
    part = pl.ds(first_move, after_move - first_move)
    pairs = ((cleans, cleans_ref), (codes.at[part], codes_smem.at[part]))
    for k, (source, to) in enumerate(pairs):
        moves.append(pltpu.make_async_copy(source, to, sems.at[k]))
        moves[-1].start()
    nothing[...] = jnp.zeros(nothing.shape, nothing.dtype)
    if step == 0:
        widened(table, 1 - half_ref[0], other_ref)

    table_single = table.reshape(table.shape[0], 1, width)
    rows_single = rows.reshape(rows.shape[0], 1, width)

    def fetch(g):
        for k in range(GROUP):
            at = cleans_ref[g * GROUP + k]
            for j in range(CHUNK):
                rows_single[k * CHUNK + j] = table_single[codes_ref[at + j]]

    def finish(g):
        size = GROUP * CHUNK
        return normalized(rows[...] + near[pl.ds(pl.multiple_of(g * size, size), size), :])

    def keep(g, done):
        size = GROUP * CHUNK
        embedded[pl.ds(pl.multiple_of(g * size, size), size), :] = done

    for move in moves:
        move.wait()
    last = cleans_ref.shape[0] - 1
    low = cleans_ref[last - STEPS + step - 1] if step > 0 else 0
    high = cleans_ref[last - STEPS + step]
    def decode(g, carry):
        done = finish(g - 1)
        fetch(g)
        keep(g - 1, done)
        return carry

    if step == 0:
        fetch(low)
    lax.fori_loop(low + (step == 0), high, decode, 0)
    if step == STEPS - 1:
        keep(high - 1, finish(high - 1))


def decode_step(
    step, half, other, codes, cleans, near, table, carried, held
):
    passages, slots = codes.shape
    width = near.shape[1]
    space = near.shape
    inside = lambda array: pinned(array, pltpu.VMEM)
    shared = [inside(codes), inside(cleans), inside(near)]
    if step == 0:
        operands = [half, inside(other)] + shared + [inside(held), inside(table)]
        in_specs = [SMEM] + [VMEM] * 6
        out_shape = [pltpu.VMEM(table.shape, jnp.float32)]
        aliases = {6: 0}
    else:
        operands = shared + [inside(table), inside(held)] + [inside(array) for array in carried]
        in_specs = [VMEM] * 7
        out_shape = []
        aliases = {5: 0, 6: 1}
    out_shape.append(pltpu.VMEM(space, jnp.bfloat16))
    out_shape.append(pltpu.VMEM((GROUP * CHUNK, width), jnp.float32))
    out_shape.append(pltpu.VMEM((16, width), jnp.bfloat16))
    results = pl.pallas_call(
        functools.partial(decode_kernel, step, passages),
        out_shape=tuple(out_shape),
        in_specs=in_specs,
        out_specs=(VMEM,) * len(out_shape),
        input_output_aliases=aliases,
        scratch_shapes=[
            pltpu.SMEM(codes.shape, jnp.int32),
            pltpu.SMEM(cleans.shape, jnp.int32),
            pltpu.SemaphoreType.DMA((2,)),
        ],
        compiler_params=granted(4),
        cost_estimate=pl.CostEstimate(flops=10**7, bytes_accessed=10**7, transcendentals=0),
        name="decode",
    )(*operands)
    if step == 0:
        table, results = results[0], results[1:]
    return table, results[:2], results[2]


def score_kernel(
    bit,
    token_count,
    local_queries,
    me_ref,
    marks,
    resets,
    queries_ref,
    embedded,
    before_ref,
    out_ref,
    marks_ref,
    resets_ref,
    turned,
    largest,
    sems,
):
    lists = []
    for k, (source, to) in enumerate(((marks, marks_ref), (resets, resets_ref))):
        lists.append(pltpu.make_async_copy(source, to, sems.at[k]))
        lists[-1].start()
    passages = out_ref.shape[1]
    query_tokens = queries_ref.shape[0]
    block = min(QUERY_BLOCK, query_tokens)
    blocks = query_tokens // block
    window = 2 * block // token_count
    window_targets = window // local_queries
    near_me = me_ref[0] & (window_targets - 1)
    far_me = quotient(me_ref[0], window_targets)
    owner = lax.broadcasted_iota(jnp.int32, (window, block), 0)
    owner_target = quotient(owner, local_queries)
    owner_row = (owner_target ^ near_me) * local_queries + owner - owner_target * local_queries
    query_of = quotient(lax.broadcasted_iota(jnp.int32, (window, block), 1), token_count)
    target_of = quotient(query_of, local_queries)
    row_of = query_of + (target_of + bit) * local_queries
    summing = (owner_row == row_of).astype(jnp.bfloat16)
    count = SCORE_GROUP // SCORE_PARTS
    size = count * CHUNK

    def score_block(b, carry):
        at = pl.ds(pl.multiple_of(b * block, block), block)
        vectors = normalized(queries_ref[at, :].astype(jnp.float32))
        turned[...] = vectors.astype(jnp.float32).T.astype(jnp.bfloat16)

        def score(first, so_far):
            at = pl.ds(pl.multiple_of(first * size, size), size)
            similar = jnp.dot(embedded[at, :], turned[...], preferred_element_type=jnp.float32)
            parts = jnp.max(similar.reshape(count, CHUNK // 8, 8, block), axis=1)
            for k in range(count):
                so_far = jnp.maximum(so_far + resets_ref[first * count + k], parts[k])
                p = marks_ref[first * count + k]
                for lane in range(block // 128):
                    largest[lane, p] = so_far[:, lane * 128 : (lane + 1) * 128]
            return so_far

        def score_parts(g, so_far):
            for part in range(SCORE_PARTS):
                so_far = score(g * SCORE_PARTS + part, so_far)
            return so_far

        @pl.when(b == 0)
        def arrived():
            for copy in lists:
                copy.wait()

        parts_used = quotient(marks_ref[marks_ref.shape[0] - 1] + count - 1, count)
        whole = quotient(parts_used, SCORE_PARTS)
        so_far = jnp.zeros((8, block), jnp.float32)
        so_far = lax.fori_loop(0, whole, score_parts, so_far)
        lax.fori_loop(whole * SCORE_PARTS, parts_used, score, so_far)
        kept = []
        for lane in range(block // 128):
            flat = largest.at[lane].reshape(8 * largest.shape[1], 128)
            best = flat[pl.ds(0, passages, stride=8), :]
            for k in range(1, 8):
                best = jnp.maximum(best, flat[pl.ds(k, passages, stride=8), :])
            kept.append(best)
        left = jnp.concatenate(kept, axis=1)
        to = pl.ds(pl.multiple_of((b ^ far_me) * window, window), window)
        sums = before_ref[to, :] if bit else jnp.zeros((window, passages), jnp.float32)
        for _ in range(3):
            part = left.astype(jnp.bfloat16)
            left = left - part.astype(jnp.float32)
            sums = sums + lax.dot_general(
                summing, part, (((1,), (1,)), ((), ())), preferred_element_type=jnp.float32
            )
        out_ref[to, :] = sums
        return carry

    lax.fori_loop(0, blocks, score_block, 0)


def score_half(bit, me, marks, resets, query_rows, embedded, before, passages, shape):
    token_count, local_queries = shape
    query_tokens, width = query_rows.shape
    block = min(QUERY_BLOCK, query_tokens)
    blocks = query_tokens // block
    return pl.pallas_call(
        functools.partial(score_kernel, bit, token_count, local_queries),
        out_shape=pltpu.VMEM((2 * query_tokens // token_count, passages), jnp.float32),
        in_specs=[SMEM] + [VMEM] * 5,
        out_specs=VMEM,
        scratch_shapes=[
            pltpu.SMEM(marks.shape, jnp.int32),
            pltpu.SMEM(resets.shape, jnp.float32),
            pltpu.VMEM((width, block), jnp.bfloat16),
            pltpu.VMEM((block // 128, passages + 1, 8, 128), jnp.float32),
            pltpu.SemaphoreType.DMA((2,)),
        ],
        compiler_params=granted(4),
        cost_estimate=pl.CostEstimate(flops=10**7, bytes_accessed=8 * 10**6, transcendentals=0),
        name="score",
    )(
        me,
        pinned(marks, pltpu.VMEM),
        pinned(resets, pltpu.VMEM),
        pinned(query_rows, pltpu.VMEM),
        pinned(embedded, pltpu.VMEM),
        pinned(before, pltpu.VMEM),
    )


def pick_kernel(passages, candidates_ref, returned_ref, out_ref):
    local_queries, count = candidates_ref.shape
    targets = returned_ref.shape[0]
    passage_numbers = lax.broadcasted_iota(jnp.int32, (passages, count), 0)
    target_numbers = lax.broadcasted_iota(jnp.int32, (targets, count), 0)
    for q in range(local_queries):
        wanted = candidates_ref[q : q + 1, :]
        target = quotient(wanted, passages)
        hits = (passage_numbers == wanted - target * passages).astype(jnp.bfloat16)
        left = returned_ref[:, q * passages : (q + 1) * passages]
        picked = jnp.zeros((targets, count), jnp.float32)
        for _ in range(3):
            part = left.astype(jnp.bfloat16)
            left = left - part.astype(jnp.float32)
            picked = picked + jnp.dot(part, hits, preferred_element_type=jnp.float32)
        kept = jnp.where(target_numbers == target, picked, 0.0)
        out_ref[q : q + 1, :] = jnp.sum(kept, axis=0, keepdims=True)


def pick(candidates, returned, passages):
    return pl.pallas_call(
        functools.partial(pick_kernel, passages),
        out_shape=jax.ShapeDtypeStruct(candidates.shape, jnp.float32),
        in_specs=[VMEM, VMEM],
        out_specs=VMEM,
        compiler_params=granted(8),
        name="pick",
    )(candidates, pltpu.with_memory_space_constraint(returned, pltpu.VMEM))


def body(queries, candidates, token_codes, residuals, lengths, centroids):
    local_queries, token_count, width = queries.shape
    targets = lax.axis_size("shard") * lax.axis_size("sub")
    passages, slots = token_codes.shape
    half = lax.axis_index("sub").astype(jnp.int32)
    me = lax.axis_index("shard").astype(jnp.int32) * lax.axis_size("sub") + half
    half = half.reshape(1)
    me = me.reshape(1)
    flat = residuals.reshape(passages * slots, width)
    other = lax.ppermute(centroids, "sub", [(0, 1), (1, 0)])

    held = queries.reshape(1, 1, local_queries * token_count, width)
    bits = targets.bit_length() - 1
    carried = None
    for turn, first in enumerate(range(bits - 1, -1, -1)):
        pairs = [(device, device ^ (1 << first)) for device in range(targets)]
        received = lax.ppermute(held, ("shard", "sub"), pairs)
        if turn == 0:
            ready = prepare(me, half, lengths, token_codes, centroids, flat)
            table, near, codes, marks, resets, cleans, nothing = ready
        elif turn <= STEPS:
            table, carried, nothing = decode_step(
                turn - 1, half, other, codes, cleans, near, table, carried, held
            )
        if first > 0:
            received = received + nothing[0:1, :]
            held = jnp.concatenate([held, received], axis=1)
            held = held.reshape((-1, 1) + held.shape[2:])
    shape = (token_count, local_queries)
    scores = carried[1]
    for bit, half_rows in enumerate((held, received)):
        rows = half_rows.reshape(targets // 2 * local_queries * token_count, width)
        scores = score_half(bit, me, marks, resets, rows, carried[0], scores, passages, shape)
    returned = lax.all_to_all(
        scores.reshape(targets, local_queries * passages),
        ("shard", "sub"),
        split_axis=0,
        concat_axis=0,
        tiled=True,
    )
    return pick(candidates, returned, passages)


def solution(mesh):
    placed = (
        P(("groups", "shard", "sub"), None, None),
        P(("groups", "shard", "sub"), None),
        P(("groups", "shard", "sub"), None),
        P(("groups", "shard", "sub"), None, None),
        P(("groups", "shard", "sub")),
        P(("groups", "shard", "sub"), None),
    )
    return jax.shard_map(
        body,
        mesh=mesh,
        in_specs=placed,
        out_specs=P(("groups", "shard", "sub"), None),
        check_vma=False,
    )
```

```python
import functools

import jax
import jax.numpy as jnp
from jax import lax
from jax.experimental import pallas as pl
from jax.experimental.pallas import tpu as pltpu
from jax.sharding import PartitionSpec as P

CHUNK = 16
GROUP = 16
SCORE_GROUP = 64
SCORE_PARTS = 2
STEPS = 2
PIECES = 4
QUERY_BLOCK = 512
SMEM = pl.BlockSpec(memory_space=pltpu.SMEM)
VMEM = pl.BlockSpec(memory_space=pltpu.VMEM)
HBM = pl.BlockSpec(memory_space=pltpu.HBM)


def normalized(vectors):
    total = jnp.sum(vectors * vectors, axis=-1, keepdims=True)
    return (vectors * lax.rsqrt(total + 1e-06)).astype(jnp.bfloat16)


def thirds(values):
    parts = []
    for _ in range(3):
        parts.append(values.astype(jnp.bfloat16))
        values = values - parts[-1].astype(jnp.float32)
    return parts


def quotient(number, divisor):
    if divisor & (divisor - 1) == 0:
        return lax.shift_right_logical(number, divisor.bit_length() - 1)
    return lax.div(number, divisor)


def pinned(array, space=pltpu.HBM):
    return pltpu.with_memory_space_constraint(array, space)


def granted(mebibytes):
    return pltpu.CompilerParams(vmem_limit_bytes=mebibytes * 1024 * 1024)


def shares_of(passages):
    edges = [0, passages * 15 // 32]
    return tuple(zip(edges, edges[1:] + [passages]))


def prepare_kernel(
    me_ref,
    lengths_hbm,
    codes_hbm,
    own_hbm,
    residuals_hbm,
    staged,
    near,
    codes,
    starts,
    cleans,
    nothing,
    lengths_ref,
    starts_ref,
    cleans_ref,
    length_rows,
    drawn,
    residuals,
    sems,
):
    del me_ref
    passages, slots = codes_hbm.shape
    width = own_hbm.shape[1]
    lengths_copy = pltpu.make_async_copy(lengths_hbm, lengths_ref, sems.at[0])
    codes_copy = pltpu.make_async_copy(codes_hbm, drawn, sems.at[1])
    residual_copy = pltpu.make_async_copy(residuals_hbm, residuals, sems.at[2])
    own_copy = pltpu.make_async_copy(own_hbm, staged, sems.at[3])
    lengths_copy.start()
    codes_copy.start()
    residual_copy.start()
    own_copy.start()
    nothing[...] = jnp.zeros(nothing.shape, nothing.dtype)
    lengths_copy.wait()

    def listing(p, chunks):
        length = lengths_ref[p]
        length_rows[pl.ds(p, 1), :] = jnp.full((1, slots), length, jnp.int32)
        for k in range(slots // CHUNK):
            starts_ref[chunks + k] = p * slots + k * CHUNK
            cleans_ref[chunks + k] = p * slots + k * CHUNK
        return chunks + quotient(length + CHUNK - 1, CHUNK)

    last = starts_ref.shape[0] - 1
    chunks = jnp.int32(0)
    for step, (low, high) in enumerate(shares_of(passages)):
        chunks = lax.fori_loop(low, high, listing, chunks, unroll=4)
        for k in range(GROUP):
            starts_ref[chunks + k] = passages * slots
            cleans_ref[chunks + k] = low * slots
        chunks = quotient(chunks + GROUP - 1, GROUP) * GROUP
        cleans_ref[last - STEPS + step] = quotient(chunks, GROUP)
    for k in range(SCORE_GROUP):
        starts_ref[chunks + k] = passages * slots
    starts_ref[last] = chunks
    starts_copy = pltpu.make_async_copy(starts_ref, starts, sems.at[4])
    cleans_copy = pltpu.make_async_copy(cleans_ref, cleans, sems.at[5])
    starts_copy.start()
    cleans_copy.start()
    codes_copy.wait()
    lanes = lax.broadcasted_iota(jnp.int32, (passages, slots), 1)
    codes[...] = jnp.where(lanes < length_rows[...], drawn[...], drawn[:, 0:1])
    residual_copy.wait()
    slot_numbers = lax.broadcasted_iota(jnp.int32, (CHUNK, width), 0)

    def place(g, carry):
        for k in range(GROUP):
            at = cleans_ref[g * GROUP + k]
            p = quotient(at, slots)
            live = lengths_ref[p] - (at - p * slots)
            first = residuals[pl.ds(pl.multiple_of(p * slots, CHUNK), CHUNK), :]
            rows = residuals[pl.ds(pl.multiple_of(at, CHUNK), CHUNK), :].astype(jnp.float32)
            rows = jnp.where(slot_numbers < live, rows, first.astype(jnp.float32)[0:1, :])
            to = pl.multiple_of((g * GROUP + k) * CHUNK, CHUNK)
            near[pl.ds(to, CHUNK), :] = rows
        return carry

    lax.fori_loop(0, quotient(chunks, GROUP), place, 0)
    own_copy.wait()
    starts_copy.wait()
    cleans_copy.wait()


def list_size(passages, slots):
    most = passages * (slots // CHUNK) + STEPS * GROUP + SCORE_GROUP + STEPS + 1
    return -(-most // 128) * 128


def list_rows(passages, slots):
    rounding = SCORE_GROUP * CHUNK
    return -(-(passages * slots + STEPS * GROUP * CHUNK) // rounding) * rounding


def prepare(me, lengths, token_codes, own, residuals):
    width = own.shape[1]
    passages, slots = token_codes.shape
    most = list_size(passages, slots)
    return pl.pallas_call(
        prepare_kernel,
        out_shape=(
            pltpu.VMEM(own.shape, jnp.bfloat16),
            pltpu.VMEM((list_rows(passages, slots), width), jnp.float32),
            pltpu.VMEM(token_codes.shape, jnp.int32),
            pltpu.VMEM((most,), jnp.int32),
            pltpu.VMEM((most,), jnp.int32),
            pltpu.VMEM((16, width), jnp.bfloat16),
        ),
        in_specs=[SMEM, HBM, HBM, HBM, HBM],
        out_specs=(VMEM,) * 6,
        scratch_shapes=[
            pltpu.SMEM(lengths.shape, jnp.int32),
            pltpu.SMEM((most,), jnp.int32),
            pltpu.SMEM((most,), jnp.int32),
            pltpu.VMEM(token_codes.shape, jnp.int32),
            pltpu.VMEM(token_codes.shape, jnp.int32),
            pltpu.VMEM(residuals.shape, jnp.bfloat16),
            pltpu.SemaphoreType.DMA((6,)),
        ],
        compiler_params=granted(4),
        cost_estimate=pl.CostEstimate(flops=10**7, bytes_accessed=8 * 10**6, transcendentals=0),
        name="prepare",
    )(me, pinned(lengths), pinned(token_codes), pinned(own), pinned(residuals))


def decode_kernel(step, passages, *refs):
    if step == 0:
        half_ref, own_ref, other_ref, codes, cleans, near, _, table = refs[:8]
    else:
        codes, cleans, near, table = refs[:4]
    embedded, rows, nothing, codes_smem, cleans_ref, sems = refs[-6:]
    slots = codes.shape[1]
    width = rows.shape[1]
    codes_ref = codes_smem.reshape(passages * slots)
    moves = []
    first, after = shares_of(passages)[step]
    first_move, after_move = first // 8 * 8, min(-(-after // 8) * 8, passages)
    part = pl.ds(first_move, after_move - first_move)
    pairs = ((cleans, cleans_ref), (codes.at[part], codes_smem.at[part]))
    for k, (source, to) in enumerate(pairs):
        moves.append(pltpu.make_async_copy(source, to, sems.at[k]))
        moves[-1].start()
    nothing[...] = jnp.zeros(nothing.shape, nothing.dtype)
    if step == 0:
        half_rows = other_ref.shape[0]
        piece = half_rows // PIECES
        for source, base in ((own_ref, half_ref[0]), (other_ref, 1 - half_ref[0])):
            for k in range(PIECES):
                to = pl.ds(pl.multiple_of(base * half_rows + k * piece, piece), piece)
                table[to, :] = source[pl.ds(k * piece, piece), :].astype(jnp.float32)

    table_single = table.reshape(table.shape[0], 1, width)
    rows_single = rows.reshape(rows.shape[0], 1, width)

    def fetch(g):
        for k in range(GROUP):
            at = cleans_ref[g * GROUP + k]
            for j in range(CHUNK):
                rows_single[k * CHUNK + j] = table_single[codes_ref[at + j]]

    def finish(g):
        size = GROUP * CHUNK
        return normalized(rows[...] + near[pl.ds(pl.multiple_of(g * size, size), size), :])

    def keep(g, done):
        size = GROUP * CHUNK
        embedded[pl.ds(pl.multiple_of(g * size, size), size), :] = done

    for move in moves:
        move.wait()
    last = cleans_ref.shape[0] - 1
    low = cleans_ref[last - STEPS + step - 1] if step > 0 else 0
    high = cleans_ref[last - STEPS + step]
    def decode(g, carry):
        done = finish(g - 1)
        fetch(g)
        keep(g - 1, done)
        return carry

    if step == 0:
        fetch(low)
    lax.fori_loop(low + (step == 0), high, decode, 0)
    if step == STEPS - 1:
        keep(high - 1, finish(high - 1))


def decode_step(
    step, half, own, other, codes, cleans, near, table, carried, held
):
    passages, slots = codes.shape
    width = near.shape[1]
    space = near.shape
    inside = lambda array: pinned(array, pltpu.VMEM)
    shared = [inside(codes), inside(cleans), inside(near)]
    if step == 0:
        operands = [half, inside(own), inside(other)] + shared + [inside(held)]
        in_specs = [SMEM] + [VMEM] * 6
        whole = (2 * own.shape[0], width)
        out_shape = [pltpu.VMEM(whole, jnp.float32)]
        aliases = {}
    else:
        operands = shared + [inside(table), inside(held)] + [inside(array) for array in carried]
        in_specs = [VMEM] * 7
        out_shape = []
        aliases = {5: 0, 6: 1}
    out_shape.append(pltpu.VMEM(space, jnp.bfloat16))
    out_shape.append(pltpu.VMEM((GROUP * CHUNK, width), jnp.float32))
    out_shape.append(pltpu.VMEM((16, width), jnp.bfloat16))
    results = pl.pallas_call(
        functools.partial(decode_kernel, step, passages),
        out_shape=tuple(out_shape),
        in_specs=in_specs,
        out_specs=(VMEM,) * len(out_shape),
        input_output_aliases=aliases,
        scratch_shapes=[
            pltpu.SMEM(codes.shape, jnp.int32),
            pltpu.SMEM(cleans.shape, jnp.int32),
            pltpu.SemaphoreType.DMA((2,)),
        ],
        compiler_params=granted(4),
        cost_estimate=pl.CostEstimate(flops=10**7, bytes_accessed=10**7, transcendentals=0),
        name="decode",
    )(*operands)
    if step == 0:
        table, results = results[0], results[1:]
    return table, results[:2], results[2]


def score_kernel(
    bit,
    token_count,
    local_queries,
    slots,
    me_ref,
    starts,
    queries_ref,
    embedded,
    before_ref,
    out_ref,
    at_ref,
    turned,
    largest,
    sem,
):
    starts_copy = pltpu.make_async_copy(starts, at_ref, sem)
    starts_copy.start()
    passages = out_ref.shape[1]
    query_tokens = queries_ref.shape[0]
    block = min(QUERY_BLOCK, query_tokens)
    blocks = query_tokens // block
    window = 2 * block // token_count
    window_targets = window // local_queries
    near_me = me_ref[0] & (window_targets - 1)
    far_me = quotient(me_ref[0], window_targets)
    owner = lax.broadcasted_iota(jnp.int32, (window, block), 0)
    owner_target = quotient(owner, local_queries)
    owner_row = (owner_target ^ near_me) * local_queries + owner - owner_target * local_queries
    query_of = quotient(lax.broadcasted_iota(jnp.int32, (window, block), 1), token_count)
    target_of = quotient(query_of, local_queries)
    row_of = query_of + (target_of + bit) * local_queries
    summing = jnp.concatenate([(owner_row == row_of).astype(jnp.bfloat16)] * 3, axis=1)
    count = SCORE_GROUP // SCORE_PARTS
    size = count * CHUNK

    def score_block(b, carry):
        at = pl.ds(pl.multiple_of(b * block, block), block)
        vectors = normalized(queries_ref[at, :].astype(jnp.float32))
        turned[...] = vectors.astype(jnp.float32).T.astype(jnp.bfloat16)

        def score(first, so_far):
            at = pl.ds(pl.multiple_of(first * size, size), size)
            similar = jnp.dot(embedded[at, :], turned[...], preferred_element_type=jnp.float32)
            parts = jnp.max(similar.reshape(count, CHUNK // 8, 8, block), axis=1)
            for k in range(count):
                start = at_ref[first * count + k]
                p = quotient(start, slots)
                so_far = jnp.where(start == p * slots, parts[k], jnp.maximum(so_far, parts[k]))
                to = pl.multiple_of(p * 8, 8)
                for lane in range(block // 128):
                    largest[lane, pl.ds(to, 8), :] = so_far[:, lane * 128 : (lane + 1) * 128]
            return so_far

        def score_parts(g, so_far):
            for part in range(SCORE_PARTS):
                so_far = score(g * SCORE_PARTS + part, so_far)
            return so_far

        @pl.when(b == 0)
        def arrived():
            starts_copy.wait()

        parts_used = quotient(at_ref[at_ref.shape[0] - 1] + count - 1, count)
        whole = quotient(parts_used, SCORE_PARTS)
        so_far = jnp.zeros((8, block), jnp.float32)
        so_far = lax.fori_loop(0, whole, score_parts, so_far)
        lax.fori_loop(whole * SCORE_PARTS, parts_used, score, so_far)
        kept = []
        for lane in range(block // 128):
            best = largest[lane, pl.ds(0, passages, stride=8), :]
            for k in range(1, 8):
                best = jnp.maximum(best, largest[lane, pl.ds(k, passages, stride=8), :])
            kept.append(best)
        left = jnp.concatenate(kept, axis=1)
        to = pl.ds(pl.multiple_of((b ^ far_me) * window, window), window)
        sums = lax.dot_general(
            summing,
            jnp.concatenate(thirds(left), axis=1),
            (((1,), (1,)), ((), ())),
            preferred_element_type=jnp.float32,
        )
        if bit:
            sums = sums + before_ref[to, :]
        out_ref[to, :] = sums
        return carry

    lax.fori_loop(0, blocks, score_block, 0)


def score_half(bit, me, starts, query_rows, embedded, before, passages, slots, shape):
    token_count, local_queries = shape
    query_tokens, width = query_rows.shape
    block = min(QUERY_BLOCK, query_tokens)
    blocks = query_tokens // block
    return pl.pallas_call(
        functools.partial(score_kernel, bit, token_count, local_queries, slots),
        out_shape=pltpu.VMEM((2 * query_tokens // token_count, passages), jnp.float32),
        in_specs=[SMEM] + [VMEM] * 4,
        out_specs=VMEM,
        scratch_shapes=[
            pltpu.SMEM(starts.shape, jnp.int32),
            pltpu.VMEM((width, block), jnp.bfloat16),
            pltpu.VMEM((block // 128, (passages + 1) * 8, 128), jnp.float32),
            pltpu.SemaphoreType.DMA,
        ],
        compiler_params=granted(4),
        cost_estimate=pl.CostEstimate(flops=10**7, bytes_accessed=8 * 10**6, transcendentals=0),
        name="score",
    )(
        me,
        pinned(starts, pltpu.VMEM),
        pinned(query_rows, pltpu.VMEM),
        pinned(embedded, pltpu.VMEM),
        pinned(before, pltpu.VMEM),
    )


def pick_kernel(passages, candidates_ref, returned_ref, out_ref):
    local_queries, count = candidates_ref.shape
    targets = returned_ref.shape[0]
    passage_numbers = lax.broadcasted_iota(jnp.int32, (passages, count), 0)
    target_numbers = lax.broadcasted_iota(jnp.int32, (targets, count), 0)
    for q in range(local_queries):
        wanted = candidates_ref[q : q + 1, :]
        target = quotient(wanted, passages)
        hits = (passage_numbers == wanted - target * passages).astype(jnp.bfloat16)
        left = returned_ref[:, q * passages : (q + 1) * passages]
        picked = jnp.dot(
            jnp.concatenate(thirds(left), axis=1),
            jnp.concatenate([hits] * 3, axis=0),
            preferred_element_type=jnp.float32,
        )
        kept = jnp.where(target_numbers == target, picked, 0.0)
        out_ref[q : q + 1, :] = jnp.sum(kept, axis=0, keepdims=True)


def pick(candidates, returned, passages):
    return pl.pallas_call(
        functools.partial(pick_kernel, passages),
        out_shape=jax.ShapeDtypeStruct(candidates.shape, jnp.float32),
        in_specs=[VMEM, VMEM],
        out_specs=VMEM,
        compiler_params=granted(8),
        name="pick",
    )(candidates, pltpu.with_memory_space_constraint(returned, pltpu.VMEM))


def body(queries, candidates, token_codes, residuals, lengths, centroids):
    local_queries, token_count, width = queries.shape
    targets = lax.axis_size("shard") * lax.axis_size("sub")
    passages, slots = token_codes.shape
    half = lax.axis_index("sub").astype(jnp.int32)
    me = lax.axis_index("shard").astype(jnp.int32) * lax.axis_size("sub") + half
    half = half.reshape(1)
    me = me.reshape(1)
    flat = residuals.reshape(passages * slots, width)
    other = lax.ppermute(centroids, "sub", [(0, 1), (1, 0)])

    held = queries.reshape(1, 1, local_queries * token_count, width)
    bits = targets.bit_length() - 1
    carried = None
    for turn, first in enumerate(range(bits - 1, -1, -1)):
        pairs = [(device, device ^ (1 << first)) for device in range(targets)]
        received = lax.ppermute(held, ("shard", "sub"), pairs)
        if turn == 0:
            ready = prepare(me, lengths, token_codes, centroids, flat)
            own, near, codes, starts, cleans, nothing = ready
            table = None
        elif turn <= STEPS:
            table, carried, nothing = decode_step(
                turn - 1, half, own, other, codes, cleans, near, table, carried, held
            )
        if first > 0:
            received = received + nothing[0:1, :]
            held = jnp.concatenate([held, received], axis=1)
            held = held.reshape((-1, 1) + held.shape[2:])
    shape = (token_count, local_queries)
    scores = carried[1]
    for bit, half_rows in enumerate((held, received)):
        rows = half_rows.reshape(targets // 2 * local_queries * token_count, width)
        scores = score_half(bit, me, starts, rows, carried[0], scores, passages, slots, shape)
    returned = lax.all_to_all(
        scores.reshape(targets, local_queries * passages),
        ("shard", "sub"),
        split_axis=0,
        concat_axis=0,
        tiled=True,
    )
    return pick(candidates, returned, passages)


def solution(mesh):
    placed = (
        P(("groups", "shard", "sub"), None, None),
        P(("groups", "shard", "sub"), None),
        P(("groups", "shard", "sub"), None),
        P(("groups", "shard", "sub"), None, None),
        P(("groups", "shard", "sub")),
        P(("groups", "shard", "sub"), None),
    )
    return jax.shard_map(
        body,
        mesh=mesh,
        in_specs=placed,
        out_specs=P(("groups", "shard", "sub"), None),
        check_vma=False,
    )
```

```python
import functools

import jax
import jax.numpy as jnp
from jax import lax
from jax.experimental import pallas as pl
from jax.experimental.pallas import tpu as pltpu
from jax.sharding import PartitionSpec as P

CHUNK = 16
GROUP = 16
SCORE_GROUP = 64
SCORE_PARTS = 2
SCORE_RUNS = (4, 2, 1)
STEPS = 2
PIECES = 4
QUERY_BLOCK = 512
SMEM = pl.BlockSpec(memory_space=pltpu.SMEM)
VMEM = pl.BlockSpec(memory_space=pltpu.VMEM)
HBM = pl.BlockSpec(memory_space=pltpu.HBM)


def normalized(vectors):
    total = jnp.sum(vectors * vectors, axis=-1, keepdims=True)
    return (vectors * lax.rsqrt(total + 1e-06)).astype(jnp.bfloat16)


def thirds(values):
    parts = []
    for _ in range(3):
        parts.append(values.astype(jnp.bfloat16))
        values = values - parts[-1].astype(jnp.float32)
    return parts


def quotient(number, divisor):
    if divisor & (divisor - 1) == 0:
        return lax.shift_right_logical(number, divisor.bit_length() - 1)
    return lax.div(number, divisor)


def pinned(array, space=pltpu.HBM):
    return pltpu.with_memory_space_constraint(array, space)


def granted(mebibytes):
    return pltpu.CompilerParams(vmem_limit_bytes=mebibytes * 1024 * 1024)


def shares_of(passages):
    edges = [0, passages // 2]
    return tuple(zip(edges, edges[1:] + [passages]))


def prepare_kernel(
    me_ref,
    lengths_hbm,
    codes_hbm,
    own_hbm,
    residuals_hbm,
    staged,
    near,
    codes,
    starts,
    cleans,
    nothing,
    lengths_ref,
    starts_ref,
    cleans_ref,
    length_rows,
    drawn,
    residuals,
    sems,
):
    del me_ref
    passages, slots = codes_hbm.shape
    width = own_hbm.shape[1]
    lengths_copy = pltpu.make_async_copy(lengths_hbm, lengths_ref, sems.at[0])
    codes_copy = pltpu.make_async_copy(codes_hbm, drawn, sems.at[1])
    residual_copy = pltpu.make_async_copy(residuals_hbm, residuals, sems.at[2])
    own_copy = pltpu.make_async_copy(own_hbm, staged, sems.at[3])
    lengths_copy.start()
    codes_copy.start()
    residual_copy.start()
    own_copy.start()
    nothing[...] = jnp.zeros(nothing.shape, nothing.dtype)
    lengths_copy.wait()

    def listing(p, chunks):
        length = lengths_ref[p]
        length_rows[pl.ds(p, 1), :] = jnp.full((1, slots), length, jnp.int32)
        for k in range(slots // CHUNK):
            starts_ref[chunks + k] = p * slots + k * CHUNK
            cleans_ref[chunks + k] = p * slots + k * CHUNK
        return chunks + quotient(length + CHUNK - 1, CHUNK)

    last = starts_ref.shape[0] - 1
    chunks = jnp.int32(0)
    for step, (low, high) in enumerate(shares_of(passages)):
        chunks = lax.fori_loop(low, high, listing, chunks, unroll=4)
        for k in range(GROUP):
            starts_ref[chunks + k] = passages * slots
            cleans_ref[chunks + k] = low * slots
        chunks = quotient(chunks + GROUP - 1, GROUP) * GROUP
        cleans_ref[last - STEPS + step] = quotient(chunks, GROUP)
    for k in range(SCORE_GROUP):
        starts_ref[chunks + k] = passages * slots
    starts_ref[last] = chunks
    starts_copy = pltpu.make_async_copy(starts_ref, starts, sems.at[4])
    cleans_copy = pltpu.make_async_copy(cleans_ref, cleans, sems.at[5])
    starts_copy.start()
    cleans_copy.start()
    codes_copy.wait()
    lanes = lax.broadcasted_iota(jnp.int32, (passages, slots), 1)
    codes[...] = jnp.where(lanes < length_rows[...], drawn[...], drawn[:, 0:1])
    residual_copy.wait()
    slot_numbers = lax.broadcasted_iota(jnp.int32, (CHUNK, width), 0)

    def place(g, carry):
        for k in range(GROUP):
            at = cleans_ref[g * GROUP + k]
            p = quotient(at, slots)
            live = lengths_ref[p] - (at - p * slots)
            first = residuals[pl.ds(pl.multiple_of(p * slots, CHUNK), CHUNK), :]
            rows = residuals[pl.ds(pl.multiple_of(at, CHUNK), CHUNK), :].astype(jnp.float32)
            rows = jnp.where(slot_numbers < live, rows, first.astype(jnp.float32)[0:1, :])
            to = pl.multiple_of((g * GROUP + k) * CHUNK, CHUNK)
            near[pl.ds(to, CHUNK), :] = rows
        return carry

    lax.fori_loop(0, quotient(chunks, GROUP), place, 0)
    own_copy.wait()
    starts_copy.wait()
    cleans_copy.wait()


def list_size(passages, slots):
    most = passages * (slots // CHUNK) + STEPS * GROUP + SCORE_GROUP + STEPS + 1
    return -(-most // 128) * 128


def list_rows(passages, slots):
    rounding = SCORE_GROUP * CHUNK
    return -(-(passages * slots + STEPS * GROUP * CHUNK) // rounding) * rounding


def prepare(me, lengths, token_codes, own, residuals):
    width = own.shape[1]
    passages, slots = token_codes.shape
    most = list_size(passages, slots)
    return pl.pallas_call(
        prepare_kernel,
        out_shape=(
            pltpu.VMEM(own.shape, jnp.bfloat16),
            pltpu.VMEM((list_rows(passages, slots), width), jnp.float32),
            pltpu.VMEM(token_codes.shape, jnp.int32),
            pltpu.VMEM((most,), jnp.int32),
            pltpu.VMEM((most,), jnp.int32),
            pltpu.VMEM((16, width), jnp.bfloat16),
        ),
        in_specs=[SMEM, HBM, HBM, HBM, HBM],
        out_specs=(VMEM,) * 6,
        scratch_shapes=[
            pltpu.SMEM(lengths.shape, jnp.int32),
            pltpu.SMEM((most,), jnp.int32),
            pltpu.SMEM((most,), jnp.int32),
            pltpu.VMEM(token_codes.shape, jnp.int32),
            pltpu.VMEM(token_codes.shape, jnp.int32),
            pltpu.VMEM(residuals.shape, jnp.bfloat16),
            pltpu.SemaphoreType.DMA((6,)),
        ],
        compiler_params=granted(4),
        cost_estimate=pl.CostEstimate(flops=10**7, bytes_accessed=8 * 10**6, transcendentals=0),
        name="prepare",
    )(me, pinned(lengths), pinned(token_codes), pinned(own), pinned(residuals))


def decode_kernel(step, passages, *refs):
    if step == 0:
        half_ref, own_ref, other_ref, codes, cleans, near, _, table = refs[:8]
    else:
        codes, cleans, near, table = refs[:4]
    embedded, rows, nothing, codes_smem, cleans_ref, sems = refs[-6:]
    slots = codes.shape[1]
    width = rows.shape[1]
    codes_ref = codes_smem.reshape(passages * slots)
    moves = []
    first, after = shares_of(passages)[step]
    first_move, after_move = first // 8 * 8, min(-(-after // 8) * 8, passages)
    part = pl.ds(first_move, after_move - first_move)
    pairs = ((cleans, cleans_ref), (codes.at[part], codes_smem.at[part]))
    for k, (source, to) in enumerate(pairs):
        moves.append(pltpu.make_async_copy(source, to, sems.at[k]))
        moves[-1].start()
    nothing[...] = jnp.zeros(nothing.shape, nothing.dtype)
    if step == 0:
        half_rows = other_ref.shape[0]
        piece = half_rows // PIECES
        for source, base in ((own_ref, half_ref[0]), (other_ref, 1 - half_ref[0])):
            for k in range(PIECES):
                to = pl.ds(pl.multiple_of(base * half_rows + k * piece, piece), piece)
                table[to, :] = source[pl.ds(k * piece, piece), :].astype(jnp.float32)

    table_single = table.reshape(table.shape[0], 1, width)
    rows_single = rows.reshape(rows.shape[0], 1, width)

    def fetch(g):
        for k in range(GROUP):
            at = cleans_ref[g * GROUP + k]
            for j in range(CHUNK):
                rows_single[k * CHUNK + j] = table_single[codes_ref[at + j]]

    def finish(g):
        size = GROUP * CHUNK
        return normalized(rows[...] + near[pl.ds(pl.multiple_of(g * size, size), size), :])

    def keep(g, done):
        size = GROUP * CHUNK
        embedded[pl.ds(pl.multiple_of(g * size, size), size), :] = done

    for move in moves:
        move.wait()
    last = cleans_ref.shape[0] - 1
    low = cleans_ref[last - STEPS + step - 1] if step > 0 else 0
    high = cleans_ref[last - STEPS + step]
    def decode(g, carry):
        done = finish(g - 1)
        fetch(g)
        keep(g - 1, done)
        return carry

    if step == 0:
        fetch(low)
    lax.fori_loop(low + (step == 0), high, decode, 0)
    if step == STEPS - 1:
        keep(high - 1, finish(high - 1))


def decode_step(
    step, half, own, other, codes, cleans, near, table, carried, held
):
    passages, slots = codes.shape
    width = near.shape[1]
    space = near.shape
    inside = lambda array: pinned(array, pltpu.VMEM)
    shared = [inside(codes), inside(cleans), inside(near)]
    if step == 0:
        operands = [half, inside(own), inside(other)] + shared + [inside(held)]
        in_specs = [SMEM] + [VMEM] * 6
        whole = (2 * own.shape[0], width)
        out_shape = [pltpu.VMEM(whole, jnp.float32)]
        aliases = {}
    else:
        operands = shared + [inside(table), inside(held)] + [inside(array) for array in carried]
        in_specs = [VMEM] * 7
        out_shape = []
        aliases = {5: 0, 6: 1}
    out_shape.append(pltpu.VMEM(space, jnp.bfloat16))
    out_shape.append(pltpu.VMEM((GROUP * CHUNK, width), jnp.float32))
    out_shape.append(pltpu.VMEM((16, width), jnp.bfloat16))
    results = pl.pallas_call(
        functools.partial(decode_kernel, step, passages),
        out_shape=tuple(out_shape),
        in_specs=in_specs,
        out_specs=(VMEM,) * len(out_shape),
        input_output_aliases=aliases,
        scratch_shapes=[
            pltpu.SMEM(codes.shape, jnp.int32),
            pltpu.SMEM(cleans.shape, jnp.int32),
            pltpu.SemaphoreType.DMA((2,)),
        ],
        compiler_params=granted(4),
        cost_estimate=pl.CostEstimate(flops=10**7, bytes_accessed=10**7, transcendentals=0),
        name="decode",
    )(*operands)
    if step == 0:
        table, results = results[0], results[1:]
    return table, results[:2], results[2]


def score_kernel(
    bit,
    token_count,
    local_queries,
    slots,
    me_ref,
    starts,
    queries_ref,
    embedded,
    before_ref,
    out_ref,
    at_ref,
    turned,
    largest,
    sem,
):
    starts_copy = pltpu.make_async_copy(starts, at_ref, sem)
    starts_copy.start()
    passages = out_ref.shape[1]
    query_tokens = queries_ref.shape[0]
    block = min(QUERY_BLOCK, query_tokens)
    blocks = query_tokens // block
    window = 2 * block // token_count
    window_targets = window // local_queries
    near_me = me_ref[0] & (window_targets - 1)
    far_me = quotient(me_ref[0], window_targets)
    owner = lax.broadcasted_iota(jnp.int32, (window, block), 0)
    owner_target = quotient(owner, local_queries)
    owner_row = (owner_target ^ near_me) * local_queries + owner - owner_target * local_queries
    query_of = quotient(lax.broadcasted_iota(jnp.int32, (window, block), 1), token_count)
    target_of = quotient(query_of, local_queries)
    row_of = query_of + (target_of + bit) * local_queries
    summing = jnp.concatenate([(owner_row == row_of).astype(jnp.bfloat16)] * 3, axis=1)
    count = SCORE_GROUP // SCORE_PARTS
    size = count * CHUNK

    def score_block(b, carry):
        at = pl.ds(pl.multiple_of(b * block, block), block)
        vectors = normalized(queries_ref[at, :].astype(jnp.float32))
        turned[...] = vectors.astype(jnp.float32).T.astype(jnp.bfloat16)

        def score(first, so_far):
            at = pl.ds(pl.multiple_of(first * size, size), size)
            similar = jnp.dot(embedded[at, :], turned[...], preferred_element_type=jnp.float32)
            parts = jnp.max(similar.reshape(count, CHUNK // 8, 8, block), axis=1)
            for k in range(count):
                start = at_ref[first * count + k]
                p = quotient(start, slots)
                so_far = jnp.where(start == p * slots, parts[k], jnp.maximum(so_far, parts[k]))
                to = pl.multiple_of(p * 8, 8)
                for lane in range(block // 128):
                    largest[lane, pl.ds(to, 8), :] = so_far[:, lane * 128 : (lane + 1) * 128]
            return so_far

        @pl.when(b == 0)
        def arrived():
            starts_copy.wait()

        parts_used = quotient(at_ref[at_ref.shape[0] - 1] + count - 1, count)
        so_far = jnp.zeros((8, block), jnp.float32)
        done = jnp.int32(0)
        for run in SCORE_RUNS:

            def score_run(g, so_far, run=run, done=done):
                for part in range(run):
                    so_far = score(done + g * run + part, so_far)
                return so_far

            runs = quotient(parts_used - done, run)
            so_far = lax.fori_loop(0, runs, score_run, so_far)
            done = done + runs * run
        kept = []
        for lane in range(block // 128):
            best = largest[lane, pl.ds(0, passages, stride=8), :]
            for k in range(1, 8):
                best = jnp.maximum(best, largest[lane, pl.ds(k, passages, stride=8), :])
            kept.append(best)
        left = jnp.concatenate(kept, axis=1)
        to = pl.ds(pl.multiple_of((b ^ far_me) * window, window), window)
        sums = lax.dot_general(
            summing,
            jnp.concatenate(thirds(left), axis=1),
            (((1,), (1,)), ((), ())),
            preferred_element_type=jnp.float32,
        )
        if bit:
            sums = sums + before_ref[to, :]
        out_ref[to, :] = sums
        return carry

    lax.fori_loop(0, blocks, score_block, 0)


def score_half(bit, me, starts, query_rows, embedded, before, passages, slots, shape):
    token_count, local_queries = shape
    query_tokens, width = query_rows.shape
    block = min(QUERY_BLOCK, query_tokens)
    blocks = query_tokens // block
    return pl.pallas_call(
        functools.partial(score_kernel, bit, token_count, local_queries, slots),
        out_shape=pltpu.VMEM((2 * query_tokens // token_count, passages), jnp.float32),
        in_specs=[SMEM] + [VMEM] * 4,
        out_specs=VMEM,
        scratch_shapes=[
            pltpu.SMEM(starts.shape, jnp.int32),
            pltpu.VMEM((width, block), jnp.bfloat16),
            pltpu.VMEM((block // 128, (passages + 1) * 8, 128), jnp.float32),
            pltpu.SemaphoreType.DMA,
        ],
        compiler_params=granted(4),
        cost_estimate=pl.CostEstimate(flops=10**7, bytes_accessed=8 * 10**6, transcendentals=0),
        name="score",
    )(
        me,
        pinned(starts, pltpu.VMEM),
        pinned(query_rows, pltpu.VMEM),
        pinned(embedded, pltpu.VMEM),
        pinned(before, pltpu.VMEM),
    )


def pick_kernel(passages, candidates_ref, returned_ref, out_ref):
    local_queries, count = candidates_ref.shape
    targets = returned_ref.shape[0]
    passage_numbers = lax.broadcasted_iota(jnp.int32, (passages, count), 0)
    target_numbers = lax.broadcasted_iota(jnp.int32, (targets, count), 0)
    for q in range(local_queries):
        wanted = candidates_ref[q : q + 1, :]
        target = quotient(wanted, passages)
        hits = (passage_numbers == wanted - target * passages).astype(jnp.bfloat16)
        left = returned_ref[:, q * passages : (q + 1) * passages]
        picked = jnp.zeros((targets, count), jnp.float32)
        for part in thirds(left):
            picked = picked + jnp.dot(part, hits, preferred_element_type=jnp.float32)
        kept = jnp.where(target_numbers == target, picked, 0.0)
        out_ref[q : q + 1, :] = jnp.sum(kept, axis=0, keepdims=True)


def pick(candidates, returned, passages):
    return pl.pallas_call(
        functools.partial(pick_kernel, passages),
        out_shape=jax.ShapeDtypeStruct(candidates.shape, jnp.float32),
        in_specs=[VMEM, VMEM],
        out_specs=VMEM,
        compiler_params=granted(8),
        name="pick",
    )(candidates, pltpu.with_memory_space_constraint(returned, pltpu.VMEM))


def body(queries, candidates, token_codes, residuals, lengths, centroids):
    local_queries, token_count, width = queries.shape
    targets = lax.axis_size("shard") * lax.axis_size("sub")
    passages, slots = token_codes.shape
    half = lax.axis_index("sub").astype(jnp.int32)
    me = lax.axis_index("shard").astype(jnp.int32) * lax.axis_size("sub") + half
    half = half.reshape(1)
    me = me.reshape(1)
    flat = residuals.reshape(passages * slots, width)
    other = lax.ppermute(centroids, "sub", [(0, 1), (1, 0)])

    held = queries.reshape(1, 1, local_queries * token_count, width)
    bits = targets.bit_length() - 1
    carried = None
    for turn, first in enumerate(range(bits - 1, -1, -1)):
        pairs = [(device, device ^ (1 << first)) for device in range(targets)]
        received = lax.ppermute(held, ("shard", "sub"), pairs)
        if turn == 0:
            ready = prepare(me, lengths, token_codes, centroids, flat)
            own, near, codes, starts, cleans, nothing = ready
            table = None
        elif turn <= STEPS:
            table, carried, nothing = decode_step(
                turn - 1, half, own, other, codes, cleans, near, table, carried, held
            )
        if first > 0:
            received = received + nothing[0:1, :]
            held = jnp.concatenate([held, received], axis=1)
            held = held.reshape((-1, 1) + held.shape[2:])
    shape = (token_count, local_queries)
    scores = carried[1]
    for bit, half_rows in enumerate((held, received)):
        rows = half_rows.reshape(targets // 2 * local_queries * token_count, width)
        scores = score_half(bit, me, starts, rows, carried[0], scores, passages, slots, shape)
    returned = lax.all_to_all(
        scores.reshape(targets, local_queries * passages),
        ("shard", "sub"),
        split_axis=0,
        concat_axis=0,
        tiled=True,
    )
    return pick(candidates, returned, passages)


def solution(mesh):
    placed = (
        P(("groups", "shard", "sub"), None, None),
        P(("groups", "shard", "sub"), None),
        P(("groups", "shard", "sub"), None),
        P(("groups", "shard", "sub"), None, None),
        P(("groups", "shard", "sub")),
        P(("groups", "shard", "sub"), None),
    )
    return jax.shard_map(
        body,
        mesh=mesh,
        in_specs=placed,
        out_specs=P(("groups", "shard", "sub"), None),
        check_vma=False,
    )
```

```python
import functools

import jax
import jax.numpy as jnp
from jax import lax
from jax.experimental import pallas as pl
from jax.experimental.pallas import tpu as pltpu
from jax.sharding import PartitionSpec as P

CHUNK = 16
GROUP = 16
SCORE_GROUP = 64
SCORE_PARTS = 2
SCORE_RUNS = (4, 2, 1)
WIDE_BITS = 2
STEPS = 2
PIECES = 4
QUERY_BLOCK = 512
SMEM = pl.BlockSpec(memory_space=pltpu.SMEM)
VMEM = pl.BlockSpec(memory_space=pltpu.VMEM)
HBM = pl.BlockSpec(memory_space=pltpu.HBM)


def normalized(vectors):
    total = jnp.sum(vectors * vectors, axis=-1, keepdims=True)
    return (vectors * lax.rsqrt(total + 1e-06)).astype(jnp.bfloat16)


def thirds(values):
    parts = []
    for _ in range(3):
        parts.append(values.astype(jnp.bfloat16))
        values = values - parts[-1].astype(jnp.float32)
    return parts


def quotient(number, divisor):
    if divisor & (divisor - 1) == 0:
        return lax.shift_right_logical(number, divisor.bit_length() - 1)
    return lax.div(number, divisor)


def pinned(array, space=pltpu.HBM):
    return pltpu.with_memory_space_constraint(array, space)


def granted(mebibytes):
    return pltpu.CompilerParams(vmem_limit_bytes=mebibytes * 1024 * 1024)


def shares_of(passages):
    edges = [0, passages // 2]
    return tuple(zip(edges, edges[1:] + [passages]))


def prepare_kernel(
    me_ref,
    lengths_hbm,
    codes_hbm,
    own_hbm,
    residuals_hbm,
    staged,
    near,
    codes,
    starts,
    cleans,
    nothing,
    lengths_ref,
    starts_ref,
    cleans_ref,
    length_rows,
    drawn,
    residuals,
    sems,
):
    del me_ref
    passages, slots = codes_hbm.shape
    width = own_hbm.shape[1]
    lengths_copy = pltpu.make_async_copy(lengths_hbm, lengths_ref, sems.at[0])
    codes_copy = pltpu.make_async_copy(codes_hbm, drawn, sems.at[1])
    residual_copy = pltpu.make_async_copy(residuals_hbm, residuals, sems.at[2])
    own_copy = pltpu.make_async_copy(own_hbm, staged, sems.at[3])
    lengths_copy.start()
    codes_copy.start()
    residual_copy.start()
    own_copy.start()
    nothing[...] = jnp.zeros(nothing.shape, nothing.dtype)
    lengths_copy.wait()

    def listing(p, chunks):
        length = lengths_ref[p]
        length_rows[pl.ds(p, 1), :] = jnp.full((1, slots), length, jnp.int32)
        for k in range(slots // CHUNK):
            starts_ref[chunks + k] = p * slots + k * CHUNK
            cleans_ref[chunks + k] = p * slots + k * CHUNK
        return chunks + quotient(length + CHUNK - 1, CHUNK)

    last = starts_ref.shape[0] - 1
    chunks = jnp.int32(0)
    for step, (low, high) in enumerate(shares_of(passages)):
        chunks = lax.fori_loop(low, high, listing, chunks, unroll=4)
        for k in range(GROUP):
            starts_ref[chunks + k] = passages * slots
            cleans_ref[chunks + k] = low * slots
        chunks = quotient(chunks + GROUP - 1, GROUP) * GROUP
        cleans_ref[last - STEPS + step] = quotient(chunks, GROUP)
    for k in range(SCORE_GROUP):
        starts_ref[chunks + k] = passages * slots
    starts_ref[last] = chunks
    starts_copy = pltpu.make_async_copy(starts_ref, starts, sems.at[4])
    cleans_copy = pltpu.make_async_copy(cleans_ref, cleans, sems.at[5])
    starts_copy.start()
    cleans_copy.start()
    codes_copy.wait()
    lanes = lax.broadcasted_iota(jnp.int32, (passages, slots), 1)
    codes[...] = jnp.where(lanes < length_rows[...], drawn[...], drawn[:, 0:1])
    residual_copy.wait()
    slot_numbers = lax.broadcasted_iota(jnp.int32, (CHUNK, width), 0)

    def place(g, carry):
        for k in range(GROUP):
            at = cleans_ref[g * GROUP + k]
            p = quotient(at, slots)
            live = lengths_ref[p] - (at - p * slots)
            first = residuals[pl.ds(pl.multiple_of(p * slots, CHUNK), CHUNK), :]
            rows = residuals[pl.ds(pl.multiple_of(at, CHUNK), CHUNK), :].astype(jnp.float32)
            rows = jnp.where(slot_numbers < live, rows, first.astype(jnp.float32)[0:1, :])
            to = pl.multiple_of((g * GROUP + k) * CHUNK, CHUNK)
            near[pl.ds(to, CHUNK), :] = rows
        return carry

    lax.fori_loop(0, quotient(chunks, GROUP), place, 0)
    own_copy.wait()
    starts_copy.wait()
    cleans_copy.wait()


def list_size(passages, slots):
    most = passages * (slots // CHUNK) + STEPS * GROUP + SCORE_GROUP + STEPS + 1
    return -(-most // 128) * 128


def list_rows(passages, slots):
    rounding = SCORE_GROUP * CHUNK
    return -(-(passages * slots + STEPS * GROUP * CHUNK) // rounding) * rounding


def prepare(me, lengths, token_codes, own, residuals):
    width = own.shape[1]
    passages, slots = token_codes.shape
    most = list_size(passages, slots)
    return pl.pallas_call(
        prepare_kernel,
        out_shape=(
            pltpu.VMEM(own.shape, jnp.bfloat16),
            pltpu.VMEM((list_rows(passages, slots), width), jnp.float32),
            pltpu.VMEM(token_codes.shape, jnp.int32),
            pltpu.VMEM((most,), jnp.int32),
            pltpu.VMEM((most,), jnp.int32),
            pltpu.VMEM((16, width), jnp.bfloat16),
        ),
        in_specs=[SMEM, HBM, HBM, HBM, HBM],
        out_specs=(VMEM,) * 6,
        scratch_shapes=[
            pltpu.SMEM(lengths.shape, jnp.int32),
            pltpu.SMEM((most,), jnp.int32),
            pltpu.SMEM((most,), jnp.int32),
            pltpu.VMEM(token_codes.shape, jnp.int32),
            pltpu.VMEM(token_codes.shape, jnp.int32),
            pltpu.VMEM(residuals.shape, jnp.bfloat16),
            pltpu.SemaphoreType.DMA((6,)),
        ],
        compiler_params=granted(4),
        cost_estimate=pl.CostEstimate(flops=10**7, bytes_accessed=8 * 10**6, transcendentals=0),
        name="prepare",
    )(me, pinned(lengths), pinned(token_codes), pinned(own), pinned(residuals))


def decode_kernel(step, passages, *refs):
    if step == 0:
        half_ref, own_ref, other_ref, codes, cleans, near, _, table = refs[:8]
    else:
        codes, cleans, near, table = refs[:4]
    embedded, rows, nothing, codes_smem, cleans_ref, sems = refs[-6:]
    slots = codes.shape[1]
    width = rows.shape[1]
    codes_ref = codes_smem.reshape(passages * slots)
    moves = []
    first, after = shares_of(passages)[step]
    first_move, after_move = first // 8 * 8, min(-(-after // 8) * 8, passages)
    part = pl.ds(first_move, after_move - first_move)
    pairs = ((cleans, cleans_ref), (codes.at[part], codes_smem.at[part]))
    for k, (source, to) in enumerate(pairs):
        moves.append(pltpu.make_async_copy(source, to, sems.at[k]))
        moves[-1].start()
    nothing[...] = jnp.zeros(nothing.shape, nothing.dtype)
    if step == 0:
        half_rows = other_ref.shape[0]
        piece = half_rows // PIECES
        for source, base in ((own_ref, half_ref[0]), (other_ref, 1 - half_ref[0])):
            for k in range(PIECES):
                to = pl.ds(pl.multiple_of(base * half_rows + k * piece, piece), piece)
                table[to, :] = source[pl.ds(k * piece, piece), :].astype(jnp.float32)

    table_single = table.reshape(table.shape[0], 1, width)
    rows_single = rows.reshape(rows.shape[0], 1, width)

    def fetch(g):
        for k in range(GROUP):
            at = cleans_ref[g * GROUP + k]
            for j in range(CHUNK):
                rows_single[k * CHUNK + j] = table_single[codes_ref[at + j]]

    def finish(g):
        size = GROUP * CHUNK
        return normalized(rows[...] + near[pl.ds(pl.multiple_of(g * size, size), size), :])

    def keep(g, done):
        size = GROUP * CHUNK
        embedded[pl.ds(pl.multiple_of(g * size, size), size), :] = done

    for move in moves:
        move.wait()
    last = cleans_ref.shape[0] - 1
    low = cleans_ref[last - STEPS + step - 1] if step > 0 else 0
    high = cleans_ref[last - STEPS + step]
    def decode(g, carry):
        done = finish(g - 1)
        fetch(g)
        keep(g - 1, done)
        return carry

    if step == 0:
        fetch(low)
    lax.fori_loop(low + (step == 0), high, decode, 0)
    if step == STEPS - 1:
        keep(high - 1, finish(high - 1))


def decode_step(
    step, half, own, other, codes, cleans, near, table, carried, held
):
    passages, slots = codes.shape
    width = near.shape[1]
    space = near.shape
    inside = lambda array: pinned(array, pltpu.VMEM)
    shared = [inside(codes), inside(cleans), inside(near)]
    if step == 0:
        operands = [half, inside(own), inside(other)] + shared + [inside(held)]
        in_specs = [SMEM] + [VMEM] * 6
        whole = (2 * own.shape[0], width)
        out_shape = [pltpu.VMEM(whole, jnp.float32)]
        aliases = {}
    else:
        operands = shared + [inside(table), inside(held)] + [inside(array) for array in carried]
        in_specs = [VMEM] * 7
        out_shape = []
        aliases = {5: 0, 6: 1}
    out_shape.append(pltpu.VMEM(space, jnp.bfloat16))
    out_shape.append(pltpu.VMEM((GROUP * CHUNK, width), jnp.float32))
    out_shape.append(pltpu.VMEM((16, width), jnp.bfloat16))
    results = pl.pallas_call(
        functools.partial(decode_kernel, step, passages),
        out_shape=tuple(out_shape),
        in_specs=in_specs,
        out_specs=(VMEM,) * len(out_shape),
        input_output_aliases=aliases,
        scratch_shapes=[
            pltpu.SMEM(codes.shape, jnp.int32),
            pltpu.SMEM(cleans.shape, jnp.int32),
            pltpu.SemaphoreType.DMA((2,)),
        ],
        compiler_params=granted(4),
        cost_estimate=pl.CostEstimate(flops=10**7, bytes_accessed=10**7, transcendentals=0),
        name="decode",
    )(*operands)
    if step == 0:
        table, results = results[0], results[1:]
    return table, results[:2], results[2]


def score_kernel(
    token_count,
    local_queries,
    slots,
    me_ref,
    starts,
    queries_ref,
    embedded,
    out_ref,
    at_ref,
    turned,
    largest,
    sem,
):
    starts_copy = pltpu.make_async_copy(starts, at_ref, sem)
    starts_copy.start()
    passages = out_ref.shape[1]
    query_tokens = queries_ref.shape[0]
    block = min(QUERY_BLOCK, query_tokens)
    blocks = query_tokens // block
    window = block // token_count
    window_targets = window // local_queries
    near_me = me_ref[0] & (window_targets - 1)
    far_me = quotient(me_ref[0], window_targets)
    owner = lax.broadcasted_iota(jnp.int32, (window, block), 0)
    owner_target = quotient(owner, local_queries)
    owner_row = (owner_target ^ near_me) * local_queries + owner - owner_target * local_queries
    query_of = quotient(lax.broadcasted_iota(jnp.int32, (window, block), 1), token_count)
    summing = jnp.concatenate([(owner_row == query_of).astype(jnp.bfloat16)] * 3, axis=1)
    count = SCORE_GROUP // SCORE_PARTS
    size = count * CHUNK

    def score_block(b, carry):
        at = pl.ds(pl.multiple_of(b * block, block), block)
        vectors = normalized(queries_ref[at, :].astype(jnp.float32))
        turned[...] = vectors.astype(jnp.float32).T.astype(jnp.bfloat16)

        def score(first, so_far):
            at = pl.ds(pl.multiple_of(first * size, size), size)
            similar = jnp.dot(embedded[at, :], turned[...], preferred_element_type=jnp.float32)
            parts = jnp.max(similar.reshape(count, CHUNK // 8, 8, block), axis=1)
            for k in range(count):
                start = at_ref[first * count + k]
                p = quotient(start, slots)
                so_far = jnp.where(start == p * slots, parts[k], jnp.maximum(so_far, parts[k]))
                to = pl.multiple_of(p * 8, 8)
                for lane in range(block // 128):
                    largest[lane, pl.ds(to, 8), :] = so_far[:, lane * 128 : (lane + 1) * 128]
            return so_far

        @pl.when(b == 0)
        def arrived():
            starts_copy.wait()

        parts_used = quotient(at_ref[at_ref.shape[0] - 1] + count - 1, count)
        so_far = jnp.zeros((8, block), jnp.float32)
        done = jnp.int32(0)
        for run in SCORE_RUNS:

            def score_run(g, so_far, run=run, done=done):
                for part in range(run):
                    so_far = score(done + g * run + part, so_far)
                return so_far

            runs = quotient(parts_used - done, run)
            so_far = lax.fori_loop(0, runs, score_run, so_far)
            done = done + runs * run
        kept = []
        for lane in range(block // 128):
            best = largest[lane, pl.ds(0, passages, stride=8), :]
            for k in range(1, 8):
                best = jnp.maximum(best, largest[lane, pl.ds(k, passages, stride=8), :])
            kept.append(best)
        left = jnp.concatenate(kept, axis=1)
        to = pl.ds(pl.multiple_of((b ^ far_me) * window, window), window)
        sums = lax.dot_general(
            summing,
            jnp.concatenate(thirds(left), axis=1),
            (((1,), (1,)), ((), ())),
            preferred_element_type=jnp.float32,
        )
        out_ref[to, :] = sums
        return carry

    lax.fori_loop(0, blocks, score_block, 0)


def score_all(me, starts, query_rows, embedded, passages, slots, shape):
    token_count, local_queries = shape
    query_tokens, width = query_rows.shape
    block = min(QUERY_BLOCK, query_tokens)
    blocks = query_tokens // block
    return pl.pallas_call(
        functools.partial(score_kernel, token_count, local_queries, slots),
        out_shape=pltpu.VMEM((query_tokens // token_count, passages), jnp.float32),
        in_specs=[SMEM] + [VMEM] * 3,
        out_specs=VMEM,
        scratch_shapes=[
            pltpu.SMEM(starts.shape, jnp.int32),
            pltpu.VMEM((width, block), jnp.bfloat16),
            pltpu.VMEM((block // 128, (passages + 1) * 8, 128), jnp.float32),
            pltpu.SemaphoreType.DMA,
        ],
        compiler_params=granted(4),
        cost_estimate=pl.CostEstimate(flops=10**7, bytes_accessed=8 * 10**6, transcendentals=0),
        name="score",
    )(
        me,
        pinned(starts, pltpu.VMEM),
        pinned(query_rows, pltpu.VMEM),
        pinned(embedded, pltpu.VMEM),
    )


def pick_kernel(passages, candidates_ref, returned_ref, out_ref):
    local_queries, count = candidates_ref.shape
    targets = returned_ref.shape[0]
    passage_numbers = lax.broadcasted_iota(jnp.int32, (passages, count), 0)
    target_numbers = lax.broadcasted_iota(jnp.int32, (targets, count), 0)
    for q in range(local_queries):
        wanted = candidates_ref[q : q + 1, :]
        target = quotient(wanted, passages)
        hits = (passage_numbers == wanted - target * passages).astype(jnp.bfloat16)
        left = returned_ref[:, q * passages : (q + 1) * passages]
        picked = jnp.zeros((targets, count), jnp.float32)
        for part in thirds(left):
            picked = picked + jnp.dot(part, hits, preferred_element_type=jnp.float32)
        kept = jnp.where(target_numbers == target, picked, 0.0)
        out_ref[q : q + 1, :] = jnp.sum(kept, axis=0, keepdims=True)


def pick(candidates, returned, passages):
    return pl.pallas_call(
        functools.partial(pick_kernel, passages),
        out_shape=jax.ShapeDtypeStruct(candidates.shape, jnp.float32),
        in_specs=[VMEM, VMEM],
        out_specs=VMEM,
        compiler_params=granted(8),
        name="pick",
    )(candidates, pltpu.with_memory_space_constraint(returned, pltpu.VMEM))


def body(queries, candidates, token_codes, residuals, lengths, centroids):
    local_queries, token_count, width = queries.shape
    targets = lax.axis_size("shard") * lax.axis_size("sub")
    passages, slots = token_codes.shape
    half = lax.axis_index("sub").astype(jnp.int32)
    me = lax.axis_index("shard").astype(jnp.int32) * lax.axis_size("sub") + half
    half = half.reshape(1)
    me = me.reshape(1)
    flat = residuals.reshape(passages * slots, width)
    other = lax.ppermute(centroids, "sub", [(0, 1), (1, 0)])

    held = queries.reshape(1, 1, local_queries * token_count, width)
    bits = targets.bit_length() - 1
    carried = None
    rounds = [(bits - WIDE_BITS, WIDE_BITS)] + [(k, 1) for k in range(bits - WIDE_BITS - 1, -1, -1)]
    for turn, (first, taken) in enumerate(rounds):
        received = []
        for value in range(1, 1 << taken):
            pairs = [(device, device ^ (value << first)) for device in range(targets)]
            received.append(lax.ppermute(held, ("shard", "sub"), pairs))
        if turn == 0:
            ready = prepare(me, lengths, token_codes, centroids, flat)
            own, near, codes, starts, cleans, nothing = ready
            table = None
        elif turn <= STEPS:
            table, carried, nothing = decode_step(
                turn - 1, half, own, other, codes, cleans, near, table, carried, held
            )
        received = [block + nothing[0:1, :] for block in received]
        held = jnp.concatenate([held] + received, axis=1)
        held = held.reshape((-1, 1) + held.shape[2:])
    shape = (token_count, local_queries)
    rows = held.reshape(targets * local_queries * token_count, width)
    scores = score_all(me, starts, rows, carried[0], passages, slots, shape)
    returned = lax.all_to_all(
        scores.reshape(targets, local_queries * passages),
        ("shard", "sub"),
        split_axis=0,
        concat_axis=0,
        tiled=True,
    )
    return pick(candidates, returned, passages)


def solution(mesh):
    placed = (
        P(("groups", "shard", "sub"), None, None),
        P(("groups", "shard", "sub"), None),
        P(("groups", "shard", "sub"), None),
        P(("groups", "shard", "sub"), None, None),
        P(("groups", "shard", "sub")),
        P(("groups", "shard", "sub"), None),
    )
    return jax.shard_map(
        body,
        mesh=mesh,
        in_specs=placed,
        out_specs=P(("groups", "shard", "sub"), None),
        check_vma=False,
    )
```

```python
import functools

import jax
import jax.numpy as jnp
from jax import lax
from jax.experimental import pallas as pl
from jax.experimental.pallas import tpu as pltpu
from jax.sharding import PartitionSpec as P

CHUNK = 16
GROUP = 16
SCORE_GROUP = 64
SCORE_PARTS = 2
SCORE_RUNS = (8, 4, 2, 1)
STEPS = 2
PIECES = 4
QUERY_BLOCK = 512
SMEM = pl.BlockSpec(memory_space=pltpu.SMEM)
VMEM = pl.BlockSpec(memory_space=pltpu.VMEM)
HBM = pl.BlockSpec(memory_space=pltpu.HBM)


def normalized(vectors):
    total = jnp.sum(vectors * vectors, axis=-1, keepdims=True)
    return (vectors * lax.rsqrt(total + 1e-06)).astype(jnp.bfloat16)


def thirds(values):
    parts = []
    for _ in range(3):
        parts.append(values.astype(jnp.bfloat16))
        values = values - parts[-1].astype(jnp.float32)
    return parts


def quotient(number, divisor):
    if divisor & (divisor - 1) == 0:
        return lax.shift_right_logical(number, divisor.bit_length() - 1)
    return lax.div(number, divisor)


def pinned(array, space=pltpu.HBM):
    return pltpu.with_memory_space_constraint(array, space)


def granted(mebibytes):
    return pltpu.CompilerParams(vmem_limit_bytes=mebibytes * 1024 * 1024)


def shares_of(passages):
    edges = [0, passages // 2]
    return tuple(zip(edges, edges[1:] + [passages]))


def prepare_kernel(
    me_ref,
    lengths_hbm,
    codes_hbm,
    own_hbm,
    residuals_hbm,
    staged,
    near,
    codes,
    starts,
    cleans,
    nothing,
    lengths_ref,
    starts_ref,
    cleans_ref,
    length_rows,
    drawn,
    residuals,
    sems,
):
    del me_ref
    passages, slots = codes_hbm.shape
    width = own_hbm.shape[1]
    lengths_copy = pltpu.make_async_copy(lengths_hbm, lengths_ref, sems.at[0])
    codes_copy = pltpu.make_async_copy(codes_hbm, drawn, sems.at[1])
    residual_copy = pltpu.make_async_copy(residuals_hbm, residuals, sems.at[2])
    own_copy = pltpu.make_async_copy(own_hbm, staged, sems.at[3])
    lengths_copy.start()
    codes_copy.start()
    residual_copy.start()
    own_copy.start()
    nothing[...] = jnp.zeros(nothing.shape, nothing.dtype)
    lengths_copy.wait()

    def listing(p, chunks):
        length = lengths_ref[p]
        length_rows[pl.ds(p, 1), :] = jnp.full((1, slots), length, jnp.int32)
        for k in range(slots // CHUNK):
            starts_ref[chunks + k] = p * slots + k * CHUNK
            cleans_ref[chunks + k] = p * slots + k * CHUNK
        return chunks + quotient(length + CHUNK - 1, CHUNK)

    last = starts_ref.shape[0] - 1
    chunks = jnp.int32(0)
    for step, (low, high) in enumerate(shares_of(passages)):
        chunks = lax.fori_loop(low, high, listing, chunks, unroll=4)
        for k in range(GROUP):
            starts_ref[chunks + k] = passages * slots
            cleans_ref[chunks + k] = low * slots
        chunks = quotient(chunks + GROUP - 1, GROUP) * GROUP
        cleans_ref[last - STEPS + step] = quotient(chunks, GROUP)
    for k in range(SCORE_GROUP):
        starts_ref[chunks + k] = passages * slots
    starts_ref[last] = chunks
    starts_copy = pltpu.make_async_copy(starts_ref, starts, sems.at[4])
    cleans_copy = pltpu.make_async_copy(cleans_ref, cleans, sems.at[5])
    starts_copy.start()
    cleans_copy.start()
    codes_copy.wait()
    lanes = lax.broadcasted_iota(jnp.int32, (passages, slots), 1)
    codes[...] = jnp.where(lanes < length_rows[...], drawn[...], drawn[:, 0:1])
    residual_copy.wait()
    slot_numbers = lax.broadcasted_iota(jnp.int32, (CHUNK, width), 0)

    def place(g, carry):
        for k in range(GROUP):
            at = cleans_ref[g * GROUP + k]
            p = quotient(at, slots)
            live = lengths_ref[p] - (at - p * slots)
            first = residuals[pl.ds(pl.multiple_of(p * slots, CHUNK), CHUNK), :]
            rows = residuals[pl.ds(pl.multiple_of(at, CHUNK), CHUNK), :].astype(jnp.float32)
            rows = jnp.where(slot_numbers < live, rows, first.astype(jnp.float32)[0:1, :])
            to = pl.multiple_of((g * GROUP + k) * CHUNK, CHUNK)
            near[pl.ds(to, CHUNK), :] = rows
        return carry

    lax.fori_loop(0, quotient(chunks, GROUP), place, 0)
    own_copy.wait()
    starts_copy.wait()
    cleans_copy.wait()


def list_size(passages, slots):
    most = passages * (slots // CHUNK) + STEPS * GROUP + SCORE_GROUP + STEPS + 1
    return -(-most // 128) * 128


def list_rows(passages, slots):
    rounding = SCORE_GROUP * CHUNK
    return -(-(passages * slots + STEPS * GROUP * CHUNK) // rounding) * rounding


def prepare(me, lengths, token_codes, own, residuals):
    width = own.shape[1]
    passages, slots = token_codes.shape
    most = list_size(passages, slots)
    return pl.pallas_call(
        prepare_kernel,
        out_shape=(
            pltpu.VMEM(own.shape, jnp.bfloat16),
            pltpu.VMEM((list_rows(passages, slots), width), jnp.float32),
            pltpu.VMEM(token_codes.shape, jnp.int32),
            pltpu.VMEM((most,), jnp.int32),
            pltpu.VMEM((most,), jnp.int32),
            pltpu.VMEM((16, width), jnp.bfloat16),
        ),
        in_specs=[SMEM, HBM, HBM, HBM, HBM],
        out_specs=(VMEM,) * 6,
        scratch_shapes=[
            pltpu.SMEM(lengths.shape, jnp.int32),
            pltpu.SMEM((most,), jnp.int32),
            pltpu.SMEM((most,), jnp.int32),
            pltpu.VMEM(token_codes.shape, jnp.int32),
            pltpu.VMEM(token_codes.shape, jnp.int32),
            pltpu.VMEM(residuals.shape, jnp.bfloat16),
            pltpu.SemaphoreType.DMA((6,)),
        ],
        compiler_params=granted(4),
        cost_estimate=pl.CostEstimate(flops=10**7, bytes_accessed=8 * 10**6, transcendentals=0),
        name="prepare",
    )(me, pinned(lengths), pinned(token_codes), pinned(own), pinned(residuals))


def decode_kernel(step, passages, *refs):
    if step == 0:
        half_ref, own_ref, other_ref, codes, cleans, near, _, table = refs[:8]
    else:
        codes, cleans, near, table = refs[:4]
    embedded, rows, nothing, codes_smem, cleans_ref, sems = refs[-6:]
    slots = codes.shape[1]
    width = rows.shape[1]
    codes_ref = codes_smem.reshape(passages * slots)
    moves = []
    first, after = shares_of(passages)[step]
    first_move, after_move = first // 8 * 8, min(-(-after // 8) * 8, passages)
    part = pl.ds(first_move, after_move - first_move)
    pairs = ((cleans, cleans_ref), (codes.at[part], codes_smem.at[part]))
    for k, (source, to) in enumerate(pairs):
        moves.append(pltpu.make_async_copy(source, to, sems.at[k]))
        moves[-1].start()
    nothing[...] = jnp.zeros(nothing.shape, nothing.dtype)
    if step == 0:
        half_rows = other_ref.shape[0]
        piece = half_rows // PIECES
        for source, base in ((own_ref, half_ref[0]), (other_ref, 1 - half_ref[0])):
            for k in range(PIECES):
                to = pl.ds(pl.multiple_of(base * half_rows + k * piece, piece), piece)
                table[to, :] = source[pl.ds(k * piece, piece), :].astype(jnp.float32)

    table_single = table.reshape(table.shape[0], 1, width)
    rows_single = rows.reshape(rows.shape[0], 1, width)

    def fetch(g):
        for k in range(GROUP):
            at = cleans_ref[g * GROUP + k]
            for j in range(CHUNK):
                rows_single[k * CHUNK + j] = table_single[codes_ref[at + j]]

    def finish(g):
        size = GROUP * CHUNK
        return normalized(rows[...] + near[pl.ds(pl.multiple_of(g * size, size), size), :])

    def keep(g, done):
        size = GROUP * CHUNK
        embedded[pl.ds(pl.multiple_of(g * size, size), size), :] = done

    for move in moves:
        move.wait()
    last = cleans_ref.shape[0] - 1
    low = cleans_ref[last - STEPS + step - 1] if step > 0 else 0
    high = cleans_ref[last - STEPS + step]
    def decode(g, carry):
        done = finish(g - 1)
        fetch(g)
        keep(g - 1, done)
        return carry

    if step == 0:
        fetch(low)
    lax.fori_loop(low + (step == 0), high, decode, 0)
    if step == STEPS - 1:
        keep(high - 1, finish(high - 1))


def decode_step(
    step, half, own, other, codes, cleans, near, table, carried, held
):
    passages, slots = codes.shape
    width = near.shape[1]
    space = near.shape
    inside = lambda array: pinned(array, pltpu.VMEM)
    shared = [inside(codes), inside(cleans), inside(near)]
    if step == 0:
        operands = [half, inside(own), inside(other)] + shared + [inside(held)]
        in_specs = [SMEM] + [VMEM] * 6
        whole = (2 * own.shape[0], width)
        out_shape = [pltpu.VMEM(whole, jnp.float32)]
        aliases = {}
    else:
        operands = shared + [inside(table), inside(held)] + [inside(array) for array in carried]
        in_specs = [VMEM] * 7
        out_shape = []
        aliases = {5: 0, 6: 1}
    out_shape.append(pltpu.VMEM(space, jnp.bfloat16))
    out_shape.append(pltpu.VMEM((GROUP * CHUNK, width), jnp.float32))
    out_shape.append(pltpu.VMEM((16, width), jnp.bfloat16))
    results = pl.pallas_call(
        functools.partial(decode_kernel, step, passages),
        out_shape=tuple(out_shape),
        in_specs=in_specs,
        out_specs=(VMEM,) * len(out_shape),
        input_output_aliases=aliases,
        scratch_shapes=[
            pltpu.SMEM(codes.shape, jnp.int32),
            pltpu.SMEM(cleans.shape, jnp.int32),
            pltpu.SemaphoreType.DMA((2,)),
        ],
        compiler_params=granted(4),
        cost_estimate=pl.CostEstimate(flops=10**7, bytes_accessed=10**7, transcendentals=0),
        name="decode",
    )(*operands)
    if step == 0:
        table, results = results[0], results[1:]
    return table, results[:2], results[2]


def score_kernel(
    bit,
    token_count,
    local_queries,
    slots,
    me_ref,
    starts,
    queries_ref,
    embedded,
    before_ref,
    out_ref,
    at_ref,
    turned,
    largest,
    sem,
):
    starts_copy = pltpu.make_async_copy(starts, at_ref, sem)
    starts_copy.start()
    passages = out_ref.shape[1]
    query_tokens = queries_ref.shape[0]
    block = min(QUERY_BLOCK, query_tokens)
    blocks = query_tokens // block
    window = 2 * block // token_count
    window_targets = window // local_queries
    near_me = me_ref[0] & (window_targets - 1)
    far_me = quotient(me_ref[0], window_targets)
    owner = lax.broadcasted_iota(jnp.int32, (window, block), 0)
    owner_target = quotient(owner, local_queries)
    owner_row = (owner_target ^ near_me) * local_queries + owner - owner_target * local_queries
    query_of = quotient(lax.broadcasted_iota(jnp.int32, (window, block), 1), token_count)
    target_of = quotient(query_of, local_queries)
    row_of = query_of + (target_of + bit) * local_queries
    summing = jnp.concatenate([(owner_row == row_of).astype(jnp.bfloat16)] * 3, axis=1)
    count = SCORE_GROUP // SCORE_PARTS
    size = count * CHUNK

    def score_block(b, carry):
        at = pl.ds(pl.multiple_of(b * block, block), block)
        vectors = normalized(queries_ref[at, :].astype(jnp.float32))
        turned[...] = vectors.astype(jnp.float32).T.astype(jnp.bfloat16)

        def score(first, so_far):
            at = pl.ds(pl.multiple_of(first * size, size), size)
            similar = jnp.dot(embedded[at, :], turned[...], preferred_element_type=jnp.float32)
            parts = jnp.max(similar.reshape(count, CHUNK // 8, 8, block), axis=1)
            for k in range(count):
                start = at_ref[first * count + k]
                p = quotient(start, slots)
                so_far = jnp.where(start == p * slots, parts[k], jnp.maximum(so_far, parts[k]))
                to = pl.multiple_of(p * 8, 8)
                for lane in range(block // 128):
                    largest[lane, pl.ds(to, 8), :] = so_far[:, lane * 128 : (lane + 1) * 128]
            return so_far

        @pl.when(b == 0)
        def arrived():
            starts_copy.wait()

        parts_used = quotient(at_ref[at_ref.shape[0] - 1] + count - 1, count)
        so_far = jnp.zeros((8, block), jnp.float32)
        done = jnp.int32(0)
        for run in SCORE_RUNS:

            def score_run(g, so_far, run=run, done=done):
                for part in range(run):
                    so_far = score(done + g * run + part, so_far)
                return so_far

            runs = quotient(parts_used - done, run)
            so_far = lax.fori_loop(0, runs, score_run, so_far)
            done = done + runs * run
        kept = []
        for lane in range(block // 128):
            best = largest[lane, pl.ds(0, passages, stride=8), :]
            for k in range(1, 8):
                best = jnp.maximum(best, largest[lane, pl.ds(k, passages, stride=8), :])
            kept.append(best)
        left = jnp.concatenate(kept, axis=1)
        to = pl.ds(pl.multiple_of((b ^ far_me) * window, window), window)
        sums = lax.dot_general(
            summing,
            jnp.concatenate(thirds(left), axis=1),
            (((1,), (1,)), ((), ())),
            preferred_element_type=jnp.float32,
        )
        if bit:
            sums = sums + before_ref[to, :]
        out_ref[to, :] = sums
        return carry

    lax.fori_loop(0, blocks, score_block, 0)


def score_half(bit, me, starts, query_rows, embedded, before, passages, slots, shape):
    token_count, local_queries = shape
    query_tokens, width = query_rows.shape
    block = min(QUERY_BLOCK, query_tokens)
    blocks = query_tokens // block
    return pl.pallas_call(
        functools.partial(score_kernel, bit, token_count, local_queries, slots),
        out_shape=pltpu.VMEM((2 * query_tokens // token_count, passages), jnp.float32),
        in_specs=[SMEM] + [VMEM] * 4,
        out_specs=VMEM,
        scratch_shapes=[
            pltpu.SMEM(starts.shape, jnp.int32),
            pltpu.VMEM((width, block), jnp.bfloat16),
            pltpu.VMEM((block // 128, (passages + 1) * 8, 128), jnp.float32),
            pltpu.SemaphoreType.DMA,
        ],
        compiler_params=granted(4),
        cost_estimate=pl.CostEstimate(flops=10**7, bytes_accessed=8 * 10**6, transcendentals=0),
        name="score",
    )(
        me,
        pinned(starts, pltpu.VMEM),
        pinned(query_rows, pltpu.VMEM),
        pinned(embedded, pltpu.VMEM),
        pinned(before, pltpu.VMEM),
    )


def pick_kernel(passages, candidates_ref, returned_ref, out_ref):
    local_queries, count = candidates_ref.shape
    targets = returned_ref.shape[0]
    passage_numbers = lax.broadcasted_iota(jnp.int32, (passages, count), 0)
    target_numbers = lax.broadcasted_iota(jnp.int32, (targets, count), 0)
    for q in range(local_queries):
        wanted = candidates_ref[q : q + 1, :]
        target = quotient(wanted, passages)
        hits = (passage_numbers == wanted - target * passages).astype(jnp.bfloat16)
        left = returned_ref[:, q * passages : (q + 1) * passages]
        picked = jnp.zeros((targets, count), jnp.float32)
        for part in thirds(left):
            picked = picked + jnp.dot(part, hits, preferred_element_type=jnp.float32)
        kept = jnp.where(target_numbers == target, picked, 0.0)
        out_ref[q : q + 1, :] = jnp.sum(kept, axis=0, keepdims=True)


def pick(candidates, returned, passages):
    return pl.pallas_call(
        functools.partial(pick_kernel, passages),
        out_shape=jax.ShapeDtypeStruct(candidates.shape, jnp.float32),
        in_specs=[VMEM, VMEM],
        out_specs=VMEM,
        compiler_params=granted(8),
        name="pick",
    )(candidates, pltpu.with_memory_space_constraint(returned, pltpu.VMEM))


def body(queries, candidates, token_codes, residuals, lengths, centroids):
    local_queries, token_count, width = queries.shape
    targets = lax.axis_size("shard") * lax.axis_size("sub")
    passages, slots = token_codes.shape
    half = lax.axis_index("sub").astype(jnp.int32)
    me = lax.axis_index("shard").astype(jnp.int32) * lax.axis_size("sub") + half
    half = half.reshape(1)
    me = me.reshape(1)
    flat = residuals.reshape(passages * slots, width)
    other = lax.ppermute(centroids, "sub", [(0, 1), (1, 0)])

    held = queries.reshape(1, 1, local_queries * token_count, width)
    bits = targets.bit_length() - 1
    carried = None
    for turn, first in enumerate(range(bits - 1, -1, -1)):
        pairs = [(device, device ^ (1 << first)) for device in range(targets)]
        received = lax.ppermute(held, ("shard", "sub"), pairs)
        if turn == 0:
            ready = prepare(me, lengths, token_codes, centroids, flat)
            own, near, codes, starts, cleans, nothing = ready
            table = None
        elif turn <= STEPS:
            table, carried, nothing = decode_step(
                turn - 1, half, own, other, codes, cleans, near, table, carried, held
            )
        if first > 0:
            received = received + nothing[0:1, :]
            held = jnp.concatenate([held, received], axis=1)
            held = held.reshape((-1, 1) + held.shape[2:])
    shape = (token_count, local_queries)
    scores = carried[1]
    for bit, half_rows in enumerate((held, received)):
        rows = half_rows.reshape(targets // 2 * local_queries * token_count, width)
        scores = score_half(bit, me, starts, rows, carried[0], scores, passages, slots, shape)
    returned = lax.all_to_all(
        scores.reshape(targets, local_queries * passages),
        ("shard", "sub"),
        split_axis=0,
        concat_axis=0,
        tiled=True,
    )
    return pick(candidates, returned, passages)


def solution(mesh):
    placed = (
        P(("groups", "shard", "sub"), None, None),
        P(("groups", "shard", "sub"), None),
        P(("groups", "shard", "sub"), None),
        P(("groups", "shard", "sub"), None, None),
        P(("groups", "shard", "sub")),
        P(("groups", "shard", "sub"), None),
    )
    return jax.shard_map(
        body,
        mesh=mesh,
        in_specs=placed,
        out_specs=P(("groups", "shard", "sub"), None),
        check_vma=False,
    )
```

```python
import functools

import jax
import jax.numpy as jnp
from jax import lax
from jax.experimental import pallas as pl
from jax.experimental.pallas import tpu as pltpu
from jax.sharding import PartitionSpec as P

CHUNK = 16
GROUP = 16
SCORE_GROUP = 64
PART = 32
SCORE_RUNS = (4, 2, 1)
STEPS = 2
PIECES = 4
QUERY_BLOCK = 512
SMEM = pl.BlockSpec(memory_space=pltpu.SMEM)
VMEM = pl.BlockSpec(memory_space=pltpu.VMEM)
HBM = pl.BlockSpec(memory_space=pltpu.HBM)


def normalized(vectors):
    total = jnp.sum(vectors * vectors, axis=-1, keepdims=True)
    return (vectors * lax.rsqrt(total + 1e-06)).astype(jnp.bfloat16)


def thirds(values):
    parts = []
    for _ in range(3):
        parts.append(values.astype(jnp.bfloat16))
        values = values - parts[-1].astype(jnp.float32)
    return parts


def quotient(number, divisor):
    if divisor & (divisor - 1) == 0:
        return lax.shift_right_logical(number, divisor.bit_length() - 1)
    return lax.div(number, divisor)


def pinned(array, space=pltpu.HBM):
    return pltpu.with_memory_space_constraint(array, space)


def granted(mebibytes):
    return pltpu.CompilerParams(vmem_limit_bytes=mebibytes * 1024 * 1024)


def shares_of(passages):
    edges = [0, passages // 2]
    return tuple(zip(edges, edges[1:] + [passages]))


def prepare_kernel(
    me_ref,
    lengths_hbm,
    codes_hbm,
    own_hbm,
    residuals_hbm,
    staged,
    near,
    codes,
    starts,
    cleans,
    nothing,
    lengths_ref,
    starts_ref,
    cleans_ref,
    length_rows,
    drawn,
    residuals,
    sems,
):
    del me_ref
    passages, slots = codes_hbm.shape
    width = own_hbm.shape[1]
    lengths_copy = pltpu.make_async_copy(lengths_hbm, lengths_ref, sems.at[0])
    codes_copy = pltpu.make_async_copy(codes_hbm, drawn, sems.at[1])
    residual_copy = pltpu.make_async_copy(residuals_hbm, residuals, sems.at[2])
    own_copy = pltpu.make_async_copy(own_hbm, staged, sems.at[3])
    lengths_copy.start()
    codes_copy.start()
    residual_copy.start()
    own_copy.start()
    nothing[...] = jnp.zeros(nothing.shape, nothing.dtype)
    lengths_copy.wait()

    def listing(p, chunks):
        length = lengths_ref[p]
        length_rows[pl.ds(p, 1), :] = jnp.full((1, slots), length, jnp.int32)
        for k in range(slots // CHUNK):
            starts_ref[chunks + k] = p * slots + k * CHUNK
            cleans_ref[chunks + k] = p * slots + k * CHUNK
        return chunks + quotient(length + CHUNK - 1, CHUNK)

    last = starts_ref.shape[0] - 1
    chunks = jnp.int32(0)
    for step, (low, high) in enumerate(shares_of(passages)):
        chunks = lax.fori_loop(low, high, listing, chunks, unroll=4)
        for k in range(PART):
            starts_ref[chunks + k] = passages * slots
            cleans_ref[chunks + k] = low * slots
        chunks = quotient(chunks + PART - 1, PART) * PART
        cleans_ref[last - STEPS + step] = quotient(chunks, GROUP)
        starts_ref[last - STEPS + step] = chunks
    starts_copy = pltpu.make_async_copy(starts_ref, starts, sems.at[4])
    cleans_copy = pltpu.make_async_copy(cleans_ref, cleans, sems.at[5])
    starts_copy.start()
    cleans_copy.start()
    codes_copy.wait()
    lanes = lax.broadcasted_iota(jnp.int32, (passages, slots), 1)
    codes[...] = jnp.where(lanes < length_rows[...], drawn[...], drawn[:, 0:1])
    residual_copy.wait()
    slot_numbers = lax.broadcasted_iota(jnp.int32, (CHUNK, width), 0)

    def place(g, carry):
        for k in range(GROUP):
            at = cleans_ref[g * GROUP + k]
            p = quotient(at, slots)
            live = lengths_ref[p] - (at - p * slots)
            first = residuals[pl.ds(pl.multiple_of(p * slots, CHUNK), CHUNK), :]
            rows = residuals[pl.ds(pl.multiple_of(at, CHUNK), CHUNK), :].astype(jnp.float32)
            rows = jnp.where(slot_numbers < live, rows, first.astype(jnp.float32)[0:1, :])
            to = pl.multiple_of((g * GROUP + k) * CHUNK, CHUNK)
            near[pl.ds(to, CHUNK), :] = rows
        return carry

    lax.fori_loop(0, quotient(chunks, GROUP), place, 0)
    own_copy.wait()
    starts_copy.wait()
    cleans_copy.wait()


def list_size(passages, slots):
    most = passages * (slots // CHUNK) + STEPS * PART + PART + STEPS + 1
    return -(-most // 128) * 128


def list_rows(passages, slots):
    rounding = SCORE_GROUP * CHUNK
    return -(-(passages * slots + STEPS * PART * CHUNK) // rounding) * rounding


def prepare(me, lengths, token_codes, own, residuals):
    width = own.shape[1]
    passages, slots = token_codes.shape
    most = list_size(passages, slots)
    return pl.pallas_call(
        prepare_kernel,
        out_shape=(
            pltpu.VMEM(own.shape, jnp.bfloat16),
            pltpu.VMEM((list_rows(passages, slots), width), jnp.float32),
            pltpu.VMEM(token_codes.shape, jnp.int32),
            pltpu.VMEM((most,), jnp.int32),
            pltpu.VMEM((most,), jnp.int32),
            pltpu.VMEM((16, width), jnp.bfloat16),
        ),
        in_specs=[SMEM, HBM, HBM, HBM, HBM],
        out_specs=(VMEM,) * 6,
        scratch_shapes=[
            pltpu.SMEM(lengths.shape, jnp.int32),
            pltpu.SMEM((most,), jnp.int32),
            pltpu.SMEM((most,), jnp.int32),
            pltpu.VMEM(token_codes.shape, jnp.int32),
            pltpu.VMEM(token_codes.shape, jnp.int32),
            pltpu.VMEM(residuals.shape, jnp.bfloat16),
            pltpu.SemaphoreType.DMA((6,)),
        ],
        compiler_params=granted(4),
        cost_estimate=pl.CostEstimate(flops=10**7, bytes_accessed=8 * 10**6, transcendentals=0),
        name="prepare",
    )(me, pinned(lengths), pinned(token_codes), pinned(own), pinned(residuals))


def decode_kernel(step, passages, *refs):
    if step == 0:
        half_ref, own_ref, other_ref, codes, cleans, near, _, table = refs[:8]
    else:
        codes, cleans, near, table = refs[:4]
    embedded, rows, nothing, codes_smem, cleans_ref, sems = refs[-6:]
    slots = codes.shape[1]
    width = rows.shape[1]
    codes_ref = codes_smem.reshape(passages * slots)
    moves = []
    first, after = shares_of(passages)[step]
    first_move, after_move = first // 8 * 8, min(-(-after // 8) * 8, passages)
    part = pl.ds(first_move, after_move - first_move)
    pairs = ((cleans, cleans_ref), (codes.at[part], codes_smem.at[part]))
    for k, (source, to) in enumerate(pairs):
        moves.append(pltpu.make_async_copy(source, to, sems.at[k]))
        moves[-1].start()
    nothing[...] = jnp.zeros(nothing.shape, nothing.dtype)
    if step == 0:
        half_rows = other_ref.shape[0]
        piece = half_rows // PIECES
        for source, base in ((own_ref, half_ref[0]), (other_ref, 1 - half_ref[0])):
            for k in range(PIECES):
                to = pl.ds(pl.multiple_of(base * half_rows + k * piece, piece), piece)
                table[to, :] = source[pl.ds(k * piece, piece), :].astype(jnp.float32)

    table_single = table.reshape(table.shape[0], 1, width)
    rows_single = rows.reshape(rows.shape[0], 1, width)

    def fetch(g):
        for k in range(GROUP):
            at = cleans_ref[g * GROUP + k]
            for j in range(CHUNK):
                rows_single[k * CHUNK + j] = table_single[codes_ref[at + j]]

    def finish(g):
        size = GROUP * CHUNK
        return normalized(rows[...] + near[pl.ds(pl.multiple_of(g * size, size), size), :])

    def keep(g, done):
        size = GROUP * CHUNK
        embedded[pl.ds(pl.multiple_of(g * size, size), size), :] = done

    for move in moves:
        move.wait()
    last = cleans_ref.shape[0] - 1
    low = cleans_ref[last - STEPS + step - 1] if step > 0 else 0
    high = cleans_ref[last - STEPS + step]
    def decode(g, carry):
        done = finish(g - 1)
        fetch(g)
        keep(g - 1, done)
        return carry

    if step == 0:
        fetch(low)
    lax.fori_loop(low + (step == 0), high, decode, 0)
    if step == STEPS - 1:
        keep(high - 1, finish(high - 1))


def decode_step(
    step, half, own, other, codes, cleans, near, table, carried, held
):
    passages, slots = codes.shape
    width = near.shape[1]
    space = near.shape
    inside = lambda array: pinned(array, pltpu.VMEM)
    shared = [inside(codes), inside(cleans), inside(near)]
    if step == 0:
        operands = [half, inside(own), inside(other)] + shared + [inside(held)]
        in_specs = [SMEM] + [VMEM] * 6
        whole = (2 * own.shape[0], width)
        out_shape = [pltpu.VMEM(whole, jnp.float32)]
        aliases = {}
    else:
        operands = shared + [inside(table), inside(held)] + [inside(array) for array in carried]
        in_specs = [VMEM] * 7
        out_shape = []
        aliases = {5: 0, 6: 1}
    out_shape.append(pltpu.VMEM(space, jnp.bfloat16))
    out_shape.append(pltpu.VMEM((GROUP * CHUNK, width), jnp.float32))
    out_shape.append(pltpu.VMEM((16, width), jnp.bfloat16))
    results = pl.pallas_call(
        functools.partial(decode_kernel, step, passages),
        out_shape=tuple(out_shape),
        in_specs=in_specs,
        out_specs=(VMEM,) * len(out_shape),
        input_output_aliases=aliases,
        scratch_shapes=[
            pltpu.SMEM(codes.shape, jnp.int32),
            pltpu.SMEM(cleans.shape, jnp.int32),
            pltpu.SemaphoreType.DMA((2,)),
        ],
        compiler_params=granted(4),
        cost_estimate=pl.CostEstimate(flops=10**7, bytes_accessed=10**7, transcendentals=0),
        name="decode",
    )(*operands)
    if step == 0:
        table, results = results[0], results[1:]
    return table, results[:2], results[2]


def score_kernel(
    bit,
    token_count,
    local_queries,
    slots,
    me_ref,
    starts,
    queries_ref,
    embedded,
    before_ref,
    out_ref,
    at_ref,
    turned,
    largest,
    sem,
):
    starts_copy = pltpu.make_async_copy(starts, at_ref, sem)
    starts_copy.start()
    passages = out_ref.shape[1]
    query_tokens = queries_ref.shape[0]
    block = min(QUERY_BLOCK, query_tokens)
    blocks = query_tokens // block
    window = 2 * block // token_count
    window_targets = window // local_queries
    near_me = me_ref[0] & (window_targets - 1)
    far_me = quotient(me_ref[0], window_targets)
    owner = lax.broadcasted_iota(jnp.int32, (window, block), 0)
    owner_target = quotient(owner, local_queries)
    owner_row = (owner_target ^ near_me) * local_queries + owner - owner_target * local_queries
    query_of = quotient(lax.broadcasted_iota(jnp.int32, (window, block), 1), token_count)
    target_of = quotient(query_of, local_queries)
    row_of = query_of + (target_of + bit) * local_queries
    summing = jnp.concatenate([(owner_row == row_of).astype(jnp.bfloat16)] * 3, axis=1)
    size = PART * CHUNK

    def score_block(b, carry):
        at = pl.ds(pl.multiple_of(b * block, block), block)
        vectors = normalized(queries_ref[at, :].astype(jnp.float32))
        turned[...] = vectors.astype(jnp.float32).T.astype(jnp.bfloat16)

        def score(first, so_far):
            at = pl.ds(pl.multiple_of(first * size, size), size)
            similar = jnp.dot(embedded[at, :], turned[...], preferred_element_type=jnp.float32)
            parts = jnp.max(similar.reshape(PART, CHUNK // 8, 8, block), axis=1)
            for k in range(PART):
                start = at_ref[first * PART + k]
                p = quotient(start, slots)
                so_far = jnp.where(start == p * slots, parts[k], jnp.maximum(so_far, parts[k]))
                to = pl.multiple_of(p * 8, 8)
                for lane in range(block // 128):
                    largest[lane, pl.ds(to, 8), :] = so_far[:, lane * 128 : (lane + 1) * 128]
            return so_far

        @pl.when(b == 0)
        def arrived():
            starts_copy.wait()

        last = at_ref.shape[0] - 1
        edge = quotient(at_ref[last - STEPS], PART)
        after = quotient(at_ref[last - STEPS + 1], PART)
        common = jnp.minimum(edge, after - edge)
        chains = (jnp.zeros((8, block), jnp.float32),) * 2
        done = jnp.int32(0)
        for run in SCORE_RUNS:

            def score_run(g, chains, run=run, done=done):
                first, second = chains
                for part in range(run):
                    i = done + g * run + part
                    first = score(i, first)
                    second = score(edge + i, second)
                return first, second

            runs = quotient(common - done, run)
            chains = lax.fori_loop(0, runs, score_run, chains)
            done = done + runs * run
        lax.fori_loop(common, edge, score, chains[0])
        lax.fori_loop(edge + common, after, score, chains[1])
        kept = []
        for lane in range(block // 128):
            best = largest[lane, pl.ds(0, passages, stride=8), :]
            for k in range(1, 8):
                best = jnp.maximum(best, largest[lane, pl.ds(k, passages, stride=8), :])
            kept.append(best)
        left = jnp.concatenate(kept, axis=1)
        to = pl.ds(pl.multiple_of((b ^ far_me) * window, window), window)
        sums = lax.dot_general(
            summing,
            jnp.concatenate(thirds(left), axis=1),
            (((1,), (1,)), ((), ())),
            preferred_element_type=jnp.float32,
        )
        if bit:
            sums = sums + before_ref[to, :]
        out_ref[to, :] = sums
        return carry

    lax.fori_loop(0, blocks, score_block, 0)


def score_half(bit, me, starts, query_rows, embedded, before, passages, slots, shape):
    token_count, local_queries = shape
    query_tokens, width = query_rows.shape
    block = min(QUERY_BLOCK, query_tokens)
    blocks = query_tokens // block
    return pl.pallas_call(
        functools.partial(score_kernel, bit, token_count, local_queries, slots),
        out_shape=pltpu.VMEM((2 * query_tokens // token_count, passages), jnp.float32),
        in_specs=[SMEM] + [VMEM] * 4,
        out_specs=VMEM,
        scratch_shapes=[
            pltpu.SMEM(starts.shape, jnp.int32),
            pltpu.VMEM((width, block), jnp.bfloat16),
            pltpu.VMEM((block // 128, (passages + 1) * 8, 128), jnp.float32),
            pltpu.SemaphoreType.DMA,
        ],
        compiler_params=granted(4),
        cost_estimate=pl.CostEstimate(flops=10**7, bytes_accessed=8 * 10**6, transcendentals=0),
        name="score",
    )(
        me,
        pinned(starts, pltpu.VMEM),
        pinned(query_rows, pltpu.VMEM),
        pinned(embedded, pltpu.VMEM),
        pinned(before, pltpu.VMEM),
    )


def pick_kernel(passages, candidates_ref, returned_ref, out_ref):
    local_queries, count = candidates_ref.shape
    targets = returned_ref.shape[0]
    passage_numbers = lax.broadcasted_iota(jnp.int32, (passages, count), 0)
    target_numbers = lax.broadcasted_iota(jnp.int32, (targets, count), 0)
    for q in range(local_queries):
        wanted = candidates_ref[q : q + 1, :]
        target = quotient(wanted, passages)
        hits = (passage_numbers == wanted - target * passages).astype(jnp.bfloat16)
        left = returned_ref[:, q * passages : (q + 1) * passages]
        picked = jnp.zeros((targets, count), jnp.float32)
        for part in thirds(left):
            picked = picked + jnp.dot(part, hits, preferred_element_type=jnp.float32)
        kept = jnp.where(target_numbers == target, picked, 0.0)
        out_ref[q : q + 1, :] = jnp.sum(kept, axis=0, keepdims=True)


def pick(candidates, returned, passages):
    return pl.pallas_call(
        functools.partial(pick_kernel, passages),
        out_shape=jax.ShapeDtypeStruct(candidates.shape, jnp.float32),
        in_specs=[VMEM, VMEM],
        out_specs=VMEM,
        compiler_params=granted(8),
        name="pick",
    )(candidates, pltpu.with_memory_space_constraint(returned, pltpu.VMEM))


def body(queries, candidates, token_codes, residuals, lengths, centroids):
    local_queries, token_count, width = queries.shape
    targets = lax.axis_size("shard") * lax.axis_size("sub")
    passages, slots = token_codes.shape
    half = lax.axis_index("sub").astype(jnp.int32)
    me = lax.axis_index("shard").astype(jnp.int32) * lax.axis_size("sub") + half
    half = half.reshape(1)
    me = me.reshape(1)
    flat = residuals.reshape(passages * slots, width)
    other = lax.ppermute(centroids, "sub", [(0, 1), (1, 0)])

    held = queries.reshape(1, 1, local_queries * token_count, width)
    bits = targets.bit_length() - 1
    carried = None
    for turn, first in enumerate(range(bits - 1, -1, -1)):
        pairs = [(device, device ^ (1 << first)) for device in range(targets)]
        received = lax.ppermute(held, ("shard", "sub"), pairs)
        if turn == 0:
            ready = prepare(me, lengths, token_codes, centroids, flat)
            own, near, codes, starts, cleans, nothing = ready
            table = None
        elif turn <= STEPS:
            table, carried, nothing = decode_step(
                turn - 1, half, own, other, codes, cleans, near, table, carried, held
            )
        if first > 0:
            received = received + nothing[0:1, :]
            held = jnp.concatenate([held, received], axis=1)
            held = held.reshape((-1, 1) + held.shape[2:])
    shape = (token_count, local_queries)
    scores = carried[1]
    for bit, half_rows in enumerate((held, received)):
        rows = half_rows.reshape(targets // 2 * local_queries * token_count, width)
        scores = score_half(bit, me, starts, rows, carried[0], scores, passages, slots, shape)
    returned = lax.all_to_all(
        scores.reshape(targets, local_queries * passages),
        ("shard", "sub"),
        split_axis=0,
        concat_axis=0,
        tiled=True,
    )
    return pick(candidates, returned, passages)


def solution(mesh):
    placed = (
        P(("groups", "shard", "sub"), None, None),
        P(("groups", "shard", "sub"), None),
        P(("groups", "shard", "sub"), None),
        P(("groups", "shard", "sub"), None, None),
        P(("groups", "shard", "sub")),
        P(("groups", "shard", "sub"), None),
    )
    return jax.shard_map(
        body,
        mesh=mesh,
        in_specs=placed,
        out_specs=P(("groups", "shard", "sub"), None),
        check_vma=False,
    )
```

```python
import functools

import jax
import jax.numpy as jnp
from jax import lax
from jax.experimental import pallas as pl
from jax.experimental.pallas import tpu as pltpu
from jax.sharding import PartitionSpec as P

CHUNK = 16
GROUP = 32
SCORE_GROUP = 64
PART = 32
SCORE_RUNS = (4, 2, 1)
STEPS = 2
PIECES = 4
QUERY_BLOCK = 512
SMEM = pl.BlockSpec(memory_space=pltpu.SMEM)
VMEM = pl.BlockSpec(memory_space=pltpu.VMEM)
HBM = pl.BlockSpec(memory_space=pltpu.HBM)


def normalized(vectors):
    total = jnp.sum(vectors * vectors, axis=-1, keepdims=True)
    return (vectors * lax.rsqrt(total + 1e-06)).astype(jnp.bfloat16)


def thirds(values):
    parts = []
    for _ in range(3):
        parts.append(values.astype(jnp.bfloat16))
        values = values - parts[-1].astype(jnp.float32)
    return parts


def quotient(number, divisor):
    if divisor & (divisor - 1) == 0:
        return lax.shift_right_logical(number, divisor.bit_length() - 1)
    return lax.div(number, divisor)


def pinned(array, space=pltpu.HBM):
    return pltpu.with_memory_space_constraint(array, space)


def granted(mebibytes):
    return pltpu.CompilerParams(vmem_limit_bytes=mebibytes * 1024 * 1024)


def shares_of(passages):
    edges = [0, passages // 2]
    return tuple(zip(edges, edges[1:] + [passages]))


def prepare_kernel(
    me_ref,
    lengths_hbm,
    codes_hbm,
    own_hbm,
    residuals_hbm,
    staged,
    near,
    codes,
    starts,
    cleans,
    nothing,
    lengths_ref,
    starts_ref,
    cleans_ref,
    length_rows,
    drawn,
    residuals,
    sems,
):
    del me_ref
    passages, slots = codes_hbm.shape
    width = own_hbm.shape[1]
    lengths_copy = pltpu.make_async_copy(lengths_hbm, lengths_ref, sems.at[0])
    codes_copy = pltpu.make_async_copy(codes_hbm, drawn, sems.at[1])
    residual_copy = pltpu.make_async_copy(residuals_hbm, residuals, sems.at[2])
    own_copy = pltpu.make_async_copy(own_hbm, staged, sems.at[3])
    lengths_copy.start()
    codes_copy.start()
    residual_copy.start()
    own_copy.start()
    nothing[...] = jnp.zeros(nothing.shape, nothing.dtype)
    lengths_copy.wait()

    def listing(p, chunks):
        length = lengths_ref[p]
        length_rows[pl.ds(p, 1), :] = jnp.full((1, slots), length, jnp.int32)
        for k in range(slots // CHUNK):
            starts_ref[chunks + k] = p * slots + k * CHUNK
            cleans_ref[chunks + k] = p * slots + k * CHUNK
        return chunks + quotient(length + CHUNK - 1, CHUNK)

    last = starts_ref.shape[0] - 1
    chunks = jnp.int32(0)
    for step, (low, high) in enumerate(shares_of(passages)):
        chunks = lax.fori_loop(low, high, listing, chunks, unroll=4)
        for k in range(PART):
            starts_ref[chunks + k] = passages * slots
            cleans_ref[chunks + k] = low * slots
        chunks = quotient(chunks + PART - 1, PART) * PART
        cleans_ref[last - STEPS + step] = quotient(chunks, GROUP)
        starts_ref[last - STEPS + step] = chunks
    starts_copy = pltpu.make_async_copy(starts_ref, starts, sems.at[4])
    cleans_copy = pltpu.make_async_copy(cleans_ref, cleans, sems.at[5])
    starts_copy.start()
    cleans_copy.start()
    codes_copy.wait()
    lanes = lax.broadcasted_iota(jnp.int32, (passages, slots), 1)
    codes[...] = jnp.where(lanes < length_rows[...], drawn[...], drawn[:, 0:1])
    residual_copy.wait()
    slot_numbers = lax.broadcasted_iota(jnp.int32, (CHUNK, width), 0)

    def place(g, carry):
        for k in range(GROUP):
            at = cleans_ref[g * GROUP + k]
            p = quotient(at, slots)
            live = lengths_ref[p] - (at - p * slots)
            first = residuals[pl.ds(pl.multiple_of(p * slots, CHUNK), CHUNK), :]
            rows = residuals[pl.ds(pl.multiple_of(at, CHUNK), CHUNK), :].astype(jnp.float32)
            rows = jnp.where(slot_numbers < live, rows, first.astype(jnp.float32)[0:1, :])
            to = pl.multiple_of((g * GROUP + k) * CHUNK, CHUNK)
            near[pl.ds(to, CHUNK), :] = rows
        return carry

    lax.fori_loop(0, quotient(chunks, GROUP), place, 0)
    own_copy.wait()
    starts_copy.wait()
    cleans_copy.wait()


def list_size(passages, slots):
    most = passages * (slots // CHUNK) + STEPS * PART + PART + STEPS + 1
    return -(-most // 128) * 128


def list_rows(passages, slots):
    rounding = SCORE_GROUP * CHUNK
    return -(-(passages * slots + STEPS * PART * CHUNK) // rounding) * rounding


def prepare(me, lengths, token_codes, own, residuals):
    width = own.shape[1]
    passages, slots = token_codes.shape
    most = list_size(passages, slots)
    return pl.pallas_call(
        prepare_kernel,
        out_shape=(
            pltpu.VMEM(own.shape, jnp.bfloat16),
            pltpu.VMEM((list_rows(passages, slots), width), jnp.float32),
            pltpu.VMEM(token_codes.shape, jnp.int32),
            pltpu.VMEM((most,), jnp.int32),
            pltpu.VMEM((most,), jnp.int32),
            pltpu.VMEM((16, width), jnp.bfloat16),
        ),
        in_specs=[SMEM, HBM, HBM, HBM, HBM],
        out_specs=(VMEM,) * 6,
        scratch_shapes=[
            pltpu.SMEM(lengths.shape, jnp.int32),
            pltpu.SMEM((most,), jnp.int32),
            pltpu.SMEM((most,), jnp.int32),
            pltpu.VMEM(token_codes.shape, jnp.int32),
            pltpu.VMEM(token_codes.shape, jnp.int32),
            pltpu.VMEM(residuals.shape, jnp.bfloat16),
            pltpu.SemaphoreType.DMA((6,)),
        ],
        compiler_params=granted(4),
        cost_estimate=pl.CostEstimate(flops=10**7, bytes_accessed=8 * 10**6, transcendentals=0),
        name="prepare",
    )(me, pinned(lengths), pinned(token_codes), pinned(own), pinned(residuals))


def decode_kernel(step, passages, *refs):
    if step == 0:
        half_ref, own_ref, other_ref, codes, cleans, near, _, table = refs[:8]
    else:
        codes, cleans, near, table = refs[:4]
    embedded, rows, nothing, codes_smem, cleans_ref, sems = refs[-6:]
    slots = codes.shape[1]
    width = rows.shape[1]
    codes_ref = codes_smem.reshape(passages * slots)
    moves = []
    first, after = shares_of(passages)[step]
    first_move, after_move = first // 8 * 8, min(-(-after // 8) * 8, passages)
    part = pl.ds(first_move, after_move - first_move)
    pairs = ((cleans, cleans_ref), (codes.at[part], codes_smem.at[part]))
    for k, (source, to) in enumerate(pairs):
        moves.append(pltpu.make_async_copy(source, to, sems.at[k]))
        moves[-1].start()
    nothing[...] = jnp.zeros(nothing.shape, nothing.dtype)
    if step == 0:
        half_rows = other_ref.shape[0]
        piece = half_rows // PIECES
        for source, base in ((own_ref, half_ref[0]), (other_ref, 1 - half_ref[0])):
            for k in range(PIECES):
                to = pl.ds(pl.multiple_of(base * half_rows + k * piece, piece), piece)
                table[to, :] = source[pl.ds(k * piece, piece), :].astype(jnp.float32)

    table_single = table.reshape(table.shape[0], 1, width)
    rows_single = rows.reshape(rows.shape[0], 1, width)

    def fetch(g):
        for k in range(GROUP):
            at = cleans_ref[g * GROUP + k]
            for j in range(CHUNK):
                rows_single[k * CHUNK + j] = table_single[codes_ref[at + j]]

    def finish(g):
        size = GROUP * CHUNK
        return normalized(rows[...] + near[pl.ds(pl.multiple_of(g * size, size), size), :])

    def keep(g, done):
        size = GROUP * CHUNK
        embedded[pl.ds(pl.multiple_of(g * size, size), size), :] = done

    for move in moves:
        move.wait()
    last = cleans_ref.shape[0] - 1
    low = cleans_ref[last - STEPS + step - 1] if step > 0 else 0
    high = cleans_ref[last - STEPS + step]
    def decode(g, carry):
        done = finish(g - 1)
        fetch(g)
        keep(g - 1, done)
        return carry

    if step == 0:
        fetch(low)
    lax.fori_loop(low + (step == 0), high, decode, 0)
    if step == STEPS - 1:
        keep(high - 1, finish(high - 1))


def decode_step(
    step, half, own, other, codes, cleans, near, table, carried, held
):
    passages, slots = codes.shape
    width = near.shape[1]
    space = near.shape
    inside = lambda array: pinned(array, pltpu.VMEM)
    shared = [inside(codes), inside(cleans), inside(near)]
    if step == 0:
        operands = [half, inside(own), inside(other)] + shared + [inside(held)]
        in_specs = [SMEM] + [VMEM] * 6
        whole = (2 * own.shape[0], width)
        out_shape = [pltpu.VMEM(whole, jnp.float32)]
        aliases = {}
    else:
        operands = shared + [inside(table), inside(held)] + [inside(array) for array in carried]
        in_specs = [VMEM] * 7
        out_shape = []
        aliases = {5: 0, 6: 1}
    out_shape.append(pltpu.VMEM(space, jnp.bfloat16))
    out_shape.append(pltpu.VMEM((GROUP * CHUNK, width), jnp.float32))
    out_shape.append(pltpu.VMEM((16, width), jnp.bfloat16))
    results = pl.pallas_call(
        functools.partial(decode_kernel, step, passages),
        out_shape=tuple(out_shape),
        in_specs=in_specs,
        out_specs=(VMEM,) * len(out_shape),
        input_output_aliases=aliases,
        scratch_shapes=[
            pltpu.SMEM(codes.shape, jnp.int32),
            pltpu.SMEM(cleans.shape, jnp.int32),
            pltpu.SemaphoreType.DMA((2,)),
        ],
        compiler_params=granted(4),
        cost_estimate=pl.CostEstimate(flops=10**7, bytes_accessed=10**7, transcendentals=0),
        name="decode",
    )(*operands)
    if step == 0:
        table, results = results[0], results[1:]
    return table, results[:2], results[2]


def score_kernel(
    bit,
    token_count,
    local_queries,
    slots,
    me_ref,
    starts,
    queries_ref,
    embedded,
    before_ref,
    out_ref,
    at_ref,
    turned,
    largest,
    sem,
):
    starts_copy = pltpu.make_async_copy(starts, at_ref, sem)
    starts_copy.start()
    passages = out_ref.shape[1]
    query_tokens = queries_ref.shape[0]
    block = min(QUERY_BLOCK, query_tokens)
    blocks = query_tokens // block
    window = 2 * block // token_count
    window_targets = window // local_queries
    near_me = me_ref[0] & (window_targets - 1)
    far_me = quotient(me_ref[0], window_targets)
    owner = lax.broadcasted_iota(jnp.int32, (window, block), 0)
    owner_target = quotient(owner, local_queries)
    owner_row = (owner_target ^ near_me) * local_queries + owner - owner_target * local_queries
    query_of = quotient(lax.broadcasted_iota(jnp.int32, (window, block), 1), token_count)
    target_of = quotient(query_of, local_queries)
    row_of = query_of + (target_of + bit) * local_queries
    summing = jnp.concatenate([(owner_row == row_of).astype(jnp.bfloat16)] * 3, axis=1)
    size = PART * CHUNK

    def score_block(b, carry):
        at = pl.ds(pl.multiple_of(b * block, block), block)
        vectors = normalized(queries_ref[at, :].astype(jnp.float32))
        turned[...] = vectors.astype(jnp.float32).T.astype(jnp.bfloat16)

        def score(first, so_far):
            at = pl.ds(pl.multiple_of(first * size, size), size)
            similar = jnp.dot(embedded[at, :], turned[...], preferred_element_type=jnp.float32)
            parts = jnp.max(similar.reshape(PART, CHUNK // 8, 8, block), axis=1)
            for k in range(PART):
                start = at_ref[first * PART + k]
                p = quotient(start, slots)
                so_far = jnp.where(start == p * slots, parts[k], jnp.maximum(so_far, parts[k]))
                to = pl.multiple_of(p * 8, 8)
                for lane in range(block // 128):
                    largest[lane, pl.ds(to, 8), :] = so_far[:, lane * 128 : (lane + 1) * 128]
            return so_far

        @pl.when(b == 0)
        def arrived():
            starts_copy.wait()

        last = at_ref.shape[0] - 1
        edge = quotient(at_ref[last - STEPS], PART)
        after = quotient(at_ref[last - STEPS + 1], PART)
        common = jnp.minimum(edge, after - edge)
        chains = (jnp.zeros((8, block), jnp.float32),) * 2
        done = jnp.int32(0)
        for run in SCORE_RUNS:

            def score_run(g, chains, run=run, done=done):
                first, second = chains
                for part in range(run):
                    i = done + g * run + part
                    first = score(i, first)
                    second = score(edge + i, second)
                return first, second

            runs = quotient(common - done, run)
            chains = lax.fori_loop(0, runs, score_run, chains)
            done = done + runs * run
        lax.fori_loop(common, edge, score, chains[0])
        lax.fori_loop(edge + common, after, score, chains[1])
        kept = []
        for lane in range(block // 128):
            best = largest[lane, pl.ds(0, passages, stride=8), :]
            for k in range(1, 8):
                best = jnp.maximum(best, largest[lane, pl.ds(k, passages, stride=8), :])
            kept.append(best)
        left = jnp.concatenate(kept, axis=1)
        to = pl.ds(pl.multiple_of((b ^ far_me) * window, window), window)
        sums = lax.dot_general(
            summing,
            jnp.concatenate(thirds(left), axis=1),
            (((1,), (1,)), ((), ())),
            preferred_element_type=jnp.float32,
        )
        if bit:
            sums = sums + before_ref[to, :]
        out_ref[to, :] = sums
        return carry

    lax.fori_loop(0, blocks, score_block, 0)


def score_half(bit, me, starts, query_rows, embedded, before, passages, slots, shape):
    token_count, local_queries = shape
    query_tokens, width = query_rows.shape
    block = min(QUERY_BLOCK, query_tokens)
    blocks = query_tokens // block
    return pl.pallas_call(
        functools.partial(score_kernel, bit, token_count, local_queries, slots),
        out_shape=pltpu.VMEM((2 * query_tokens // token_count, passages), jnp.float32),
        in_specs=[SMEM] + [VMEM] * 4,
        out_specs=VMEM,
        scratch_shapes=[
            pltpu.SMEM(starts.shape, jnp.int32),
            pltpu.VMEM((width, block), jnp.bfloat16),
            pltpu.VMEM((block // 128, (passages + 1) * 8, 128), jnp.float32),
            pltpu.SemaphoreType.DMA,
        ],
        compiler_params=granted(4),
        cost_estimate=pl.CostEstimate(flops=10**7, bytes_accessed=8 * 10**6, transcendentals=0),
        name="score",
    )(
        me,
        pinned(starts, pltpu.VMEM),
        pinned(query_rows, pltpu.VMEM),
        pinned(embedded, pltpu.VMEM),
        pinned(before, pltpu.VMEM),
    )


def pick_kernel(passages, candidates_ref, returned_ref, out_ref):
    local_queries, count = candidates_ref.shape
    targets = returned_ref.shape[0]
    passage_numbers = lax.broadcasted_iota(jnp.int32, (passages, count), 0)
    target_numbers = lax.broadcasted_iota(jnp.int32, (targets, count), 0)
    for q in range(local_queries):
        wanted = candidates_ref[q : q + 1, :]
        target = quotient(wanted, passages)
        hits = (passage_numbers == wanted - target * passages).astype(jnp.bfloat16)
        left = returned_ref[:, q * passages : (q + 1) * passages]
        picked = jnp.zeros((targets, count), jnp.float32)
        for part in thirds(left):
            picked = picked + jnp.dot(part, hits, preferred_element_type=jnp.float32)
        kept = jnp.where(target_numbers == target, picked, 0.0)
        out_ref[q : q + 1, :] = jnp.sum(kept, axis=0, keepdims=True)


def pick(candidates, returned, passages):
    return pl.pallas_call(
        functools.partial(pick_kernel, passages),
        out_shape=jax.ShapeDtypeStruct(candidates.shape, jnp.float32),
        in_specs=[VMEM, VMEM],
        out_specs=VMEM,
        compiler_params=granted(8),
        name="pick",
    )(candidates, pltpu.with_memory_space_constraint(returned, pltpu.VMEM))


def body(queries, candidates, token_codes, residuals, lengths, centroids):
    local_queries, token_count, width = queries.shape
    targets = lax.axis_size("shard") * lax.axis_size("sub")
    passages, slots = token_codes.shape
    half = lax.axis_index("sub").astype(jnp.int32)
    me = lax.axis_index("shard").astype(jnp.int32) * lax.axis_size("sub") + half
    half = half.reshape(1)
    me = me.reshape(1)
    flat = residuals.reshape(passages * slots, width)
    other = lax.ppermute(centroids, "sub", [(0, 1), (1, 0)])

    held = queries.reshape(1, 1, local_queries * token_count, width)
    bits = targets.bit_length() - 1
    carried = None
    for turn, first in enumerate(range(bits - 1, -1, -1)):
        pairs = [(device, device ^ (1 << first)) for device in range(targets)]
        received = lax.ppermute(held, ("shard", "sub"), pairs)
        if turn == 0:
            ready = prepare(me, lengths, token_codes, centroids, flat)
            own, near, codes, starts, cleans, nothing = ready
            table = None
        elif turn <= STEPS:
            table, carried, nothing = decode_step(
                turn - 1, half, own, other, codes, cleans, near, table, carried, held
            )
        if first > 0:
            received = received + nothing[0:1, :]
            held = jnp.concatenate([held, received], axis=1)
            held = held.reshape((-1, 1) + held.shape[2:])
    shape = (token_count, local_queries)
    scores = carried[1]
    for bit, half_rows in enumerate((held, received)):
        rows = half_rows.reshape(targets // 2 * local_queries * token_count, width)
        scores = score_half(bit, me, starts, rows, carried[0], scores, passages, slots, shape)
    returned = lax.all_to_all(
        scores.reshape(targets, local_queries * passages),
        ("shard", "sub"),
        split_axis=0,
        concat_axis=0,
        tiled=True,
    )
    return pick(candidates, returned, passages)


def solution(mesh):
    placed = (
        P(("groups", "shard", "sub"), None, None),
        P(("groups", "shard", "sub"), None),
        P(("groups", "shard", "sub"), None),
        P(("groups", "shard", "sub"), None, None),
        P(("groups", "shard", "sub")),
        P(("groups", "shard", "sub"), None),
    )
    return jax.shard_map(
        body,
        mesh=mesh,
        in_specs=placed,
        out_specs=P(("groups", "shard", "sub"), None),
        check_vma=False,
    )
```
